32 devices in a mesh: ctx: 4 (over z), tp: 4 (over y, x), fsdp: 2 (over core).
Axes of the slice: x: 2, y: 2, z: 4, core: 2. Of those that a mesh axis runs over, the one named last changes fastest.
Arguments:
- tokens: bfloat16 [2, 4096, 2048], P('fsdp', 'ctx'), may hold values from -6 to 6
- query_weight: bfloat16 [2048, 2048], P('fsdp', 'tp'), may hold values from -0.125 to 0.125
- key_weight: bfloat16 [2048, 2048], P('fsdp', 'tp'), may hold values from -0.125 to 0.125
- value_weight: bfloat16 [2048, 2048], P('fsdp', 'tp'), may hold values from -0.125 to 0.125
- gate_weight: bfloat16 [2048, 2048], P('fsdp', 'tp'), may hold values from -0.125 to 0.125
- out_weight: bfloat16 [2048, 2048], P('tp', 'fsdp'), may hold values from -0.125 to 0.125
- log_decay: float32 [2, 4096, 8], P('fsdp', 'ctx', 'tp'), may hold values from -1 to 0
Outputs:
- mixed: bfloat16 [2, 4096, 2048], P('fsdp', 'ctx', 'tp')
The draws below stay inside these ranges and needn't reach their ends.
All inputs are finite; a program needn't handle non-finite values.
Results may differ from the reference program's by a relative error of at most 0.013.
Values may be sent and summed in bfloat16 or wider, within the bound.
No kernel may reach another device: no remote copies, remote signals or barrier semaphores. Data moves between devices by JAX's collectives and lax.ppermute only.
A program may use at most 128 MiB of HBM per device.

```python
import jax
import jax.numpy as jnp
from jax import lax

D = 2048
RETENTION_HEADS = 8
DH = 256
BLOCK = 512
TOK_DEV = 1024
SEQUENCE_COUNT = 2
SEQUENCE_LENGTH = 4096


def draw_log_decay(key, part):
    head_order = jax.random.permutation(jax.random.fold_in(key, 11), RETENTION_HEADS)
    fast_count = RETENTION_HEADS // 2
    fast_heads = head_order < fast_count
    fast_rate = jnp.exp(jax.random.uniform(jax.random.fold_in(key, 12), (RETENTION_HEADS,), jnp.float32, jnp.log(1.0 / 50.0), jnp.log(1.0 / 30.0)))
    slow_low = jnp.log(jnp.float32(0.05) / SEQUENCE_LENGTH)
    slow_high = jnp.log(jnp.float32(0.25) / SEQUENCE_LENGTH)
    slow_rate = jnp.exp(jax.random.uniform(jax.random.fold_in(key, 13), (RETENTION_HEADS,), jnp.float32, slow_low, slow_high))
    baseline_rate = jnp.where(fast_heads, fast_rate, slow_rate)
    device_multiplier = jnp.exp(jax.random.uniform(jax.random.fold_in(key, 14), (SEQUENCE_COUNT, SEQUENCE_LENGTH // TOK_DEV, 1, RETENTION_HEADS), jnp.float32, jnp.log(0.5), jnp.log(2.0)))
    device_multiplier = jnp.repeat(device_multiplier, TOK_DEV, axis=2).reshape(SEQUENCE_COUNT, SEQUENCE_LENGTH, RETENTION_HEADS)
    token_multiplier = jax.random.uniform(jax.random.fold_in(key, 15), (SEQUENCE_COUNT, SEQUENCE_LENGTH, RETENTION_HEADS), jnp.float32, 0.5, 1.5)
    spike_first_index = jax.random.randint(jax.random.fold_in(key, 16), (SEQUENCE_COUNT, 1), 0, SEQUENCE_LENGTH)
    spike_stride = jax.random.randint(jax.random.fold_in(key, 18), (SEQUENCE_COUNT, 1), 1, SEQUENCE_LENGTH)
    spike_positions = jnp.concatenate([spike_first_index, (spike_first_index + spike_stride) % SEQUENCE_LENGTH], axis=1)
    spike_penalty = jax.random.uniform(jax.random.fold_in(key, 17), (SEQUENCE_COUNT, 2, RETENTION_HEADS), jnp.float32, 0.2, 0.5)
    spike_hit_count = jnp.arange(SEQUENCE_LENGTH)[None, :, None] == spike_positions[:, None, :]
    spike_total_sum = jnp.sum(jnp.where(spike_hit_count[..., None], jnp.log(1.0 - spike_penalty)[:, None, :, :], 0.0), axis=2)
    return -baseline_rate[None, None, :] * device_multiplier * token_multiplier + spike_total_sum


def shard_levels(key, shape, pieces, low, largest):
    factor_of, own = 1.0, jax.random.fold_in(key, 6)
    for dim, shards_of in pieces:
        heights = jnp.exp(jax.random.uniform(jax.random.fold_in(own, dim), (shards_of,), jnp.float32, low / len(pieces), largest / len(pieces)))
        factor_of = factor_of * jnp.repeat(heights, shape[dim] // shards_of).reshape([-1 if axis == dim else 1 for axis in range(len(shape))])
    return factor_of


def scatter_about(rng, extent, deviation, limit, cuts=(), dtype=jnp.bfloat16):
    values = deviation * jax.random.normal(rng, extent, jnp.float32)
    if cuts:
        values = values * shard_levels(rng, extent, cuts, -0.22, 0.18)
    return jnp.clip(values, -limit, limit).astype(dtype)


def setup_inputs(seed: int = 0) -> dict:
    arg_keys = jax.random.split(jax.random.key(seed), 8)
    tokens = scatter_about(arg_keys[0], (SEQUENCE_COUNT, SEQUENCE_LENGTH, D), 1.0, 6.0, ((0, 2), (1, 4)))
    query_weight = scatter_about(arg_keys[1], (D, D), D ** -0.5, 0.125, ((0, 2), (1, 4)))
    key_weight = scatter_about(arg_keys[2], (D, D), D ** -0.5, 0.125, ((0, 2), (1, 4)))
    value_weight = scatter_about(arg_keys[3], (D, D), D ** -0.5, 0.125, ((0, 2), (1, 4)))
    gate_weight = scatter_about(arg_keys[4], (D, D), D ** -0.5, 0.125, ((0, 2), (1, 4)))
    out_weight = scatter_about(arg_keys[5], (D, D), D ** -0.5, 0.125, ((0, 4), (1, 2)))
    log_decay = draw_log_decay(jax.random.fold_in(arg_keys[7], 71), 0)
    return {"tokens": tokens, "query_weight": query_weight, "key_weight": key_weight, "value_weight": value_weight, "gate_weight": gate_weight, "out_weight": out_weight, "log_decay": log_decay}


def rotate(values, positions):
    half_dim = values.shape[-1] // 2
    index_row = jnp.arange(half_dim).astype(jnp.float32)
    frequency = jnp.power(jnp.float32(10000.0), -index_row / half_dim)
    angles = positions[:, None] * frequency[None, :]
    cosine = jnp.concatenate([jnp.cos(angles), jnp.cos(angles)], axis=-1)[:, None, :]
    sine_part = jnp.concatenate([jnp.sin(angles), jnp.sin(angles)], axis=-1)[:, None, :]
    turned = jnp.concatenate([-values[..., half_dim:], values[..., :half_dim]], axis=-1)
    return values * cosine + turned * sine_part

def group_norm(retained):
    center = retained - lax.optimization_barrier(jnp.mean(retained, axis=-1, keepdims=True))
    spread = lax.optimization_barrier(jnp.mean(center * center, axis=-1, keepdims=True))
    return center * lax.rsqrt(spread + 1e-05)

def reference(tokens, query_weight, key_weight, value_weight, gate_weight, out_weight, log_decay):

    def one_sequence(inputs):
        token_rows, decay_rows = inputs
        positions = jnp.arange(SEQUENCE_LENGTH).astype(jnp.float32)

        def project(weight):
            return jnp.dot(token_rows, weight, preferred_element_type=jnp.float32)
        queries = rotate(project(query_weight).reshape(SEQUENCE_LENGTH, RETENTION_HEADS, DH), positions).astype(jnp.bfloat16)
        keys_all = rotate(project(key_weight).reshape(SEQUENCE_LENGTH, RETENTION_HEADS, DH), positions).astype(jnp.bfloat16)
        values_all = project(value_weight).reshape(SEQUENCE_LENGTH, RETENTION_HEADS, DH).astype(jnp.bfloat16)
        gate_values = project(gate_weight).astype(jnp.bfloat16)
        blocks = SEQUENCE_LENGTH // BLOCK
        causal = jnp.arange(BLOCK)[:, None] >= jnp.arange(BLOCK)[None, :]

        def advance(carried, block_data):
            q_block, k_block, v_block, d_block = block_data
            cumulative = jnp.cumsum(d_block, axis=0)
            scores = jnp.einsum('thd,shd->hts', q_block.astype(jnp.float32), k_block.astype(jnp.float32))
            leading = cumulative.T
            differ = leading[:, :, None] - leading[:, None, :]
            weights = jnp.where(causal, jnp.exp(jnp.where(causal, differ, 0.0)), 0.0)
            mixed_weights = (scores * weights).astype(jnp.bfloat16)
            intra_part = jnp.einsum('hts,shd->thd', mixed_weights.astype(jnp.float32), v_block.astype(jnp.float32))
            inter_part = jnp.exp(cumulative)[:, :, None] * jnp.einsum('thd,hde->the', q_block.astype(jnp.float32), carried, precision=lax.Precision.HIGHEST)
            ending = cumulative[-1]
            weighted = k_block.astype(jnp.float32) * jnp.exp(ending[None, :] - cumulative)[:, :, None]
            update = jnp.einsum('shd,she->hde', weighted, v_block.astype(jnp.float32), precision=lax.Precision.HIGHEST)
            return (jnp.exp(ending)[:, None, None] * carried + update, intra_part + inter_part)
        final_state, retained = lax.scan(advance, jnp.zeros((RETENTION_HEADS, DH, DH), jnp.float32), (queries.reshape(blocks, BLOCK, RETENTION_HEADS, DH), keys_all.reshape(blocks, BLOCK, RETENTION_HEADS, DH), values_all.reshape(blocks, BLOCK, RETENTION_HEADS, DH), decay_rows.reshape(blocks, BLOCK, RETENTION_HEADS)))
        normed = group_norm(retained.reshape(SEQUENCE_LENGTH, RETENTION_HEADS, DH)).reshape(SEQUENCE_LENGTH, D)
        hidden = (jax.nn.silu(gate_values.astype(jnp.float32)) * normed).astype(jnp.bfloat16)
        return jnp.dot(hidden, out_weight, preferred_element_type=jnp.float32).astype(jnp.bfloat16)
    return lax.map(one_sequence, (tokens, log_decay))
```

```python
import functools

import jax
import jax.numpy as jnp
from jax import lax
from jax.experimental import pallas as pl
from jax.experimental.pallas import tpu as pltpu
from jax.sharding import PartitionSpec as P

DH = 256
BLOCK = 512
VMEM_LIMIT = 40 * 1024 * 1024
F32 = jnp.float32
BF16 = jnp.bfloat16


def mm(left, right):
    return jnp.dot(left, right, preferred_element_type=F32)


def mm_nt(left, right):
    return lax.dot_general(left, right, (((1,), (1,)), ((), ())), preferred_element_type=F32)


def mm_tn(left, right):
    return lax.dot_general(left, right, (((0,), (0,)), ((), ())), preferred_element_type=F32)


def swap(value, axis, mask):
    size = lax.axis_size(axis)
    return lax.ppermute(value, axis, [(place, place ^ mask) for place in range(size)])


def rotated(values, cosine, sine):
    half = DH // 2
    parts = []
    for start in range(0, values.shape[1], DH):
        low = values[:, start : start + half]
        high = values[:, start + half : start + DH]
        parts.append((low * cosine - high * sine).astype(BF16))
        parts.append((high * cosine + low * sine).astype(BF16))
    return jnp.concatenate(parts, axis=1)


def key_value_kernel(
    heads, other, x, wk, wv, acc_k, acc_v, cosine, sine, decay, k_out, v_out, before_out, state_out, sent_out
):
    block = pl.program_id(0)

    @pl.when(block == 0)
    def _():
        state_out[...] = jnp.zeros_like(state_out)

    keys = rotated(acc_k[...] + mm(x[...], wk[...]), cosine[...], sine[...])
    values = (acc_v[...] + mm(x[...], wv[...])).astype(BF16)
    k_out[...] = keys
    v_out[...] = values
    columns = decay[...].T
    for head in range(heads):
        span = slice(head * DH, (head + 1) * DH)
        ending = columns[BLOCK - 1 : BLOCK, head : head + 1]
        faded = jnp.exp(ending - columns[:, head : head + 1])
        weighted = (keys[:, span].astype(F32) * faded).astype(BF16)
        old = state_out[head]
        before_out[0, head] = old.astype(BF16)
        state_out[head] = jnp.exp(ending) * old + mm_tn(weighted, values[:, span])
    sent_out[...] = state_out[...].astype(BF16)


def query_gate_kernel(heads, other, x, wq, wg, acc_q, acc_g, cosine, sine, decay, k, v, q_out, g_out, intra_out):
    queries = rotated(acc_q[...] + mm(x[...], wq[...]), cosine[...], sine[...])
    q_out[...] = queries
    g_out[...] = (acc_g[...] + mm(x[...], wg[...])).astype(BF16)
    columns = decay[...].T
    rows = decay[...]
    part = BLOCK // 2
    for head in range(heads):
        span = slice(head * DH, (head + 1) * DH)
        for piece in range(2):
            first, last = piece * part, (piece + 1) * part
            scores = mm_nt(queries[first:last, span], k[:last, span])
            differ = columns[first:last, head : head + 1] - rows[head : head + 1, :last]
            place_t = lax.broadcasted_iota(jnp.int32, (part, last), 0) + first
            place_s = lax.broadcasted_iota(jnp.int32, (part, last), 1)
            causal = place_t >= place_s
            weights = jnp.where(causal, jnp.exp(jnp.where(causal, differ, 0.0)), 0.0)
            intra_out[first:last, span] = mm((scores * weights).astype(BF16), v[:last, span])


def hidden_kernel(heads, block, scale, q, gate, intra, decay, entering, before, out):
    columns = decay[...].T
    for head in range(heads):
        span = slice(head * DH, (head + 1) * DH)
        prior = scale[block, head] * entering[head].astype(F32) + before[0, head].astype(F32)
        inter = jnp.exp(columns[:, head : head + 1]) * mm(q[:, span], prior.astype(BF16))
        retained = intra[:, span] + inter
        center = retained - jnp.mean(retained, axis=1, keepdims=True)
        spread = jnp.mean(center * center, axis=1, keepdims=True)
        value = gate[:, span].astype(F32)
        silu = value / (1.0 + jnp.exp(-value))
        out[:, span] = (silu * center * lax.rsqrt(spread + 1e-5)).astype(BF16)


def params(*semantics):
    return pltpu.CompilerParams(vmem_limit_bytes=VMEM_LIMIT, dimension_semantics=semantics)


def cost(flops, bytes_accessed, transcendentals=0):
    return pl.CostEstimate(flops=flops, bytes_accessed=bytes_accessed, transcendentals=transcendentals)


def turn_tables(row_count, width):
    half = width // 2
    fine = 32
    index_row = jnp.arange(half).astype(F32)
    frequency = jnp.power(F32(10000.0), -index_row / half)
    offset = lax.axis_index("ctx") * row_count
    coarse_at = (offset + fine * jnp.arange(row_count // fine)).astype(F32)
    fine_at = jnp.arange(fine).astype(F32)
    coarse = coarse_at[:, None] * frequency[None, :]
    small = fine_at[:, None] * frequency[None, :]
    cos_c, sin_c = jnp.cos(coarse)[:, None, :], jnp.sin(coarse)[:, None, :]
    cos_f, sin_f = jnp.cos(small)[None], jnp.sin(small)[None]
    cosine = (cos_c * cos_f - sin_c * sin_f).reshape(row_count, half)
    sine = (sin_c * cos_f + cos_c * sin_f).reshape(row_count, half)
    return cosine, sine


def on_device(tokens, query_weight, key_weight, value_weight, gate_weight, out_weight, log_decay):
    x = tokens[0]
    rows, width = x.shape
    part, cols = query_weight.shape
    heads = cols // DH
    blocks = rows // BLOCK
    ctx = lax.axis_size("ctx")
    core = lax.axis_index("fsdp")
    place = lax.axis_index("tp")

    key_far = swap(key_weight, "fsdp", 1)
    value_far = swap(value_weight, "fsdp", 1)
    query_far = swap(query_weight, "fsdp", 1)
    gate_far = swap(gate_weight, "fsdp", 1)
    out_far = swap(out_weight, "fsdp", 1)

    lower = (jnp.arange(BLOCK)[:, None] <= jnp.arange(BLOCK)[None, :]).astype(F32)
    per_block = log_decay[0].T.reshape(heads * blocks, BLOCK)
    sums = jnp.dot(per_block, lower, precision=lax.Precision.HIGHEST).reshape(heads, blocks, BLOCK)
    ending = sums[:, :, -1]
    decay_rows = jnp.pad(sums.reshape(heads, rows), ((0, 8 - heads), (0, 0)))
    earlier = jnp.cumsum(ending, axis=1) - ending
    block_scale = jnp.exp(earlier).T
    total = jnp.sum(ending, axis=1)

    cosine, sine = turn_tables(rows, DH)

    x_own = lax.dynamic_slice_in_dim(x, core * part, part, axis=1)
    acc_k = mm(x_own, key_weight)
    acc_v = mm(x_own, value_weight)
    acc_q = mm(x_own, query_weight)
    acc_g = mm(x_own, gate_weight)

    other = (1 - core).astype(jnp.int32).reshape(1)
    whole_w = pl.BlockSpec((part, cols), lambda b, o: (0, 0))
    rows_spec = pl.BlockSpec((BLOCK, cols), lambda b, o: (b, 0))
    turn_spec = pl.BlockSpec((BLOCK, DH // 2), lambda b, o: (b, 0))
    decay_spec = pl.BlockSpec((8, BLOCK), lambda b, o: (0, b))
    x_spec = pl.BlockSpec((BLOCK, part), lambda b, o: (b, o[0]))
    state_spec = pl.BlockSpec((heads, DH, DH), lambda b, o: (0, 0, 0))

    keys, values, before, state, sent = pl.pallas_call(
        functools.partial(key_value_kernel, heads),
        grid_spec=pltpu.PrefetchScalarGridSpec(
            num_scalar_prefetch=1,
            grid=(blocks,),
            in_specs=[x_spec, whole_w, whole_w, rows_spec, rows_spec, turn_spec, turn_spec, decay_spec],
            out_specs=[
                rows_spec,
                rows_spec,
                pl.BlockSpec((1, heads, DH, DH), lambda b, o: (b, 0, 0, 0)),
                state_spec,
                state_spec,
            ],
        ),
        out_shape=[
            jax.ShapeDtypeStruct((rows, cols), BF16),
            jax.ShapeDtypeStruct((rows, cols), BF16),
            jax.ShapeDtypeStruct((blocks, heads, DH, DH), BF16),
            jax.ShapeDtypeStruct((heads, DH, DH), F32),
            jax.ShapeDtypeStruct((heads, DH, DH), BF16),
        ],
        compiler_params=params("arbitrary"),
        cost_estimate=cost(4 * rows * part * cols, 12 << 20),
        name="key_value",
    )(other, x, key_far, value_far, acc_k, acc_v, cosine, sine, decay_rows)

    entering = jnp.zeros_like(state)
    entering_log = jnp.zeros_like(total)
    window, window_log, message = state, total, sent
    hop = 1
    while hop < ctx:
        pairs = [(source, source + hop) for source in range(ctx - hop)]
        got = lax.ppermute(message, "ctx", pairs).astype(F32)
        entering = entering + jnp.exp(entering_log)[:, None, None] * got
        if 2 * hop < ctx:
            got_log = lax.ppermute(window_log, "ctx", pairs)
            window = window + jnp.exp(window_log)[:, None, None] * got
            message = window.astype(BF16)
            entering_log = entering_log + got_log
            window_log = window_log + got_log
        hop *= 2
    entering = entering.astype(BF16)

    queries, gates, intra = pl.pallas_call(
        functools.partial(query_gate_kernel, heads),
        grid_spec=pltpu.PrefetchScalarGridSpec(
            num_scalar_prefetch=1,
            grid=(blocks,),
            in_specs=[
                x_spec, whole_w, whole_w, rows_spec, rows_spec, turn_spec, turn_spec, decay_spec, rows_spec, rows_spec,
            ],
            out_specs=[rows_spec, rows_spec, rows_spec],
        ),
        out_shape=[
            jax.ShapeDtypeStruct((rows, cols), BF16),
            jax.ShapeDtypeStruct((rows, cols), BF16),
            jax.ShapeDtypeStruct((rows, cols), F32),
        ],
        compiler_params=params("arbitrary"),
        cost_estimate=cost(4 * rows * part * cols + 4 * rows * BLOCK * cols, 16 << 20, rows * BLOCK * heads),
        name="query_gate",
    )(other, x, query_far, gate_far, acc_q, acc_g, cosine, sine, decay_rows, keys, values)

    out_rows = jnp.where(
        core == 0,
        jnp.concatenate([out_weight, out_far], axis=1),
        jnp.concatenate([out_far, out_weight], axis=1),
    )

    def out_columns(at):
        return lax.dynamic_slice_in_dim(out_rows, at * cols, cols, axis=1)

    masks = (1, 2)
    mine = out_columns(place)
    across = [out_columns(place ^ mask) for mask in masks]
    diagonal = out_columns(place ^ (masks[0] | masks[1]))
    gathered_rows = []
    for index, mask in enumerate(masks):
        both = jnp.concatenate([across[index], diagonal], axis=1)
        gathered_rows.append(swap(both, "tp", mask))

    def hidden_rows(block):
        at = pl.BlockSpec((BLOCK, cols), lambda i: (block, 0))
        return pl.pallas_call(
            functools.partial(hidden_kernel, heads, block),
            grid=(1,),
            in_specs=[
                pl.BlockSpec(memory_space=pltpu.SMEM),
                at,
                at,
                at,
                pl.BlockSpec((8, BLOCK), lambda i: (0, block)),
                pl.BlockSpec((heads, DH, DH), lambda i: (0, 0, 0)),
                pl.BlockSpec((1, heads, DH, DH), lambda i: (block, 0, 0, 0)),
            ],
            out_specs=pl.BlockSpec((BLOCK, cols), lambda i: (0, 0)),
            out_shape=jax.ShapeDtypeStruct((BLOCK, cols), BF16),
            compiler_params=params("arbitrary"),
            cost_estimate=cost(2 * BLOCK * DH * cols, 4 << 20, BLOCK * cols),
            name="hidden",
        )(block_scale, queries, gates, intra, decay_rows, entering, before)

    hidden = [hidden_rows(block) for block in range(blocks)]
    outs = []
    for block in range(blocks):
        gather_at, sum_at = block % 2, 1 - block % 2
        far = swap(hidden[block], "tp", masks[gather_at])
        far_weight = gathered_rows[gather_at]
        give = mm(hidden[block], across[sum_at]) + mm(far, far_weight[:, cols:])
        keep = mm(hidden[block], mine) + mm(far, far_weight[:, :cols])
        got = swap(give.astype(BF16), "tp", masks[sum_at])
        outs.append((keep + got.astype(F32)).astype(BF16))
    return jnp.concatenate(outs, axis=0)[None]


def solution(mesh):
    in_specs = (
        P("fsdp", "ctx", None),
        P("fsdp", "tp"),
        P("fsdp", "tp"),
        P("fsdp", "tp"),
        P("fsdp", "tp"),
        P("tp", "fsdp"),
        P("fsdp", "ctx", "tp"),
    )
    out_specs = P("fsdp", "ctx", "tp")
    return jax.shard_map(
        on_device, mesh=mesh, in_specs=in_specs, out_specs=out_specs, check_vma=False
    )
```

```python
import functools

import jax
import jax.numpy as jnp
from jax import lax
from jax.experimental import pallas as pl
from jax.experimental.pallas import tpu as pltpu
from jax.sharding import PartitionSpec as P

DH = 256
BLOCK = 512
TILE = 256
FINE = 32
VMEM_LIMIT = 14 * 1024 * 1024
F32 = jnp.float32
BF16 = jnp.bfloat16


def mm(left, right):
    return jnp.dot(left, right, preferred_element_type=F32)


def mm_nt(left, right):
    return lax.dot_general(left, right, (((1,), (1,)), ((), ())), preferred_element_type=F32)


def mm_tn(left, right):
    return lax.dot_general(left, right, (((0,), (0,)), ((), ())), preferred_element_type=F32)


def swap(value, axis, mask):
    size = lax.axis_size(axis)
    return lax.ppermute(value, axis, [(place, place ^ mask) for place in range(size)])


def kernel_call(kernel, outs, operands, scalars, name, flops, transcendentals=0):
    arrays = [pltpu.with_memory_space_constraint(array, pltpu.VMEM) for array in operands]
    moved = sum(array.size * array.dtype.itemsize for array in operands)
    return pl.pallas_call(
        kernel,
        in_specs=[pl.BlockSpec(memory_space=pltpu.SMEM)] * len(scalars)
        + [pl.BlockSpec(memory_space=pltpu.VMEM)] * len(operands),
        out_specs=[pl.BlockSpec(memory_space=pltpu.VMEM)] * len(outs),
        out_shape=[pltpu.VMEM(shape, dtype) for shape, dtype in outs],
        compiler_params=pltpu.CompilerParams(vmem_limit_bytes=VMEM_LIMIT),
        cost_estimate=pl.CostEstimate(
            flops=flops, bytes_accessed=moved, transcendentals=transcendentals
        ),
        name=name,
    )(*scalars, *arrays)


def turned(values, cosine, sine):
    half = DH // 2
    parts = []
    for start in range(0, values.shape[1], DH):
        low = values[:, start : start + half]
        high = values[:, start + half : start + DH]
        parts.append((low * cosine - high * sine).astype(BF16))
        parts.append((high * cosine + low * sine).astype(BF16))
    return jnp.concatenate(parts, axis=1)


def angles(coarse, fine, first, count):
    at = first // FINE
    far = coarse[:, pl.ds(at, count // FINE), :]
    near = fine[...]
    cos_c, sin_c = far[0][:, None, :], far[1][:, None, :]
    cos_f, sin_f = near[0][None], near[1][None]
    cosine = cos_c * cos_f - sin_c * sin_f
    sine = sin_c * cos_f + cos_c * sin_f
    return cosine.reshape(count, DH // 2), sine.reshape(count, DH // 2)


def half_of(x, first, count, index, part):
    return x[pl.ds(first, count), pl.ds(pl.multiple_of(index * part, part), part)]


def key_value_own_kernel(where, x, wk, wv, acc_k, acc_v):
    part = wk.shape[0]
    core = where[0]

    def step(tile, carry):
        first = pl.multiple_of(tile * TILE, TILE)
        rows = half_of(x, first, TILE, core, part)
        acc_k[pl.ds(first, TILE), :] = mm(rows, wk[...])
        acc_v[pl.ds(first, TILE), :] = mm(rows, wv[...])
        return carry

    lax.fori_loop(0, x.shape[0] // TILE, step, 0)


def key_value_kernel(
    heads, where, x, wk, wv, acc_k, acc_v, coarse, fine, decay, k_out, v_out, before_out, state_out, sent_out
):
    part = wk.shape[0]
    far = 1 - where[0]
    state_out[...] = jnp.zeros_like(state_out)

    def block_step(block, carry):
        start = pl.multiple_of(block * BLOCK, BLOCK)
        columns = decay[:, pl.ds(start, BLOCK)].T
        ending = columns[BLOCK - 1 : BLOCK, :]
        faded = jnp.exp(ending - columns)
        updates = [None] * heads
        for piece in range(BLOCK // TILE):
            first = pl.multiple_of(start + piece * TILE, TILE)
            at = pl.ds(first, TILE)
            rows = half_of(x, first, TILE, far, part)
            cosine, sine = angles(coarse, fine, first, TILE)
            keys = turned(acc_k[at, :] + mm(rows, wk[...]), cosine, sine)
            values = (acc_v[at, :] + mm(rows, wv[...])).astype(BF16)
            k_out[at, :] = keys
            v_out[at, :] = values
            for head in range(heads):
                span = slice(head * DH, (head + 1) * DH)
                fade = faded[piece * TILE : (piece + 1) * TILE, head : head + 1]
                weighted = (keys[:, span].astype(F32) * fade).astype(BF16)
                update = mm_tn(weighted, values[:, span])
                updates[head] = update if piece == 0 else updates[head] + update
        for head in range(heads):
            old = state_out[head]
            before_out[block, head] = old.astype(BF16)
            state_out[head] = jnp.exp(ending[:, head : head + 1]) * old + updates[head]
        return carry

    lax.fori_loop(0, x.shape[0] // BLOCK, block_step, 0)
    sent_out[...] = state_out[...].astype(BF16)


def query_gate_kernel(
    heads, where, x, wq, wq_far, wg, wg_far, coarse, fine, decay, k, v, q_out, g_out, intra_out
):
    part = wq.shape[0]
    core = where[0]

    def block_step(block, carry):
        start = pl.multiple_of(block * BLOCK, BLOCK)
        lines = decay[:, pl.ds(start, BLOCK)]
        columns = lines.T
        for piece in range(BLOCK // TILE):
            low, last = piece * TILE, (piece + 1) * TILE
            first = pl.multiple_of(start + low, TILE)
            at = pl.ds(first, TILE)
            own = half_of(x, first, TILE, core, part)
            far = half_of(x, first, TILE, 1 - core, part)
            cosine, sine = angles(coarse, fine, first, TILE)
            queries = turned(mm(own, wq[...]) + mm(far, wq_far[...]), cosine, sine)
            q_out[at, :] = queries
            g_out[at, :] = (mm(own, wg[...]) + mm(far, wg_far[...])).astype(BF16)
            place_t = lax.broadcasted_iota(jnp.int32, (TILE, last), 0) + low
            place_s = lax.broadcasted_iota(jnp.int32, (TILE, last), 1)
            causal = place_t >= place_s
            for head in range(heads):
                span = slice(head * DH, (head + 1) * DH)
                scores = mm_nt(queries[:, span], k[pl.ds(start, last), span])
                differ = columns[low:last, head : head + 1] - lines[head : head + 1, :last]
                weights = jnp.where(causal, jnp.exp(jnp.where(causal, differ, 0.0)), 0.0)
                intra_out[at, span] = mm((scores * weights).astype(BF16), v[pl.ds(start, last), span])
        return carry

    lax.fori_loop(0, x.shape[0] // BLOCK, block_step, 0)


def hidden_kernel(heads, block, scale, q, gate, intra, decay, entering, before, out):
    start = block * BLOCK
    columns = jnp.exp(decay[:, start : start + BLOCK].T)
    for head in range(heads):
        span = slice(head * DH, (head + 1) * DH)
        prior = scale[block, head] * entering[head].astype(F32) + before[block, head].astype(F32)
        prior = prior.astype(BF16)
        for low in range(0, BLOCK, TILE):
            at = slice(start + low, start + low + TILE)
            inter = columns[low : low + TILE, head : head + 1] * mm(q[at, span], prior)
            retained = intra[at, span] + inter
            center = retained - jnp.mean(retained, axis=1, keepdims=True)
            spread = jnp.mean(center * center, axis=1, keepdims=True)
            value = gate[at, span].astype(F32)
            silu = value / (1.0 + jnp.exp(-value))
            out[low : low + TILE, span] = (silu * center * lax.rsqrt(spread + 1e-5)).astype(BF16)


def column_of(first, second, is_first, index, cols):
    at = pl.ds(pl.multiple_of(index * cols, cols), cols)
    return jnp.where(is_first, first[:, at], second[:, at])


def product_kernel(parts, where, *refs):
    out = refs[-1]
    cols = out.shape[1]
    total = None
    for number, (half, index) in enumerate(parts):
        rows, first, second = refs[3 * number : 3 * number + 3]
        weight = column_of(first, second, where[half] == 1, where[index], cols)
        term = mm(rows[...], weight)
        total = term if total is None else total + term
    out[...] = total.astype(out.dtype)


def finish_kernel(*refs):
    out = refs[-1]
    count = (len(refs) - 1) // 2
    for block in range(count):
        value = refs[2 * block][...] + refs[2 * block + 1][...].astype(F32)
        out[0, block * BLOCK : (block + 1) * BLOCK, :] = value.astype(BF16)


def turn_tables(row_count):
    half = DH // 2
    index_row = jnp.arange(half).astype(F32)
    frequency = jnp.power(F32(10000.0), -index_row / half)
    offset = lax.axis_index("ctx") * row_count
    coarse_at = (offset + FINE * jnp.arange(row_count // FINE)).astype(F32)
    fine_at = jnp.arange(FINE).astype(F32)
    coarse = coarse_at[:, None] * frequency[None, :]
    fine = fine_at[:, None] * frequency[None, :]
    return jnp.stack([jnp.cos(coarse), jnp.sin(coarse)]), jnp.stack([jnp.cos(fine), jnp.sin(fine)])


def on_device(tokens, query_weight, key_weight, value_weight, gate_weight, out_weight, log_decay):
    x = tokens[0]
    rows, width = x.shape
    part, cols = query_weight.shape
    heads = cols // DH
    blocks = rows // BLOCK
    ctx = lax.axis_size("ctx")
    tp, cores = lax.axis_size("tp"), lax.axis_size("fsdp")
    core = lax.axis_index("fsdp")
    place = lax.axis_index("tp")
    assert tp == 4 and cores == 2
    high, low = place // 2, place % 2
    near_mask, far_mask = 1, 2

    key_far = swap(key_weight, "fsdp", 1)
    value_far = swap(value_weight, "fsdp", 1)
    near_first = swap(out_weight, "tp", near_mask)
    high_pairs = [
        ((at ^ far_mask) * cores + at // 2, at * cores + at // 2) for at in range(tp)
    ]
    high_pass = lax.ppermute(out_weight, ("tp", "fsdp"), high_pairs)
    query_far = swap(query_weight, "fsdp", 1)
    gate_far = swap(gate_weight, "fsdp", 1)
    own_second = swap(out_weight, "fsdp", 1)
    near_second = swap(near_first, "fsdp", 1)
    core_pairs = [(at * cores + at // 2, at * cores + 1 - at // 2) for at in range(tp)]
    high_other = lax.ppermute(high_pass, ("tp", "fsdp"), core_pairs)

    lower = (jnp.arange(BLOCK)[:, None] <= jnp.arange(BLOCK)[None, :]).astype(F32)
    per_block = log_decay[0].T.reshape(heads * blocks, BLOCK)
    sums = jnp.dot(per_block, lower, precision=lax.Precision.HIGHEST).reshape(heads, blocks, BLOCK)
    ending = sums[:, :, -1]
    decay_rows = jnp.pad(sums.reshape(heads, rows), ((0, 8 - heads), (0, 0)))
    earlier = jnp.cumsum(ending, axis=1) - ending
    block_scale = jnp.exp(earlier).T
    total = jnp.sum(ending, axis=1)
    coarse, fine = turn_tables(rows)

    same_half = (core == high).astype(jnp.int32)
    where = jnp.stack([core, same_half, 1 - same_half, low, 1 - low]).astype(jnp.int32)
    at_same, at_other, at_low, at_flip = 1, 2, 3, 4
    product = 2 * rows * part * cols

    acc_k, acc_v = kernel_call(
        key_value_own_kernel,
        [((rows, cols), F32)] * 2,
        [x, key_weight, value_weight],
        [where],
        "key_value_own",
        2 * product,
    )
    keys, values, before, state, sent = kernel_call(
        functools.partial(key_value_kernel, heads),
        [
            ((rows, cols), BF16),
            ((rows, cols), BF16),
            ((blocks, heads, DH, DH), BF16),
            ((heads, DH, DH), F32),
            ((heads, DH, DH), BF16),
        ],
        [x, key_far, value_far, acc_k, acc_v, coarse, fine, decay_rows],
        [where],
        "key_value",
        2 * product,
    )

    entering = jnp.zeros_like(state)
    entering_log = jnp.zeros_like(total)
    window, window_log, message = state, total, sent
    hop = 1
    while hop < ctx:
        pairs = [(source, source + hop) for source in range(ctx - hop)]
        got = lax.ppermute(message, "ctx", pairs).astype(F32)
        entering = entering + jnp.exp(entering_log)[:, None, None] * got
        if 2 * hop < ctx:
            got_log = lax.ppermute(window_log, "ctx", pairs)
            window = window + jnp.exp(window_log)[:, None, None] * got
            message = window.astype(BF16)
            entering_log = entering_log + got_log
            window_log = window_log + got_log
        hop *= 2
    entering = entering.astype(BF16)

    queries, gates, intra = kernel_call(
        functools.partial(query_gate_kernel, heads),
        [((rows, cols), BF16), ((rows, cols), BF16), ((rows, cols), F32)],
        [x, query_weight, query_far, gate_weight, gate_far, coarse, fine, decay_rows, keys, values],
        [where],
        "query_gate",
        4 * product + 4 * rows * BLOCK * cols,
        rows * BLOCK * heads,
    )

    hidden = [
        kernel_call(
            functools.partial(hidden_kernel, heads, block),
            [((BLOCK, cols), BF16)],
            [queries, gates, intra, decay_rows, entering, before],
            [block_scale],
            "hidden",
            2 * BLOCK * DH * cols,
            BLOCK * cols,
        )[0]
        for block in range(blocks)
    ]
    own_pair = (out_weight, own_second)
    plans = [
        (near_mask, far_mask, (near_first, near_second), (at_other, at_low), (at_same, at_low)),
        (far_mask, near_mask, (high_pass, high_other), (at_same, at_flip), (at_same, at_low)),
    ]
    keeps = []
    for block in range(blocks):
        gather_at, sum_at, pair, give_at, keep_at = plans[block % 2]
        far = swap(hidden[block], "tp", gather_at)
        flops = 4 * BLOCK * cols * cols

        def product_of(at, dtype, name):
            return kernel_call(
                functools.partial(product_kernel, (at, at)),
                [((BLOCK, cols), dtype)],
                [hidden[block], *own_pair, far, *pair],
                [where],
                name,
                flops,
            )[0]

        give = product_of(give_at, BF16, "give")
        keep = product_of(keep_at, F32, "keep")
        keeps += [keep, swap(give, "tp", sum_at)]
    arrays = [pltpu.with_memory_space_constraint(array, pltpu.VMEM) for array in keeps]
    return pl.pallas_call(
        finish_kernel,
        in_specs=[pl.BlockSpec(memory_space=pltpu.VMEM)] * len(arrays),
        out_specs=pl.BlockSpec(memory_space=pltpu.VMEM),
        out_shape=jax.ShapeDtypeStruct((1, rows, cols), BF16),
        compiler_params=pltpu.CompilerParams(vmem_limit_bytes=VMEM_LIMIT),
        name="finish",
    )(*arrays)


def solution(mesh):
    in_specs = (
        P("fsdp", "ctx", None),
        P("fsdp", "tp"),
        P("fsdp", "tp"),
        P("fsdp", "tp"),
        P("fsdp", "tp"),
        P("tp", "fsdp"),
        P("fsdp", "ctx", "tp"),
    )
    out_specs = P("fsdp", "ctx", "tp")
    return jax.shard_map(
        on_device, mesh=mesh, in_specs=in_specs, out_specs=out_specs, check_vma=False
    )
```

```python
import functools
import math

import jax
import jax.numpy as jnp
from jax import lax
from jax.experimental import pallas as pl
from jax.experimental.pallas import tpu as pltpu
from jax.sharding import PartitionSpec as P

DH = 256
BLOCK = 512
TILE = 256
FINE = 32
EXTRA = 16
VMEM_LIMIT = 14 * 1024 * 1024
F32 = jnp.float32
BF16 = jnp.bfloat16


def mm(left, right):
    return jnp.dot(left, right, preferred_element_type=F32)


def mm_nt(left, right):
    return lax.dot_general(left, right, (((1,), (1,)), ((), ())), preferred_element_type=F32)


def mm_tn(left, right):
    return lax.dot_general(left, right, (((0,), (0,)), ((), ())), preferred_element_type=F32)


def swap(value, axis, mask):
    size = lax.axis_size(axis)
    return lax.ppermute(value, axis, [(place, place ^ mask) for place in range(size)])


def kernel_call(kernel, outs, operands, name, flops, transcendentals=0):
    arrays = [pltpu.with_memory_space_constraint(array, pltpu.VMEM) for array in operands]
    moved = sum(array.size * array.dtype.itemsize for array in operands)
    return pl.pallas_call(
        kernel,
        in_specs=[pl.BlockSpec(memory_space=pltpu.VMEM)] * len(operands),
        out_specs=[pl.BlockSpec(memory_space=pltpu.VMEM)] * len(outs),
        out_shape=[pltpu.VMEM(shape, dtype) for shape, dtype in outs],
        compiler_params=pltpu.CompilerParams(vmem_limit_bytes=VMEM_LIMIT),
        cost_estimate=pl.CostEstimate(
            flops=flops, bytes_accessed=moved, transcendentals=transcendentals
        ),
        name=name,
    )(*arrays)


def turned(values, cosine, sine):
    half = DH // 2
    parts = []
    for start in range(0, values.shape[1], DH):
        low = values[:, start : start + half]
        high = values[:, start + half : start + DH]
        parts.append((low * cosine - high * sine).astype(BF16))
        parts.append((high * cosine + low * sine).astype(BF16))
    return jnp.concatenate(parts, axis=1)


def angles(coarse, fine, first, count):
    at = first // FINE
    far = coarse[:, pl.ds(at, count // FINE), :]
    near = fine[...]
    cos_c, sin_c = far[0][:, None, :], far[1][:, None, :]
    cos_f, sin_f = near[0][None], near[1][None]
    cosine = cos_c * cos_f - sin_c * sin_f
    sine = sin_c * cos_f + cos_c * sin_f
    return cosine.reshape(count, DH // 2), sine.reshape(count, DH // 2)


def half_of(x, first, count, index, part):
    return x[pl.ds(first, count), pl.ds(pl.multiple_of(index * part, part), part)]


def decay_sums(log_decay, decay):
    heads, rows = log_decay.shape
    place_s = lax.broadcasted_iota(jnp.int32, (BLOCK, BLOCK), 0)
    place_t = lax.broadcasted_iota(jnp.int32, (BLOCK, BLOCK), 1)
    upper = jnp.where(place_s <= place_t, 1.0, 0.0).astype(BF16)
    value = jnp.concatenate([log_decay[...], jnp.zeros((8 - heads, rows), F32)], axis=0)
    parts = []
    for _ in range(3):
        parts.append(value.astype(BF16))
        value = value - parts[-1].astype(F32)
    stacked = jnp.concatenate([part.astype(F32) for part in parts], axis=0).astype(BF16)
    for start in range(0, rows, BLOCK):
        sums = mm(stacked[:, start : start + BLOCK], upper)
        decay[:, start : start + BLOCK] = sums[:8] + sums[8:16] + sums[16:]


def angle_tables(coarse, fine):
    half = DH // 2

    def fill(table, start, stride):
        count = table.shape[1]
        place = lax.broadcasted_iota(jnp.int32, (count, half), 0) * stride + start
        index = lax.broadcasted_iota(jnp.int32, (count, half), 1).astype(F32)
        angle = place.astype(F32) * jnp.exp(index * (-math.log(10000.0) / half))
        table[0] = jnp.cos(angle)
        table[1] = jnp.sin(angle)

    fill(coarse, lax.axis_index("ctx") * coarse.shape[1] * FINE, FINE)
    fill(fine, 0, 1)


def key_value_own_kernel(x, wk, wv, log_decay, acc_k, acc_v, decay, coarse, fine):
    part = wk.shape[0]
    core = lax.axis_index("fsdp")

    def step(tile, carry):
        first = pl.multiple_of(tile * TILE, TILE)
        rows = half_of(x, first, TILE, core, part)
        acc_k[pl.ds(first, TILE), :] = mm(rows, wk[...])
        acc_v[pl.ds(first, TILE), :] = mm(rows, wv[...])
        return carry

    lax.fori_loop(0, x.shape[0] // TILE, step, 0)
    decay_sums(log_decay, decay)
    angle_tables(coarse, fine)


def pack_message(message, states, logs):
    heads = len(states)
    place = lax.broadcasted_iota(jnp.int32, (EXTRA, DH), 0)
    tail = jnp.zeros((EXTRA, DH), F32)
    for head in range(heads):
        message[head * DH : (head + 1) * DH, :] = states[head].astype(BF16)
        rest = logs[head]
        for number in range(3):
            piece = rest.astype(BF16).astype(F32)
            tail = jnp.where(place == 3 * head + number, piece, tail)
            rest = rest - piece
    message[heads * DH :, :] = tail.astype(BF16)


def message_log(message, heads, head):
    tail = message[heads * DH :, :].astype(F32)
    return tail[3 * head : 3 * head + 1] + tail[3 * head + 1 : 3 * head + 2] + tail[3 * head + 2 : 3 * head + 3]


def key_value_kernel(
    heads, x, wk, wv, acc_k, acc_v, decay, coarse, fine, k_out, v_out, before_out, state_out, message
):
    part = wk.shape[0]
    far = 1 - lax.axis_index("fsdp")
    state_out[...] = jnp.zeros_like(state_out)

    def block_step(block, totals):
        start = pl.multiple_of(block * BLOCK, BLOCK)
        columns = decay[:, pl.ds(start, BLOCK)].T
        ending = columns[BLOCK - 1 : BLOCK, :]
        faded = jnp.exp(ending - columns)
        updates = [None] * heads
        for piece in range(BLOCK // TILE):
            first = pl.multiple_of(start + piece * TILE, TILE)
            at = pl.ds(first, TILE)
            rows = half_of(x, first, TILE, far, part)
            cosine, sine = angles(coarse, fine, first, TILE)
            keys = turned(acc_k[at, :] + mm(rows, wk[...]), cosine, sine)
            values = (acc_v[at, :] + mm(rows, wv[...])).astype(BF16)
            k_out[at, :] = keys
            v_out[at, :] = values
            for head in range(heads):
                span = slice(head * DH, (head + 1) * DH)
                fade = faded[piece * TILE : (piece + 1) * TILE, head : head + 1]
                weighted = (keys[:, span].astype(F32) * fade).astype(BF16)
                update = mm_tn(weighted, values[:, span])
                updates[head] = update if piece == 0 else updates[head] + update
        for head in range(heads):
            span = slice(head * DH, (head + 1) * DH)
            old = state_out[span, :]
            before_out[block, span, :] = old.astype(BF16)
            state_out[span, :] = jnp.exp(ending[:, head : head + 1]) * old + updates[head]
        return totals + ending

    totals = lax.fori_loop(0, x.shape[0] // BLOCK, block_step, jnp.zeros((1, 8), F32))
    states = [state_out[head * DH : (head + 1) * DH, :] for head in range(heads)]
    pack_message(message, states, [totals[:, head : head + 1] for head in range(heads)])


def combine_kernel(heads, first, decay, *refs):
    if first:
        state, got, window, entering, message = refs
    else:
        state, old_message, old_entering, got, window, entering, message = refs
    states, logs = [], []
    for head in range(heads):
        span = slice(head * DH, (head + 1) * DH)
        arrived = got[span, :].astype(F32)
        arrived_log = message_log(got, heads, head)[:, :1]
        if first:
            ends = [decay[head : head + 1, end - 1 : end] for end in range(BLOCK, decay.shape[1] + 1, BLOCK)]
            window_log = functools.reduce(lambda a, b: a + b, ends)
            entering[span, :] = arrived
            entering_log = arrived_log
        else:
            window_log = message_log(old_message, heads, head)[:, :1]
            before_log = old_entering[heads * DH + head : heads * DH + head + 1, :1]
            entering[span, :] = old_entering[span, :] + jnp.exp(before_log) * arrived
            entering_log = before_log + arrived_log
        entering[heads * DH + head : heads * DH + head + 1, :] = jnp.broadcast_to(entering_log, (1, DH))
        new = state[span, :] + jnp.exp(window_log) * arrived
        window[span, :] = new
        states.append(new)
        logs.append(window_log + arrived_log)
    pack_message(message, states, logs)


def query_gate_kernel(
    heads, x, wq, wq_far, wg, wg_far, decay, coarse, fine, k, v, q_out, g_out, intra_out
):
    part = wq.shape[0]
    core = lax.axis_index("fsdp")

    def block_step(block, carry):
        start = pl.multiple_of(block * BLOCK, BLOCK)
        lines = decay[:, pl.ds(start, BLOCK)]
        columns = lines.T
        for piece in range(BLOCK // TILE):
            low, last = piece * TILE, (piece + 1) * TILE
            first = pl.multiple_of(start + low, TILE)
            at = pl.ds(first, TILE)
            own = half_of(x, first, TILE, core, part)
            far = half_of(x, first, TILE, 1 - core, part)
            cosine, sine = angles(coarse, fine, first, TILE)
            queries = turned(mm(own, wq[...]) + mm(far, wq_far[...]), cosine, sine)
            q_out[at, :] = queries
            g_out[at, :] = (mm(own, wg[...]) + mm(far, wg_far[...])).astype(BF16)
            place_t = lax.broadcasted_iota(jnp.int32, (TILE, last), 0) + low
            place_s = lax.broadcasted_iota(jnp.int32, (TILE, last), 1)
            causal = place_t >= place_s
            for head in range(heads):
                span = slice(head * DH, (head + 1) * DH)
                scores = mm_nt(queries[:, span], k[pl.ds(start, last), span])
                differ = columns[low:last, head : head + 1] - lines[head : head + 1, :last]
                weights = jnp.where(causal, jnp.exp(jnp.where(causal, differ, 0.0)), 0.0)
                intra_out[at, span] = mm((scores * weights).astype(BF16), v[pl.ds(start, last), span])
        return carry

    lax.fori_loop(0, x.shape[0] // BLOCK, block_step, 0)


def hidden_kernel(heads, start, q, gate, intra, decay, entering, got, before, out):
    block, low = start // BLOCK, start % BLOCK
    lines = decay[:, start : start + TILE]
    columns = jnp.exp(lines.T)
    at = slice(start, start + TILE)
    for head in range(heads):
        span = slice(head * DH, (head + 1) * DH)
        entering_log = entering[heads * DH + head : heads * DH + head + 1, :1]
        state = entering[span, :] + jnp.exp(entering_log) * got[span, :].astype(F32)
        scale_log = jnp.zeros((1, 1), F32)
        for earlier in range(block):
            end = (earlier + 1) * BLOCK
            scale_log = scale_log + decay[head : head + 1, end - 1 : end]
        prior = (jnp.exp(scale_log) * state + before[block, span, :].astype(F32)).astype(BF16)
        inter = columns[:, head : head + 1] * mm(q[at, span], prior)
        retained = intra[at, span] + inter
        center = retained - jnp.mean(retained, axis=1, keepdims=True)
        spread = jnp.mean(center * center, axis=1, keepdims=True)
        value = gate[at, span].astype(F32)
        silu = value / (1.0 + jnp.exp(-value))
        out[:, span] = (silu * center * lax.rsqrt(spread + 1e-5)).astype(BF16)


def column_of(first, second, is_first, index, cols):
    at = pl.ds(pl.multiple_of(index * cols, cols), cols)
    return jnp.where(is_first, first[:, at], second[:, at])


def product_kernel(by_low, flip, *refs):
    out = refs[-1]
    cols = out.shape[1]
    place, core = lax.axis_index("tp"), lax.axis_index("fsdp")
    high, low = place // 2, place % 2
    if by_low:
        wanted_high, wanted_low = (1 - high if flip else high), low
    else:
        wanted_high, wanted_low = high, (1 - low if flip else low)
    own, own_first, own_second, far, far_first, far_second = refs[:-1]
    own_weight = column_of(own_first, own_second, core == wanted_high, wanted_low, cols)
    if by_low:
        far_weight = jnp.where(core == wanted_high, far_first[...], far_second[...])
    else:
        far_weight = column_of(far_first, far_second, core == high, wanted_low, cols)
    out[...] = (mm(own[...], own_weight) + mm(far[...], far_weight)).astype(out.dtype)


def slice_kernel(weight, out):
    cols = out.shape[1]
    low = lax.axis_index("tp") % 2
    out[...] = weight[:, pl.ds(pl.multiple_of((1 - low) * cols, cols), cols)]


def finish_kernel(*refs):
    out = refs[-1]
    for number in range((len(refs) - 1) // 2):
        value = refs[2 * number][...] + refs[2 * number + 1][...].astype(F32)
        out[0, number * TILE : (number + 1) * TILE, :] = value.astype(BF16)


def after(value, *others):
    return lax.optimization_barrier((value, *others))[0]


def on_device(tokens, query_weight, key_weight, value_weight, gate_weight, out_weight, log_decay):
    x = tokens[0]
    rows, width = x.shape
    part, cols = query_weight.shape
    heads = cols // DH
    blocks = rows // BLOCK
    ctx, tp, cores = lax.axis_size("ctx"), lax.axis_size("tp"), lax.axis_size("fsdp")
    assert tp == 4 and cores == 2 and ctx > 2
    near_mask, far_mask = 1, 2
    product = 2 * rows * part * cols
    tables = [((2, rows // FINE, DH // 2), F32), ((2, FINE, DH // 2), F32)]

    key_far = swap(key_weight, "fsdp", 1)
    value_far = swap(value_weight, "fsdp", 1)

    acc_k, acc_v, decay, coarse, fine = kernel_call(
        key_value_own_kernel,
        [((rows, cols), F32)] * 2 + [((8, rows), F32)] + tables,
        [x, key_weight, value_weight, log_decay[0].T],
        "key_value_own",
        2 * product,
    )
    state_shape = (heads * DH, DH)
    message_shape = (heads * DH + EXTRA, DH)
    keys, values, before, state, message = kernel_call(
        functools.partial(key_value_kernel, heads),
        [
            ((rows, cols), BF16),
            ((rows, cols), BF16),
            ((blocks, *state_shape), BF16),
            (state_shape, F32),
            (message_shape, BF16),
        ],
        [x, key_far, value_far, acc_k, acc_v, decay, coarse, fine],
        "key_value",
        2 * product,
    )

    window, entering, hop = state, None, 1
    while hop < ctx:
        pairs = [(source, source + hop) for source in range(ctx - hop)]
        got = lax.ppermute(message, "ctx", pairs)
        hop *= 2
        if hop < ctx:
            held = [decay, window] + ([] if entering is None else [message, entering]) + [got]
            window, entering, message = kernel_call(
                functools.partial(combine_kernel, heads, entering is None),
                [(state_shape, F32), (message_shape, F32), (message_shape, BF16)],
                held,
                "combine",
                0,
            )

    query_far = swap(query_weight, "fsdp", 1)
    gate_far = swap(gate_weight, "fsdp", 1)
    [for_near] = kernel_call(slice_kernel, [((cols, cols), BF16)], [out_weight], "near_columns", 0)
    near_first = swap(for_near, "tp", near_mask)
    near_second = swap(near_first, "fsdp", 1)
    high_pairs = [((at ^ far_mask) * cores + at // 2, at * cores + at // 2) for at in range(tp)]
    core_pairs = [(at * cores + at // 2, at * cores + 1 - at // 2) for at in range(tp)]
    high_pass = lax.ppermute(out_weight, ("tp", "fsdp"), high_pairs)
    high_other = lax.ppermute(high_pass, ("tp", "fsdp"), core_pairs)
    own_second = swap(out_weight, "fsdp", 1)

    queries, gates, intra = kernel_call(
        functools.partial(query_gate_kernel, heads),
        [((rows, cols), BF16), ((rows, cols), BF16), ((rows, cols), F32)],
        [x, query_weight, query_far, gate_weight, gate_far, decay, coarse, fine, keys, values],
        "query_gate",
        4 * product + 4 * rows * BLOCK * cols,
        rows * BLOCK * heads,
    )

    starts = list(range(0, rows, TILE))
    order = [start for pair in zip(starts[: len(starts) // 2], starts[len(starts) // 2 :]) for start in pair]
    pieces = {}
    for start in order:
        by_low = start < rows // 2
        [hidden] = kernel_call(
            functools.partial(hidden_kernel, heads, start),
            [((TILE, cols), BF16)],
            [queries, gates, intra, decay, entering, got, before],
            "hidden",
            2 * TILE * DH * cols,
            TILE * cols,
        )
        pieces[start] = hidden, swap(hidden, "tp", near_mask if by_low else far_mask)
    sums = {}
    for start in order:
        by_low = start < rows // 2
        hidden, far = pieces[start]
        pair = (near_first, near_second) if by_low else (high_pass, high_other)

        def product_of(flip, dtype, name):
            return kernel_call(
                functools.partial(product_kernel, by_low, flip),
                [((TILE, cols), dtype)],
                [hidden, out_weight, own_second, far, *pair],
                name,
                4 * TILE * cols * cols,
            )[0]

        give = product_of(True, BF16, "give")
        keep = product_of(False, F32, "keep")
        sums[start] = keep, swap(give, "tp", far_mask if by_low else near_mask)
    arrays = [
        pltpu.with_memory_space_constraint(array, pltpu.VMEM) for start in starts for array in sums[start]
    ]
    return pl.pallas_call(
        finish_kernel,
        in_specs=[pl.BlockSpec(memory_space=pltpu.VMEM)] * len(arrays),
        out_specs=pl.BlockSpec(memory_space=pltpu.VMEM),
        out_shape=jax.ShapeDtypeStruct((1, rows, cols), BF16),
        compiler_params=pltpu.CompilerParams(vmem_limit_bytes=VMEM_LIMIT),
        name="finish",
    )(*arrays)


def solution(mesh):
    in_specs = (
        P("fsdp", "ctx", None),
        P("fsdp", "tp"),
        P("fsdp", "tp"),
        P("fsdp", "tp"),
        P("fsdp", "tp"),
        P("tp", "fsdp"),
        P("fsdp", "ctx", "tp"),
    )
    out_specs = P("fsdp", "ctx", "tp")
    return jax.shard_map(
        on_device, mesh=mesh, in_specs=in_specs, out_specs=out_specs, check_vma=False
    )
```

```python
import functools
import math

import jax
import jax.numpy as jnp
from jax import lax
from jax.experimental import pallas as pl
from jax.experimental.pallas import tpu as pltpu
from jax.sharding import PartitionSpec as P

DH = 256
BLOCK = 512
TILE = 256
FINE = 32
EXTRA = 16
VMEM_LIMIT = 14 * 1024 * 1024
F32 = jnp.float32
BF16 = jnp.bfloat16


def mm(left, right):
    return jnp.dot(left, right, preferred_element_type=F32)


def mm_nt(left, right):
    return lax.dot_general(left, right, (((1,), (1,)), ((), ())), preferred_element_type=F32)


def mm_tn(left, right):
    return lax.dot_general(left, right, (((0,), (0,)), ((), ())), preferred_element_type=F32)


def swap(value, axis, mask):
    size = lax.axis_size(axis)
    return lax.ppermute(value, axis, [(place, place ^ mask) for place in range(size)])


def kernel_call(kernel, outs, operands, name):
    arrays = [pltpu.with_memory_space_constraint(array, pltpu.VMEM) for array in operands]
    return pl.pallas_call(
        kernel,
        in_specs=[pl.BlockSpec(memory_space=pltpu.VMEM)] * len(operands),
        out_specs=[pl.BlockSpec(memory_space=pltpu.VMEM)] * len(outs),
        out_shape=[pltpu.VMEM(shape, dtype) for shape, dtype in outs],
        compiler_params=pltpu.CompilerParams(vmem_limit_bytes=VMEM_LIMIT),
        cost_estimate=pl.CostEstimate(
            flops=1, bytes_accessed=1, transcendentals=0
        ),
        name=name,
    )(*arrays)


def turned(values, cosine, sine):
    half = DH // 2
    parts = []
    for start in range(0, values.shape[1], DH):
        low = values[:, start : start + half]
        high = values[:, start + half : start + DH]
        parts.append((low * cosine - high * sine).astype(BF16))
        parts.append((high * cosine + low * sine).astype(BF16))
    return jnp.concatenate(parts, axis=1)


def angles(coarse, fine, first, count):
    at = first // FINE
    far = coarse[:, pl.ds(at, count // FINE), :]
    near = fine[...]
    cos_c, sin_c = far[0][:, None, :], far[1][:, None, :]
    cos_f, sin_f = near[0][None], near[1][None]
    cosine = cos_c * cos_f - sin_c * sin_f
    sine = sin_c * cos_f + cos_c * sin_f
    return cosine.reshape(count, DH // 2), sine.reshape(count, DH // 2)


def half_of(x, first, count, index, part):
    return x[pl.ds(first, count), pl.ds(pl.multiple_of(index * part, part), part)]


def decay_sums(log_decay, decay):
    heads, rows = log_decay.shape
    place_s = lax.broadcasted_iota(jnp.int32, (BLOCK, BLOCK), 0)
    place_t = lax.broadcasted_iota(jnp.int32, (BLOCK, BLOCK), 1)
    upper = jnp.where(place_s <= place_t, 1.0, 0.0).astype(BF16)
    value = jnp.concatenate([log_decay[...], jnp.zeros((8 - heads, rows), F32)], axis=0)
    parts = []
    for _ in range(3):
        parts.append(value.astype(BF16))
        value = value - parts[-1].astype(F32)
    stacked = jnp.concatenate([part.astype(F32) for part in parts], axis=0).astype(BF16)
    for start in range(0, rows, BLOCK):
        sums = mm(stacked[:, start : start + BLOCK], upper)
        decay[:, start : start + BLOCK] = sums[:8] + sums[8:16] + sums[16:]


def angle_tables(coarse, fine):
    half = DH // 2

    def fill(table, start, stride):
        count = table.shape[1]
        place = lax.broadcasted_iota(jnp.int32, (count, half), 0) * stride + start
        index = lax.broadcasted_iota(jnp.int32, (count, half), 1).astype(F32)
        angle = place.astype(F32) * jnp.exp(index * (-math.log(10000.0) / half))
        table[0] = jnp.cos(angle)
        table[1] = jnp.sin(angle)

    fill(coarse, lax.axis_index("ctx") * coarse.shape[1] * FINE, FINE)
    fill(fine, 0, 1)


def key_value_own_kernel(
    x_far, wk_far, wv_far, wq_far, wg_far, wo_far, log_decay_far,
    x, acc_k, acc_v, decay, coarse, fine, wqg, wo, near_columns, wk, wv, log_decay, arrived,
):
    rows, part = x.shape[0], wk.shape[0]
    core = lax.axis_index("fsdp")
    low = lax.axis_index("tp") % 2
    steps = rows // TILE
    cols = near_columns.shape[1]
    copies = []

    def load(source, target):
        copy = pltpu.make_async_copy(source, target, arrived.at[len(copies)])
        copies.append(copy)
        copy.start()
        return copy

    def load_x(tile, half):
        at = (pl.ds(tile * TILE, TILE), pl.ds(pl.multiple_of(half * part, part), part))
        return load(x_far.at[at], x.at[at])

    logs = load(log_decay_far, log_decay)
    first = [load(wk_far, wk), load_x(0, core)]
    value = load(wv_far, wv)
    own = [load_x(tile, core) for tile in range(1, steps)]
    weight = load(wo_far, wo)
    rest = [load_x(tile, 1 - core) for tile in range(steps)]
    rest += [load(wq_far, wqg.at[pl.ds(0, part)]), load(wg_far, wqg.at[pl.ds(part, part)])]
    angle_tables(coarse, fine)
    logs.wait()
    decay_sums(log_decay, decay)
    for tile in range(steps):
        at = slice(tile * TILE, (tile + 1) * TILE)
        for copy in first if tile == 0 else [own[tile - 1]]:
            copy.wait()
        block = half_of(x, tile * TILE, TILE, core, part)
        acc_k[at, :] = mm(block, wk[...])
        if tile == 0:
            value.wait()
        acc_v[at, :] = mm(block, wv[...])
    weight.wait()
    near_columns[...] = wo[:, pl.ds(pl.multiple_of((1 - low) * cols, cols), cols)]
    for copy in rest:
        copy.wait()


def pack_message(message, states, logs):
    heads = len(states)
    place = lax.broadcasted_iota(jnp.int32, (EXTRA, DH), 0)
    tail = jnp.zeros((EXTRA, DH), F32)
    for head in range(heads):
        message[head * DH : (head + 1) * DH, :] = states[head].astype(BF16)
        rest = logs[head]
        for number in range(3):
            piece = rest.astype(BF16).astype(F32)
            tail = jnp.where(place == 3 * head + number, piece, tail)
            rest = rest - piece
    message[heads * DH :, :] = tail.astype(BF16)


def message_log(message, heads, head):
    tail = message[heads * DH :, :].astype(F32)
    return tail[3 * head : 3 * head + 1] + tail[3 * head + 1 : 3 * head + 2] + tail[3 * head + 2 : 3 * head + 3]


def key_value_kernel(
    heads, x, wk, wv, acc_k, acc_v, decay, coarse, fine, k_out, v_out, before_out, state_out, message
):
    part = wk.shape[0]
    far = 1 - lax.axis_index("fsdp")
    state_out[...] = jnp.zeros_like(state_out)

    def block_step(block, totals):
        start = pl.multiple_of(block * BLOCK, BLOCK)
        columns = decay[:, pl.ds(start, BLOCK)].T
        ending = columns[BLOCK - 1 : BLOCK, :]
        faded = jnp.exp(ending - columns)
        updates = [None] * heads
        for piece in range(BLOCK // TILE):
            first = pl.multiple_of(start + piece * TILE, TILE)
            at = pl.ds(first, TILE)
            rows = half_of(x, first, TILE, far, part)
            cosine, sine = angles(coarse, fine, first, TILE)
            keys = turned(acc_k[at, :] + mm(rows, wk[...]), cosine, sine)
            values = (acc_v[at, :] + mm(rows, wv[...])).astype(BF16)
            k_out[at, :] = keys
            v_out[at, :] = values
            for head in range(heads):
                span = slice(head * DH, (head + 1) * DH)
                fade = faded[piece * TILE : (piece + 1) * TILE, head : head + 1]
                weighted = (keys[:, span].astype(F32) * fade).astype(BF16)
                update = mm_tn(weighted, values[:, span])
                updates[head] = update if piece == 0 else updates[head] + update
        for head in range(heads):
            span = slice(head * DH, (head + 1) * DH)
            old = state_out[span, :]
            before_out[block, span, :] = old.astype(BF16)
            state_out[span, :] = jnp.exp(ending[:, head : head + 1]) * old + updates[head]
        return totals + ending

    totals = lax.fori_loop(0, x.shape[0] // BLOCK, block_step, jnp.zeros((1, 8), F32))
    states = [state_out[head * DH : (head + 1) * DH, :] for head in range(heads)]
    pack_message(message, states, [totals[:, head : head + 1] for head in range(heads)])


def combine_kernel(heads, first, ins, decay, state, *refs):
    if not first:
        old_message, old_entering = refs[:2]
        refs = refs[2:]
    arrivals = refs[:ins]
    window, entering, message = refs[ins:]
    states, logs = [], []
    for head in range(heads):
        span = slice(head * DH, (head + 1) * DH)
        arrived = functools.reduce(lambda a, b: a + b, [got[span, :].astype(F32) for got in arrivals])
        arrived_log = functools.reduce(
            lambda a, b: a + b, [message_log(got, heads, head)[:, :1] for got in arrivals]
        )
        if first:
            ends = [decay[head : head + 1, end - 1 : end] for end in range(BLOCK, decay.shape[1] + 1, BLOCK)]
            window_log = functools.reduce(lambda a, b: a + b, ends)
            entering[span, :] = arrived
            entering_log = arrived_log
        else:
            window_log = message_log(old_message, heads, head)[:, :1]
            before_log = old_entering[heads * DH + head : heads * DH + head + 1, :1]
            entering[span, :] = old_entering[span, :] + jnp.exp(before_log) * arrived
            entering_log = before_log + arrived_log
        entering[heads * DH + head : heads * DH + head + 1, :] = jnp.broadcast_to(entering_log, (1, DH))
        new = state[span, :] + jnp.exp(window_log) * arrived
        window[span, :] = new
        states.append(new)
        logs.append(window_log + arrived_log)
    pack_message(message, states, logs)


def query_gate_kernel(
    heads, block, x, wqg, wqg_far, decay, coarse, fine, k, v, q_out, g_out, intra_out
):
    part = wqg.shape[0] // 2
    core = lax.axis_index("fsdp")
    start = block * BLOCK
    lines = decay[:, start : start + BLOCK]
    columns = lines.T

    def project(piece, carry):
        first = pl.multiple_of(start + piece * TILE, TILE)
        at = pl.ds(pl.multiple_of(piece * TILE, TILE), TILE)
        own = half_of(x, first, TILE, core, part)
        far = half_of(x, first, TILE, 1 - core, part)
        cosine, sine = angles(coarse, fine, first, TILE)
        q_out[at, :] = turned(mm(own, wqg[:part, :]) + mm(far, wqg_far[:part, :]), cosine, sine)
        g_out[at, :] = (mm(own, wqg[part:, :]) + mm(far, wqg_far[part:, :])).astype(BF16)
        return carry

    lax.fori_loop(0, BLOCK // TILE, project, 0)
    for piece in range(BLOCK // TILE):
        low, last = piece * TILE, (piece + 1) * TILE
        place_t = lax.broadcasted_iota(jnp.int32, (TILE, last), 0) + low
        place_s = lax.broadcasted_iota(jnp.int32, (TILE, last), 1)
        causal = place_t >= place_s
        for head in range(heads):
            span = slice(head * DH, (head + 1) * DH)
            scores = mm_nt(q_out[low:last, span], k[start : start + last, span])
            differ = columns[low:last, head : head + 1] - lines[head : head + 1, :last]
            weights = jnp.where(causal, jnp.exp(jnp.where(causal, differ, 0.0)), 0.0)
            intra_out[low:last, span] = mm((scores * weights).astype(BF16), v[start : start + last, span])


def hidden_kernel(heads, starts, ins, decay, entering, before, *refs):
    arrivals, projected, outs = refs[:ins], refs[ins : -len(starts)], refs[-len(starts) :]
    for head in range(heads):
        span = slice(head * DH, (head + 1) * DH)
        entering_log = entering[heads * DH + head : heads * DH + head + 1, :1]
        got = functools.reduce(lambda a, b: a + b, [ref[span, :].astype(F32) for ref in arrivals])
        state = entering[span, :] + jnp.exp(entering_log) * got
        for start, out in zip(starts, outs):
            block = start // BLOCK
            q, gate, intra = projected[3 * block : 3 * block + 3]
            at = slice(start % BLOCK, start % BLOCK + TILE)
            column = jnp.exp(decay[:, start : start + TILE].T[:, head : head + 1])
            scale_log = jnp.zeros((1, 1), F32)
            for earlier in range(block):
                end = (earlier + 1) * BLOCK
                scale_log = scale_log + decay[head : head + 1, end - 1 : end]
            prior = (jnp.exp(scale_log) * state + before[block, span, :].astype(F32)).astype(BF16)
            retained = intra[at, span] + column * mm(q[at, span], prior)
            center = retained - jnp.mean(retained, axis=1, keepdims=True)
            spread = jnp.mean(center * center, axis=1, keepdims=True)
            value = gate[at, span].astype(F32)
            silu = value / (1.0 + jnp.exp(-value))
            out[:, span] = (silu * center * lax.rsqrt(spread + 1e-5)).astype(BF16)


def arrange_kernel(near_first, near_second, high_first, high_second, low_out, high_out):
    cols = near_first.shape[1]
    place, core = lax.axis_index("tp"), lax.axis_index("fsdp")
    high, low = place // 2, place % 2
    here = core == high
    mine = pl.ds(pl.multiple_of(low * cols, cols), cols)
    flipped = pl.ds(pl.multiple_of((1 - low) * cols, cols), cols)
    low_out[:, :cols] = jnp.where(here, near_second[...], near_first[...])
    low_out[:, cols:] = jnp.where(here, near_first[...], near_second[...])
    high_out[:, :cols] = jnp.where(here, high_first[:, flipped], high_second[:, flipped])
    high_out[:, cols:] = jnp.where(here, high_first[:, mine], high_second[:, mine])


def own_kernel(order, own_first, own_second, *refs):
    pieces, outs = refs[: len(order)], refs[len(order) :]
    cols = pieces[0].shape[1]
    place, core = lax.axis_index("tp"), lax.axis_index("fsdp")
    high, low = place // 2, place % 2
    here = core == high
    mine = pl.ds(pl.multiple_of(low * cols, cols), cols)
    flipped = pl.ds(pl.multiple_of((1 - low) * cols, cols), cols)
    keep = jnp.where(here, own_first[:, mine], own_second[:, mine])
    gives = [
        jnp.where(here, own_second[:, mine], own_first[:, mine]),
        jnp.where(here, own_first[:, flipped], own_second[:, flipped]),
    ]
    for (half, number), piece in zip(order, pieces):
        at = slice(number * TILE, (number + 1) * TILE)
        outs[half][at, :cols] = mm(piece[...], gives[half])
        outs[half][at, cols:] = mm(piece[...], keep)


def give_kernel(number, own, far, weight, out):
    cols = out.shape[1]
    at = slice(number * TILE, (number + 1) * TILE)
    out[...] = (own[at, :cols] + mm(far[...], weight[:, :cols])).astype(BF16)


def keep_kernel(order, *refs):
    count = len(order)
    fars, owns, weights, outs = refs[:count], refs[count : count + 2], refs[count + 2 : count + 4], refs[count + 4 :]
    for (half, number), far in zip(order, fars):
        cols = far.shape[1]
        at = slice(number * TILE, (number + 1) * TILE)
        outs[half][at, :] = owns[half][at, cols:] + mm(far[...], weights[half][:, cols:])


def finish_kernel(order, *refs):
    gots, keeps, out = refs[: len(order)], refs[len(order) : -1], refs[-1]
    for (half, number), got in zip(order, gots):
        keep = keeps[half]
        at = slice(number * TILE, (number + 1) * TILE)
        value = keep[at, :] + got[...].astype(F32)
        start = half * keep.shape[0] + number * TILE
        out[0, start : start + TILE, :] = value.astype(BF16)


def after(value, *others):
    return lax.optimization_barrier((value, *others))[0]


def on_device(tokens, query_weight, key_weight, value_weight, gate_weight, out_weight, log_decay):
    x = tokens[0]
    rows, width = x.shape
    part, cols = query_weight.shape
    heads = cols // DH
    blocks = rows // BLOCK
    ctx, tp, cores = lax.axis_size("ctx"), lax.axis_size("tp"), lax.axis_size("fsdp")
    assert tp == 4 and cores == 2 and ctx > 2
    near_mask, far_mask = 1, 2
    tables = [((2, rows // FINE, DH // 2), F32), ((2, FINE, DH // 2), F32)]

    key_far = swap(key_weight, "fsdp", 1)
    value_far = swap(value_weight, "fsdp", 1)

    own_outs = [((rows, width), BF16), ((rows, cols), F32), ((rows, cols), F32), ((8, rows), F32)] + tables
    own_outs += [((2 * part, cols), BF16), (out_weight.shape, BF16), ((cols, cols), BF16)]
    loaded = (x, key_weight, value_weight, query_weight, gate_weight, out_weight, log_decay[0].T)
    in_hbm = [pltpu.with_memory_space_constraint(array, pltpu.HBM) for array in loaded]
    x, acc_k, acc_v, decay, coarse, fine, own_qg, out_weight, for_near = pl.pallas_call(
        key_value_own_kernel,
        in_specs=[pl.BlockSpec(memory_space=pltpu.HBM)] * len(in_hbm),
        out_specs=[pl.BlockSpec(memory_space=pltpu.VMEM)] * len(own_outs),
        out_shape=[pltpu.VMEM(shape, dtype) for shape, dtype in own_outs],
        scratch_shapes=[
            pltpu.VMEM((part, cols), BF16),
            pltpu.VMEM((part, cols), BF16),
            pltpu.VMEM((heads, rows), F32),
            pltpu.SemaphoreType.DMA((2 * (rows // TILE) + 6,)),
        ],
        compiler_params=pltpu.CompilerParams(vmem_limit_bytes=VMEM_LIMIT),
        cost_estimate=pl.CostEstimate(flops=1, bytes_accessed=1, transcendentals=0),
        name="key_value_own",
    )(*in_hbm)
    state_shape = (heads * DH, DH)
    message_shape = (heads * DH + EXTRA, DH)
    keys, values, before, state, message = kernel_call(
        functools.partial(key_value_kernel, heads),
        [
            ((rows, cols), BF16),
            ((rows, cols), BF16),
            ((blocks, *state_shape), BF16),
            (state_shape, F32),
            (message_shape, BF16),
        ],
        [x, key_far, value_far, acc_k, acc_v, decay, coarse, fine],
        "key_value",
    )

    far_qg = swap(after(own_qg, message), "fsdp", 1)

    def query_gate(block, decay):
        return kernel_call(
            functools.partial(query_gate_kernel, heads, block),
            [((BLOCK, cols), BF16), ((BLOCK, cols), BF16), ((BLOCK, cols), F32)],
            [x, own_qg, far_qg, decay, coarse, fine, keys, values],
            "query_gate",
        )

    near_first = swap(after(for_near, message), "tp", near_mask)
    high_pairs = [((at ^ far_mask) * cores + at // 2, at * cores + at // 2) for at in range(tp)]
    core_pairs = [(at * cores + at // 2, at * cores + 1 - at // 2) for at in range(tp)]
    late_weight = after(out_weight, message)
    high_pass = lax.ppermute(late_weight, ("tp", "fsdp"), high_pairs)
    own_second = swap(late_weight, "fsdp", 1)

    projected = [query_gate(0, decay)]
    window, entering, hop, early = state, None, 1, None
    held = after(decay, *projected[0])
    while True:
        grown = hop // 2
        late = [(source, source + hop) for source in range(grown, ctx - hop)]
        arrivals = [lax.ppermute(message, "ctx", late)] + ([early] if early is not None else [])
        if 2 * hop >= ctx:
            break
        unchanged = [(source, source + 2 * hop) for source in range(hop) if source + 2 * hop < ctx]
        early = lax.ppermute(message, "ctx", unchanged)
        old = [] if entering is None else [message, entering]
        window, entering, message = kernel_call(
            functools.partial(combine_kernel, heads, entering is None, len(arrivals)),
            [(state_shape, F32), (message_shape, F32), (message_shape, BF16)],
            [held, window, *old, *arrivals],
            "combine",
        )
        hop *= 2

    held = after(decay, message, near_first, *arrivals[1:])
    for block in range(1, blocks):
        projected.append(query_gate(block, held))
    projected = [array for arrays in projected for array in arrays]

    count = rows // 2 // TILE
    masks = (near_mask, far_mask)
    hidden, far = [[], []], [[], []]
    for number in range(count):
        held = after(decay, pair[0]) if number else decay
        pair = kernel_call(
            functools.partial(hidden_kernel, heads, [(half * count + number) * TILE for half in range(2)], len(arrivals)),
            [((TILE, cols), BF16)] * 2,
            [held, entering, before, *arrivals, *projected],
            "hidden",
        )
        for half in range(2):
            hidden[half].append(pair[half])
            far[half].append(swap(pair[half], "tp", masks[half]))
    near_second = swap(after(near_first, hidden[0][-1]), "fsdp", 1)
    high_other = lax.ppermute(after(high_pass, hidden[0][-1]), ("tp", "fsdp"), core_pairs)
    weights = kernel_call(
        arrange_kernel,
        [((cols, 2 * cols), BF16)] * 2,
        [near_first, near_second, high_pass, high_other],
        "arrange",
    )
    order = [(half, number) for number in reversed(range(count)) for half in (1, 0)]
    owns = kernel_call(
        functools.partial(own_kernel, order),
        [((count * TILE, 2 * cols), F32)] * 2,
        [out_weight, own_second, *(hidden[half][number] for half, number in order)],
        "own_products",
    )
    gots = []
    for half, number in order:
        [give] = kernel_call(
            functools.partial(give_kernel, number),
            [((TILE, cols), BF16)],
            [owns[half], far[half][number], weights[half]],
            "give",
        )
        gots.append(swap(give, "tp", masks[1 - half]))
    keeps = kernel_call(
        functools.partial(keep_kernel, order),
        [((count * TILE, cols), F32)] * 2,
        [*(far[half][number] for half, number in order), *owns, *weights],
        "keep",
    )
    arrays = [pltpu.with_memory_space_constraint(array, pltpu.VMEM) for array in (*gots, *keeps)]
    return pl.pallas_call(
        functools.partial(finish_kernel, order),
        in_specs=[pl.BlockSpec(memory_space=pltpu.VMEM)] * len(arrays),
        out_specs=pl.BlockSpec(memory_space=pltpu.VMEM),
        out_shape=jax.ShapeDtypeStruct((1, rows, cols), BF16),
        compiler_params=pltpu.CompilerParams(vmem_limit_bytes=VMEM_LIMIT),
        name="finish",
    )(*arrays)


def solution(mesh):
    in_specs = (
        P("fsdp", "ctx", None),
        P("fsdp", "tp"),
        P("fsdp", "tp"),
        P("fsdp", "tp"),
        P("fsdp", "tp"),
        P("tp", "fsdp"),
        P("fsdp", "ctx", "tp"),
    )
    out_specs = P("fsdp", "ctx", "tp")
    return jax.shard_map(
        on_device, mesh=mesh, in_specs=in_specs, out_specs=out_specs, check_vma=False
    )
```

```python
import functools
import math

import jax
import jax.numpy as jnp
from jax import lax
from jax.experimental import pallas as pl
from jax.experimental.pallas import tpu as pltpu
from jax.sharding import PartitionSpec as P

DH = 256
BLOCK = 512
TILE = 256
FINE = 32
EXTRA = 16
VMEM_LIMIT = 14 * 1024 * 1024
F32 = jnp.float32
BF16 = jnp.bfloat16


def mm(left, right):
    return jnp.dot(left, right, preferred_element_type=F32)


def mm_nt(left, right):
    return lax.dot_general(left, right, (((1,), (1,)), ((), ())), preferred_element_type=F32)


def mm_tn(left, right):
    return lax.dot_general(left, right, (((0,), (0,)), ((), ())), preferred_element_type=F32)


def swap(value, axis, mask):
    size = lax.axis_size(axis)
    return lax.ppermute(value, axis, [(place, place ^ mask) for place in range(size)])


def kernel_call(kernel, outs, operands, name):
    arrays = [pltpu.with_memory_space_constraint(array, pltpu.VMEM) for array in operands]
    return pl.pallas_call(
        kernel,
        in_specs=[pl.BlockSpec(memory_space=pltpu.VMEM)] * len(operands),
        out_specs=[pl.BlockSpec(memory_space=pltpu.VMEM)] * len(outs),
        out_shape=[pltpu.VMEM(shape, dtype) for shape, dtype in outs],
        compiler_params=pltpu.CompilerParams(vmem_limit_bytes=VMEM_LIMIT),
        cost_estimate=pl.CostEstimate(
            flops=1, bytes_accessed=1, transcendentals=0
        ),
        name=name,
    )(*arrays)


def loading_call(kernel, outs, loaded, operands, scratch, loads, name):
    arrays = [pltpu.with_memory_space_constraint(array, pltpu.HBM) for array in loaded]
    arrays += [pltpu.with_memory_space_constraint(array, pltpu.VMEM) for array in operands]
    return pl.pallas_call(
        kernel,
        in_specs=[pl.BlockSpec(memory_space=pltpu.HBM)] * len(loaded)
        + [pl.BlockSpec(memory_space=pltpu.VMEM)] * len(operands),
        out_specs=[pl.BlockSpec(memory_space=pltpu.VMEM)] * len(outs),
        out_shape=[pltpu.VMEM(shape, dtype) for shape, dtype in outs],
        scratch_shapes=[*scratch, pltpu.SemaphoreType.DMA((loads,))],
        compiler_params=pltpu.CompilerParams(vmem_limit_bytes=VMEM_LIMIT),
        cost_estimate=pl.CostEstimate(flops=1, bytes_accessed=1, transcendentals=0),
        name=name,
    )(*arrays)


def turned(values, cosine, sine):
    half = DH // 2
    parts = []
    for start in range(0, values.shape[1], DH):
        low = values[:, start : start + half]
        high = values[:, start + half : start + DH]
        parts.append((low * cosine - high * sine).astype(BF16))
        parts.append((high * cosine + low * sine).astype(BF16))
    return jnp.concatenate(parts, axis=1)


def angles(coarse, fine, first, count):
    at = first // FINE
    far = coarse[:, pl.ds(at, count // FINE), :]
    near = fine[...]
    cos_c, sin_c = far[0][:, None, :], far[1][:, None, :]
    cos_f, sin_f = near[0][None], near[1][None]
    cosine = cos_c * cos_f - sin_c * sin_f
    sine = sin_c * cos_f + cos_c * sin_f
    return cosine.reshape(count, DH // 2), sine.reshape(count, DH // 2)


def decay_sums(log_decay, decay):
    heads, rows = log_decay.shape
    place_s = lax.broadcasted_iota(jnp.int32, (BLOCK, BLOCK), 0)
    place_t = lax.broadcasted_iota(jnp.int32, (BLOCK, BLOCK), 1)
    upper = jnp.where(place_s <= place_t, 1.0, 0.0).astype(BF16)
    value = jnp.concatenate([log_decay[...], jnp.zeros((8 - heads, rows), F32)], axis=0)
    parts = []
    for _ in range(3):
        parts.append(value.astype(BF16))
        value = value - parts[-1].astype(F32)
    stacked = jnp.concatenate([part.astype(F32) for part in parts], axis=0).astype(BF16)
    for start in range(0, rows, BLOCK):
        sums = mm(stacked[:, start : start + BLOCK], upper)
        decay[:, start : start + BLOCK] = sums[:8] + sums[8:16] + sums[16:]


def angle_tables(coarse, fine):
    half = DH // 2

    def fill(table, start, stride):
        count = table.shape[1]
        place = lax.broadcasted_iota(jnp.int32, (count, half), 0) * stride + start
        index = lax.broadcasted_iota(jnp.int32, (count, half), 1).astype(F32)
        angle = place.astype(F32) * jnp.exp(index * (-math.log(10000.0) / half))
        table[0] = jnp.cos(angle)
        table[1] = jnp.sin(angle)

    fill(coarse, lax.axis_index("ctx") * coarse.shape[1] * FINE, FINE)
    fill(fine, 0, 1)


class Loads:
    def __init__(self, arrived):
        self.arrived, self.count = arrived, 0

    def start(self, source, target):
        copy = pltpu.make_async_copy(source, target, self.arrived.at[self.count])
        self.count += 1
        copy.start()
        return copy


def half_tiles(x_far, x, half, loads):
    rows, part = x.shape
    columns = pl.ds(pl.multiple_of(half * part, part), part)
    return [
        functools.partial(loads.start, x_far.at[pl.ds(at, TILE), columns], x.at[pl.ds(at, TILE)])
        for at in range(0, rows, TILE)
    ]


def key_value_own_kernel(
    x_far, wk_far, wv_far, log_decay_far, wo_far, wq_far, wg_far,
    x, acc_k, acc_v, decay, coarse, fine, wo, wq, wg, wk, wv, log_decay, arrived,
):
    loads = Loads(arrived)
    tiles = half_tiles(x_far, x, lax.axis_index("fsdp"), loads)
    logs = loads.start(log_decay_far, log_decay)
    key, first = loads.start(wk_far, wk), tiles[0]()
    value = loads.start(wv_far, wv)
    rest = [tile() for tile in tiles[1:]]
    others = [loads.start(wo_far, wo), loads.start(wq_far, wq), loads.start(wg_far, wg)]
    angle_tables(coarse, fine)
    logs.wait()
    decay_sums(log_decay, decay)
    key.wait()
    for number, copy in enumerate([first, *rest]):
        at = slice(number * TILE, (number + 1) * TILE)
        copy.wait()
        acc_k[at, :] = mm(x[at, :], wk[...])
        if number == 0:
            value.wait()
        acc_v[at, :] = mm(x[at, :], wv[...])
    for copy in others:
        copy.wait()


def pack_message(message, state, log):
    place = lax.broadcasted_iota(jnp.int32, (EXTRA, DH), 0)
    tail = jnp.zeros((EXTRA, DH), F32)
    message[:DH, :] = state.astype(BF16)
    for number in range(3):
        piece = log.astype(BF16).astype(F32)
        tail = jnp.where(place == number, piece, tail)
        log = log - piece
    message[DH:, :] = tail.astype(BF16)


def message_log(message):
    tail = message[DH:, :].astype(F32)
    return (tail[:1] + tail[1:2] + tail[2:3])[:, :1]


def key_value_kernel(
    heads, x_far, wk, wv, acc_k, acc_v, decay, coarse, fine, x, k_out, v_out, before_out, *refs
):
    states, messages, arrived = refs[:heads], refs[heads : 2 * heads], refs[-1]
    loads = Loads(arrived)
    tiles = [tile() for tile in half_tiles(x_far, x, 1 - lax.axis_index("fsdp"), loads)]
    totals, blocks = 0.0, x.shape[0] // BLOCK
    for block in range(blocks):
        start = block * BLOCK
        columns = decay[:, start : start + BLOCK].T
        ending = columns[BLOCK - 1 : BLOCK, :]
        totals = totals + ending
        faded = jnp.exp(ending - columns)
        updates = [None] * heads
        for piece in range(BLOCK // TILE):
            first = start + piece * TILE
            at = slice(first, first + TILE)
            tiles[first // TILE].wait()
            cosine, sine = angles(coarse, fine, first, TILE)
            keys = turned(acc_k[at, :] + mm(x[at, :], wk[...]), cosine, sine)
            values = (acc_v[at, :] + mm(x[at, :], wv[...])).astype(BF16)
            k_out[at, :] = keys
            v_out[at, :] = values
            for head in range(heads):
                span = slice(head * DH, (head + 1) * DH)
                fade = faded[piece * TILE : (piece + 1) * TILE, head : head + 1]
                weighted = (keys[:, span].astype(F32) * fade).astype(BF16)
                update = mm_tn(weighted, values[:, span])
                updates[head] = update if piece == 0 else updates[head] + update
        for head in range(heads):
            span = slice(head * DH, (head + 1) * DH)
            old = states[head][...] if block else jnp.zeros((DH, DH), F32)
            before_out[block, span, :] = old.astype(BF16)
            new = jnp.exp(ending[:, head : head + 1]) * old + updates[head]
            states[head][...] = new
            if block == blocks - 1:
                pack_message(messages[head], new, totals[:, head : head + 1])


def combine_kernel(hop, first, window, sent, *refs):
    if first:
        got, new_window, new_entering, message = refs
    else:
        entering, got, new_window, new_entering, message = refs
    upper = (lax.axis_index("ctx") // hop) % 2 == 1
    arrived = got[:DH, :].astype(F32)
    window_log, arrived_log = message_log(sent), message_log(got)
    if first:
        new_entering[:DH, :] = jnp.where(upper, arrived, 0.0)
        entering_log = jnp.zeros((1, 1), F32)
    else:
        entering_log = entering[DH : DH + 1, :1]
        new_entering[:DH, :] = entering[:DH, :] + jnp.where(upper, jnp.exp(entering_log), 0.0) * arrived
    entering_log = entering_log + jnp.where(upper, arrived_log, 0.0)
    new_entering[DH:, :] = jnp.broadcast_to(entering_log, (8, DH))
    own_fade = jnp.where(upper, 1.0, jnp.exp(arrived_log))
    arrived_fade = jnp.where(upper, jnp.exp(window_log), 1.0)
    joined = own_fade * window[...] + arrived_fade * arrived
    new_window[...] = joined
    pack_message(message, joined, window_log + arrived_log)


def query_gate_kernel(
    heads, block, x_own, x_other, wq, wq_far, wg, wg_far, decay, coarse, fine, k, v, q_out, g_out, intra_out
):
    start = block * BLOCK
    lines = decay[:, start : start + BLOCK]
    columns = lines.T

    def project(piece, carry):
        first = pl.multiple_of(start + piece * TILE, TILE)
        at = pl.ds(pl.multiple_of(piece * TILE, TILE), TILE)
        own, far = x_own[pl.ds(first, TILE), :], x_other[pl.ds(first, TILE), :]
        cosine, sine = angles(coarse, fine, first, TILE)
        q_out[at, :] = turned(mm(own, wq[...]) + mm(far, wq_far[...]), cosine, sine)
        g_out[at, :] = (mm(own, wg[...]) + mm(far, wg_far[...])).astype(BF16)
        return carry

    lax.fori_loop(0, BLOCK // TILE, project, 0)
    for piece in range(BLOCK // TILE):
        low, last = piece * TILE, (piece + 1) * TILE
        place_t = lax.broadcasted_iota(jnp.int32, (TILE, last), 0) + low
        place_s = lax.broadcasted_iota(jnp.int32, (TILE, last), 1)
        causal = place_t >= place_s
        for head in range(heads):
            span = slice(head * DH, (head + 1) * DH)
            scores = mm_nt(q_out[low:last, span], k[start : start + last, span])
            differ = columns[low:last, head : head + 1] - lines[head : head + 1, :last]
            weights = jnp.where(causal, jnp.exp(jnp.where(causal, differ, 0.0)), 0.0)
            intra_out[low:last, span] = mm((scores * weights).astype(BF16), v[start : start + last, span])


def hidden_kernel(heads, hop, starts, decay, before, *refs):
    refs, token = refs[:-1], refs[-1]
    token[...] = jnp.zeros_like(token)
    entering, arrivals, projected, outs = (
        refs[:heads], refs[heads : 2 * heads], refs[2 * heads : -len(starts)], refs[-len(starts) :]
    )
    upper = (lax.axis_index("ctx") // hop) % 2 == 1
    for head in range(heads):
        span = slice(head * DH, (head + 1) * DH)
        fade = jnp.where(upper, jnp.exp(entering[head][DH : DH + 1, :1]), 0.0)
        state = entering[head][:DH, :] + fade * arrivals[head][:DH, :].astype(F32)
        for start, out in zip(starts, outs):
            block = start // BLOCK
            q, gate, intra = projected[3 * block : 3 * block + 3]
            at = slice(start % BLOCK, start % BLOCK + TILE)
            column = jnp.exp(decay[:, start : start + TILE].T[:, head : head + 1])
            scale_log = jnp.zeros((1, 1), F32)
            for earlier in range(block):
                end = (earlier + 1) * BLOCK
                scale_log = scale_log + decay[head : head + 1, end - 1 : end]
            prior = (jnp.exp(scale_log) * state + before[block, span, :].astype(F32)).astype(BF16)
            retained = intra[at, span] + column * mm(q[at, span], prior)
            center = retained - jnp.mean(retained, axis=1, keepdims=True)
            spread = jnp.mean(center * center, axis=1, keepdims=True)
            value = gate[at, span].astype(F32)
            silu = value / (1.0 + jnp.exp(-value))
            out[:, span] = (silu * center * lax.rsqrt(spread + 1e-5)).astype(BF16)


def arrange_kernel(near_first, near_second, high_first, high_second, low_out, high_out):
    cols = near_first.shape[1]
    place, core = lax.axis_index("tp"), lax.axis_index("fsdp")
    high, low = place // 2, place % 2
    here = core == high
    same = core == low
    low_out[:, :cols] = jnp.where(here, near_second[...], near_first[...])
    low_out[:, cols:] = jnp.where(here, near_first[...], near_second[...])
    high_out[:, :cols] = jnp.where(same, high_second[...], high_first[...])
    high_out[:, cols:] = jnp.where(same, high_first[...], high_second[...])


def columns_kernel(own_first, own_second, near, high_out):
    cols = near.shape[1]
    place, core = lax.axis_index("tp"), lax.axis_index("fsdp")
    high, low = place // 2, place % 2
    near[...] = own_first[:, pl.ds(pl.multiple_of((1 - low) * cols, cols), cols)]
    at = pl.ds(pl.multiple_of(core * cols, cols), cols)
    high_out[...] = jnp.where(core == high, own_second[:, at], own_first[:, at])


def own_kernel(order, own_first, own_second, *refs):
    pieces, outs = refs[: len(order)], refs[len(order) :]
    cols = pieces[0].shape[1]
    place, core = lax.axis_index("tp"), lax.axis_index("fsdp")
    high, low = place // 2, place % 2
    here = core == high
    mine = pl.ds(pl.multiple_of(low * cols, cols), cols)
    flipped = pl.ds(pl.multiple_of((1 - low) * cols, cols), cols)
    keep = jnp.where(here, own_first[:, mine], own_second[:, mine])
    gives = [
        jnp.where(here, own_second[:, mine], own_first[:, mine]),
        jnp.where(here, own_first[:, flipped], own_second[:, flipped]),
    ]
    for (half, number), piece in zip(order, pieces):
        at = slice(number * TILE, (number + 1) * TILE)
        outs[half][at, :cols] = mm(piece[...], gives[half])
        outs[half][at, cols:] = mm(piece[...], keep)


def give_kernel(number, own, far, weight, out):
    cols = out.shape[1]
    at = slice(number * TILE, (number + 1) * TILE)
    out[...] = (own[at, :cols] + mm(far[...], weight[:, :cols])).astype(BF16)


def keep_kernel(order, *refs):
    count = len(order)
    fars, owns, weights, outs = refs[:count], refs[count : count + 2], refs[count + 2 : count + 4], refs[count + 4 :]
    for (half, number), far in zip(order, fars):
        cols = far.shape[1]
        at = slice(number * TILE, (number + 1) * TILE)
        outs[half][at, :] = owns[half][at, cols:] + mm(far[...], weights[half][:, cols:])


def finish_kernel(order, *refs):
    gots, keeps, out = refs[: len(order)], refs[len(order) : -1], refs[-1]
    for (half, number), got in zip(order, gots):
        keep = keeps[half]
        at = slice(number * TILE, (number + 1) * TILE)
        value = keep[at, :] + got[...].astype(F32)
        start = half * keep.shape[0] + number * TILE
        out[0, start : start + TILE, :] = value.astype(BF16)


def after(value, *others):
    return lax.optimization_barrier((value, *others))[0]


def on_device(tokens, query_weight, key_weight, value_weight, gate_weight, out_weight, log_decay):
    x = tokens[0]
    rows, width = x.shape
    part, cols = query_weight.shape
    heads = cols // DH
    blocks = rows // BLOCK
    ctx, tp, cores = lax.axis_size("ctx"), lax.axis_size("tp"), lax.axis_size("fsdp")
    assert tp == 4 and cores == 2 and ctx >= 4 and ctx & (ctx - 1) == 0
    near_mask, far_mask = 1, 2
    tables = [((2, rows // FINE, DH // 2), F32), ((2, FINE, DH // 2), F32)]

    key_far = swap(key_weight, "fsdp", 1)
    value_far = swap(value_weight, "fsdp", 1)

    x_own, acc_k, acc_v, decay, coarse, fine, out_first, own_q, own_g = loading_call(
        key_value_own_kernel,
        [((rows, part), BF16), ((rows, cols), F32), ((rows, cols), F32), ((8, rows), F32)]
        + tables
        + [(out_weight.shape, BF16), ((part, cols), BF16), ((part, cols), BF16)],
        [x, key_weight, value_weight, log_decay[0].T, out_weight, query_weight, gate_weight],
        [],
        [pltpu.VMEM((part, cols), BF16)] * 2 + [pltpu.VMEM((heads, rows), F32)],
        rows // TILE + 6,
        "key_value_own",
    )
    message_shape, state_shape = (DH + EXTRA, DH), (DH, DH)
    x_other, keys, values, before, *states = loading_call(
        functools.partial(key_value_kernel, heads),
        [
            ((rows, part), BF16),
            ((rows, cols), BF16),
            ((rows, cols), BF16),
            ((blocks, heads * DH, DH), BF16),
        ]
        + [(state_shape, F32)] * heads
        + [(message_shape, BF16)] * heads,
        [x],
        [key_far, value_far, acc_k, acc_v, decay, coarse, fine],
        [],
        rows // TILE,
        "key_value",
    )
    windows, messages = states[:heads], states[heads:]
    last_message = messages[-1]

    entering = [None] * heads
    hop = 1
    while True:
        arrivals = [swap(message, "ctx", hop) for message in messages]
        if 2 * hop >= ctx:
            break
        for head in range(heads):
            old = [] if entering[head] is None else [entering[head]]
            windows[head], entering[head], messages[head] = kernel_call(
                functools.partial(combine_kernel, hop, not old),
                [(state_shape, F32), ((DH + 8, DH), F32), (message_shape, BF16)],
                [windows[head], messages[head], *old, arrivals[head]],
                "combine",
            )
        hop *= 2

    far_q, far_g = swap(own_q, "fsdp", 1), swap(own_g, "fsdp", 1)
    own_second = swap(out_first, "fsdp", 1)
    for_near, for_high = kernel_call(
        columns_kernel,
        [((cols, cols), BF16)] * 2,
        [after(out_first, last_message), own_second],
        "columns",
    )
    near_first = swap(for_near, "tp", near_mask)
    high_first = swap(for_high, "tp", far_mask)

    held, projected = after(decay, *messages), []
    for block in range(blocks):
        projected += kernel_call(
            functools.partial(query_gate_kernel, heads, block),
            [((BLOCK, cols), BF16), ((BLOCK, cols), BF16), ((BLOCK, cols), F32)],
            [x_own, x_other, own_q, far_q, own_g, far_g, held, coarse, fine, keys, values],
            "query_gate",
        )
    count = rows // 2 // TILE
    masks = (near_mask, far_mask)
    hidden, far = [[], []], [[], []]
    for number in range(count):
        held = after(decay, swap(pair[2], "fsdp", 1)) if number else decay
        pair = kernel_call(
            functools.partial(hidden_kernel, heads, hop, [(half * count + number) * TILE for half in range(2)]),
            [((TILE, cols), BF16)] * 2 + [((16, 128), BF16)],
            [held, before, *entering, *arrivals, *projected],
            "hidden",
        )
        if number == 0:
            near_second = swap(after(near_first, pair[0]), "fsdp", 1)
            high_second = swap(after(high_first, pair[0]), "fsdp", 1)
        for half in range(2):
            hidden[half].append(pair[half])
            far[half].append(swap(pair[half], "tp", masks[half]))
    weights = kernel_call(
        arrange_kernel,
        [((cols, 2 * cols), BF16)] * 2,
        [near_first, near_second, high_first, high_second],
        "arrange",
    )
    order = [(half, number) for number in reversed(range(count)) for half in (1, 0)]
    owns = kernel_call(
        functools.partial(own_kernel, order),
        [((count * TILE, 2 * cols), F32)] * 2,
        [out_first, own_second, *(hidden[half][number] for half, number in order)],
        "own_products",
    )
    gots = []
    for half, number in order:
        [give] = kernel_call(
            functools.partial(give_kernel, number),
            [((TILE, cols), BF16)],
            [owns[half], far[half][number], weights[half]],
            "give",
        )
        gots.append(swap(give, "tp", masks[1 - half]))
    keeps = kernel_call(
        functools.partial(keep_kernel, order),
        [((count * TILE, cols), F32)] * 2,
        [*(far[half][number] for half, number in order), *owns, *weights],
        "keep",
    )
    arrays = [pltpu.with_memory_space_constraint(array, pltpu.VMEM) for array in (*gots, *keeps)]
    return pl.pallas_call(
        functools.partial(finish_kernel, order),
        in_specs=[pl.BlockSpec(memory_space=pltpu.VMEM)] * len(arrays),
        out_specs=pl.BlockSpec(memory_space=pltpu.VMEM),
        out_shape=jax.ShapeDtypeStruct((1, rows, cols), BF16),
        compiler_params=pltpu.CompilerParams(vmem_limit_bytes=VMEM_LIMIT),
        name="finish",
    )(*arrays)


def solution(mesh):
    in_specs = (
        P("fsdp", "ctx", None),
        P("fsdp", "tp"),
        P("fsdp", "tp"),
        P("fsdp", "tp"),
        P("fsdp", "tp"),
        P("tp", "fsdp"),
        P("fsdp", "ctx", "tp"),
    )
    out_specs = P("fsdp", "ctx", "tp")
    return jax.shard_map(
        on_device, mesh=mesh, in_specs=in_specs, out_specs=out_specs, check_vma=False
    )
```

```python
import functools
import math

import jax
import jax.numpy as jnp
from jax import lax
from jax.experimental import pallas as pl
from jax.experimental.pallas import tpu as pltpu
from jax.sharding import PartitionSpec as P

DH = 256
BLOCK = 512
TILE = 256
FINE = 32
EXTRA = 16
VMEM_LIMIT = 14 * 1024 * 1024
F32 = jnp.float32
BF16 = jnp.bfloat16


def mm(left, right):
    return jnp.dot(left, right, preferred_element_type=F32)


def mm_nt(left, right):
    return lax.dot_general(left, right, (((1,), (1,)), ((), ())), preferred_element_type=F32)


def mm_tn(left, right):
    return lax.dot_general(left, right, (((0,), (0,)), ((), ())), preferred_element_type=F32)


def swap(value, axis, mask):
    size = lax.axis_size(axis)
    return lax.ppermute(value, axis, [(place, place ^ mask) for place in range(size)])


def kernel_call(kernel, outs, operands, name):
    arrays = [pltpu.with_memory_space_constraint(array, pltpu.VMEM) for array in operands]
    return pl.pallas_call(
        kernel,
        in_specs=[pl.BlockSpec(memory_space=pltpu.VMEM)] * len(operands),
        out_specs=[pl.BlockSpec(memory_space=pltpu.VMEM)] * len(outs),
        out_shape=[pltpu.VMEM(shape, dtype) for shape, dtype in outs],
        compiler_params=pltpu.CompilerParams(vmem_limit_bytes=VMEM_LIMIT),
        cost_estimate=pl.CostEstimate(
            flops=1, bytes_accessed=1, transcendentals=0
        ),
        name=name,
    )(*arrays)


def loading_call(kernel, outs, loaded, operands, scratch, loads, name):
    arrays = [pltpu.with_memory_space_constraint(array, pltpu.HBM) for array in loaded]
    arrays += [pltpu.with_memory_space_constraint(array, pltpu.VMEM) for array in operands]
    return pl.pallas_call(
        kernel,
        in_specs=[pl.BlockSpec(memory_space=pltpu.HBM)] * len(loaded)
        + [pl.BlockSpec(memory_space=pltpu.VMEM)] * len(operands),
        out_specs=[pl.BlockSpec(memory_space=pltpu.VMEM)] * len(outs),
        out_shape=[pltpu.VMEM(shape, dtype) for shape, dtype in outs],
        scratch_shapes=[*scratch, pltpu.SemaphoreType.DMA((loads,))],
        compiler_params=pltpu.CompilerParams(vmem_limit_bytes=VMEM_LIMIT),
        cost_estimate=pl.CostEstimate(flops=1, bytes_accessed=1, transcendentals=0),
        name=name,
    )(*arrays)


def turned(values, cosine, sine):
    half = DH // 2
    parts = []
    for start in range(0, values.shape[1], DH):
        low = values[:, start : start + half]
        high = values[:, start + half : start + DH]
        parts.append((low * cosine - high * sine).astype(BF16))
        parts.append((high * cosine + low * sine).astype(BF16))
    return jnp.concatenate(parts, axis=1)


def angles(coarse, fine, first, count):
    at = first // FINE
    far = coarse[:, pl.ds(at, count // FINE), :]
    near = fine[...]
    cos_c, sin_c = far[0][:, None, :], far[1][:, None, :]
    cos_f, sin_f = near[0][None], near[1][None]
    cosine = cos_c * cos_f - sin_c * sin_f
    sine = sin_c * cos_f + cos_c * sin_f
    return cosine.reshape(count, DH // 2), sine.reshape(count, DH // 2)


def decay_sums(log_decay, decay):
    heads, rows = log_decay.shape
    place_s = lax.broadcasted_iota(jnp.int32, (BLOCK, BLOCK), 0)
    place_t = lax.broadcasted_iota(jnp.int32, (BLOCK, BLOCK), 1)
    upper = jnp.where(place_s <= place_t, 1.0, 0.0).astype(BF16)
    value = jnp.concatenate([log_decay[...], jnp.zeros((8 - heads, rows), F32)], axis=0)
    parts = []
    for _ in range(3):
        parts.append(value.astype(BF16))
        value = value - parts[-1].astype(F32)
    stacked = jnp.concatenate([part.astype(F32) for part in parts], axis=0).astype(BF16)
    for start in range(0, rows, BLOCK):
        sums = mm(stacked[:, start : start + BLOCK], upper)
        decay[:, start : start + BLOCK] = sums[:8] + sums[8:16] + sums[16:]


def angle_tables(coarse, fine):
    half = DH // 2

    def fill(table, start, stride):
        count = table.shape[1]
        place = lax.broadcasted_iota(jnp.int32, (count, half), 0) * stride + start
        index = lax.broadcasted_iota(jnp.int32, (count, half), 1).astype(F32)
        angle = place.astype(F32) * jnp.exp(index * (-math.log(10000.0) / half))
        table[0] = jnp.cos(angle)
        table[1] = jnp.sin(angle)

    fill(coarse, lax.axis_index("ctx") * coarse.shape[1] * FINE, FINE)
    fill(fine, 0, 1)


class Loads:
    def __init__(self, arrived):
        self.arrived, self.count = arrived, 0

    def start(self, source, target):
        copy = pltpu.make_async_copy(source, target, self.arrived.at[self.count])
        self.count += 1
        copy.start()
        return copy


def key_value_own_kernel(
    x_far, wk_far, wv_far, log_decay_far, wo_far,
    x_own, x_other, acc_k, acc_v, decay, coarse, fine, wo, wk, wv, log_decay, arrived,
):
    rows, part = x_own.shape
    core = lax.axis_index("fsdp")
    loads = Loads(arrived)

    def tile(x, half, number):
        at = pl.ds(number * TILE, TILE)
        columns = pl.ds(pl.multiple_of(half * part, part), part)
        return loads.start(x_far.at[at, columns], x.at[at])

    count = rows // TILE
    logs = loads.start(log_decay_far, log_decay)
    key, tiles = loads.start(wk_far, wk), [tile(x_own, core, 0)]
    value = loads.start(wv_far, wv)
    angle_tables(coarse, fine)
    logs.wait()
    decay_sums(log_decay, decay)
    key.wait()
    others = []
    for number in range(count):
        at = slice(number * TILE, (number + 1) * TILE)
        tiles[number].wait()
        if number == 0:
            tiles += [tile(x_own, core, later) for later in range(1, count)]
        else:
            others += [tile(x_other, 1 - core, later) for later in range(count) if later % (count - 1) == number - 1]
            if number == count - 1:
                others.append(loads.start(wo_far, wo))
        acc_k[at, :] = mm(x_own[at, :], wk[...])
        if number == 0:
            value.wait()
        acc_v[at, :] = mm(x_own[at, :], wv[...])
    for copy in others:
        copy.wait()


def pack_message(message, states, logs):
    heads = len(states)
    place = lax.broadcasted_iota(jnp.int32, (EXTRA, DH), 0)
    tail = jnp.zeros((EXTRA, DH), F32)
    for head in range(heads):
        message[head * DH : (head + 1) * DH, :] = states[head].astype(BF16)
        rest = logs[head]
        for number in range(3):
            piece = rest.astype(BF16).astype(F32)
            tail = jnp.where(place == 3 * head + number, piece, tail)
            rest = rest - piece
    message[heads * DH :, :] = tail.astype(BF16)


def message_log(message, heads, head):
    tail = message[heads * DH :, :].astype(F32)
    return (tail[3 * head : 3 * head + 1] + tail[3 * head + 1 : 3 * head + 2] + tail[3 * head + 2 : 3 * head + 3])[:, :1]


def exchanges(ctx, hop):
    lower = range(ctx - hop)
    early = [at for at in lower if at < hop // 2]
    even = [at for at in lower if at >= hop // 2 and at // hop % 2 == 0]
    odd = [at for at in lower if at // hop % 2 == 1]
    return early, even, odd


def is_upper(lowers, hop):
    place = lax.axis_index("ctx")
    found = place < 0
    for lower in lowers:
        found = jnp.logical_or(found, place == lower + hop)
    return found


def arrived_state(arrivals, sets, hop, span):
    parts = [jnp.where(is_upper(lowers, hop), ref[span, :].astype(F32), 0.0) for ref, lowers in zip(arrivals, sets)]
    return functools.reduce(lambda a, b: a + b, parts)


def arrived_log(arrivals, sets, hop, heads, head):
    parts = [jnp.where(is_upper(lowers, hop), message_log(ref, heads, head), 0.0) for ref, lowers in zip(arrivals, sets)]
    return functools.reduce(lambda a, b: a + b, parts)


def key_value_kernel(
    heads, wq_far, wg_far, x, wk, wv, acc_k, acc_v, decay, coarse, fine,
    wq, wg, k_out, v_out, before_out, state_out, message, arrived,
):
    loads = Loads(arrived)
    others = [loads.start(wq_far, wq), loads.start(wg_far, wg)]
    state_out[...] = jnp.zeros_like(state_out)

    def block_step(block, totals):
        start = pl.multiple_of(block * BLOCK, BLOCK)
        columns = decay[:, pl.ds(start, BLOCK)].T
        ending = columns[BLOCK - 1 : BLOCK, :]
        faded = jnp.exp(ending - columns)
        updates = [None] * heads
        for piece in range(BLOCK // TILE):
            first = pl.multiple_of(start + piece * TILE, TILE)
            at = pl.ds(first, TILE)
            cosine, sine = angles(coarse, fine, first, TILE)
            keys = turned(acc_k[at, :] + mm(x[at, :], wk[...]), cosine, sine)
            values = (acc_v[at, :] + mm(x[at, :], wv[...])).astype(BF16)
            k_out[at, :] = keys
            v_out[at, :] = values
            for head in range(heads):
                span = slice(head * DH, (head + 1) * DH)
                fade = faded[piece * TILE : (piece + 1) * TILE, head : head + 1]
                weighted = (keys[:, span].astype(F32) * fade).astype(BF16)
                update = mm_tn(weighted, values[:, span])
                updates[head] = update if piece == 0 else updates[head] + update
        for head in range(heads):
            span = slice(head * DH, (head + 1) * DH)
            old = state_out[span, :]
            before_out[block, span, :] = old.astype(BF16)
            state_out[span, :] = jnp.exp(ending[:, head : head + 1]) * old + updates[head]
        return totals + ending

    totals = lax.fori_loop(0, x.shape[0] // BLOCK, block_step, jnp.zeros((1, 8), F32))
    states = [state_out[head * DH : (head + 1) * DH, :] for head in range(heads)]
    pack_message(message, states, [totals[:, head : head + 1] for head in range(heads)])
    for copy in others:
        copy.wait()


def combine_kernel(heads, hop, sets, first, state, sent, *refs):
    if not first:
        old_entering, refs = refs[0], refs[1:]
    arrivals = refs[: len(sets)]
    window, entering, message = refs[len(sets) :]
    states, logs = [], []
    for head in range(heads):
        span = slice(head * DH, (head + 1) * DH)
        row = slice(heads * DH + head, heads * DH + head + 1)
        arrived = arrived_state(arrivals, sets, hop, span)
        log = arrived_log(arrivals, sets, hop, heads, head)
        window_log = message_log(sent, heads, head)
        if first:
            entering[span, :] = arrived
            entering_log = log
        else:
            before_log = old_entering[row, :1]
            entering[span, :] = old_entering[span, :] + jnp.exp(before_log) * arrived
            entering_log = before_log + log
        entering[row, :] = jnp.broadcast_to(entering_log, (1, DH))
        new = state[span, :] + jnp.exp(window_log) * arrived
        window[span, :] = new
        states.append(new)
        logs.append(window_log + log)
    pack_message(message, states, logs)


def query_gate_kernel(
    heads, block, x_own, x_other, wq, wq_far, wg, wg_far, decay, coarse, fine, k, v, q_out, g_out, intra_out
):
    start = block * BLOCK
    lines = decay[:, start : start + BLOCK]
    columns = lines.T

    def project(piece, carry):
        first = pl.multiple_of(start + piece * TILE, TILE)
        at = pl.ds(pl.multiple_of(piece * TILE, TILE), TILE)
        own, far = x_own[pl.ds(first, TILE), :], x_other[pl.ds(first, TILE), :]
        cosine, sine = angles(coarse, fine, first, TILE)
        q_out[at, :] = turned(mm(own, wq[...]) + mm(far, wq_far[...]), cosine, sine)
        g_out[at, :] = (mm(own, wg[...]) + mm(far, wg_far[...])).astype(BF16)
        return carry

    lax.fori_loop(0, BLOCK // TILE, project, 0)
    for piece in range(BLOCK // TILE):
        low, last = piece * TILE, (piece + 1) * TILE
        place_t = lax.broadcasted_iota(jnp.int32, (TILE, last), 0) + low
        place_s = lax.broadcasted_iota(jnp.int32, (TILE, last), 1)
        causal = place_t >= place_s
        for head in range(heads):
            span = slice(head * DH, (head + 1) * DH)
            scores = mm_nt(q_out[low:last, span], k[start : start + last, span])
            differ = columns[low:last, head : head + 1] - lines[head : head + 1, :last]
            weights = jnp.where(causal, jnp.exp(jnp.where(causal, differ, 0.0)), 0.0)
            intra_out[low:last, span] = mm((scores * weights).astype(BF16), v[start : start + last, span])


def hidden_kernel(heads, hop, sets, starts, decay, before, entering, *refs):
    arrivals, refs, token = refs[: len(sets)], refs[len(sets) : -1], refs[-1]
    projected, outs = refs[: -len(starts)], refs[-len(starts) :]
    token[...] = jnp.zeros_like(token)
    for head in range(heads):
        span = slice(head * DH, (head + 1) * DH)
        entering_log = entering[heads * DH + head : heads * DH + head + 1, :1]
        state = entering[span, :] + jnp.exp(entering_log) * arrived_state(arrivals, sets, hop, span)
        for start, out in zip(starts, outs):
            block = start // BLOCK
            q, gate, intra = projected[3 * block : 3 * block + 3]
            at = slice(start % BLOCK, start % BLOCK + TILE)
            column = jnp.exp(decay[:, start : start + TILE].T[:, head : head + 1])
            scale_log = jnp.zeros((1, 1), F32)
            for earlier in range(block):
                end = (earlier + 1) * BLOCK
                scale_log = scale_log + decay[head : head + 1, end - 1 : end]
            prior = (jnp.exp(scale_log) * state + before[block, span, :].astype(F32)).astype(BF16)
            retained = intra[at, span] + column * mm(q[at, span], prior)
            center = retained - jnp.mean(retained, axis=1, keepdims=True)
            spread = jnp.mean(center * center, axis=1, keepdims=True)
            value = gate[at, span].astype(F32)
            silu = value / (1.0 + jnp.exp(-value))
            out[:, span] = (silu * center * lax.rsqrt(spread + 1e-5)).astype(BF16)


def arrange_kernel(near_first, near_second, high_first, high_second, low_out, high_out):
    cols = near_first.shape[1]
    place, core = lax.axis_index("tp"), lax.axis_index("fsdp")
    high, low = place // 2, place % 2
    here = core == high
    same = core == low
    low_out[:, :cols] = jnp.where(here, near_second[...], near_first[...])
    low_out[:, cols:] = jnp.where(here, near_first[...], near_second[...])
    high_out[:, :cols] = jnp.where(same, high_second[...], high_first[...])
    high_out[:, cols:] = jnp.where(same, high_first[...], high_second[...])


def columns_kernel(own_first, own_second, near, high_out):
    cols = near.shape[1]
    place, core = lax.axis_index("tp"), lax.axis_index("fsdp")
    high, low = place // 2, place % 2
    near[...] = own_first[:, pl.ds(pl.multiple_of((1 - low) * cols, cols), cols)]
    at = pl.ds(pl.multiple_of(core * cols, cols), cols)
    high_out[...] = jnp.where(core == high, own_second[:, at], own_first[:, at])


def own_kernel(order, own_first, own_second, *refs):
    pieces, outs = refs[: len(order)], refs[len(order) :]
    cols = pieces[0].shape[1]
    place, core = lax.axis_index("tp"), lax.axis_index("fsdp")
    high, low = place // 2, place % 2
    here = core == high
    mine = pl.ds(pl.multiple_of(low * cols, cols), cols)
    flipped = pl.ds(pl.multiple_of((1 - low) * cols, cols), cols)
    keep = jnp.where(here, own_first[:, mine], own_second[:, mine])
    gives = [
        jnp.where(here, own_second[:, mine], own_first[:, mine]),
        jnp.where(here, own_first[:, flipped], own_second[:, flipped]),
    ]
    for (half, number), piece in zip(order, pieces):
        at = slice(number * TILE, (number + 1) * TILE)
        outs[half][at, :cols] = mm(piece[...], gives[half])
        outs[half][at, cols:] = mm(piece[...], keep)


def give_kernel(number, own, far, weight, out):
    cols = out.shape[1]
    at = slice(number * TILE, (number + 1) * TILE)
    out[...] = (own[at, :cols] + mm(far[...], weight[:, :cols])).astype(BF16)


def keep_kernel(order, *refs):
    count = len(order)
    fars, owns, weights, outs = refs[:count], refs[count : count + 2], refs[count + 2 : count + 4], refs[count + 4 :]
    for (half, number), far in zip(order, fars):
        cols = far.shape[1]
        at = slice(number * TILE, (number + 1) * TILE)
        outs[half][at, :] = owns[half][at, cols:] + mm(far[...], weights[half][:, cols:])


def finish_kernel(order, *refs):
    gots, keeps, out = refs[: len(order)], refs[len(order) : -1], refs[-1]
    for (half, number), got in zip(order, gots):
        keep = keeps[half]
        at = slice(number * TILE, (number + 1) * TILE)
        value = keep[at, :] + got[...].astype(F32)
        start = half * keep.shape[0] + number * TILE
        out[0, start : start + TILE, :] = value.astype(BF16)


def after(value, *others):
    return lax.optimization_barrier((value, *others))[0]


def on_device(tokens, query_weight, key_weight, value_weight, gate_weight, out_weight, log_decay):
    x = tokens[0]
    rows, width = x.shape
    part, cols = query_weight.shape
    heads = cols // DH
    blocks = rows // BLOCK
    ctx, tp, cores = lax.axis_size("ctx"), lax.axis_size("tp"), lax.axis_size("fsdp")
    assert tp == 4 and cores == 2 and ctx >= 4 and ctx & (ctx - 1) == 0
    near_mask, far_mask = 1, 2
    tables = [((2, rows // FINE, DH // 2), F32), ((2, FINE, DH // 2), F32)]

    key_far = swap(key_weight, "fsdp", 1)
    value_far = swap(value_weight, "fsdp", 1)

    x_own, x_other, acc_k, acc_v, decay, coarse, fine, out_first = loading_call(
        key_value_own_kernel,
        [((rows, part), BF16)] * 2
        + [((rows, cols), F32)] * 2
        + [((8, rows), F32)]
        + tables
        + [(out_weight.shape, BF16)],
        [x, key_weight, value_weight, log_decay[0].T, out_weight],
        [],
        [pltpu.VMEM((part, cols), BF16)] * 2 + [pltpu.VMEM((heads, rows), F32)],
        2 * (rows // TILE) + 4,
        "key_value_own",
    )
    state_shape, message_shape = (heads * DH, DH), (heads * DH + EXTRA, DH)
    own_q, own_g, keys, values, before, window, message = loading_call(
        functools.partial(key_value_kernel, heads),
        [((part, cols), BF16)] * 2
        + [((rows, cols), BF16)] * 2
        + [((blocks, heads * DH, DH), BF16), (state_shape, F32), (message_shape, BF16)],
        [query_weight, gate_weight],
        [x_other, key_far, value_far, acc_k, acc_v, decay, coarse, fine],
        [],
        2,
        "key_value",
    )

    def exchange(message, lowers, hop):
        return lax.ppermute(
            message, "ctx", [pair for at in lowers for pair in ((at, at + hop), (at + hop, at))]
        )

    entering, hop, early, last_message = None, 1, [], message
    while True:
        first_set, *later_sets = exchanges(ctx, hop)
        later_sets = [lowers for lowers in later_sets if lowers]
        sets = later_sets + ([first_set] if first_set else [])
        arrivals = [exchange(message, lowers, hop) for lowers in later_sets] + early
        if 2 * hop >= ctx:
            break
        unchanged = exchanges(ctx, 2 * hop)[0]
        early = [exchange(message, unchanged, 2 * hop)]
        old = [] if entering is None else [entering]
        window, entering, message = kernel_call(
            functools.partial(combine_kernel, heads, hop, sets, entering is None),
            [(state_shape, F32), ((heads * DH + 8, DH), F32), (message_shape, BF16)],
            [window, message, *old, *arrivals],
            "combine",
        )
        hop *= 2

    far_q, far_g = swap(own_q, "fsdp", 1), swap(own_g, "fsdp", 1)
    own_second = swap(out_first, "fsdp", 1)
    for_near, for_high = kernel_call(
        columns_kernel,
        [((cols, cols), BF16)] * 2,
        [after(out_first, last_message), own_second],
        "columns",
    )
    near_first = swap(for_near, "tp", near_mask)
    high_first = swap(for_high, "tp", far_mask)

    held, projected = after(decay, message), []
    for block in range(blocks):
        projected += kernel_call(
            functools.partial(query_gate_kernel, heads, block),
            [((BLOCK, cols), BF16), ((BLOCK, cols), BF16), ((BLOCK, cols), F32)],
            [x_own, x_other, own_q, far_q, own_g, far_g, held, coarse, fine, keys, values],
            "query_gate",
        )
    count = rows // 2 // TILE
    masks = (near_mask, far_mask)
    hidden, far = [[], []], [[], []]
    for number in range(count):
        held = after(decay, swap(pair[2], "fsdp", 1)) if number else decay
        pair = kernel_call(
            functools.partial(hidden_kernel, heads, hop, sets, [(half * count + number) * TILE for half in range(2)]),
            [((TILE, cols), BF16)] * 2 + [((16, 128), BF16)],
            [held, before, entering, *arrivals, *projected],
            "hidden",
        )
        if number == 0:
            near_second = swap(after(near_first, pair[0]), "fsdp", 1)
            high_second = swap(after(high_first, pair[0]), "fsdp", 1)
        for half in range(2):
            hidden[half].append(pair[half])
            far[half].append(swap(pair[half], "tp", masks[half]))
    weights = kernel_call(
        arrange_kernel,
        [((cols, 2 * cols), BF16)] * 2,
        [near_first, near_second, high_first, high_second],
        "arrange",
    )
    order = [(half, number) for number in reversed(range(count)) for half in (1, 0)]
    owns = kernel_call(
        functools.partial(own_kernel, order),
        [((count * TILE, 2 * cols), F32)] * 2,
        [out_first, own_second, *(hidden[half][number] for half, number in order)],
        "own_products",
    )
    gots = []
    for half, number in order:
        [give] = kernel_call(
            functools.partial(give_kernel, number),
            [((TILE, cols), BF16)],
            [owns[half], far[half][number], weights[half]],
            "give",
        )
        gots.append(swap(give, "tp", masks[1 - half]))
    keeps = kernel_call(
        functools.partial(keep_kernel, order),
        [((count * TILE, cols), F32)] * 2,
        [*(far[half][number] for half, number in order), *owns, *weights],
        "keep",
    )
    arrays = [pltpu.with_memory_space_constraint(array, pltpu.VMEM) for array in (*gots, *keeps)]
    return pl.pallas_call(
        functools.partial(finish_kernel, order),
        in_specs=[pl.BlockSpec(memory_space=pltpu.VMEM)] * len(arrays),
        out_specs=pl.BlockSpec(memory_space=pltpu.VMEM),
        out_shape=jax.ShapeDtypeStruct((1, rows, cols), BF16),
        compiler_params=pltpu.CompilerParams(vmem_limit_bytes=VMEM_LIMIT),
        name="finish",
    )(*arrays)


def solution(mesh):
    in_specs = (
        P("fsdp", "ctx", None),
        P("fsdp", "tp"),
        P("fsdp", "tp"),
        P("fsdp", "tp"),
        P("fsdp", "tp"),
        P("tp", "fsdp"),
        P("fsdp", "ctx", "tp"),
    )
    out_specs = P("fsdp", "ctx", "tp")
    return jax.shard_map(
        on_device, mesh=mesh, in_specs=in_specs, out_specs=out_specs, check_vma=False
    )
```

```python
import functools
import math

import jax
import jax.numpy as jnp
from jax import lax
from jax.experimental import pallas as pl
from jax.experimental.pallas import tpu as pltpu
from jax.sharding import PartitionSpec as P

DH = 256
BLOCK = 512
TILE = 256
FINE = 32
EXTRA = 16
VMEM_LIMIT = 14 * 1024 * 1024
F32 = jnp.float32
BF16 = jnp.bfloat16


def mm(left, right):
    return jnp.dot(left, right, preferred_element_type=F32)


def mm_nt(left, right):
    return lax.dot_general(left, right, (((1,), (1,)), ((), ())), preferred_element_type=F32)


def mm_tn(left, right):
    return lax.dot_general(left, right, (((0,), (0,)), ((), ())), preferred_element_type=F32)


def swap(value, axis, mask):
    size = lax.axis_size(axis)
    return lax.ppermute(value, axis, [(place, place ^ mask) for place in range(size)])


def kernel_call(kernel, outs, operands, name):
    arrays = [pltpu.with_memory_space_constraint(array, pltpu.VMEM) for array in operands]
    return pl.pallas_call(
        kernel,
        in_specs=[pl.BlockSpec(memory_space=pltpu.VMEM)] * len(operands),
        out_specs=[pl.BlockSpec(memory_space=pltpu.VMEM)] * len(outs),
        out_shape=[pltpu.VMEM(shape, dtype) for shape, dtype in outs],
        compiler_params=pltpu.CompilerParams(vmem_limit_bytes=VMEM_LIMIT),
        cost_estimate=pl.CostEstimate(
            flops=1, bytes_accessed=1, transcendentals=0
        ),
        name=name,
    )(*arrays)


def loading_call(kernel, outs, loaded, operands, scratch, loads, name):
    arrays = [pltpu.with_memory_space_constraint(array, pltpu.HBM) for array in loaded]
    arrays += [pltpu.with_memory_space_constraint(array, pltpu.VMEM) for array in operands]
    return pl.pallas_call(
        kernel,
        in_specs=[pl.BlockSpec(memory_space=pltpu.HBM)] * len(loaded)
        + [pl.BlockSpec(memory_space=pltpu.VMEM)] * len(operands),
        out_specs=[pl.BlockSpec(memory_space=pltpu.VMEM)] * len(outs),
        out_shape=[pltpu.VMEM(shape, dtype) for shape, dtype in outs],
        scratch_shapes=[*scratch, pltpu.SemaphoreType.DMA((loads,))],
        compiler_params=pltpu.CompilerParams(vmem_limit_bytes=VMEM_LIMIT),
        cost_estimate=pl.CostEstimate(flops=1, bytes_accessed=1, transcendentals=0),
        name=name,
    )(*arrays)


def turned(values, cosine, sine):
    half = DH // 2
    parts = []
    for start in range(0, values.shape[1], DH):
        low = values[:, start : start + half]
        high = values[:, start + half : start + DH]
        parts.append((low * cosine - high * sine).astype(BF16))
        parts.append((high * cosine + low * sine).astype(BF16))
    return jnp.concatenate(parts, axis=1)


def angles(coarse, fine, first, count):
    at = first // FINE
    far = coarse[:, pl.ds(at, count // FINE), :]
    near = fine[...]
    cos_c, sin_c = far[0][:, None, :], far[1][:, None, :]
    cos_f, sin_f = near[0][None], near[1][None]
    cosine = cos_c * cos_f - sin_c * sin_f
    sine = sin_c * cos_f + cos_c * sin_f
    return cosine.reshape(count, DH // 2), sine.reshape(count, DH // 2)


def decay_sums(log_decay, decay):
    heads, rows = log_decay.shape
    place_s = lax.broadcasted_iota(jnp.int32, (BLOCK, BLOCK), 0)
    place_t = lax.broadcasted_iota(jnp.int32, (BLOCK, BLOCK), 1)
    upper = jnp.where(place_s <= place_t, 1.0, 0.0).astype(BF16)
    value = jnp.concatenate([log_decay[...], jnp.zeros((8 - heads, rows), F32)], axis=0)
    parts = []
    for _ in range(3):
        parts.append(value.astype(BF16))
        value = value - parts[-1].astype(F32)
    stacked = jnp.concatenate([part.astype(F32) for part in parts], axis=0).astype(BF16)
    for start in range(0, rows, BLOCK):
        sums = mm(stacked[:, start : start + BLOCK], upper)
        decay[:, start : start + BLOCK] = sums[:8] + sums[8:16] + sums[16:]


def angle_tables(coarse, fine):
    half = DH // 2

    def fill(table, start, stride):
        count = table.shape[1]
        place = lax.broadcasted_iota(jnp.int32, (count, half), 0) * stride + start
        index = lax.broadcasted_iota(jnp.int32, (count, half), 1).astype(F32)
        angle = place.astype(F32) * jnp.exp(index * (-math.log(10000.0) / half))
        table[0] = jnp.cos(angle)
        table[1] = jnp.sin(angle)

    fill(coarse, lax.axis_index("ctx") * coarse.shape[1] * FINE, FINE)
    fill(fine, 0, 1)


class Loads:
    def __init__(self, arrived):
        self.arrived, self.count = arrived, 0

    def start(self, source, target):
        copy = pltpu.make_async_copy(source, target, self.arrived.at[self.count])
        self.count += 1
        copy.start()
        return copy


def key_value_own_kernel(
    x_far, wk_far, wv_far, log_decay_far, x_own, x_other, acc_k, acc_v, decay, coarse, fine, wk, wv, log_decay, arrived
):
    rows, part = x_own.shape
    core = lax.axis_index("fsdp")
    loads = Loads(arrived)

    def tile(x, half, start):
        columns = pl.ds(pl.multiple_of(half * part, part), part)
        return loads.start(x_far.at[pl.ds(start, TILE), columns], x.at[pl.ds(start, TILE)])

    logs = loads.start(log_decay_far, log_decay)
    key, tiles = loads.start(wk_far, wk), [tile(x_own, core, 0)]
    value = loads.start(wv_far, wv)
    tiles += [tile(x_own, core, start) for start in range(TILE, rows, TILE)]
    others = [tile(x_other, 1 - core, start) for start in range(0, rows, TILE)]
    angle_tables(coarse, fine)
    logs.wait()
    decay_sums(log_decay, decay)
    key.wait()
    for number, copy in enumerate(tiles):
        at = slice(number * TILE, (number + 1) * TILE)
        copy.wait()
        acc_k[at, :] = mm(x_own[at, :], wk[...])
        if number == 0:
            value.wait()
        acc_v[at, :] = mm(x_own[at, :], wv[...])
    for copy in others:
        copy.wait()


def pack_message(message, states, logs):
    heads = len(states)
    place = lax.broadcasted_iota(jnp.int32, (EXTRA, DH), 0)
    tail = jnp.zeros((EXTRA, DH), F32)
    for head in range(heads):
        message[head * DH : (head + 1) * DH, :] = states[head].astype(BF16)
        rest = logs[head]
        for number in range(3):
            piece = rest.astype(BF16).astype(F32)
            tail = jnp.where(place == 3 * head + number, piece, tail)
            rest = rest - piece
    message[heads * DH :, :] = tail.astype(BF16)


def message_log(message, heads, head):
    tail = message[heads * DH :, :].astype(F32)
    return (tail[3 * head : 3 * head + 1] + tail[3 * head + 1 : 3 * head + 2] + tail[3 * head + 2 : 3 * head + 3])[:, :1]


def exchanges(ctx, hop):
    lower = range(ctx - hop)
    if hop == 1:
        return [], list(lower), []
    early = [at for at in lower if at < hop // 2]
    even = [at for at in lower if at >= hop // 2 and at // hop % 2 == 0]
    odd = [at for at in lower if at // hop % 2 == 1]
    return early, even, odd


def is_upper(lowers, hop):
    place = lax.axis_index("ctx")
    found = place < 0
    for lower in lowers:
        found = jnp.logical_or(found, place == lower + hop)
    return found


def arrived_state(arrivals, sets, hop, span):
    parts = [jnp.where(is_upper(lowers, hop), ref[span, :].astype(F32), 0.0) for ref, lowers in zip(arrivals, sets)]
    return functools.reduce(lambda a, b: a + b, parts)


def arrived_log(arrivals, sets, hop, heads, head):
    parts = [jnp.where(is_upper(lowers, hop), message_log(ref, heads, head), 0.0) for ref, lowers in zip(arrivals, sets)]
    return functools.reduce(lambda a, b: a + b, parts)


def key_value_kernel(
    heads, wo_far, wq_far, wg_far, x, wk, wv, acc_k, acc_v, decay, coarse, fine,
    wo, wq, wg, k_out, v_out, before_out, state_out, message, arrived,
):
    loads = Loads(arrived)
    others = [loads.start(wo_far, wo), loads.start(wq_far, wq), loads.start(wg_far, wg)]
    state_out[...] = jnp.zeros_like(state_out)

    def block_step(block, totals):
        start = pl.multiple_of(block * BLOCK, BLOCK)
        columns = decay[:, pl.ds(start, BLOCK)].T
        ending = columns[BLOCK - 1 : BLOCK, :]
        faded = jnp.exp(ending - columns)
        updates = [None] * heads
        for piece in range(BLOCK // TILE):
            first = pl.multiple_of(start + piece * TILE, TILE)
            at = pl.ds(first, TILE)
            cosine, sine = angles(coarse, fine, first, TILE)
            keys = turned(acc_k[at, :] + mm(x[at, :], wk[...]), cosine, sine)
            values = (acc_v[at, :] + mm(x[at, :], wv[...])).astype(BF16)
            k_out[at, :] = keys
            v_out[at, :] = values
            for head in range(heads):
                span = slice(head * DH, (head + 1) * DH)
                fade = faded[piece * TILE : (piece + 1) * TILE, head : head + 1]
                weighted = (keys[:, span].astype(F32) * fade).astype(BF16)
                update = mm_tn(weighted, values[:, span])
                updates[head] = update if piece == 0 else updates[head] + update
        for head in range(heads):
            span = slice(head * DH, (head + 1) * DH)
            old = state_out[span, :]
            before_out[block, span, :] = old.astype(BF16)
            state_out[span, :] = jnp.exp(ending[:, head : head + 1]) * old + updates[head]
        return totals + ending

    totals = lax.fori_loop(0, x.shape[0] // BLOCK, block_step, jnp.zeros((1, 8), F32))
    states = [state_out[head * DH : (head + 1) * DH, :] for head in range(heads)]
    pack_message(message, states, [totals[:, head : head + 1] for head in range(heads)])
    for copy in others:
        copy.wait()


def combine_kernel(heads, hop, sets, first, state, sent, *refs):
    if not first:
        old_entering, refs = refs[0], refs[1:]
    arrivals = refs[: len(sets)]
    window, entering, message = refs[len(sets) :]
    states, logs = [], []
    for head in range(heads):
        span = slice(head * DH, (head + 1) * DH)
        row = slice(heads * DH + head, heads * DH + head + 1)
        arrived = arrived_state(arrivals, sets, hop, span)
        log = arrived_log(arrivals, sets, hop, heads, head)
        window_log = message_log(sent, heads, head)
        if first:
            entering[span, :] = arrived
            entering_log = log
        else:
            before_log = old_entering[row, :1]
            entering[span, :] = old_entering[span, :] + jnp.exp(before_log) * arrived
            entering_log = before_log + log
        entering[row, :] = jnp.broadcast_to(entering_log, (1, DH))
        new = state[span, :] + jnp.exp(window_log) * arrived
        window[span, :] = new
        states.append(new)
        logs.append(window_log + log)
    pack_message(message, states, logs)


def query_gate_kernel(
    heads, block, x_own, x_other, wq, wq_far, wg, wg_far, decay, coarse, fine, k, v, q_out, g_out, intra_out
):
    start = block * BLOCK
    lines = decay[:, start : start + BLOCK]
    columns = lines.T

    def project(piece, carry):
        first = pl.multiple_of(start + piece * TILE, TILE)
        at = pl.ds(pl.multiple_of(piece * TILE, TILE), TILE)
        own, far = x_own[pl.ds(first, TILE), :], x_other[pl.ds(first, TILE), :]
        cosine, sine = angles(coarse, fine, first, TILE)
        q_out[at, :] = turned(mm(own, wq[...]) + mm(far, wq_far[...]), cosine, sine)
        g_out[at, :] = (mm(own, wg[...]) + mm(far, wg_far[...])).astype(BF16)
        return carry

    lax.fori_loop(0, BLOCK // TILE, project, 0)
    for piece in range(BLOCK // TILE):
        low, last = piece * TILE, (piece + 1) * TILE
        place_t = lax.broadcasted_iota(jnp.int32, (TILE, last), 0) + low
        place_s = lax.broadcasted_iota(jnp.int32, (TILE, last), 1)
        causal = place_t >= place_s
        for head in range(heads):
            span = slice(head * DH, (head + 1) * DH)
            scores = mm_nt(q_out[low:last, span], k[start : start + last, span])
            differ = columns[low:last, head : head + 1] - lines[head : head + 1, :last]
            weights = jnp.where(causal, jnp.exp(jnp.where(causal, differ, 0.0)), 0.0)
            intra_out[low:last, span] = mm((scores * weights).astype(BF16), v[start : start + last, span])


def hidden_kernel(heads, hop, sets, starts, decay, before, entering, *refs):
    arrivals, refs, token = refs[: len(sets)], refs[len(sets) : -1], refs[-1]
    projected, outs = refs[: -len(starts)], refs[-len(starts) :]
    token[...] = jnp.zeros_like(token)
    for head in range(heads):
        span = slice(head * DH, (head + 1) * DH)
        entering_log = entering[heads * DH + head : heads * DH + head + 1, :1]
        state = entering[span, :] + jnp.exp(entering_log) * arrived_state(arrivals, sets, hop, span)
        for start, out in zip(starts, outs):
            block = start // BLOCK
            q, gate, intra = projected[3 * block : 3 * block + 3]
            at = slice(start % BLOCK, start % BLOCK + TILE)
            column = jnp.exp(decay[:, start : start + TILE].T[:, head : head + 1])
            scale_log = jnp.zeros((1, 1), F32)
            for earlier in range(block):
                end = (earlier + 1) * BLOCK
                scale_log = scale_log + decay[head : head + 1, end - 1 : end]
            prior = (jnp.exp(scale_log) * state + before[block, span, :].astype(F32)).astype(BF16)
            retained = intra[at, span] + column * mm(q[at, span], prior)
            center = retained - jnp.mean(retained, axis=1, keepdims=True)
            spread = jnp.mean(center * center, axis=1, keepdims=True)
            value = gate[at, span].astype(F32)
            silu = value / (1.0 + jnp.exp(-value))
            out[:, span] = (silu * center * lax.rsqrt(spread + 1e-5)).astype(BF16)


def arrange_kernel(near_first, near_second, high_first, high_second, low_out, high_out):
    cols = near_first.shape[1]
    place, core = lax.axis_index("tp"), lax.axis_index("fsdp")
    high, low = place // 2, place % 2
    here = core == high
    same = core == low
    low_out[:, :cols] = jnp.where(here, near_second[...], near_first[...])
    low_out[:, cols:] = jnp.where(here, near_first[...], near_second[...])
    high_out[:, :cols] = jnp.where(same, high_second[...], high_first[...])
    high_out[:, cols:] = jnp.where(same, high_first[...], high_second[...])


def columns_kernel(own_first, own_second, near, high_out):
    cols = near.shape[1]
    place, core = lax.axis_index("tp"), lax.axis_index("fsdp")
    high, low = place // 2, place % 2
    near[...] = own_first[:, pl.ds(pl.multiple_of((1 - low) * cols, cols), cols)]
    at = pl.ds(pl.multiple_of(core * cols, cols), cols)
    high_out[...] = jnp.where(core == high, own_second[:, at], own_first[:, at])


def own_kernel(order, own_first, own_second, *refs):
    pieces, outs = refs[: len(order)], refs[len(order) :]
    cols = pieces[0].shape[1]
    place, core = lax.axis_index("tp"), lax.axis_index("fsdp")
    high, low = place // 2, place % 2
    here = core == high
    mine = pl.ds(pl.multiple_of(low * cols, cols), cols)
    flipped = pl.ds(pl.multiple_of((1 - low) * cols, cols), cols)
    keep = jnp.where(here, own_first[:, mine], own_second[:, mine])
    gives = [
        jnp.where(here, own_second[:, mine], own_first[:, mine]),
        jnp.where(here, own_first[:, flipped], own_second[:, flipped]),
    ]
    for (half, number), piece in zip(order, pieces):
        at = slice(number * TILE, (number + 1) * TILE)
        outs[half][at, :cols] = mm(piece[...], gives[half])
        outs[half][at, cols:] = mm(piece[...], keep)


def give_kernel(number, own, far, weight, out):
    cols = out.shape[1]
    at = slice(number * TILE, (number + 1) * TILE)
    out[...] = (own[at, :cols] + mm(far[...], weight[:, :cols])).astype(BF16)


def keep_kernel(order, *refs):
    count = len(order)
    fars, owns, weights, outs = refs[:count], refs[count : count + 2], refs[count + 2 : count + 4], refs[count + 4 :]
    for (half, number), far in zip(order, fars):
        cols = far.shape[1]
        at = slice(number * TILE, (number + 1) * TILE)
        outs[half][at, :] = owns[half][at, cols:] + mm(far[...], weights[half][:, cols:])


def finish_kernel(order, *refs):
    gots, keeps, out = refs[: len(order)], refs[len(order) : -1], refs[-1]
    for (half, number), got in zip(order, gots):
        keep = keeps[half]
        at = slice(number * TILE, (number + 1) * TILE)
        value = keep[at, :] + got[...].astype(F32)
        start = half * keep.shape[0] + number * TILE
        out[0, start : start + TILE, :] = value.astype(BF16)


def after(value, *others):
    return lax.optimization_barrier((value, *others))[0]


def on_device(tokens, query_weight, key_weight, value_weight, gate_weight, out_weight, log_decay):
    x = tokens[0]
    rows, width = x.shape
    part, cols = query_weight.shape
    heads = cols // DH
    blocks = rows // BLOCK
    ctx, tp, cores = lax.axis_size("ctx"), lax.axis_size("tp"), lax.axis_size("fsdp")
    assert tp == 4 and cores == 2 and ctx >= 4 and ctx & (ctx - 1) == 0
    near_mask, far_mask = 1, 2
    tables = [((2, rows // FINE, DH // 2), F32), ((2, FINE, DH // 2), F32)]

    key_far = swap(key_weight, "fsdp", 1)
    value_far = swap(value_weight, "fsdp", 1)

    x_own, x_other, acc_k, acc_v, decay, coarse, fine = loading_call(
        key_value_own_kernel,
        [((rows, part), BF16)] * 2
        + [((rows, cols), F32)] * 2
        + [((8, rows), F32)]
        + tables,
        [x, key_weight, value_weight, log_decay[0].T],
        [],
        [pltpu.VMEM((part, cols), BF16)] * 2 + [pltpu.VMEM((heads, rows), F32)],
        2 * (rows // TILE) + 3,
        "key_value_own",
    )
    state_shape, message_shape = (heads * DH, DH), (heads * DH + EXTRA, DH)
    out_first, own_q, own_g, keys, values, before, window, message = loading_call(
        functools.partial(key_value_kernel, heads),
        [(out_weight.shape, BF16)]
        + [((part, cols), BF16)] * 2
        + [((rows, cols), BF16)] * 2
        + [((blocks, heads * DH, DH), BF16), (state_shape, F32), (message_shape, BF16)],
        [out_weight, query_weight, gate_weight],
        [x_other, key_far, value_far, acc_k, acc_v, decay, coarse, fine],
        [],
        3,
        "key_value",
    )

    def exchange(message, lowers, hop):
        pairs = [(at, at + hop) for at in lowers]
        if hop > 1:
            pairs += [(upper, at) for at, upper in pairs]
        return lax.ppermute(message, "ctx", pairs)

    entering, hop, early, last_message = None, 1, [], message
    while True:
        first_set, *later_sets = exchanges(ctx, hop)
        later_sets = [lowers for lowers in later_sets if lowers]
        sets = later_sets + ([first_set] if first_set else [])
        arrivals = [exchange(message, lowers, hop) for lowers in later_sets] + early
        if 2 * hop >= ctx:
            break
        unchanged = exchanges(ctx, 2 * hop)[0]
        early = [exchange(message, unchanged, 2 * hop)]
        old = [] if entering is None else [entering]
        window, entering, message = kernel_call(
            functools.partial(combine_kernel, heads, hop, sets, entering is None),
            [(state_shape, F32), ((heads * DH + 8, DH), F32), (message_shape, BF16)],
            [window, message, *old, *arrivals],
            "combine",
        )
        hop *= 2

    far_q, far_g = swap(own_q, "fsdp", 1), swap(own_g, "fsdp", 1)
    own_second = swap(out_first, "fsdp", 1)
    for_near, for_high = kernel_call(
        columns_kernel,
        [((cols, cols), BF16)] * 2,
        [after(out_first, last_message), own_second],
        "columns",
    )
    near_first = swap(for_near, "tp", near_mask)
    high_first = swap(for_high, "tp", far_mask)

    held, projected = after(decay, message, *early), []
    for block in range(blocks):
        if block == blocks - 1 and early:
            held = after(held, *early, high_first, near_first)
        projected += kernel_call(
            functools.partial(query_gate_kernel, heads, block),
            [((BLOCK, cols), BF16), ((BLOCK, cols), BF16), ((BLOCK, cols), F32)],
            [x_own, x_other, own_q, far_q, own_g, far_g, held, coarse, fine, keys, values],
            "query_gate",
        )
    count = rows // 2 // TILE
    masks = (near_mask, far_mask)
    hidden, far = [[], []], [[], []]
    for number in range(count):
        held = after(decay, swap(pair[2], "fsdp", 1)) if number else decay
        pair = kernel_call(
            functools.partial(hidden_kernel, heads, hop, sets, [(half * count + number) * TILE for half in range(2)]),
            [((TILE, cols), BF16)] * 2 + [((16, 128), BF16)],
            [held, before, entering, *arrivals, *projected],
            "hidden",
        )
        if number == 1:
            near_second = swap(after(near_first, pair[0]), "fsdp", 1)
            high_second = swap(after(high_first, pair[0]), "fsdp", 1)
        for half in range(2):
            hidden[half].append(pair[half])
            far[half].append(swap(pair[half], "tp", masks[half]))
    weights = kernel_call(
        arrange_kernel,
        [((cols, 2 * cols), BF16)] * 2,
        [near_first, near_second, high_first, high_second],
        "arrange",
    )
    order = [(half, number) for number in reversed(range(count)) for half in (1, 0)]
    owns = kernel_call(
        functools.partial(own_kernel, order),
        [((count * TILE, 2 * cols), F32)] * 2,
        [out_first, own_second, *(hidden[half][number] for half, number in order)],
        "own_products",
    )
    gots = []
    for half, number in order:
        [give] = kernel_call(
            functools.partial(give_kernel, number),
            [((TILE, cols), BF16)],
            [owns[half], far[half][number], weights[half]],
            "give",
        )
        gots.append(swap(give, "tp", masks[1 - half]))
    keeps = kernel_call(
        functools.partial(keep_kernel, order),
        [((count * TILE, cols), F32)] * 2,
        [*(far[half][number] for half, number in order), *owns, *weights],
        "keep",
    )
    arrays = [pltpu.with_memory_space_constraint(array, pltpu.VMEM) for array in (*gots, *keeps)]
    return pl.pallas_call(
        functools.partial(finish_kernel, order),
        in_specs=[pl.BlockSpec(memory_space=pltpu.VMEM)] * len(arrays),
        out_specs=pl.BlockSpec(memory_space=pltpu.VMEM),
        out_shape=jax.ShapeDtypeStruct((1, rows, cols), BF16),
        compiler_params=pltpu.CompilerParams(vmem_limit_bytes=VMEM_LIMIT),
        name="finish",
    )(*arrays)


def solution(mesh):
    in_specs = (
        P("fsdp", "ctx", None),
        P("fsdp", "tp"),
        P("fsdp", "tp"),
        P("fsdp", "tp"),
        P("fsdp", "tp"),
        P("tp", "fsdp"),
        P("fsdp", "ctx", "tp"),
    )
    out_specs = P("fsdp", "ctx", "tp")
    return jax.shard_map(
        on_device, mesh=mesh, in_specs=in_specs, out_specs=out_specs, check_vma=False
    )
```

```python
import functools
import math

import jax
import jax.numpy as jnp
from jax import lax
from jax.experimental import pallas as pl
from jax.experimental.pallas import tpu as pltpu
from jax.sharding import PartitionSpec as P

DH = 256
BLOCK = 512
TILE = 256
FINE = 32
EXTRA = 16
IN_FLIGHT = 5
VMEM_LIMIT = 14 * 1024 * 1024
F32 = jnp.float32
BF16 = jnp.bfloat16


def mm(left, right):
    return jnp.dot(left, right, preferred_element_type=F32)


def mm_nt(left, right):
    return lax.dot_general(left, right, (((1,), (1,)), ((), ())), preferred_element_type=F32)


def mm_tn(left, right):
    return lax.dot_general(left, right, (((0,), (0,)), ((), ())), preferred_element_type=F32)


def swap(value, axis, mask):
    size = lax.axis_size(axis)
    return lax.ppermute(value, axis, [(place, place ^ mask) for place in range(size)])


def kernel_call(kernel, outs, operands, name):
    arrays = [pltpu.with_memory_space_constraint(array, pltpu.VMEM) for array in operands]
    return pl.pallas_call(
        kernel,
        in_specs=[pl.BlockSpec(memory_space=pltpu.VMEM)] * len(operands),
        out_specs=[pl.BlockSpec(memory_space=pltpu.VMEM)] * len(outs),
        out_shape=[pltpu.VMEM(shape, dtype) for shape, dtype in outs],
        compiler_params=pltpu.CompilerParams(vmem_limit_bytes=VMEM_LIMIT),
        cost_estimate=pl.CostEstimate(
            flops=1, bytes_accessed=1, transcendentals=0
        ),
        name=name,
    )(*arrays)


def loading_call(kernel, outs, loaded, operands, scratch, loads, name):
    arrays = [pltpu.with_memory_space_constraint(array, pltpu.HBM) for array in loaded]
    arrays += [pltpu.with_memory_space_constraint(array, pltpu.VMEM) for array in operands]
    return pl.pallas_call(
        kernel,
        in_specs=[pl.BlockSpec(memory_space=pltpu.HBM)] * len(loaded)
        + [pl.BlockSpec(memory_space=pltpu.VMEM)] * len(operands),
        out_specs=[pl.BlockSpec(memory_space=pltpu.VMEM)] * len(outs),
        out_shape=[pltpu.VMEM(shape, dtype) for shape, dtype in outs],
        scratch_shapes=[*scratch, pltpu.SemaphoreType.DMA((loads,))],
        compiler_params=pltpu.CompilerParams(vmem_limit_bytes=VMEM_LIMIT),
        cost_estimate=pl.CostEstimate(flops=1, bytes_accessed=1, transcendentals=0),
        name=name,
    )(*arrays)


def turned(values, cosine, sine):
    half = DH // 2
    parts = []
    for start in range(0, values.shape[1], DH):
        low = values[:, start : start + half]
        high = values[:, start + half : start + DH]
        parts.append((low * cosine - high * sine).astype(BF16))
        parts.append((high * cosine + low * sine).astype(BF16))
    return jnp.concatenate(parts, axis=1)


def angles(coarse, fine, first, count):
    at = first // FINE
    far = coarse[:, pl.ds(at, count // FINE), :]
    near = fine[...]
    cos_c, sin_c = far[0][:, None, :], far[1][:, None, :]
    cos_f, sin_f = near[0][None], near[1][None]
    cosine = cos_c * cos_f - sin_c * sin_f
    sine = sin_c * cos_f + cos_c * sin_f
    return cosine.reshape(count, DH // 2), sine.reshape(count, DH // 2)


def decay_sums(log_decay, decay):
    heads, rows = log_decay.shape
    place_s = lax.broadcasted_iota(jnp.int32, (BLOCK, BLOCK), 0)
    place_t = lax.broadcasted_iota(jnp.int32, (BLOCK, BLOCK), 1)
    upper = jnp.where(place_s <= place_t, 1.0, 0.0).astype(BF16)
    value = jnp.concatenate([log_decay[...], jnp.zeros((8 - heads, rows), F32)], axis=0)
    parts = []
    for _ in range(3):
        parts.append(value.astype(BF16))
        value = value - parts[-1].astype(F32)
    stacked = jnp.concatenate([part.astype(F32) for part in parts], axis=0).astype(BF16)
    for start in range(0, rows, BLOCK):
        sums = mm(stacked[:, start : start + BLOCK], upper)
        decay[:, start : start + BLOCK] = sums[:8] + sums[8:16] + sums[16:]


def angle_tables(coarse, fine):
    half = DH // 2

    def fill(table, start, stride):
        count = table.shape[1]
        place = lax.broadcasted_iota(jnp.int32, (count, half), 0) * stride + start
        index = lax.broadcasted_iota(jnp.int32, (count, half), 1).astype(F32)
        angle = place.astype(F32) * jnp.exp(index * (-math.log(10000.0) / half))
        table[0] = jnp.cos(angle)
        table[1] = jnp.sin(angle)

    fill(coarse, lax.axis_index("ctx") * coarse.shape[1] * FINE, FINE)
    fill(fine, 0, 1)


class Loads:
    def __init__(self, arrived):
        self.arrived, self.count = arrived, 0

    def start(self, source, target):
        copy = pltpu.make_async_copy(source, target, self.arrived.at[self.count])
        self.count += 1
        copy.start()
        return copy


def key_value_own_kernel(
    x_far, wk_far, wv_far, log_decay_far, wo_far,
    x_own, x_other, acc_k, acc_v, decay, coarse, fine, wo, wk, wv, log_decay, arrived,
):
    rows, part = x_own.shape
    core = lax.axis_index("fsdp")
    loads = Loads(arrived)

    def tile(x, half, start):
        columns = pl.ds(pl.multiple_of(half * part, part), part)
        return functools.partial(loads.start, x_far.at[pl.ds(start, TILE), columns], x.at[pl.ds(start, TILE)])

    starts = range(0, rows, TILE)
    half = part // 2
    queue = [functools.partial(loads.start, log_decay_far, log_decay)]
    queue += [functools.partial(loads.start, wk_far.at[pl.ds(at, half)], wk.at[pl.ds(at, half)]) for at in (0, half)]
    queue += [tile(x_own, core, start) for start in starts]
    queue += [functools.partial(loads.start, wv_far.at[pl.ds(at, half)], wv.at[pl.ds(at, half)]) for at in (0, half)]
    queue += [tile(x_other, 1 - core, start) for start in starts]
    queue += [functools.partial(loads.start, wo_far, wo)]
    flight, done = [], 0

    def fill(limit):
        while len(flight) < min(len(queue), done + limit):
            flight.append(queue[len(flight)]())

    def need(count):
        nonlocal done
        while done < count:
            flight[done].wait()
            done += 1
            fill(IN_FLIGHT)

    fill(IN_FLIGHT)
    angle_tables(coarse, fine)
    need(1)
    decay_sums(log_decay, decay)
    for number, start in enumerate(starts):
        need(4 + number)
        at = slice(start, start + TILE)
        acc_k[at, :] = mm(x_own[at, :], wk[...])
    need(5 + len(starts))
    for start in starts:
        at = slice(start, start + TILE)
        acc_v[at, :] = mm(x_own[at, :], wv[...])
        need(min(len(queue), done + 2))
    need(len(queue))


def pack_message(message, states, logs):
    heads = len(states)
    place = lax.broadcasted_iota(jnp.int32, (EXTRA, DH), 0)
    tail = jnp.zeros((EXTRA, DH), F32)
    for head in range(heads):
        message[head * DH : (head + 1) * DH, :] = states[head].astype(BF16)
        rest = logs[head]
        for number in range(3):
            piece = rest.astype(BF16).astype(F32)
            tail = jnp.where(place == 3 * head + number, piece, tail)
            rest = rest - piece
    message[heads * DH :, :] = tail.astype(BF16)


def message_log(message, heads, head):
    tail = message[heads * DH :, :].astype(F32)
    return (tail[3 * head : 3 * head + 1] + tail[3 * head + 1 : 3 * head + 2] + tail[3 * head + 2 : 3 * head + 3])[:, :1]


def exchanges(ctx, hop):
    lower = range(ctx - hop)
    if hop == 1:
        return [], list(lower), []
    early = [at for at in lower if at < hop // 2]
    even = [at for at in lower if at >= hop // 2 and at // hop % 2 == 0]
    odd = [at for at in lower if at // hop % 2 == 1]
    return early, even, odd


def is_upper(lowers, hop):
    place = lax.axis_index("ctx")
    found = place < 0
    for lower in lowers:
        found = jnp.logical_or(found, place == lower + hop)
    return found


def arrived_state(arrivals, sets, hop, span):
    parts = [jnp.where(is_upper(lowers, hop), ref[span, :].astype(F32), 0.0) for ref, lowers in zip(arrivals, sets)]
    return functools.reduce(lambda a, b: a + b, parts)


def arrived_log(arrivals, sets, hop, heads, head):
    parts = [jnp.where(is_upper(lowers, hop), message_log(ref, heads, head), 0.0) for ref, lowers in zip(arrivals, sets)]
    return functools.reduce(lambda a, b: a + b, parts)


def key_value_kernel(
    heads, wq_far, wg_far, x, wk, wv, acc_k, acc_v, decay, coarse, fine, wqg,
    k_out, v_out, before_out, state_out, message, arrived,
):
    loads = Loads(arrived)
    part = wk.shape[0]
    others = [loads.start(far, wqg.at[pl.ds(at, part)]) for far, at in ((wq_far, 0), (wg_far, part))]
    state_out[...] = jnp.zeros_like(state_out)

    def block_step(block, totals):
        start = pl.multiple_of(block * BLOCK, BLOCK)
        columns = decay[:, pl.ds(start, BLOCK)].T
        ending = columns[BLOCK - 1 : BLOCK, :]
        faded = jnp.exp(ending - columns)
        updates = [None] * heads
        for piece in range(BLOCK // TILE):
            first = pl.multiple_of(start + piece * TILE, TILE)
            at = pl.ds(first, TILE)
            cosine, sine = angles(coarse, fine, first, TILE)
            keys = turned(acc_k[at, :] + mm(x[at, :], wk[...]), cosine, sine)
            values = (acc_v[at, :] + mm(x[at, :], wv[...])).astype(BF16)
            k_out[at, :] = keys
            v_out[at, :] = values
            for head in range(heads):
                span = slice(head * DH, (head + 1) * DH)
                fade = faded[piece * TILE : (piece + 1) * TILE, head : head + 1]
                weighted = (keys[:, span].astype(F32) * fade).astype(BF16)
                update = mm_tn(weighted, values[:, span])
                updates[head] = update if piece == 0 else updates[head] + update
        for head in range(heads):
            span = slice(head * DH, (head + 1) * DH)
            old = state_out[span, :]
            before_out[block, span, :] = old.astype(BF16)
            state_out[span, :] = jnp.exp(ending[:, head : head + 1]) * old + updates[head]
        return totals + ending

    totals = lax.fori_loop(0, x.shape[0] // BLOCK, block_step, jnp.zeros((1, 8), F32))
    states = [state_out[head * DH : (head + 1) * DH, :] for head in range(heads)]
    pack_message(message, states, [totals[:, head : head + 1] for head in range(heads)])
    for copy in others:
        copy.wait()


def combine_kernel(heads, hop, sets, first, state, sent, *refs):
    if not first:
        old_entering, refs = refs[0], refs[1:]
    arrivals = refs[: len(sets)]
    window, entering, message = refs[len(sets) :]
    states, logs = [], []
    for head in range(heads):
        span = slice(head * DH, (head + 1) * DH)
        row = slice(heads * DH + head, heads * DH + head + 1)
        arrived = arrived_state(arrivals, sets, hop, span)
        log = arrived_log(arrivals, sets, hop, heads, head)
        window_log = message_log(sent, heads, head)
        if first:
            entering[span, :] = arrived
            entering_log = log
        else:
            before_log = old_entering[row, :1]
            entering[span, :] = old_entering[span, :] + jnp.exp(before_log) * arrived
            entering_log = before_log + log
        entering[row, :] = jnp.broadcast_to(entering_log, (1, DH))
        new = state[span, :] + jnp.exp(window_log) * arrived
        window[span, :] = new
        states.append(new)
        logs.append(window_log + log)
    pack_message(message, states, logs)


def query_gate_kernel(
    heads, block, x_own, x_other, wqg, wqg_far, decay, coarse, fine, k, v, q_out, g_out, intra_out
):
    part = x_own.shape[1]
    start = block * BLOCK
    lines = decay[:, start : start + BLOCK]
    columns = lines.T

    def project(piece, carry):
        first = pl.multiple_of(start + piece * TILE, TILE)
        at = pl.ds(pl.multiple_of(piece * TILE, TILE), TILE)
        own, far = x_own[pl.ds(first, TILE), :], x_other[pl.ds(first, TILE), :]
        cosine, sine = angles(coarse, fine, first, TILE)
        q_out[at, :] = turned(mm(own, wqg[:part, :]) + mm(far, wqg_far[:part, :]), cosine, sine)
        g_out[at, :] = (mm(own, wqg[part:, :]) + mm(far, wqg_far[part:, :])).astype(BF16)
        return carry

    lax.fori_loop(0, BLOCK // TILE, project, 0)
    for piece in range(BLOCK // TILE):
        low, last = piece * TILE, (piece + 1) * TILE
        place_t = lax.broadcasted_iota(jnp.int32, (TILE, last), 0) + low
        place_s = lax.broadcasted_iota(jnp.int32, (TILE, last), 1)
        causal = place_t >= place_s
        for head in range(heads):
            span = slice(head * DH, (head + 1) * DH)
            scores = mm_nt(q_out[low:last, span], k[start : start + last, span])
            differ = columns[low:last, head : head + 1] - lines[head : head + 1, :last]
            weights = jnp.where(causal, jnp.exp(jnp.where(causal, differ, 0.0)), 0.0)
            intra_out[low:last, span] = mm((scores * weights).astype(BF16), v[start : start + last, span])


def hidden_kernel(heads, hop, sets, starts, decay, before, entering, *refs):
    arrivals, refs, token = refs[: len(sets)], refs[len(sets) : -1], refs[-1]
    projected, outs = refs[: -len(starts)], refs[-len(starts) :]
    token[...] = jnp.zeros_like(token)
    for head in range(heads):
        span = slice(head * DH, (head + 1) * DH)
        entering_log = entering[heads * DH + head : heads * DH + head + 1, :1]
        state = entering[span, :] + jnp.exp(entering_log) * arrived_state(arrivals, sets, hop, span)
        for start, out in zip(starts, outs):
            block = start // BLOCK
            q, gate, intra = projected[3 * block : 3 * block + 3]
            at = slice(start % BLOCK, start % BLOCK + TILE)
            column = jnp.exp(decay[:, start : start + TILE].T[:, head : head + 1])
            scale_log = jnp.zeros((1, 1), F32)
            for earlier in range(block):
                end = (earlier + 1) * BLOCK
                scale_log = scale_log + decay[head : head + 1, end - 1 : end]
            prior = (jnp.exp(scale_log) * state + before[block, span, :].astype(F32)).astype(BF16)
            retained = intra[at, span] + column * mm(q[at, span], prior)
            center = retained - jnp.mean(retained, axis=1, keepdims=True)
            spread = jnp.mean(center * center, axis=1, keepdims=True)
            value = gate[at, span].astype(F32)
            silu = value / (1.0 + jnp.exp(-value))
            out[:, span] = (silu * center * lax.rsqrt(spread + 1e-5)).astype(BF16)


def columns_kernel(first, second, out):
    cols = out.shape[1] // 2
    place, core = lax.axis_index("tp"), lax.axis_index("fsdp")
    high, low = place // 2, place % 2

    @pl.when(core == 0)
    def _():
        at = pl.ds(pl.multiple_of((1 - low) * cols, cols), cols)
        out[:, :cols] = first[:, at]
        out[:, cols:] = second[:, at]

    @pl.when(core == 1)
    def _():
        out[...] = jnp.where(high == 0, first[...], second[...])


def arrange_kernel(mine, other, low_out, high_out):
    cols = mine.shape[1] // 2
    place, core = lax.axis_index("tp"), lax.axis_index("fsdp")
    for gathered, bit, out in ((core == 0, place // 2, low_out), (core == 1, place % 2, high_out)):
        give = pl.ds(pl.multiple_of((1 - bit) * cols, cols), cols)
        keep = pl.ds(pl.multiple_of(bit * cols, cols), cols)
        out[:, :cols] = jnp.where(gathered, mine[:, give], other[:, give])
        out[:, cols:] = jnp.where(gathered, mine[:, keep], other[:, keep])


def own_kernel(order, own_first, own_second, *refs):
    pieces, outs = refs[: len(order)], refs[len(order) :]
    cols = pieces[0].shape[1]
    place, core = lax.axis_index("tp"), lax.axis_index("fsdp")
    high, low = place // 2, place % 2
    here = core == high
    mine = pl.ds(pl.multiple_of(low * cols, cols), cols)
    flipped = pl.ds(pl.multiple_of((1 - low) * cols, cols), cols)
    keep = jnp.where(here, own_first[:, mine], own_second[:, mine])
    gives = [
        jnp.where(here, own_second[:, mine], own_first[:, mine]),
        jnp.where(here, own_first[:, flipped], own_second[:, flipped]),
    ]
    for (half, number), piece in zip(order, pieces):
        at = slice(number * TILE, (number + 1) * TILE)
        outs[half][at, :cols] = mm(piece[...], gives[half])
        outs[half][at, cols:] = mm(piece[...], keep)


def give_kernel(number, own, far, weight, out):
    cols = out.shape[1]
    at = slice(number * TILE, (number + 1) * TILE)
    out[...] = (own[at, :cols] + mm(far[...], weight[:, :cols])).astype(BF16)


def keep_kernel(order, *refs):
    count = len(order)
    fars, owns, weights, outs = refs[:count], refs[count : count + 2], refs[count + 2 : count + 4], refs[count + 4 :]
    for (half, number), far in zip(order, fars):
        cols = far.shape[1]
        at = slice(number * TILE, (number + 1) * TILE)
        outs[half][at, :] = owns[half][at, cols:] + mm(far[...], weights[half][:, cols:])


def finish_kernel(order, *refs):
    gots, keeps, out = refs[: len(order)], refs[len(order) : -1], refs[-1]
    for (half, number), got in zip(order, gots):
        keep = keeps[half]
        at = slice(number * TILE, (number + 1) * TILE)
        value = keep[at, :] + got[...].astype(F32)
        start = half * keep.shape[0] + number * TILE
        out[0, start : start + TILE, :] = value.astype(BF16)


def after(value, *others):
    return lax.optimization_barrier((value, *others))[0]


def on_device(tokens, query_weight, key_weight, value_weight, gate_weight, out_weight, log_decay):
    x = tokens[0]
    rows, width = x.shape
    part, cols = query_weight.shape
    heads = cols // DH
    blocks = rows // BLOCK
    ctx, tp, cores = lax.axis_size("ctx"), lax.axis_size("tp"), lax.axis_size("fsdp")
    assert tp == 4 and cores == 2 and ctx >= 4 and ctx & (ctx - 1) == 0
    near_mask, far_mask = 1, 2
    tables = [((2, rows // FINE, DH // 2), F32), ((2, FINE, DH // 2), F32)]

    key_far = swap(key_weight, "fsdp", 1)
    value_far = swap(value_weight, "fsdp", 1)

    x_own, x_other, acc_k, acc_v, decay, coarse, fine, out_first = loading_call(
        key_value_own_kernel,
        [((rows, part), BF16)] * 2
        + [((rows, cols), F32)] * 2
        + [((8, rows), F32)]
        + tables
        + [(out_weight.shape, BF16)],
        [x, key_weight, value_weight, log_decay[0].T, out_weight],
        [],
        [pltpu.VMEM((part, cols), BF16)] * 2 + [pltpu.VMEM((heads, rows), F32)],
        2 * (rows // TILE) + 6,
        "key_value_own",
    )
    state_shape, message_shape = (heads * DH, DH), (heads * DH + EXTRA, DH)
    own_qg, keys, values, before, window, message = loading_call(
        functools.partial(key_value_kernel, heads),
        [((2 * part, cols), BF16)]
        + [((rows, cols), BF16)] * 2
        + [((blocks, heads * DH, DH), BF16), (state_shape, F32), (message_shape, BF16)],
        [query_weight, gate_weight],
        [x_other, key_far, value_far, acc_k, acc_v, decay, coarse, fine],
        [],
        2,
        "key_value",
    )

    def exchange(message, lowers, hop):
        pairs = [(at, at + hop) for at in lowers]
        if hop > 1:
            pairs += [(upper, at) for at, upper in pairs]
        return lax.ppermute(message, "ctx", pairs)

    entering, hop, early, message_sent = None, 1, [], message
    while True:
        first_set, *later_sets = exchanges(ctx, hop)
        later_sets = [lowers for lowers in later_sets if lowers]
        sets = later_sets + ([first_set] if first_set else [])
        arrivals = [exchange(message, lowers, hop) for lowers in later_sets] + early
        if 2 * hop >= ctx:
            break
        unchanged = exchanges(ctx, 2 * hop)[0]
        early = [exchange(message, unchanged, 2 * hop)]
        old = [] if entering is None else [entering]
        window, entering, message = kernel_call(
            functools.partial(combine_kernel, heads, hop, sets, entering is None),
            [(state_shape, F32), ((heads * DH + 8, DH), F32), (message_shape, BF16)],
            [window, message, *old, *arrivals],
            "combine",
        )
        hop *= 2

    far_qg = swap(own_qg, "fsdp", 1)
    own_second = swap(out_first, "fsdp", 1)
    [for_partner] = kernel_call(
        columns_kernel,
        [(out_weight.shape, BF16)],
        [out_first, own_second],
        "columns",
    )
    pairs = [(at * cores + at_core, (at ^ mask) * cores + at_core) for at in range(tp) for at_core, mask in enumerate((near_mask, far_mask))]
    out_mine = lax.ppermute(for_partner, ("tp", "fsdp"), pairs)

    held, projected = after(decay, message), []
    for block in range(blocks):
        if block == blocks - 1 and early:
            held = after(held, *early, out_mine)
        projected += kernel_call(
            functools.partial(query_gate_kernel, heads, block),
            [((BLOCK, cols), BF16), ((BLOCK, cols), BF16), ((BLOCK, cols), F32)],
            [x_own, x_other, own_qg, far_qg, held, coarse, fine, keys, values],
            "query_gate",
        )
    count = rows // 2 // TILE
    masks = (near_mask, far_mask)
    hidden, far = [[], []], [[], []]
    for number in range(count):
        held = after(decay, swap(pair[2], "fsdp", 1)) if number else decay
        pair = kernel_call(
            functools.partial(hidden_kernel, heads, hop, sets, [(half * count + number) * TILE for half in range(2)]),
            [((TILE, cols), BF16)] * 2 + [((16, 128), BF16)],
            [held, before, entering, *arrivals, *projected],
            "hidden",
        )
        if number == 1:
            out_other = swap(after(out_mine, pair[0]), "fsdp", 1)
        for half in range(2):
            hidden[half].append(pair[half])
            far[half].append(swap(pair[half], "tp", masks[half]))
    weights = kernel_call(
        arrange_kernel,
        [((cols, 2 * cols), BF16)] * 2,
        [out_mine, out_other],
        "arrange",
    )
    order = [(half, number) for number in reversed(range(count)) for half in (1, 0)]
    owns = kernel_call(
        functools.partial(own_kernel, order),
        [((count * TILE, 2 * cols), F32)] * 2,
        [out_first, own_second, *(hidden[half][number] for half, number in order)],
        "own_products",
    )
    gots = []
    for half, number in order:
        [give] = kernel_call(
            functools.partial(give_kernel, number),
            [((TILE, cols), BF16)],
            [owns[half], far[half][number], weights[half]],
            "give",
        )
        gots.append(swap(give, "tp", masks[1 - half]))
    keeps = kernel_call(
        functools.partial(keep_kernel, order),
        [((count * TILE, cols), F32)] * 2,
        [*(far[half][number] for half, number in order), *owns, *weights],
        "keep",
    )
    arrays = [pltpu.with_memory_space_constraint(array, pltpu.VMEM) for array in (*gots, *keeps)]
    return pl.pallas_call(
        functools.partial(finish_kernel, order),
        in_specs=[pl.BlockSpec(memory_space=pltpu.VMEM)] * len(arrays),
        out_specs=pl.BlockSpec(memory_space=pltpu.VMEM),
        out_shape=jax.ShapeDtypeStruct((1, rows, cols), BF16),
        compiler_params=pltpu.CompilerParams(vmem_limit_bytes=VMEM_LIMIT),
        name="finish",
    )(*arrays)


def solution(mesh):
    in_specs = (
        P("fsdp", "ctx", None),
        P("fsdp", "tp"),
        P("fsdp", "tp"),
        P("fsdp", "tp"),
        P("fsdp", "tp"),
        P("tp", "fsdp"),
        P("fsdp", "ctx", "tp"),
    )
    out_specs = P("fsdp", "ctx", "tp")
    return jax.shard_map(
        on_device, mesh=mesh, in_specs=in_specs, out_specs=out_specs, check_vma=False
    )
```

```python
import functools
import math

import jax
import jax.numpy as jnp
from jax import lax
from jax.experimental import pallas as pl
from jax.experimental.pallas import tpu as pltpu
from jax.sharding import PartitionSpec as P

DH = 256
BLOCK = 512
TILE = 256
FINE = 32
EXTRA = 16
VMEM_LIMIT = 14 * 1024 * 1024
F32 = jnp.float32
BF16 = jnp.bfloat16


def mm(left, right):
    return jnp.dot(left, right, preferred_element_type=F32)


def mm_nt(left, right):
    return lax.dot_general(left, right, (((1,), (1,)), ((), ())), preferred_element_type=F32)


def mm_tn(left, right):
    return lax.dot_general(left, right, (((0,), (0,)), ((), ())), preferred_element_type=F32)


def swap(value, axis, mask):
    size = lax.axis_size(axis)
    return lax.ppermute(value, axis, [(place, place ^ mask) for place in range(size)])


def kernel_call(kernel, outs, operands, name):
    arrays = [pltpu.with_memory_space_constraint(array, pltpu.VMEM) for array in operands]
    return pl.pallas_call(
        kernel,
        in_specs=[pl.BlockSpec(memory_space=pltpu.VMEM)] * len(operands),
        out_specs=[pl.BlockSpec(memory_space=pltpu.VMEM)] * len(outs),
        out_shape=[pltpu.VMEM(shape, dtype) for shape, dtype in outs],
        compiler_params=pltpu.CompilerParams(vmem_limit_bytes=VMEM_LIMIT),
        cost_estimate=pl.CostEstimate(
            flops=1, bytes_accessed=1, transcendentals=0
        ),
        name=name,
    )(*arrays)


def loading_call(kernel, outs, loaded, operands, scratch, loads, name):
    arrays = [pltpu.with_memory_space_constraint(array, pltpu.HBM) for array in loaded]
    arrays += [pltpu.with_memory_space_constraint(array, pltpu.VMEM) for array in operands]
    return pl.pallas_call(
        kernel,
        in_specs=[pl.BlockSpec(memory_space=pltpu.HBM)] * len(loaded)
        + [pl.BlockSpec(memory_space=pltpu.VMEM)] * len(operands),
        out_specs=[pl.BlockSpec(memory_space=pltpu.VMEM)] * len(outs),
        out_shape=[pltpu.VMEM(shape, dtype) for shape, dtype in outs],
        scratch_shapes=[*scratch, pltpu.SemaphoreType.DMA((loads,))],
        compiler_params=pltpu.CompilerParams(vmem_limit_bytes=VMEM_LIMIT),
        cost_estimate=pl.CostEstimate(flops=1, bytes_accessed=1, transcendentals=0),
        name=name,
    )(*arrays)


def turned(values, cosine, sine):
    half = DH // 2
    parts = []
    for start in range(0, values.shape[1], DH):
        low = values[:, start : start + half]
        high = values[:, start + half : start + DH]
        parts.append((low * cosine - high * sine).astype(BF16))
        parts.append((high * cosine + low * sine).astype(BF16))
    return jnp.concatenate(parts, axis=1)


def angles(coarse, fine, first, count):
    at = first // FINE
    far = coarse[:, pl.ds(at, count // FINE), :]
    near = fine[...]
    cos_c, sin_c = far[0][:, None, :], far[1][:, None, :]
    cos_f, sin_f = near[0][None], near[1][None]
    cosine = cos_c * cos_f - sin_c * sin_f
    sine = sin_c * cos_f + cos_c * sin_f
    return cosine.reshape(count, DH // 2), sine.reshape(count, DH // 2)


def decay_sums(log_decay, decay):
    heads, rows = log_decay.shape
    place_s = lax.broadcasted_iota(jnp.int32, (BLOCK, BLOCK), 0)
    place_t = lax.broadcasted_iota(jnp.int32, (BLOCK, BLOCK), 1)
    upper = jnp.where(place_s <= place_t, 1.0, 0.0).astype(BF16)
    value = jnp.concatenate([log_decay[...], jnp.zeros((8 - heads, rows), F32)], axis=0)
    parts = []
    for _ in range(3):
        parts.append(value.astype(BF16))
        value = value - parts[-1].astype(F32)
    stacked = jnp.concatenate([part.astype(F32) for part in parts], axis=0).astype(BF16)
    for start in range(0, rows, BLOCK):
        sums = mm(stacked[:, start : start + BLOCK], upper)
        decay[:, start : start + BLOCK] = sums[:8] + sums[8:16] + sums[16:]


def turn(first, second):
    (cos_a, sin_a), (cos_b, sin_b) = first, second
    return cos_a * cos_b - sin_a * sin_b, sin_a * cos_b + cos_a * sin_b


def joined(first, second):
    return tuple(jnp.concatenate(pair, axis=0) for pair in zip(first, second))


def angle_tables(coarse, fine):
    half, seeds = DH // 2, 8
    index = lax.broadcasted_iota(jnp.int32, (seeds, half), 1).astype(F32)
    frequency = jnp.exp(index * (-math.log(10000.0) / half))
    place = lax.broadcasted_iota(jnp.int32, (seeds, half), 0).astype(F32)
    offset = (lax.axis_index("ctx") * (coarse.shape[1] * FINE)).astype(F32)
    near = jnp.cos(place * frequency), jnp.sin(place * frequency)
    base = jnp.cos(offset * frequency), jnp.sin(offset * frequency)
    step = turn([part[seeds - 1 : seeds] for part in near], [part[1:2] for part in near])
    while near[0].shape[0] < FINE:
        near = joined(near, turn(near, step))
        step = turn(step, step)
    far = tuple(part[:1] for part in base)
    while far[0].shape[0] < coarse.shape[1]:
        far = joined(far, turn(far, step))
        step = turn(step, step)
    for table, parts in ((coarse, far), (fine, near)):
        table[0], table[1] = (part[: table.shape[1]] for part in parts)


class Loads:
    def __init__(self, arrived):
        self.arrived, self.count = arrived, 0

    def start(self, source, target):
        copy = pltpu.make_async_copy(source, target, self.arrived.at[self.count])
        self.count += 1
        copy.start()
        return copy


def key_value_own_kernel(
    x_far, wk_far, wv_far, log_decay_far, wo_far, wq_far, wg_far,
    x_own, x_other, acc_k, acc_v, decay, coarse, fine, wo, wq, wg, wk, wv, log_decay, arrived,
):
    rows, part = x_own.shape
    core = lax.axis_index("fsdp")
    loads = Loads(arrived)

    def tile(x, half, start):
        columns = pl.ds(pl.multiple_of(half * part, part), part)
        return loads.start(x_far.at[pl.ds(start, TILE), columns], x.at[pl.ds(start, TILE)])

    starts = range(0, rows, TILE)
    logs, key = loads.start(log_decay_far, log_decay), loads.start(wk_far, wk)
    tiles = [tile(x_own, core, start) for start in starts]
    value = loads.start(wv_far, wv)
    others = [tile(x_other, 1 - core, start) for start in starts]
    others += [loads.start(wo_far, wo), loads.start(wq_far, wq), loads.start(wg_far, wg)]
    angle_tables(coarse, fine)
    logs.wait()
    decay_sums(log_decay, decay)
    key.wait()
    for copy, start in zip(tiles, starts):
        at = slice(start, start + TILE)
        copy.wait()
        acc_k[at, :] = mm(x_own[at, :], wk[...])
    value.wait()
    for start in starts:
        at = slice(start, start + TILE)
        acc_v[at, :] = mm(x_own[at, :], wv[...])
    for copy in others:
        copy.wait()


def pack_message(message, states, logs):
    heads = len(states)
    place = lax.broadcasted_iota(jnp.int32, (EXTRA, DH), 0)
    tail = jnp.zeros((EXTRA, DH), F32)
    for head in range(heads):
        message[head * DH : (head + 1) * DH, :] = states[head].astype(BF16)
        rest = logs[head]
        for number in range(3):
            piece = rest.astype(BF16).astype(F32)
            tail = jnp.where(place == 3 * head + number, piece, tail)
            rest = rest - piece
    message[heads * DH :, :] = tail.astype(BF16)


def message_log(message, heads, head):
    tail = message[heads * DH :, :].astype(F32)
    return (tail[3 * head : 3 * head + 1] + tail[3 * head + 1 : 3 * head + 2] + tail[3 * head + 2 : 3 * head + 3])[:, :1]


def exchanges(ctx, hop):
    lower = range(ctx - hop)
    if hop == 1:
        return [], list(lower), []
    early = [at for at in lower if at < hop // 2]
    even = [at for at in lower if at >= hop // 2 and at // hop % 2 == 0]
    odd = [at for at in lower if at // hop % 2 == 1]
    return early, even, odd


def is_upper(lowers, hop):
    place = lax.axis_index("ctx")
    found = place < 0
    for lower in lowers:
        found = jnp.logical_or(found, place == lower + hop)
    return found


def arrived_state(arrivals, sets, hop, span):
    parts = [jnp.where(is_upper(lowers, hop), ref[span, :].astype(F32), 0.0) for ref, lowers in zip(arrivals, sets)]
    return functools.reduce(lambda a, b: a + b, parts)


def arrived_log(arrivals, sets, hop, heads, head):
    parts = [jnp.where(is_upper(lowers, hop), message_log(ref, heads, head), 0.0) for ref, lowers in zip(arrivals, sets)]
    return functools.reduce(lambda a, b: a + b, parts)


def key_value_kernel(
    heads, x, wk, wv, acc_k, acc_v, decay, coarse, fine, k_out, v_out, before_out, state_out, message
):
    state_out[...] = jnp.zeros_like(state_out)

    def block_step(block, totals):
        start = pl.multiple_of(block * BLOCK, BLOCK)
        columns = decay[:, pl.ds(start, BLOCK)].T
        ending = columns[BLOCK - 1 : BLOCK, :]
        faded = jnp.exp(ending - columns)
        updates = [None] * heads
        for piece in range(BLOCK // TILE):
            first = pl.multiple_of(start + piece * TILE, TILE)
            at = pl.ds(first, TILE)
            cosine, sine = angles(coarse, fine, first, TILE)
            keys = turned(acc_k[at, :] + mm(x[at, :], wk[...]), cosine, sine)
            values = (acc_v[at, :] + mm(x[at, :], wv[...])).astype(BF16)
            k_out[at, :] = keys
            v_out[at, :] = values
            for head in range(heads):
                span = slice(head * DH, (head + 1) * DH)
                fade = faded[piece * TILE : (piece + 1) * TILE, head : head + 1]
                weighted = (keys[:, span].astype(F32) * fade).astype(BF16)
                update = mm_tn(weighted, values[:, span])
                updates[head] = update if piece == 0 else updates[head] + update
        for head in range(heads):
            span = slice(head * DH, (head + 1) * DH)
            old = state_out[span, :]
            before_out[block, span, :] = old.astype(BF16)
            state_out[span, :] = jnp.exp(ending[:, head : head + 1]) * old + updates[head]
        return totals + ending

    totals = lax.fori_loop(0, x.shape[0] // BLOCK, block_step, jnp.zeros((1, 8), F32))
    states = [state_out[head * DH : (head + 1) * DH, :] for head in range(heads)]
    pack_message(message, states, [totals[:, head : head + 1] for head in range(heads)])


def combine_kernel(heads, hop, sets, first, state, sent, *refs):
    if not first:
        old_entering, refs = refs[0], refs[1:]
    arrivals = refs[: len(sets)]
    window, entering, message = refs[len(sets) :]
    states, logs = [], []
    for head in range(heads):
        span = slice(head * DH, (head + 1) * DH)
        row = slice(heads * DH + head, heads * DH + head + 1)
        arrived = arrived_state(arrivals, sets, hop, span)
        log = arrived_log(arrivals, sets, hop, heads, head)
        window_log = message_log(sent, heads, head)
        if first:
            entering[span, :] = arrived
            entering_log = log
        else:
            before_log = old_entering[row, :1]
            entering[span, :] = old_entering[span, :] + jnp.exp(before_log) * arrived
            entering_log = before_log + log
        entering[row, :] = jnp.broadcast_to(entering_log, (1, DH))
        new = state[span, :] + jnp.exp(window_log) * arrived
        window[span, :] = new
        states.append(new)
        logs.append(window_log + log)
    pack_message(message, states, logs)


def query_gate_kernel(
    heads, block, x_own, x_other, wq, wq_far, wg, wg_far, decay, coarse, fine, k, v, q_out, g_out, intra_out
):
    start = block * BLOCK
    lines = decay[:, start : start + BLOCK]
    columns = lines.T

    def project(piece, carry):
        first = pl.multiple_of(start + piece * TILE, TILE)
        at = pl.ds(pl.multiple_of(piece * TILE, TILE), TILE)
        own, far = x_own[pl.ds(first, TILE), :], x_other[pl.ds(first, TILE), :]
        cosine, sine = angles(coarse, fine, first, TILE)
        q_out[at, :] = turned(mm(own, wq[...]) + mm(far, wq_far[...]), cosine, sine)
        g_out[at, :] = (mm(own, wg[...]) + mm(far, wg_far[...])).astype(BF16)
        return carry

    lax.fori_loop(0, BLOCK // TILE, project, 0)
    for piece in range(BLOCK // TILE):
        low, last = piece * TILE, (piece + 1) * TILE
        place_t = lax.broadcasted_iota(jnp.int32, (TILE, last), 0) + low
        place_s = lax.broadcasted_iota(jnp.int32, (TILE, last), 1)
        causal = place_t >= place_s
        for head in range(heads):
            span = slice(head * DH, (head + 1) * DH)
            scores = mm_nt(q_out[low:last, span], k[start : start + last, span])
            differ = columns[low:last, head : head + 1] - lines[head : head + 1, :last]
            weights = jnp.where(causal, jnp.exp(jnp.where(causal, differ, 0.0)), 0.0)
            intra_out[low:last, span] = mm((scores * weights).astype(BF16), v[start : start + last, span])


def hidden_kernel(heads, hop, sets, starts, decay, before, entering, *refs):
    arrivals, refs, token = refs[: len(sets)], refs[len(sets) : -1], refs[-1]
    projected, outs = refs[: -len(starts)], refs[-len(starts) :]
    token[...] = jnp.zeros_like(token)
    for head in range(heads):
        span = slice(head * DH, (head + 1) * DH)
        entering_log = entering[heads * DH + head : heads * DH + head + 1, :1]
        state = entering[span, :] + jnp.exp(entering_log) * arrived_state(arrivals, sets, hop, span)
        for start, out in zip(starts, outs):
            block = start // BLOCK
            q, gate, intra = projected[3 * block : 3 * block + 3]
            at = slice(start % BLOCK, start % BLOCK + TILE)
            column = jnp.exp(decay[:, start : start + TILE].T[:, head : head + 1])
            scale_log = jnp.zeros((1, 1), F32)
            for earlier in range(block):
                end = (earlier + 1) * BLOCK
                scale_log = scale_log + decay[head : head + 1, end - 1 : end]
            prior = (jnp.exp(scale_log) * state + before[block, span, :].astype(F32)).astype(BF16)
            retained = intra[at, span] + column * mm(q[at, span], prior)
            center = retained - jnp.mean(retained, axis=1, keepdims=True)
            spread = jnp.mean(center * center, axis=1, keepdims=True)
            value = gate[at, span].astype(F32)
            silu = value / (1.0 + jnp.exp(-value))
            out[:, span] = (silu * center * lax.rsqrt(spread + 1e-5)).astype(BF16)


def columns_kernel(first, second, out):
    cols = out.shape[1] // 2
    place, core = lax.axis_index("tp"), lax.axis_index("fsdp")
    high, low = place // 2, place % 2

    @pl.when(core == 0)
    def _():
        at = pl.ds(pl.multiple_of((1 - low) * cols, cols), cols)
        out[:, :cols] = first[:, at]
        out[:, cols:] = second[:, at]

    @pl.when(core == 1)
    def _():
        out[...] = jnp.where(high == 0, first[...], second[...])


def arrange_kernel(mine, other, low_out, high_out):
    cols = mine.shape[1] // 2
    place, core = lax.axis_index("tp"), lax.axis_index("fsdp")
    for gathered, bit, out in ((core == 0, place // 2, low_out), (core == 1, place % 2, high_out)):
        give = pl.ds(pl.multiple_of((1 - bit) * cols, cols), cols)
        keep = pl.ds(pl.multiple_of(bit * cols, cols), cols)
        out[:, :cols] = jnp.where(gathered, mine[:, give], other[:, give])
        out[:, cols:] = jnp.where(gathered, mine[:, keep], other[:, keep])


def own_kernel(order, own_first, own_second, *refs):
    pieces, outs = refs[: len(order)], refs[len(order) :]
    cols = pieces[0].shape[1]
    place, core = lax.axis_index("tp"), lax.axis_index("fsdp")
    high, low = place // 2, place % 2
    here = core == high
    mine = pl.ds(pl.multiple_of(low * cols, cols), cols)
    flipped = pl.ds(pl.multiple_of((1 - low) * cols, cols), cols)
    keep = jnp.where(here, own_first[:, mine], own_second[:, mine])
    gives = [
        jnp.where(here, own_second[:, mine], own_first[:, mine]),
        jnp.where(here, own_first[:, flipped], own_second[:, flipped]),
    ]
    for (half, number), piece in zip(order, pieces):
        at = slice(number * TILE, (number + 1) * TILE)
        outs[half][at, :cols] = mm(piece[...], gives[half])
        outs[half][at, cols:] = mm(piece[...], keep)


def give_kernel(number, own, far, weight, out):
    cols = out.shape[1]
    at = slice(number * TILE, (number + 1) * TILE)
    out[...] = (own[at, :cols] + mm(far[...], weight[:, :cols])).astype(BF16)


def keep_kernel(order, *refs):
    count = len(order)
    fars, owns, weights, outs = refs[:count], refs[count : count + 2], refs[count + 2 : count + 4], refs[count + 4 :]
    for (half, number), far in zip(order, fars):
        cols = far.shape[1]
        at = slice(number * TILE, (number + 1) * TILE)
        outs[half][at, :] = owns[half][at, cols:] + mm(far[...], weights[half][:, cols:])


def finish_kernel(order, *refs):
    gots, keeps, out = refs[: len(order)], refs[len(order) : -1], refs[-1]
    for (half, number), got in zip(order, gots):
        keep = keeps[half]
        at = slice(number * TILE, (number + 1) * TILE)
        value = keep[at, :] + got[...].astype(F32)
        start = half * keep.shape[0] + number * TILE
        out[0, start : start + TILE, :] = value.astype(BF16)


def after(value, *others):
    return lax.optimization_barrier((value, *others))[0]


def on_device(tokens, query_weight, key_weight, value_weight, gate_weight, out_weight, log_decay):
    x = tokens[0]
    rows, width = x.shape
    part, cols = query_weight.shape
    heads = cols // DH
    blocks = rows // BLOCK
    ctx, tp, cores = lax.axis_size("ctx"), lax.axis_size("tp"), lax.axis_size("fsdp")
    assert tp == 4 and cores == 2 and ctx >= 4 and ctx & (ctx - 1) == 0
    near_mask, far_mask = 1, 2
    tables = [((2, rows // FINE, DH // 2), F32), ((2, FINE, DH // 2), F32)]

    key_far = swap(key_weight, "fsdp", 1)
    value_far = swap(value_weight, "fsdp", 1)

    x_own, x_other, acc_k, acc_v, decay, coarse, fine, out_first, own_q, own_g = loading_call(
        key_value_own_kernel,
        [((rows, part), BF16)] * 2
        + [((rows, cols), F32)] * 2
        + [((8, rows), F32)]
        + tables
        + [(out_weight.shape, BF16), ((part, cols), BF16), ((part, cols), BF16)],
        [x, key_weight, value_weight, log_decay[0].T, out_weight, query_weight, gate_weight],
        [],
        [pltpu.VMEM((part, cols), BF16)] * 2 + [pltpu.VMEM((heads, rows), F32)],
        2 * (rows // TILE) + 6,
        "key_value_own",
    )
    state_shape, message_shape = (heads * DH, DH), (heads * DH + EXTRA, DH)
    keys, values, before, window, message = kernel_call(
        functools.partial(key_value_kernel, heads),
        [((rows, cols), BF16)] * 2
        + [((blocks, heads * DH, DH), BF16), (state_shape, F32), (message_shape, BF16)],
        [x_other, key_far, value_far, acc_k, acc_v, decay, coarse, fine],
        "key_value",
    )
    far_q, far_g = swap(own_q, "fsdp", 1), swap(own_g, "fsdp", 1)

    def query_gate(block, decay):
        return kernel_call(
            functools.partial(query_gate_kernel, heads, block),
            [((BLOCK, cols), BF16), ((BLOCK, cols), BF16), ((BLOCK, cols), F32)],
            [x_own, x_other, own_q, far_q, own_g, far_g, decay, coarse, fine, keys, values],
            "query_gate",
        )

    def exchange(message, lowers, hop):
        pairs = [(at, at + hop) for at in lowers]
        if hop > 1:
            pairs += [(upper, at) for at, upper in pairs]
        return lax.ppermute(message, "ctx", pairs)

    projected = list(query_gate(0, decay))
    window = after(window, projected[0])
    entering, hop, early, first_message = None, 1, [], message
    while True:
        first_set, *later_sets = exchanges(ctx, hop)
        later_sets = [lowers for lowers in later_sets if lowers]
        sets = later_sets + ([first_set] if first_set else [])
        arrivals = [exchange(message, lowers, hop) for lowers in later_sets] + early
        if 2 * hop >= ctx:
            break
        unchanged = exchanges(ctx, 2 * hop)[0]
        early = [exchange(message, unchanged, 2 * hop)]
        old = [] if entering is None else [entering]
        window, entering, message = kernel_call(
            functools.partial(combine_kernel, heads, hop, sets, entering is None),
            [(state_shape, F32), ((heads * DH + 8, DH), F32), (message_shape, BF16)],
            [window, message, *old, *arrivals],
            "combine",
        )
        hop *= 2

    own_second = swap(out_first, "fsdp", 1)
    [for_partner] = kernel_call(
        columns_kernel,
        [(out_weight.shape, BF16)],
        [after(out_first, first_message), own_second],
        "columns",
    )
    pairs = [(at * cores + at_core, (at ^ mask) * cores + at_core) for at in range(tp) for at_core, mask in enumerate((near_mask, far_mask))]
    out_mine = lax.ppermute(for_partner, ("tp", "fsdp"), pairs)

    held = after(decay, message, *early)
    for block in range(1, blocks):
        projected += query_gate(block, held)

    count = rows // 2 // TILE
    masks = (near_mask, far_mask)
    hidden, far = [[], []], [[], []]
    for number in range(count):
        held = after(decay, swap(pair[2], "fsdp", 1)) if number else decay
        pair = kernel_call(
            functools.partial(hidden_kernel, heads, hop, sets, [(half * count + number) * TILE for half in range(2)]),
            [((TILE, cols), BF16)] * 2 + [((16, 128), BF16)],
            [held, before, entering, *arrivals, *projected],
            "hidden",
        )
        if number == 0:
            out_other = swap(after(out_mine, pair[0]), "fsdp", 1)
        for half in range(2):
            hidden[half].append(pair[half])
            far[half].append(swap(pair[half], "tp", masks[half]))
    weights = kernel_call(
        arrange_kernel,
        [((cols, 2 * cols), BF16)] * 2,
        [out_mine, out_other],
        "arrange",
    )
    order = [(half, number) for number in reversed(range(count)) for half in (1, 0)]
    owns = kernel_call(
        functools.partial(own_kernel, order),
        [((count * TILE, 2 * cols), F32)] * 2,
        [out_first, own_second, *(hidden[half][number] for half, number in order)],
        "own_products",
    )
    gots = []
    for half, number in order:
        [give] = kernel_call(
            functools.partial(give_kernel, number),
            [((TILE, cols), BF16)],
            [owns[half], far[half][number], weights[half]],
            "give",
        )
        gots.append(swap(give, "tp", masks[1 - half]))
    keeps = kernel_call(
        functools.partial(keep_kernel, order),
        [((count * TILE, cols), F32)] * 2,
        [*(far[half][number] for half, number in order), *owns, *weights],
        "keep",
    )
    arrays = [pltpu.with_memory_space_constraint(array, pltpu.VMEM) for array in (*gots, *keeps)]
    return pl.pallas_call(
        functools.partial(finish_kernel, order),
        in_specs=[pl.BlockSpec(memory_space=pltpu.VMEM)] * len(arrays),
        out_specs=pl.BlockSpec(memory_space=pltpu.VMEM),
        out_shape=jax.ShapeDtypeStruct((1, rows, cols), BF16),
        compiler_params=pltpu.CompilerParams(vmem_limit_bytes=VMEM_LIMIT),
        name="finish",
    )(*arrays)


def solution(mesh):
    in_specs = (
        P("fsdp", "ctx", None),
        P("fsdp", "tp"),
        P("fsdp", "tp"),
        P("fsdp", "tp"),
        P("fsdp", "tp"),
        P("tp", "fsdp"),
        P("fsdp", "ctx", "tp"),
    )
    out_specs = P("fsdp", "ctx", "tp")
    return jax.shard_map(
        on_device, mesh=mesh, in_specs=in_specs, out_specs=out_specs, check_vma=False
    )
```

```python
import functools
import math

import jax
import jax.numpy as jnp
from jax import lax
from jax.experimental import pallas as pl
from jax.experimental.pallas import tpu as pltpu
from jax.sharding import PartitionSpec as P

DH = 256
BLOCK = 512
TILE = 256
FINE = 32
EXTRA = 16
VMEM_LIMIT = 14 * 1024 * 1024
F32 = jnp.float32
BF16 = jnp.bfloat16


def mm(left, right):
    return jnp.dot(left, right, preferred_element_type=F32)


def mm_nt(left, right):
    return lax.dot_general(left, right, (((1,), (1,)), ((), ())), preferred_element_type=F32)


def mm_tn(left, right):
    return lax.dot_general(left, right, (((0,), (0,)), ((), ())), preferred_element_type=F32)


def swap(value, axis, mask):
    size = lax.axis_size(axis)
    return lax.ppermute(value, axis, [(place, place ^ mask) for place in range(size)])


def kernel_call(kernel, outs, operands, name):
    arrays = [pltpu.with_memory_space_constraint(array, pltpu.VMEM) for array in operands]
    return pl.pallas_call(
        kernel,
        in_specs=[pl.BlockSpec(memory_space=pltpu.VMEM)] * len(operands),
        out_specs=[pl.BlockSpec(memory_space=pltpu.VMEM)] * len(outs),
        out_shape=[pltpu.VMEM(shape, dtype) for shape, dtype in outs],
        compiler_params=pltpu.CompilerParams(vmem_limit_bytes=VMEM_LIMIT),
        cost_estimate=pl.CostEstimate(
            flops=1, bytes_accessed=1, transcendentals=0
        ),
        name=name,
    )(*arrays)


def loading_call(kernel, outs, loaded, operands, scratch, loads, name):
    arrays = [pltpu.with_memory_space_constraint(array, pltpu.HBM) for array in loaded]
    arrays += [pltpu.with_memory_space_constraint(array, pltpu.VMEM) for array in operands]
    return pl.pallas_call(
        kernel,
        in_specs=[pl.BlockSpec(memory_space=pltpu.HBM)] * len(loaded)
        + [pl.BlockSpec(memory_space=pltpu.VMEM)] * len(operands),
        out_specs=[pl.BlockSpec(memory_space=pltpu.VMEM)] * len(outs),
        out_shape=[pltpu.VMEM(shape, dtype) for shape, dtype in outs],
        scratch_shapes=[*scratch, pltpu.SemaphoreType.DMA((loads,))],
        compiler_params=pltpu.CompilerParams(vmem_limit_bytes=VMEM_LIMIT),
        cost_estimate=pl.CostEstimate(flops=1, bytes_accessed=1, transcendentals=0),
        name=name,
    )(*arrays)


def turned(values, cosine, sine):
    half = DH // 2
    parts = []
    for start in range(0, values.shape[1], DH):
        low = values[:, start : start + half]
        high = values[:, start + half : start + DH]
        parts.append((low * cosine - high * sine).astype(BF16))
        parts.append((high * cosine + low * sine).astype(BF16))
    return jnp.concatenate(parts, axis=1)


def angles(coarse, fine, first, count):
    at = first // FINE
    far = coarse[:, pl.ds(at, count // FINE), :]
    near = fine[...]
    cos_c, sin_c = far[0][:, None, :], far[1][:, None, :]
    cos_f, sin_f = near[0][None], near[1][None]
    cosine = cos_c * cos_f - sin_c * sin_f
    sine = sin_c * cos_f + cos_c * sin_f
    return cosine.reshape(count, DH // 2), sine.reshape(count, DH // 2)


def decay_sums(log_decay, decay):
    heads, rows = log_decay.shape
    place_s = lax.broadcasted_iota(jnp.int32, (BLOCK, BLOCK), 0)
    place_t = lax.broadcasted_iota(jnp.int32, (BLOCK, BLOCK), 1)
    upper = jnp.where(place_s <= place_t, 1.0, 0.0).astype(BF16)
    value = jnp.concatenate([log_decay[...], jnp.zeros((8 - heads, rows), F32)], axis=0)
    parts = []
    for _ in range(3):
        parts.append(value.astype(BF16))
        value = value - parts[-1].astype(F32)
    stacked = jnp.concatenate([part.astype(F32) for part in parts], axis=0).astype(BF16)
    for start in range(0, rows, BLOCK):
        sums = mm(stacked[:, start : start + BLOCK], upper)
        decay[:, start : start + BLOCK] = sums[:8] + sums[8:16] + sums[16:]


def turn(first, second):
    (cos_a, sin_a), (cos_b, sin_b) = first, second
    return cos_a * cos_b - sin_a * sin_b, sin_a * cos_b + cos_a * sin_b


def joined(first, second):
    return tuple(jnp.concatenate(pair, axis=0) for pair in zip(first, second))


def angle_tables(coarse, fine):
    half, seeds = DH // 2, 8
    index = lax.broadcasted_iota(jnp.int32, (seeds, half), 1).astype(F32)
    frequency = jnp.exp(index * (-math.log(10000.0) / half))
    place = lax.broadcasted_iota(jnp.int32, (seeds, half), 0).astype(F32)
    offset = (lax.axis_index("ctx") * (coarse.shape[1] * FINE)).astype(F32)
    near = jnp.cos(place * frequency), jnp.sin(place * frequency)
    base = jnp.cos(offset * frequency), jnp.sin(offset * frequency)
    step = turn([part[seeds - 1 : seeds] for part in near], [part[1:2] for part in near])
    while near[0].shape[0] < FINE:
        near = joined(near, turn(near, step))
        step = turn(step, step)
    far = tuple(part[:1] for part in base)
    while far[0].shape[0] < coarse.shape[1]:
        far = joined(far, turn(far, step))
        step = turn(step, step)
    for table, parts in ((coarse, far), (fine, near)):
        table[0], table[1] = (part[: table.shape[1]] for part in parts)


class Loads:
    def __init__(self, arrived):
        self.arrived, self.count = arrived, 0

    def start(self, source, target):
        copy = pltpu.make_async_copy(source, target, self.arrived.at[self.count])
        self.count += 1
        copy.start()
        return copy


def key_value_own_kernel(
    x_far, wk_far, wv_far, log_decay_far, wo_far, wq_far, wg_far,
    x_own, x_other, acc_k, acc_v, decay, coarse, fine, wo, wq, wg, wk, wv, log_decay, arrived,
):
    rows, part = x_own.shape
    core = lax.axis_index("fsdp")
    loads = Loads(arrived)

    def tile(x, half, start):
        at = pl.ds(start, BLOCK)
        columns = pl.ds(pl.multiple_of(half * part, part), part)
        return loads.start(x_far.at[at, columns], x.at[at])

    starts = range(0, rows, BLOCK)
    logs, key = loads.start(log_decay_far, log_decay), loads.start(wk_far, wk)
    tiles = [tile(x_own, core, start) for start in starts]
    value = loads.start(wv_far, wv)
    others = [tile(x_other, 1 - core, start) for start in starts]
    others += [loads.start(wo_far, wo), loads.start(wq_far, wq), loads.start(wg_far, wg)]
    angle_tables(coarse, fine)
    logs.wait()
    decay_sums(log_decay, decay)
    key.wait()
    for copy, start in zip(tiles, starts):
        at = slice(start, start + BLOCK)
        copy.wait()
        acc_k[at, :] = mm(x_own[at, :], wk[...])
    value.wait()
    for start in starts:
        at = slice(start, start + BLOCK)
        acc_v[at, :] = mm(x_own[at, :], wv[...])
    for copy in others:
        copy.wait()


def pack_message(message, states, logs):
    heads = len(states)
    place = lax.broadcasted_iota(jnp.int32, (EXTRA, DH), 0)
    tail = jnp.zeros((EXTRA, DH), F32)
    for head in range(heads):
        message[head * DH : (head + 1) * DH, :] = states[head].astype(BF16)
        rest = logs[head]
        for number in range(3):
            piece = rest.astype(BF16).astype(F32)
            tail = jnp.where(place == 3 * head + number, piece, tail)
            rest = rest - piece
    message[heads * DH :, :] = tail.astype(BF16)


def message_log(message, heads, head):
    tail = message[heads * DH :, :].astype(F32)
    return (tail[3 * head : 3 * head + 1] + tail[3 * head + 1 : 3 * head + 2] + tail[3 * head + 2 : 3 * head + 3])[:, :1]


def exchanges(ctx, hop):
    lower = range(ctx - hop)
    if hop == 1:
        return [], list(lower), []
    early = [at for at in lower if at < hop // 2]
    even = [at for at in lower if at >= hop // 2 and at // hop % 2 == 0]
    odd = [at for at in lower if at // hop % 2 == 1]
    return early, even, odd


def is_upper(lowers, hop):
    place = lax.axis_index("ctx")
    found = place < 0
    for lower in lowers:
        found = jnp.logical_or(found, place == lower + hop)
    return found


def arrived_state(arrivals, sets, hop, span):
    parts = [jnp.where(is_upper(lowers, hop), ref[span, :].astype(F32), 0.0) for ref, lowers in zip(arrivals, sets)]
    return functools.reduce(lambda a, b: a + b, parts)


def arrived_log(arrivals, sets, hop, heads, head):
    parts = [jnp.where(is_upper(lowers, hop), message_log(ref, heads, head), 0.0) for ref, lowers in zip(arrivals, sets)]
    return functools.reduce(lambda a, b: a + b, parts)


def key_value_kernel(
    heads, x, wk, wv, acc_k, acc_v, decay, coarse, fine, k_out, v_out, before_out, state_out, message
):
    state_out[...] = jnp.zeros_like(state_out)

    def block_step(block, totals):
        start = pl.multiple_of(block * BLOCK, BLOCK)
        columns = decay[:, pl.ds(start, BLOCK)].T
        ending = columns[BLOCK - 1 : BLOCK, :]
        faded = jnp.exp(ending - columns)
        at = pl.ds(start, BLOCK)
        cosine, sine = angles(coarse, fine, start, BLOCK)
        keys = turned(acc_k[at, :] + mm(x[at, :], wk[...]), cosine, sine)
        k_out[at, :] = keys
        values = (acc_v[at, :] + mm(x[at, :], wv[...])).astype(BF16)
        v_out[at, :] = values
        for head in range(heads):
            span = slice(head * DH, (head + 1) * DH)
            weighted = (keys[:, span].astype(F32) * faded[:, head : head + 1]).astype(BF16)
            old = state_out[span, :]
            before_out[block, span, :] = old.astype(BF16)
            state_out[span, :] = jnp.exp(ending[:, head : head + 1]) * old + mm_tn(weighted, values[:, span])
        return totals + ending

    totals = lax.fori_loop(0, x.shape[0] // BLOCK, block_step, jnp.zeros((1, 8), F32))
    states = [state_out[head * DH : (head + 1) * DH, :] for head in range(heads)]
    pack_message(message, states, [totals[:, head : head + 1] for head in range(heads)])


def combine_kernel(heads, hop, sets, first, state, sent, *refs):
    if not first:
        old_entering, refs = refs[0], refs[1:]
    arrivals = refs[: len(sets)]
    window, entering, message = refs[len(sets) :]
    states, logs = [], []
    for head in range(heads):
        span = slice(head * DH, (head + 1) * DH)
        row = slice(heads * DH + head, heads * DH + head + 1)
        arrived = arrived_state(arrivals, sets, hop, span)
        log = arrived_log(arrivals, sets, hop, heads, head)
        window_log = message_log(sent, heads, head)
        if first:
            entering[span, :] = arrived
            entering_log = log
        else:
            before_log = old_entering[row, :1]
            entering[span, :] = old_entering[span, :] + jnp.exp(before_log) * arrived
            entering_log = before_log + log
        entering[row, :] = jnp.broadcast_to(entering_log, (1, DH))
        new = state[span, :] + jnp.exp(window_log) * arrived
        window[span, :] = new
        states.append(new)
        logs.append(window_log + log)
    pack_message(message, states, logs)


def query_gate_kernel(
    heads, block, x_own, x_other, wq, wq_far, wg, wg_far, decay, coarse, fine, k, v, q_out, g_out, intra_out
):
    start = block * BLOCK
    lines = decay[:, start : start + BLOCK]
    columns = lines.T

    at = slice(start, start + BLOCK)
    cosine, sine = angles(coarse, fine, start, BLOCK)
    q_out[...] = turned(mm(x_own[at, :], wq[...]) + mm(x_other[at, :], wq_far[...]), cosine, sine)
    g_out[...] = (mm(x_own[at, :], wg[...]) + mm(x_other[at, :], wg_far[...])).astype(BF16)
    for piece in range(BLOCK // TILE):
        low, last = piece * TILE, (piece + 1) * TILE
        place_t = lax.broadcasted_iota(jnp.int32, (TILE, last), 0) + low
        place_s = lax.broadcasted_iota(jnp.int32, (TILE, last), 1)
        causal = place_t >= place_s
        for head in range(heads):
            span = slice(head * DH, (head + 1) * DH)
            scores = mm_nt(q_out[low:last, span], k[start : start + last, span])
            differ = columns[low:last, head : head + 1] - lines[head : head + 1, :last]
            weights = jnp.where(causal, jnp.exp(jnp.where(causal, differ, 0.0)), 0.0)
            intra_out[low:last, span] = mm((scores * weights).astype(BF16), v[start : start + last, span])


def hidden_kernel(heads, hop, sets, starts, decay, before, entering, *refs):
    arrivals, refs, token = refs[: len(sets)], refs[len(sets) : -1], refs[-1]
    projected, outs = refs[: -len(starts)], refs[-len(starts) :]
    token[...] = jnp.zeros_like(token)
    for head in range(heads):
        span = slice(head * DH, (head + 1) * DH)
        entering_log = entering[heads * DH + head : heads * DH + head + 1, :1]
        state = entering[span, :] + jnp.exp(entering_log) * arrived_state(arrivals, sets, hop, span)
        for start, out in zip(starts, outs):
            block = start // BLOCK
            q, gate, intra = projected[3 * block : 3 * block + 3]
            at = slice(start % BLOCK, start % BLOCK + TILE)
            column = jnp.exp(decay[:, start : start + TILE].T[:, head : head + 1])
            scale_log = jnp.zeros((1, 1), F32)
            for earlier in range(block):
                end = (earlier + 1) * BLOCK
                scale_log = scale_log + decay[head : head + 1, end - 1 : end]
            prior = (jnp.exp(scale_log) * state + before[block, span, :].astype(F32)).astype(BF16)
            retained = intra[at, span] + column * mm(q[at, span], prior)
            center = retained - jnp.mean(retained, axis=1, keepdims=True)
            spread = jnp.mean(center * center, axis=1, keepdims=True)
            value = gate[at, span].astype(F32)
            silu = value / (1.0 + jnp.exp(-value))
            out[:, span] = (silu * center * lax.rsqrt(spread + 1e-5)).astype(BF16)


def columns_kernel(first, second, out):
    cols = out.shape[1] // 2
    place, core = lax.axis_index("tp"), lax.axis_index("fsdp")
    high, low = place // 2, place % 2

    @pl.when(core == 0)
    def _():
        at = pl.ds(pl.multiple_of((1 - low) * cols, cols), cols)
        out[:, :cols] = first[:, at]
        out[:, cols:] = second[:, at]

    @pl.when(core == 1)
    def _():
        out[...] = jnp.where(high == 0, first[...], second[...])


def arrange_kernel(mine, other, low_out, high_out):
    cols = mine.shape[1] // 2
    place, core = lax.axis_index("tp"), lax.axis_index("fsdp")
    for gathered, bit, out in ((core == 0, place // 2, low_out), (core == 1, place % 2, high_out)):
        give = pl.ds(pl.multiple_of((1 - bit) * cols, cols), cols)
        keep = pl.ds(pl.multiple_of(bit * cols, cols), cols)
        out[:, :cols] = jnp.where(gathered, mine[:, give], other[:, give])
        out[:, cols:] = jnp.where(gathered, mine[:, keep], other[:, keep])


def own_kernel(order, own_first, own_second, *refs):
    pieces, outs = refs[: len(order)], refs[len(order) :]
    cols = pieces[0].shape[1]
    place, core = lax.axis_index("tp"), lax.axis_index("fsdp")
    high, low = place // 2, place % 2
    here = core == high
    mine = pl.ds(pl.multiple_of(low * cols, cols), cols)
    flipped = pl.ds(pl.multiple_of((1 - low) * cols, cols), cols)
    keep = jnp.where(here, own_first[:, mine], own_second[:, mine])
    gives = [
        jnp.where(here, own_second[:, mine], own_first[:, mine]),
        jnp.where(here, own_first[:, flipped], own_second[:, flipped]),
    ]
    for (half, number), piece in zip(order, pieces):
        at = slice(number * TILE, (number + 1) * TILE)
        outs[half][at, :cols] = mm(piece[...], gives[half])
        outs[half][at, cols:] = mm(piece[...], keep)


def give_kernel(number, own, far, weight, out):
    cols = out.shape[1]
    at = slice(number * TILE, (number + 1) * TILE)
    out[...] = (own[at, :cols] + mm(far[...], weight[:, :cols])).astype(BF16)


def keep_kernel(order, *refs):
    count = len(order)
    fars, owns, weights, outs = refs[:count], refs[count : count + 2], refs[count + 2 : count + 4], refs[count + 4 :]
    for (half, number), far in zip(order, fars):
        cols = far.shape[1]
        at = slice(number * TILE, (number + 1) * TILE)
        outs[half][at, :] = owns[half][at, cols:] + mm(far[...], weights[half][:, cols:])


def finish_kernel(order, *refs):
    gots, keeps, out = refs[: len(order)], refs[len(order) : -1], refs[-1]
    for (half, number), got in zip(order, gots):
        keep = keeps[half]
        at = slice(number * TILE, (number + 1) * TILE)
        value = keep[at, :] + got[...].astype(F32)
        start = half * keep.shape[0] + number * TILE
        out[0, start : start + TILE, :] = value.astype(BF16)


def after(value, *others):
    return lax.optimization_barrier((value, *others))[0]


def on_device(tokens, query_weight, key_weight, value_weight, gate_weight, out_weight, log_decay):
    x = tokens[0]
    rows, width = x.shape
    part, cols = query_weight.shape
    heads = cols // DH
    blocks = rows // BLOCK
    ctx, tp, cores = lax.axis_size("ctx"), lax.axis_size("tp"), lax.axis_size("fsdp")
    assert tp == 4 and cores == 2 and ctx >= 4 and ctx & (ctx - 1) == 0
    near_mask, far_mask = 1, 2
    tables = [((2, rows // FINE, DH // 2), F32), ((2, FINE, DH // 2), F32)]

    key_far = swap(key_weight, "fsdp", 1)
    value_far = swap(value_weight, "fsdp", 1)

    x_own, x_other, acc_k, acc_v, decay, coarse, fine, out_first, own_q, own_g = loading_call(
        key_value_own_kernel,
        [((rows, part), BF16)] * 2
        + [((rows, cols), F32)] * 2
        + [((8, rows), F32)]
        + tables
        + [(out_weight.shape, BF16), ((part, cols), BF16), ((part, cols), BF16)],
        [x, key_weight, value_weight, log_decay[0].T, out_weight, query_weight, gate_weight],
        [],
        [pltpu.VMEM((part, cols), BF16)] * 2 + [pltpu.VMEM((heads, rows), F32)],
        2 * (rows // BLOCK) + 6,
        "key_value_own",
    )
    state_shape, message_shape = (heads * DH, DH), (heads * DH + EXTRA, DH)
    keys, values, before, window, message = kernel_call(
        functools.partial(key_value_kernel, heads),
        [((rows, cols), BF16)] * 2
        + [((blocks, heads * DH, DH), BF16), (state_shape, F32), (message_shape, BF16)],
        [x_other, key_far, value_far, acc_k, acc_v, decay, coarse, fine],
        "key_value",
    )
    far_q, far_g = swap(own_q, "fsdp", 1), swap(own_g, "fsdp", 1)

    def query_gate(block, decay):
        return kernel_call(
            functools.partial(query_gate_kernel, heads, block),
            [((BLOCK, cols), BF16), ((BLOCK, cols), BF16), ((BLOCK, cols), F32)],
            [x_own, x_other, own_q, far_q, own_g, far_g, decay, coarse, fine, keys, values],
            "query_gate",
        )

    def exchange(message, lowers, hop):
        pairs = [(at, at + hop) for at in lowers]
        if hop > 1:
            pairs += [(upper, at) for at, upper in pairs]
        return lax.ppermute(message, "ctx", pairs)

    projected = list(query_gate(0, decay))
    window = after(window, projected[0])
    entering, hop, early, first_message = None, 1, [], message
    while True:
        first_set, *later_sets = exchanges(ctx, hop)
        later_sets = [lowers for lowers in later_sets if lowers]
        sets = later_sets + ([first_set] if first_set else [])
        arrivals = [exchange(message, lowers, hop) for lowers in later_sets] + early
        if 2 * hop >= ctx:
            break
        unchanged = exchanges(ctx, 2 * hop)[0]
        early = [exchange(message, unchanged, 2 * hop)]
        old = [] if entering is None else [entering]
        window, entering, message = kernel_call(
            functools.partial(combine_kernel, heads, hop, sets, entering is None),
            [(state_shape, F32), ((heads * DH + 8, DH), F32), (message_shape, BF16)],
            [window, message, *old, *arrivals],
            "combine",
        )
        hop *= 2

    own_second = swap(out_first, "fsdp", 1)
    [for_partner] = kernel_call(
        columns_kernel,
        [(out_weight.shape, BF16)],
        [after(out_first, first_message), own_second],
        "columns",
    )
    pairs = [(at * cores + at_core, (at ^ mask) * cores + at_core) for at in range(tp) for at_core, mask in enumerate((near_mask, far_mask))]
    out_mine = lax.ppermute(for_partner, ("tp", "fsdp"), pairs)

    held = after(decay, message, *early)
    for block in range(1, blocks):
        projected += query_gate(block, held)

    count = rows // 2 // TILE
    masks = (near_mask, far_mask)
    hidden, far = [[], []], [[], []]
    for number in range(count):
        held = after(decay, swap(pair[2], "fsdp", 1)) if number else decay
        pair = kernel_call(
            functools.partial(hidden_kernel, heads, hop, sets, [(half * count + number) * TILE for half in range(2)]),
            [((TILE, cols), BF16)] * 2 + [((16, 128), BF16)],
            [held, before, entering, *arrivals, *projected],
            "hidden",
        )
        if number == 0:
            out_other = swap(after(out_mine, pair[0]), "fsdp", 1)
        for half in range(2):
            hidden[half].append(pair[half])
            far[half].append(swap(pair[half], "tp", masks[half]))
    weights = kernel_call(
        arrange_kernel,
        [((cols, 2 * cols), BF16)] * 2,
        [out_mine, out_other],
        "arrange",
    )
    order = [(half, number) for number in reversed(range(count)) for half in (1, 0)]
    owns = kernel_call(
        functools.partial(own_kernel, order),
        [((count * TILE, 2 * cols), F32)] * 2,
        [out_first, own_second, *(hidden[half][number] for half, number in order)],
        "own_products",
    )
    gots = []
    for half, number in order:
        [give] = kernel_call(
            functools.partial(give_kernel, number),
            [((TILE, cols), BF16)],
            [owns[half], far[half][number], weights[half]],
            "give",
        )
        gots.append(swap(give, "tp", masks[1 - half]))
    keeps = kernel_call(
        functools.partial(keep_kernel, order),
        [((count * TILE, cols), F32)] * 2,
        [*(far[half][number] for half, number in order), *owns, *weights],
        "keep",
    )
    arrays = [pltpu.with_memory_space_constraint(array, pltpu.VMEM) for array in (*gots, *keeps)]
    return pl.pallas_call(
        functools.partial(finish_kernel, order),
        in_specs=[pl.BlockSpec(memory_space=pltpu.VMEM)] * len(arrays),
        out_specs=pl.BlockSpec(memory_space=pltpu.VMEM),
        out_shape=jax.ShapeDtypeStruct((1, rows, cols), BF16),
        compiler_params=pltpu.CompilerParams(vmem_limit_bytes=VMEM_LIMIT),
        name="finish",
    )(*arrays)


def solution(mesh):
    in_specs = (
        P("fsdp", "ctx", None),
        P("fsdp", "tp"),
        P("fsdp", "tp"),
        P("fsdp", "tp"),
        P("fsdp", "tp"),
        P("tp", "fsdp"),
        P("fsdp", "ctx", "tp"),
    )
    out_specs = P("fsdp", "ctx", "tp")
    return jax.shard_map(
        on_device, mesh=mesh, in_specs=in_specs, out_specs=out_specs, check_vma=False
    )
```

```python
import functools
import math

import jax
import jax.numpy as jnp
from jax import lax
from jax.experimental import pallas as pl
from jax.experimental.pallas import tpu as pltpu
from jax.sharding import PartitionSpec as P

DH = 256
BLOCK = 512
TILE = 256
FINE = 32
EXTRA = 16
VMEM_LIMIT = 14 * 1024 * 1024
F32 = jnp.float32
BF16 = jnp.bfloat16


def mm(left, right):
    return jnp.dot(left, right, preferred_element_type=F32)


def mm_nt(left, right):
    return lax.dot_general(left, right, (((1,), (1,)), ((), ())), preferred_element_type=F32)


def mm_tn(left, right):
    return lax.dot_general(left, right, (((0,), (0,)), ((), ())), preferred_element_type=F32)


def swap(value, axis, mask):
    size = lax.axis_size(axis)
    return lax.ppermute(value, axis, [(place, place ^ mask) for place in range(size)])


def kernel_call(kernel, outs, operands, name):
    arrays = [pltpu.with_memory_space_constraint(array, pltpu.VMEM) for array in operands]
    return pl.pallas_call(
        kernel,
        in_specs=[pl.BlockSpec(memory_space=pltpu.VMEM)] * len(operands),
        out_specs=[pl.BlockSpec(memory_space=pltpu.VMEM)] * len(outs),
        out_shape=[pltpu.VMEM(shape, dtype) for shape, dtype in outs],
        compiler_params=pltpu.CompilerParams(vmem_limit_bytes=VMEM_LIMIT),
        cost_estimate=pl.CostEstimate(
            flops=1, bytes_accessed=1, transcendentals=0
        ),
        name=name,
    )(*arrays)


def loading_call(kernel, outs, loaded, operands, scratch, loads, name):
    arrays = [pltpu.with_memory_space_constraint(array, pltpu.HBM) for array in loaded]
    arrays += [pltpu.with_memory_space_constraint(array, pltpu.VMEM) for array in operands]
    return pl.pallas_call(
        kernel,
        in_specs=[pl.BlockSpec(memory_space=pltpu.HBM)] * len(loaded)
        + [pl.BlockSpec(memory_space=pltpu.VMEM)] * len(operands),
        out_specs=[pl.BlockSpec(memory_space=pltpu.VMEM)] * len(outs),
        out_shape=[pltpu.VMEM(shape, dtype) for shape, dtype in outs],
        scratch_shapes=[*scratch, pltpu.SemaphoreType.DMA((loads,))],
        compiler_params=pltpu.CompilerParams(vmem_limit_bytes=VMEM_LIMIT),
        cost_estimate=pl.CostEstimate(flops=1, bytes_accessed=1, transcendentals=0),
        name=name,
    )(*arrays)


def turned(values, cosine, sine):
    half = DH // 2
    parts = []
    for start in range(0, values.shape[1], DH):
        low = values[:, start : start + half]
        high = values[:, start + half : start + DH]
        parts.append((low * cosine - high * sine).astype(BF16))
        parts.append((high * cosine + low * sine).astype(BF16))
    return jnp.concatenate(parts, axis=1)


def angles(coarse, fine, first, count):
    at = first // FINE
    far = coarse[:, pl.ds(at, count // FINE), :]
    near = fine[...]
    cos_c, sin_c = far[0][:, None, :], far[1][:, None, :]
    cos_f, sin_f = near[0][None], near[1][None]
    cosine = cos_c * cos_f - sin_c * sin_f
    sine = sin_c * cos_f + cos_c * sin_f
    return cosine.reshape(count, DH // 2), sine.reshape(count, DH // 2)


def decay_sums(log_decay, decay):
    heads, rows = log_decay.shape
    place_s = lax.broadcasted_iota(jnp.int32, (BLOCK, BLOCK), 0)
    place_t = lax.broadcasted_iota(jnp.int32, (BLOCK, BLOCK), 1)
    upper = jnp.where(place_s <= place_t, 1.0, 0.0).astype(BF16)
    value = jnp.concatenate([log_decay[...], jnp.zeros((8 - heads, rows), F32)], axis=0)
    parts = []
    for _ in range(3):
        parts.append(value.astype(BF16))
        value = value - parts[-1].astype(F32)
    stacked = jnp.concatenate([part.astype(F32) for part in parts], axis=0).astype(BF16)
    for start in range(0, rows, BLOCK):
        sums = mm(stacked[:, start : start + BLOCK], upper)
        decay[:, start : start + BLOCK] = sums[:8] + sums[8:16] + sums[16:]


def turn(first, second):
    (cos_a, sin_a), (cos_b, sin_b) = first, second
    return cos_a * cos_b - sin_a * sin_b, sin_a * cos_b + cos_a * sin_b


def joined(first, second):
    return tuple(jnp.concatenate(pair, axis=0) for pair in zip(first, second))


def angle_tables(coarse, fine):
    half, seeds = DH // 2, 8
    index = lax.broadcasted_iota(jnp.int32, (seeds, half), 1).astype(F32)
    frequency = jnp.exp(index * (-math.log(10000.0) / half))
    place = lax.broadcasted_iota(jnp.int32, (seeds, half), 0).astype(F32)
    offset = (lax.axis_index("ctx") * (coarse.shape[1] * FINE)).astype(F32)
    near = jnp.cos(place * frequency), jnp.sin(place * frequency)
    base = jnp.cos(offset * frequency), jnp.sin(offset * frequency)
    step = turn([part[seeds - 1 : seeds] for part in near], [part[1:2] for part in near])
    while near[0].shape[0] < FINE:
        near = joined(near, turn(near, step))
        step = turn(step, step)
    far = tuple(part[:1] for part in base)
    while far[0].shape[0] < coarse.shape[1]:
        far = joined(far, turn(far, step))
        step = turn(step, step)
    for table, parts in ((coarse, far), (fine, near)):
        table[0], table[1] = (part[: table.shape[1]] for part in parts)


class Loads:
    def __init__(self, arrived):
        self.arrived, self.count = arrived, 0

    def start(self, source, target):
        copy = pltpu.make_async_copy(source, target, self.arrived.at[self.count])
        self.count += 1
        copy.start()
        return copy


def key_value_own_kernel(
    x_far, wk_far, wv_far, log_decay_far, wo_far, wq_far, wg_far,
    x_own, x_other, acc_k, acc_v, decay, coarse, fine, wo, wq, wg, wk, wv, log_decay, arrived,
):
    rows, part = x_own.shape
    core = lax.axis_index("fsdp")
    loads = Loads(arrived)

    def tile(x, half, start):
        at = pl.ds(start, BLOCK)
        columns = pl.ds(pl.multiple_of(half * part, part), part)
        return loads.start(x_far.at[at, columns], x.at[at])

    starts = range(0, rows, BLOCK)
    logs, key = loads.start(log_decay_far, log_decay), loads.start(wk_far, wk)
    tiles = [tile(x_own, core, start) for start in starts]
    value = loads.start(wv_far, wv)
    others = [tile(x_other, 1 - core, start) for start in starts]
    others += [loads.start(wo_far, wo), loads.start(wq_far, wq), loads.start(wg_far, wg)]
    key.wait()
    tiles[0].wait()
    for number, start in enumerate(starts):
        at = slice(start, start + BLOCK)
        if number:
            tiles[number].wait()
        acc_k[at, :] = mm(x_own[at, :], wk[...])
    value.wait()
    logs.wait()
    angle_tables(coarse, fine)
    decay_sums(log_decay, decay)
    for start in starts:
        at = slice(start, start + BLOCK)
        acc_v[at, :] = mm(x_own[at, :], wv[...])
    for copy in others:
        copy.wait()


def pack_message(message, states, logs):
    heads = len(states)
    place = lax.broadcasted_iota(jnp.int32, (EXTRA, DH), 0)
    tail = jnp.zeros((EXTRA, DH), F32)
    for head in range(heads):
        message[head * DH : (head + 1) * DH, :] = states[head].astype(BF16)
        rest = logs[head]
        for number in range(3):
            piece = rest.astype(BF16).astype(F32)
            tail = jnp.where(place == 3 * head + number, piece, tail)
            rest = rest - piece
    message[heads * DH :, :] = tail.astype(BF16)


def message_log(message, heads, head):
    tail = message[heads * DH :, :].astype(F32)
    return (tail[3 * head : 3 * head + 1] + tail[3 * head + 1 : 3 * head + 2] + tail[3 * head + 2 : 3 * head + 3])[:, :1]


def exchanges(ctx, hop):
    lower = range(ctx - hop)
    if hop == 1:
        return [], list(lower), []
    early = [at for at in lower if at < hop // 2]
    even = [at for at in lower if at >= hop // 2 and at // hop % 2 == 0]
    odd = [at for at in lower if at // hop % 2 == 1]
    return early, even, odd


def is_upper(lowers, hop):
    place = lax.axis_index("ctx")
    found = place < 0
    for lower in lowers:
        found = jnp.logical_or(found, place == lower + hop)
    return found


def arrived_state(arrivals, sets, hop, span):
    parts = [jnp.where(is_upper(lowers, hop), ref[span, :].astype(F32), 0.0) for ref, lowers in zip(arrivals, sets)]
    return functools.reduce(lambda a, b: a + b, parts)


def arrived_log(arrivals, sets, hop, heads, head):
    parts = [jnp.where(is_upper(lowers, hop), message_log(ref, heads, head), 0.0) for ref, lowers in zip(arrivals, sets)]
    return functools.reduce(lambda a, b: a + b, parts)


def key_value_kernel(
    heads, x, wk, wv, acc_k, acc_v, decay, coarse, fine, k_out, v_out, before_out, state_out, message
):
    state_out[...] = jnp.zeros_like(state_out)

    totals = jnp.zeros((1, 8), F32)
    for block in range(x.shape[0] // BLOCK):
        start = block * BLOCK
        columns = decay[:, slice(start, start + BLOCK)].T
        ending = columns[BLOCK - 1 : BLOCK, :]
        faded = jnp.exp(ending - columns)
        at = slice(start, start + BLOCK)
        cosine, sine = angles(coarse, fine, start, BLOCK)
        keys = turned(acc_k[at, :] + mm(x[at, :], wk[...]), cosine, sine)
        k_out[at, :] = keys
        values = (acc_v[at, :] + mm(x[at, :], wv[...])).astype(BF16)
        v_out[at, :] = values
        for head in range(heads):
            span = slice(head * DH, (head + 1) * DH)
            weighted = (keys[:, span].astype(F32) * faded[:, head : head + 1]).astype(BF16)
            old = state_out[span, :]
            before_out[block, span, :] = old.astype(BF16)
            state_out[span, :] = jnp.exp(ending[:, head : head + 1]) * old + mm_tn(weighted, values[:, span])
        totals = totals + ending
    states = [state_out[head * DH : (head + 1) * DH, :] for head in range(heads)]
    pack_message(message, states, [totals[:, head : head + 1] for head in range(heads)])


def combine_kernel(heads, hop, sets, first, state, sent, *refs):
    if not first:
        old_entering, refs = refs[0], refs[1:]
    arrivals = refs[: len(sets)]
    window, entering, message = refs[len(sets) :]
    states, logs = [], []
    for head in range(heads):
        span = slice(head * DH, (head + 1) * DH)
        row = slice(heads * DH + head, heads * DH + head + 1)
        arrived = arrived_state(arrivals, sets, hop, span)
        log = arrived_log(arrivals, sets, hop, heads, head)
        window_log = message_log(sent, heads, head)
        if first:
            entering[span, :] = arrived
            entering_log = log
        else:
            before_log = old_entering[row, :1]
            entering[span, :] = old_entering[span, :] + jnp.exp(before_log) * arrived
            entering_log = before_log + log
        entering[row, :] = jnp.broadcast_to(entering_log, (1, DH))
        new = state[span, :] + jnp.exp(window_log) * arrived
        window[span, :] = new
        states.append(new)
        logs.append(window_log + log)
    pack_message(message, states, logs)


def query_gate_kernel(
    heads, block, x_own, x_other, wq, wq_far, wg, wg_far, decay, coarse, fine, k, v, q_out, g_out, intra_out
):
    start = block * BLOCK
    lines = decay[:, start : start + BLOCK]
    columns = lines.T

    at = slice(start, start + BLOCK)
    cosine, sine = angles(coarse, fine, start, BLOCK)
    q_out[...] = turned(mm(x_own[at, :], wq[...]) + mm(x_other[at, :], wq_far[...]), cosine, sine)
    gates = (mm(x_own[at, :], wg[...]) + mm(x_other[at, :], wg_far[...])).astype(BF16).astype(F32)
    g_out[...] = gates / (1.0 + jnp.exp(-gates))
    for piece in range(BLOCK // TILE):
        low, last = piece * TILE, (piece + 1) * TILE
        place_t = lax.broadcasted_iota(jnp.int32, (TILE, last), 0) + low
        place_s = lax.broadcasted_iota(jnp.int32, (TILE, last), 1)
        causal = place_t >= place_s
        for head in range(heads):
            span = slice(head * DH, (head + 1) * DH)
            scores = mm_nt(q_out[low:last, span], k[start : start + last, span])
            differ = columns[low:last, head : head + 1] - lines[head : head + 1, :last]
            weights = jnp.where(causal, jnp.exp(jnp.where(causal, differ, 0.0)), 0.0)
            intra_out[low:last, span] = mm((scores * weights).astype(BF16), v[start : start + last, span])


def hidden_kernel(heads, hop, sets, starts, decay, before, entering, *refs):
    arrivals, refs, token = refs[: len(sets)], refs[len(sets) : -1], refs[-1]
    projected, outs = refs[: -len(starts)], refs[-len(starts) :]
    token[...] = jnp.zeros_like(token)
    for head in range(heads):
        span = slice(head * DH, (head + 1) * DH)
        entering_log = entering[heads * DH + head : heads * DH + head + 1, :1]
        state = entering[span, :] + jnp.exp(entering_log) * arrived_state(arrivals, sets, hop, span)
        for start, out in zip(starts, outs):
            block = start // BLOCK
            q, gate, intra = projected[3 * block : 3 * block + 3]
            at = slice(start % BLOCK, start % BLOCK + TILE)
            column = jnp.exp(decay[:, start : start + TILE].T[:, head : head + 1])
            scale_log = jnp.zeros((1, 1), F32)
            for earlier in range(block):
                end = (earlier + 1) * BLOCK
                scale_log = scale_log + decay[head : head + 1, end - 1 : end]
            prior = (jnp.exp(scale_log) * state + before[block, span, :].astype(F32)).astype(BF16)
            retained = intra[at, span] + column * mm(q[at, span], prior)
            center = retained - jnp.mean(retained, axis=1, keepdims=True)
            spread = jnp.mean(center * center, axis=1, keepdims=True)
            out[:, span] = (gate[at, span] * center * lax.rsqrt(spread + 1e-5)).astype(BF16)


def columns_kernel(first, second, out):
    cols = out.shape[1] // 2
    place, core = lax.axis_index("tp"), lax.axis_index("fsdp")
    high, low = place // 2, place % 2

    @pl.when(core == 0)
    def _():
        at = pl.ds(pl.multiple_of((1 - low) * cols, cols), cols)
        out[:, :cols] = first[:, at]
        out[:, cols:] = second[:, at]

    @pl.when(core == 1)
    def _():
        out[...] = jnp.where(high == 0, first[...], second[...])


def arrange_kernel(mine, other, low_out, high_out):
    cols = mine.shape[1] // 2
    place, core = lax.axis_index("tp"), lax.axis_index("fsdp")
    for gathered, bit, out in ((core == 0, place // 2, low_out), (core == 1, place % 2, high_out)):
        give = pl.ds(pl.multiple_of((1 - bit) * cols, cols), cols)
        keep = pl.ds(pl.multiple_of(bit * cols, cols), cols)
        out[:, :cols] = jnp.where(gathered, mine[:, give], other[:, give])
        out[:, cols:] = jnp.where(gathered, mine[:, keep], other[:, keep])


def own_kernel(order, own_first, own_second, *refs):
    pieces, outs = refs[: len(order)], refs[len(order) :]
    cols = pieces[0].shape[1]
    place, core = lax.axis_index("tp"), lax.axis_index("fsdp")
    high, low = place // 2, place % 2
    here = core == high
    mine = pl.ds(pl.multiple_of(low * cols, cols), cols)
    flipped = pl.ds(pl.multiple_of((1 - low) * cols, cols), cols)
    keep = jnp.where(here, own_first[:, mine], own_second[:, mine])
    gives = [
        jnp.where(here, own_second[:, mine], own_first[:, mine]),
        jnp.where(here, own_first[:, flipped], own_second[:, flipped]),
    ]
    for (half, number), piece in zip(order, pieces):
        at = slice(number * TILE, (number + 1) * TILE)
        outs[half][at, :cols] = mm(piece[...], gives[half])
        outs[half][at, cols:] = mm(piece[...], keep)


def give_kernel(number, own, far, weight, out):
    cols = out.shape[1]
    at = slice(number * TILE, (number + 1) * TILE)
    out[...] = (own[at, :cols] + mm(far[...], weight[:, :cols])).astype(BF16)


def keep_kernel(order, *refs):
    count = len(order)
    fars, owns, weights, outs = refs[:count], refs[count : count + 2], refs[count + 2 : count + 4], refs[count + 4 :]
    for (half, number), far in zip(order, fars):
        cols = far.shape[1]
        at = slice(number * TILE, (number + 1) * TILE)
        outs[half][at, :] = owns[half][at, cols:] + mm(far[...], weights[half][:, cols:])


def finish_kernel(order, *refs):
    count = len(order)
    gots, keeps, out, ready, written = refs[:count], refs[count : count + 2], refs[-3], refs[-2], refs[-1]
    copies = []
    for slot, ((half, number), got) in enumerate(zip(order, gots)):
        keep = keeps[half]
        at = slice(number * TILE, (number + 1) * TILE)
        ready[slot] = (keep[at, :] + got[...].astype(F32)).astype(BF16)
        start = half * keep.shape[0] + number * TILE
        copies.append(pltpu.make_async_copy(ready.at[slot], out.at[0, pl.ds(start, TILE)], written.at[slot]))
        copies[-1].start()
    for copy in copies:
        copy.wait()


def after(value, *others):
    return lax.optimization_barrier((value, *others))[0]


def on_device(tokens, query_weight, key_weight, value_weight, gate_weight, out_weight, log_decay):
    x = tokens[0]
    rows, width = x.shape
    part, cols = query_weight.shape
    heads = cols // DH
    blocks = rows // BLOCK
    ctx, tp, cores = lax.axis_size("ctx"), lax.axis_size("tp"), lax.axis_size("fsdp")
    assert tp == 4 and cores == 2 and ctx >= 4 and ctx & (ctx - 1) == 0
    near_mask, far_mask = 1, 2
    tables = [((2, rows // FINE, DH // 2), F32), ((2, FINE, DH // 2), F32)]

    key_far = swap(key_weight, "fsdp", 1)
    value_far = swap(value_weight, "fsdp", 1)

    x_own, x_other, acc_k, acc_v, decay, coarse, fine, out_first, own_q, own_g = loading_call(
        key_value_own_kernel,
        [((rows, part), BF16)] * 2
        + [((rows, cols), F32)] * 2
        + [((8, rows), F32)]
        + tables
        + [(out_weight.shape, BF16), ((part, cols), BF16), ((part, cols), BF16)],
        [x, key_weight, value_weight, log_decay[0].T, out_weight, query_weight, gate_weight],
        [],
        [pltpu.VMEM((part, cols), BF16)] * 2 + [pltpu.VMEM((heads, rows), F32)],
        2 * (rows // BLOCK) + 6,
        "key_value_own",
    )
    state_shape, message_shape = (heads * DH, DH), (heads * DH + EXTRA, DH)
    keys, values, before, window, message = kernel_call(
        functools.partial(key_value_kernel, heads),
        [((rows, cols), BF16)] * 2
        + [((blocks, heads * DH, DH), BF16), (state_shape, F32), (message_shape, BF16)],
        [x_other, key_far, value_far, acc_k, acc_v, decay, coarse, fine],
        "key_value",
    )
    far_q, far_g = swap(own_q, "fsdp", 1), swap(own_g, "fsdp", 1)

    def query_gate(block, decay):
        return kernel_call(
            functools.partial(query_gate_kernel, heads, block),
            [((BLOCK, cols), BF16), ((BLOCK, cols), F32), ((BLOCK, cols), F32)],
            [x_own, x_other, own_q, far_q, own_g, far_g, decay, coarse, fine, keys, values],
            "query_gate",
        )

    def exchange(message, lowers, hop):
        pairs = [(at, at + hop) for at in lowers]
        if hop > 1:
            pairs += [(upper, at) for at, upper in pairs]
        return lax.ppermute(message, "ctx", pairs)

    projected = list(query_gate(0, decay))
    window = after(window, projected[0])
    entering, hop, early, first_message = None, 1, [], message
    while True:
        first_set, *later_sets = exchanges(ctx, hop)
        later_sets = [lowers for lowers in later_sets if lowers]
        sets = later_sets + ([first_set] if first_set else [])
        arrivals = [exchange(message, lowers, hop) for lowers in later_sets] + early
        if 2 * hop >= ctx:
            break
        unchanged = exchanges(ctx, 2 * hop)[0]
        early = [exchange(message, unchanged, 2 * hop)]
        old = [] if entering is None else [entering]
        window, entering, message = kernel_call(
            functools.partial(combine_kernel, heads, hop, sets, entering is None),
            [(state_shape, F32), ((heads * DH + 8, DH), F32), (message_shape, BF16)],
            [window, message, *old, *arrivals],
            "combine",
        )
        hop *= 2

    own_second = swap(out_first, "fsdp", 1)
    [for_partner] = kernel_call(
        columns_kernel,
        [(out_weight.shape, BF16)],
        [after(out_first, first_message), own_second],
        "columns",
    )
    pairs = [(at * cores + at_core, (at ^ mask) * cores + at_core) for at in range(tp) for at_core, mask in enumerate((near_mask, far_mask))]
    out_mine = lax.ppermute(for_partner, ("tp", "fsdp"), pairs)

    held = after(decay, message, *early)
    for block in range(1, blocks):
        projected += query_gate(block, held)

    count = rows // 2 // TILE
    masks = (near_mask, far_mask)
    hidden, far = [[], []], [[], []]
    for number in range(count):
        held = after(decay, swap(pair[2], "fsdp", 1)) if number else decay
        pair = kernel_call(
            functools.partial(hidden_kernel, heads, hop, sets, [(half * count + number) * TILE for half in range(2)]),
            [((TILE, cols), BF16)] * 2 + [((16, 128), BF16)],
            [held, before, entering, *arrivals, *projected],
            "hidden",
        )
        if number == 0:
            out_other = swap(after(out_mine, pair[0]), "fsdp", 1)
        for half in range(2):
            hidden[half].append(pair[half])
            far[half].append(swap(pair[half], "tp", masks[half]))
    weights = kernel_call(
        arrange_kernel,
        [((cols, 2 * cols), BF16)] * 2,
        [out_mine, out_other],
        "arrange",
    )
    order = [(half, number) for number in reversed(range(count)) for half in (1, 0)]
    owns = kernel_call(
        functools.partial(own_kernel, order),
        [((count * TILE, 2 * cols), F32)] * 2,
        [out_first, own_second, *(hidden[half][number] for half, number in order)],
        "own_products",
    )
    gots = []
    for half, number in order:
        [give] = kernel_call(
            functools.partial(give_kernel, number),
            [((TILE, cols), BF16)],
            [owns[half], far[half][number], weights[half]],
            "give",
        )
        gots.append(swap(give, "tp", masks[1 - half]))
    keeps = kernel_call(
        functools.partial(keep_kernel, order),
        [((count * TILE, cols), F32)] * 2,
        [*(far[half][number] for half, number in order), *owns, *weights],
        "keep",
    )
    result = None
    for part_order, part_gots in ((order[2:], gots[2:]), (order[:2], gots[:2])):
        arrays = [pltpu.with_memory_space_constraint(array, pltpu.VMEM) for array in (*part_gots, *keeps)]
        held = [] if result is None else [result]
        result = pl.pallas_call(
            functools.partial(finish_kernel, part_order),
            in_specs=[pl.BlockSpec(memory_space=pltpu.VMEM)] * len(arrays)
            + [pl.BlockSpec(memory_space=pltpu.HBM)] * len(held),
            out_specs=pl.BlockSpec(memory_space=pltpu.HBM),
            out_shape=jax.ShapeDtypeStruct((1, rows, cols), BF16),
            input_output_aliases={len(arrays): 0} if held else {},
            scratch_shapes=[
                pltpu.VMEM((len(part_order), TILE, cols), BF16),
                pltpu.SemaphoreType.DMA((len(part_order),)),
            ],
            compiler_params=pltpu.CompilerParams(vmem_limit_bytes=VMEM_LIMIT),
            name="finish",
        )(*arrays, *held)
    return result


def solution(mesh):
    in_specs = (
        P("fsdp", "ctx", None),
        P("fsdp", "tp"),
        P("fsdp", "tp"),
        P("fsdp", "tp"),
        P("fsdp", "tp"),
        P("tp", "fsdp"),
        P("fsdp", "ctx", "tp"),
    )
    out_specs = P("fsdp", "ctx", "tp")
    return jax.shard_map(
        on_device, mesh=mesh, in_specs=in_specs, out_specs=out_specs, check_vma=False
    )
```

```python
import functools
import math

import jax
import jax.numpy as jnp
from jax import lax
from jax.experimental import pallas as pl
from jax.experimental.pallas import tpu as pltpu
from jax.sharding import PartitionSpec as P

DH = 256
BLOCK = 512
TILE = 256
FINE = 32
EXTRA = 16
VMEM_LIMIT = 14 * 1024 * 1024
F32 = jnp.float32
BF16 = jnp.bfloat16


def mm(left, right):
    return jnp.dot(left, right, preferred_element_type=F32)


def mm_nt(left, right):
    return lax.dot_general(left, right, (((1,), (1,)), ((), ())), preferred_element_type=F32)


def mm_tn(left, right):
    return lax.dot_general(left, right, (((0,), (0,)), ((), ())), preferred_element_type=F32)


def swap(value, axis, mask):
    size = lax.axis_size(axis)
    return lax.ppermute(value, axis, [(place, place ^ mask) for place in range(size)])


def kernel_call(kernel, outs, operands, name):
    arrays = [pltpu.with_memory_space_constraint(array, pltpu.VMEM) for array in operands]
    return pl.pallas_call(
        kernel,
        in_specs=[pl.BlockSpec(memory_space=pltpu.VMEM)] * len(operands),
        out_specs=[pl.BlockSpec(memory_space=pltpu.VMEM)] * len(outs),
        out_shape=[pltpu.VMEM(shape, dtype) for shape, dtype in outs],
        compiler_params=pltpu.CompilerParams(vmem_limit_bytes=VMEM_LIMIT),
        cost_estimate=pl.CostEstimate(
            flops=1, bytes_accessed=1, transcendentals=0
        ),
        name=name,
    )(*arrays)


def loading_call(kernel, outs, loaded, operands, scratch, loads, name):
    arrays = [pltpu.with_memory_space_constraint(array, pltpu.HBM) for array in loaded]
    arrays += [pltpu.with_memory_space_constraint(array, pltpu.VMEM) for array in operands]
    return pl.pallas_call(
        kernel,
        in_specs=[pl.BlockSpec(memory_space=pltpu.HBM)] * len(loaded)
        + [pl.BlockSpec(memory_space=pltpu.VMEM)] * len(operands),
        out_specs=[pl.BlockSpec(memory_space=pltpu.VMEM)] * len(outs),
        out_shape=[pltpu.VMEM(shape, dtype) for shape, dtype in outs],
        scratch_shapes=[*scratch, pltpu.SemaphoreType.DMA((loads,))],
        compiler_params=pltpu.CompilerParams(vmem_limit_bytes=VMEM_LIMIT),
        cost_estimate=pl.CostEstimate(flops=1, bytes_accessed=1, transcendentals=0),
        name=name,
    )(*arrays)


def turned(values, cosine, sine):
    half = DH // 2
    parts = []
    for start in range(0, values.shape[1], DH):
        low = values[:, start : start + half]
        high = values[:, start + half : start + DH]
        parts.append((low * cosine - high * sine).astype(BF16))
        parts.append((high * cosine + low * sine).astype(BF16))
    return jnp.concatenate(parts, axis=1)


def angles(coarse, fine, first, count):
    at = first // FINE
    far = coarse[:, pl.ds(at, count // FINE), :]
    near = fine[...]
    cos_c, sin_c = far[0][:, None, :], far[1][:, None, :]
    cos_f, sin_f = near[0][None], near[1][None]
    cosine = cos_c * cos_f - sin_c * sin_f
    sine = sin_c * cos_f + cos_c * sin_f
    return cosine.reshape(count, DH // 2), sine.reshape(count, DH // 2)


def decay_sums(log_decay, decay):
    heads, rows = log_decay.shape
    place_s = lax.broadcasted_iota(jnp.int32, (BLOCK, BLOCK), 0)
    place_t = lax.broadcasted_iota(jnp.int32, (BLOCK, BLOCK), 1)
    upper = jnp.where(place_s <= place_t, 1.0, 0.0).astype(BF16)
    value = jnp.concatenate([log_decay[...], jnp.zeros((8 - heads, rows), F32)], axis=0)
    parts = []
    for _ in range(3):
        parts.append(value.astype(BF16))
        value = value - parts[-1].astype(F32)
    stacked = jnp.concatenate([part.astype(F32) for part in parts], axis=0).astype(BF16)
    for start in range(0, rows, BLOCK):
        sums = mm(stacked[:, start : start + BLOCK], upper)
        decay[:, start : start + BLOCK] = sums[:8] + sums[8:16] + sums[16:]


def turn(first, second):
    (cos_a, sin_a), (cos_b, sin_b) = first, second
    return cos_a * cos_b - sin_a * sin_b, sin_a * cos_b + cos_a * sin_b


def joined(first, second):
    return tuple(jnp.concatenate(pair, axis=0) for pair in zip(first, second))


def angle_tables(coarse, fine):
    half, seeds = DH // 2, 8
    index = lax.broadcasted_iota(jnp.int32, (seeds, half), 1).astype(F32)
    frequency = jnp.exp(index * (-math.log(10000.0) / half))
    place = lax.broadcasted_iota(jnp.int32, (seeds, half), 0).astype(F32)
    offset = (lax.axis_index("ctx") * (coarse.shape[1] * FINE)).astype(F32)
    near = jnp.cos(place * frequency), jnp.sin(place * frequency)
    base = jnp.cos(offset * frequency), jnp.sin(offset * frequency)
    step = turn([part[seeds - 1 : seeds] for part in near], [part[1:2] for part in near])
    while near[0].shape[0] < FINE:
        near = joined(near, turn(near, step))
        step = turn(step, step)
    far = tuple(part[:1] for part in base)
    while far[0].shape[0] < coarse.shape[1]:
        far = joined(far, turn(far, step))
        step = turn(step, step)
    for table, parts in ((coarse, far), (fine, near)):
        table[0], table[1] = (part[: table.shape[1]] for part in parts)


class Loads:
    def __init__(self, arrived):
        self.arrived, self.count = arrived, 0

    def start(self, source, target):
        copy = pltpu.make_async_copy(source, target, self.arrived.at[self.count])
        self.count += 1
        copy.start()
        return copy


def key_value_own_kernel(
    x_far, wk_far, wv_far, log_decay_far, wo_far, wq_far, wg_far,
    x_own, x_other, acc_k, acc_v, decay, coarse, fine, wo, wq, wg, wk, wv, log_decay, arrived,
):
    rows, part = x_own.shape
    core = lax.axis_index("fsdp")
    loads = Loads(arrived)

    def tile(x, half, start):
        at = pl.ds(start, BLOCK)
        columns = pl.ds(pl.multiple_of(half * part, part), part)
        return loads.start(x_far.at[at, columns], x.at[at])

    starts = range(0, rows, BLOCK)
    logs, key = loads.start(log_decay_far, log_decay), loads.start(wk_far, wk)
    tiles = [tile(x_own, core, start) for start in starts]
    value = loads.start(wv_far, wv)
    others = [tile(x_other, 1 - core, start) for start in starts]
    others += [loads.start(wo_far, wo), loads.start(wq_far, wq), loads.start(wg_far, wg)]
    key.wait()
    tiles[0].wait()
    for number, start in enumerate(starts):
        at = slice(start, start + BLOCK)
        if number:
            tiles[number].wait()
        acc_k[at, :] = mm(x_own[at, :], wk[...])
    value.wait()
    logs.wait()
    angle_tables(coarse, fine)
    decay_sums(log_decay, decay)
    for start in starts:
        at = slice(start, start + BLOCK)
        acc_v[at, :] = mm(x_own[at, :], wv[...])
    for copy in others:
        copy.wait()


def pack_message(message, states, logs):
    heads = len(states)
    place = lax.broadcasted_iota(jnp.int32, (EXTRA, DH), 0)
    tail = jnp.zeros((EXTRA, DH), F32)
    for head in range(heads):
        message[head * DH : (head + 1) * DH, :] = states[head].astype(BF16)
        rest = logs[head]
        for number in range(3):
            piece = rest.astype(BF16).astype(F32)
            tail = jnp.where(place == 3 * head + number, piece, tail)
            rest = rest - piece
    message[heads * DH :, :] = tail.astype(BF16)


def message_log(message, heads, head):
    tail = message[heads * DH :, :].astype(F32)
    return (tail[3 * head : 3 * head + 1] + tail[3 * head + 1 : 3 * head + 2] + tail[3 * head + 2 : 3 * head + 3])[:, :1]


def exchanges(ctx, hop):
    lower = range(ctx - hop)
    if hop == 1:
        return [], list(lower), []
    early = [at for at in lower if at < hop // 2]
    even = [at for at in lower if at >= hop // 2 and at // hop % 2 == 0]
    odd = [at for at in lower if at // hop % 2 == 1]
    return early, even, odd


def is_upper(lowers, hop):
    place = lax.axis_index("ctx")
    found = place < 0
    for lower in lowers:
        found = jnp.logical_or(found, place == lower + hop)
    return found


def arrived_state(arrivals, sets, hop, span):
    parts = [jnp.where(is_upper(lowers, hop), ref[span, :].astype(F32), 0.0) for ref, lowers in zip(arrivals, sets)]
    return functools.reduce(lambda a, b: a + b, parts)


def arrived_log(arrivals, sets, hop, heads, head):
    parts = [jnp.where(is_upper(lowers, hop), message_log(ref, heads, head), 0.0) for ref, lowers in zip(arrivals, sets)]
    return functools.reduce(lambda a, b: a + b, parts)


def key_value_kernel(
    heads, x, wk, wv, acc_k, acc_v, decay, coarse, fine, k_out, v_out, before_out, state_out, message
):
    state_out[...] = jnp.zeros_like(state_out)

    totals = jnp.zeros((1, 8), F32)
    for block in range(x.shape[0] // BLOCK):
        start = block * BLOCK
        columns = decay[:, slice(start, start + BLOCK)].T
        ending = columns[BLOCK - 1 : BLOCK, :]
        faded = jnp.exp(ending - columns)
        at = slice(start, start + BLOCK)
        cosine, sine = angles(coarse, fine, start, BLOCK)
        keys = turned(acc_k[at, :] + mm(x[at, :], wk[...]), cosine, sine)
        k_out[at, :] = keys
        values = (acc_v[at, :] + mm(x[at, :], wv[...])).astype(BF16)
        v_out[at, :] = values
        for head in range(heads):
            span = slice(head * DH, (head + 1) * DH)
            weighted = (keys[:, span].astype(F32) * faded[:, head : head + 1]).astype(BF16)
            old = state_out[span, :]
            before_out[block, span, :] = old.astype(BF16)
            state_out[span, :] = jnp.exp(ending[:, head : head + 1]) * old + mm_tn(weighted, values[:, span])
        totals = totals + ending
    states = [state_out[head * DH : (head + 1) * DH, :] for head in range(heads)]
    pack_message(message, states, [totals[:, head : head + 1] for head in range(heads)])


def combine_kernel(heads, hop, sets, first, last, state, sent, *refs):
    if not first:
        old_entering, refs = refs[0], refs[1:]
    arrivals, entering = refs[: len(sets)], refs[len(sets)]
    outs = refs[len(sets) + 1 :]
    states, logs = [], []
    for head in range(heads):
        span = slice(head * DH, (head + 1) * DH)
        row = slice(heads * DH + head, heads * DH + head + 1)
        arrived = arrived_state(arrivals, sets, hop, span)
        log = arrived_log(arrivals, sets, hop, heads, head)
        window_log = message_log(sent, heads, head)
        if first:
            entering[span, :] = arrived
            entering_log = log
        else:
            before_log = old_entering[row, :1]
            entering[span, :] = old_entering[span, :] + jnp.exp(before_log) * arrived
            entering_log = before_log + log
        entering[row, :] = jnp.broadcast_to(entering_log, (1, DH))
        new = state[span, :] + jnp.exp(window_log) * arrived
        if last:
            outs[head][...] = new.astype(BF16)
        else:
            outs[0][span, :] = new
        states.append(new)
        logs.append(window_log + log)
    if not last:
        pack_message(outs[1], states, logs)


def query_gate_kernel(
    heads, block, x_own, x_other, wq, wq_far, wg, wg_far, decay, coarse, fine, k, v, q_out, g_out, intra_out
):
    start = block * BLOCK
    lines = decay[:, start : start + BLOCK]
    columns = lines.T

    at = slice(start, start + BLOCK)
    cosine, sine = angles(coarse, fine, start, BLOCK)
    q_out[...] = turned(mm(x_own[at, :], wq[...]) + mm(x_other[at, :], wq_far[...]), cosine, sine)
    gates = (mm(x_own[at, :], wg[...]) + mm(x_other[at, :], wg_far[...])).astype(BF16).astype(F32)
    g_out[...] = gates / (1.0 + jnp.exp(-gates))
    for piece in range(BLOCK // TILE):
        low, last = piece * TILE, (piece + 1) * TILE
        place_t = lax.broadcasted_iota(jnp.int32, (TILE, last), 0) + low
        place_s = lax.broadcasted_iota(jnp.int32, (TILE, last), 1)
        causal = place_t >= place_s
        for head in range(heads):
            span = slice(head * DH, (head + 1) * DH)
            scores = mm_nt(q_out[low:last, span], k[start : start + last, span])
            differ = columns[low:last, head : head + 1] - lines[head : head + 1, :last]
            weights = jnp.where(causal, jnp.exp(jnp.where(causal, differ, 0.0)), 0.0)
            intra_out[low:last, span] = mm((scores * weights).astype(BF16), v[start : start + last, span])


def hidden_kernel(heads, head, hop, early_sets, late_sets, pieces, decay, before, entering, *refs):
    early, refs = refs[: len(early_sets)], refs[len(early_sets) :]
    late, refs = refs[: len(late_sets)], refs[len(late_sets) :]
    projected, outs, token = refs[: -len(pieces) - 1], refs[-len(pieces) - 1 : -1], refs[-1]
    token[...] = jnp.zeros_like(token)
    span = slice(head * DH, (head + 1) * DH)
    arrived = arrived_state(late, late_sets, hop, slice(0, DH))
    if early_sets:
        arrived = arrived + arrived_state(early, early_sets, hop, span)
    entering_log = entering[heads * DH + head : heads * DH + head + 1, :1]
    state = entering[span, :] + jnp.exp(entering_log) * arrived
    for (start, count), out in zip(pieces, outs):
        block = start // BLOCK
        q, gate, intra = projected[3 * block : 3 * block + 3]
        scale_log = jnp.zeros((1, 1), F32)
        for earlier in range(block):
            end = (earlier + 1) * BLOCK
            scale_log = scale_log + decay[head : head + 1, end - 1 : end]
        prior = (jnp.exp(scale_log) * state + before[block, span, :].astype(F32)).astype(BF16)
        for low in range(0, count, TILE):
            first = start % BLOCK + low
            at = slice(first, first + TILE)
            column = jnp.exp(decay[:, start + low : start + low + TILE].T[:, head : head + 1])
            retained = intra[at, span] + column * mm(q[at, span], prior)
            center = retained - jnp.mean(retained, axis=1, keepdims=True)
            spread = jnp.mean(center * center, axis=1, keepdims=True)
            out[low : low + TILE, :] = (gate[at, span] * center * lax.rsqrt(spread + 1e-5)).astype(BF16)


def columns_kernel(first, second, out):
    cols = out.shape[1] // 2
    place, core = lax.axis_index("tp"), lax.axis_index("fsdp")
    high, low = place // 2, place % 2

    @pl.when(core == 0)
    def _():
        at = pl.ds(pl.multiple_of((1 - low) * cols, cols), cols)
        out[:, :cols] = first[:, at]
        out[:, cols:] = second[:, at]

    @pl.when(core == 1)
    def _():
        out[...] = jnp.where(high == 0, first[...], second[...])


def arrange_kernel(mine, other, low_out, high_out):
    cols = mine.shape[1] // 2
    place, core = lax.axis_index("tp"), lax.axis_index("fsdp")
    for gathered, bit, out in ((core == 0, place // 2, low_out), (core == 1, place % 2, high_out)):
        give = pl.ds(pl.multiple_of((1 - bit) * cols, cols), cols)
        keep = pl.ds(pl.multiple_of(bit * cols, cols), cols)
        out[:, :cols] = jnp.where(gathered, mine[:, give], other[:, give])
        out[:, cols:] = jnp.where(gathered, mine[:, keep], other[:, keep])


def own_kernel(order, own_first, own_second, *refs):
    pieces, outs = refs[: len(order)], refs[len(order) :]
    cols = outs[0].shape[1] // 2
    place, core = lax.axis_index("tp"), lax.axis_index("fsdp")
    high, low = place // 2, place % 2
    here = core == high
    mine = pl.ds(pl.multiple_of(low * cols, cols), cols)
    flipped = pl.ds(pl.multiple_of((1 - low) * cols, cols), cols)
    keep = jnp.where(here, own_first[:, mine], own_second[:, mine])
    gives = [
        jnp.where(here, own_second[:, mine], own_first[:, mine]),
        jnp.where(here, own_first[:, flipped], own_second[:, flipped]),
    ]
    for half in range(2):
        for (head, first, count), piece in sorted(
            ((key[1:], ref) for key, ref in zip(order, pieces) if key[0] == half), key=lambda pair: pair[0]
        ):
            at, span = slice(first, first + count), slice(head * DH, (head + 1) * DH)
            for target, weight in ((slice(0, cols), gives[half]), (slice(cols, 2 * cols), keep)):
                term = mm(piece[...], weight[span, :])
                outs[half][at, target] = term if head == 0 else outs[half][at, target] + term


def far_product(first, keys, fars, weight, columns):
    total = None
    for (head, start, count), far in zip(keys, fars):
        if start <= first < start + count:
            term = mm(far[first - start : first - start + TILE, :], weight[head * DH : (head + 1) * DH, columns])
            total = term if total is None else total + term
    return total


def give_kernel(first, keys, own, weight, *refs):
    fars, out = refs[:-1], refs[-1]
    cols = out.shape[1]
    at = slice(first, first + TILE)
    out[...] = (own[at, :cols] + far_product(first, keys, fars, weight, slice(0, cols))).astype(BF16)


def keep_kernel(order, *refs):
    count = len(order)
    fars, owns, weights, outs = refs[:count], refs[count : count + 2], refs[count + 2 : count + 4], refs[count + 4 :]
    for half in range(2):
        mine = [(key[1:], far) for key, far in zip(order, fars) if key[0] == half]
        keys, pieces = [key for key, _ in mine], [far for _, far in mine]
        cols = outs[half].shape[1]
        for first in range(0, outs[half].shape[0], TILE):
            at = slice(first, first + TILE)
            term = far_product(first, keys, pieces, weights[half], slice(cols, 2 * cols))
            outs[half][at, :] = owns[half][at, cols:] + term


def finish_kernel(order, *refs):
    count = len(order)
    gots, keeps, out, ready, written = refs[:count], refs[count : count + 2], refs[-3], refs[-2], refs[-1]
    copies = []
    for slot, ((half, first), got) in enumerate(zip(order, gots)):
        keep = keeps[half]
        at = slice(first, first + TILE)
        ready[slot] = (keep[at, :] + got[...].astype(F32)).astype(BF16)
        start = half * keep.shape[0] + first
        copies.append(pltpu.make_async_copy(ready.at[slot], out.at[0, pl.ds(start, TILE)], written.at[slot]))
        copies[-1].start()
    for copy in copies:
        copy.wait()


def after(value, *others):
    return lax.optimization_barrier((value, *others))[0]


def on_device(tokens, query_weight, key_weight, value_weight, gate_weight, out_weight, log_decay):
    x = tokens[0]
    rows, width = x.shape
    part, cols = query_weight.shape
    heads = cols // DH
    blocks = rows // BLOCK
    ctx, tp, cores = lax.axis_size("ctx"), lax.axis_size("tp"), lax.axis_size("fsdp")
    assert tp == 4 and cores == 2 and ctx >= 4 and ctx & (ctx - 1) == 0
    near_mask, far_mask = 1, 2
    tables = [((2, rows // FINE, DH // 2), F32), ((2, FINE, DH // 2), F32)]

    key_far = swap(key_weight, "fsdp", 1)
    value_far = swap(value_weight, "fsdp", 1)

    x_own, x_other, acc_k, acc_v, decay, coarse, fine, out_first, own_q, own_g = loading_call(
        key_value_own_kernel,
        [((rows, part), BF16)] * 2
        + [((rows, cols), F32)] * 2
        + [((8, rows), F32)]
        + tables
        + [(out_weight.shape, BF16), ((part, cols), BF16), ((part, cols), BF16)],
        [x, key_weight, value_weight, log_decay[0].T, out_weight, query_weight, gate_weight],
        [],
        [pltpu.VMEM((part, cols), BF16)] * 2 + [pltpu.VMEM((heads, rows), F32)],
        2 * (rows // BLOCK) + 6,
        "key_value_own",
    )
    state_shape, message_shape = (heads * DH, DH), (heads * DH + EXTRA, DH)
    keys, values, before, window, message = kernel_call(
        functools.partial(key_value_kernel, heads),
        [((rows, cols), BF16)] * 2
        + [((blocks, heads * DH, DH), BF16), (state_shape, F32), (message_shape, BF16)],
        [x_other, key_far, value_far, acc_k, acc_v, decay, coarse, fine],
        "key_value",
    )
    far_q, far_g = swap(own_q, "fsdp", 1), swap(own_g, "fsdp", 1)

    def query_gate(block, decay):
        return kernel_call(
            functools.partial(query_gate_kernel, heads, block),
            [((BLOCK, cols), BF16), ((BLOCK, cols), F32), ((BLOCK, cols), F32)],
            [x_own, x_other, own_q, far_q, own_g, far_g, decay, coarse, fine, keys, values],
            "query_gate",
        )

    def exchange(message, lowers, hop):
        pairs = [(at, at + hop) for at in lowers]
        if hop > 1:
            pairs += [(upper, at) for at, upper in pairs]
        return lax.ppermute(message, "ctx", pairs)

    projected = list(query_gate(0, decay))
    window = after(window, projected[0])
    entering, hop, early, first_message = None, 1, [], message
    while True:
        early_sets, late_sets = [], []
        first_set, *late_sets = exchanges(ctx, hop)
        late_sets = [lowers for lowers in late_sets if lowers]
        early_sets = [first_set] if first_set else []
        if 2 * hop >= ctx:
            break
        arrivals = [exchange(message, lowers, hop) for lowers in late_sets] + early
        unchanged = exchanges(ctx, 2 * hop)[0]
        early = [exchange(message, unchanged, 2 * hop)]
        old = [] if entering is None else [entering]
        last = 4 * hop >= ctx
        combined = [((heads * DH + 8, DH), F32)]
        combined += [((DH, DH), BF16)] * heads if last else [(state_shape, F32), (message_shape, BF16)]
        entering, *outs = kernel_call(
            functools.partial(combine_kernel, heads, hop, late_sets + early_sets, entering is None, last),
            combined,
            [window, message, *old, *arrivals],
            "combine",
        )
        if not last:
            window, message = outs
        hop *= 2
    own_second = swap(out_first, "fsdp", 1)
    late = [[exchange(state, lowers, hop) for lowers in late_sets] for state in outs]

    [for_partner] = kernel_call(
        columns_kernel,
        [(out_weight.shape, BF16)],
        [after(out_first, first_message), own_second],
        "columns",
    )
    pairs = [(at * cores + at_core, (at ^ mask) * cores + at_core) for at in range(tp) for at_core, mask in enumerate((near_mask, far_mask))]
    out_mine = lax.ppermute(for_partner, ("tp", "fsdp"), pairs)

    held = after(decay, *outs, *early)
    for block in range(1, blocks):
        projected += query_gate(block, held)

    masks, middle = (near_mask, far_mask), rows // 2
    out_other = swap(after(out_mine, outs[0], *early), "fsdp", 1)
    cuts = [(head, 0, middle) for head in range(heads - 1)]
    cuts += [(heads - 1, first, TILE) for first in range(0, middle, TILE)]
    hidden, far, token = {}, {}, None
    for head, first, count in cuts:
        held = decay if token is None else after(decay, swap(token, "fsdp", 1))
        *pair, token = kernel_call(
            functools.partial(
                hidden_kernel, heads, head, hop, early_sets, late_sets, [(half * middle + first, count) for half in range(2)]
            ),
            [((count, DH), BF16)] * 2 + [((16, 128), BF16)],
            [held, before, entering, *early, *late[head], *projected],
            "hidden",
        )
        for half in range(2):
            key = half, head, first, count
            hidden[key], far[key] = pair[half], swap(pair[half], "tp", masks[half])
    weights = kernel_call(
        arrange_kernel,
        [((cols, 2 * cols), BF16)] * 2,
        [out_mine, out_other],
        "arrange",
    )
    order = [(half, *cut) for cut in reversed(cuts) for half in (1, 0)]
    owns = kernel_call(
        functools.partial(own_kernel, order),
        [((middle, 2 * cols), F32)] * 2,
        [out_first, own_second, *(hidden[key] for key in order)],
        "own_products",
    )
    tiles = [(half, first) for first in reversed(range(0, middle, TILE)) for half in (1, 0)]
    gots = []
    for half, first in tiles:
        keys = [key for key in order if key[0] == half and key[2] <= first < key[2] + key[3]]
        [give] = kernel_call(
            functools.partial(give_kernel, first, [key[1:] for key in keys]),
            [((TILE, cols), BF16)],
            [owns[half], weights[half], *(far[key] for key in keys)],
            "give",
        )
        gots.append(swap(give, "tp", masks[1 - half]))
    keeps = kernel_call(
        functools.partial(keep_kernel, order),
        [((middle, cols), F32)] * 2,
        [*(far[key] for key in order), *owns, *weights],
        "keep",
    )
    result = None
    for part_order, part_gots in ((tiles[2:], gots[2:]), (tiles[:2], gots[:2])):
        arrays = [pltpu.with_memory_space_constraint(array, pltpu.VMEM) for array in (*part_gots, *keeps)]
        held = [] if result is None else [result]
        result = pl.pallas_call(
            functools.partial(finish_kernel, part_order),
            in_specs=[pl.BlockSpec(memory_space=pltpu.VMEM)] * len(arrays)
            + [pl.BlockSpec(memory_space=pltpu.HBM)] * len(held),
            out_specs=pl.BlockSpec(memory_space=pltpu.HBM),
            out_shape=jax.ShapeDtypeStruct((1, rows, cols), BF16),
            input_output_aliases={len(arrays): 0} if held else {},
            scratch_shapes=[
                pltpu.VMEM((len(part_order), TILE, cols), BF16),
                pltpu.SemaphoreType.DMA((len(part_order),)),
            ],
            compiler_params=pltpu.CompilerParams(vmem_limit_bytes=VMEM_LIMIT),
            name="finish",
        )(*arrays, *held)
    return result


def solution(mesh):
    in_specs = (
        P("fsdp", "ctx", None),
        P("fsdp", "tp"),
        P("fsdp", "tp"),
        P("fsdp", "tp"),
        P("fsdp", "tp"),
        P("tp", "fsdp"),
        P("fsdp", "ctx", "tp"),
    )
    out_specs = P("fsdp", "ctx", "tp")
    return jax.shard_map(
        on_device, mesh=mesh, in_specs=in_specs, out_specs=out_specs, check_vma=False
    )
```

```python
import functools
import math

import jax
import jax.numpy as jnp
from jax import lax
from jax.experimental import pallas as pl
from jax.experimental.pallas import tpu as pltpu
from jax.sharding import PartitionSpec as P

DH = 256
BLOCK = 512
TILE = 256
FINE = 32
EXTRA = 16
VMEM_LIMIT = 14 * 1024 * 1024
F32 = jnp.float32
BF16 = jnp.bfloat16


def mm(left, right):
    return jnp.dot(left, right, preferred_element_type=F32)


def mm_nt(left, right):
    return lax.dot_general(left, right, (((1,), (1,)), ((), ())), preferred_element_type=F32)


def mm_tn(left, right):
    return lax.dot_general(left, right, (((0,), (0,)), ((), ())), preferred_element_type=F32)


def swap(value, axis, mask):
    size = lax.axis_size(axis)
    return lax.ppermute(value, axis, [(place, place ^ mask) for place in range(size)])


def kernel_call(kernel, outs, operands, name):
    arrays = [pltpu.with_memory_space_constraint(array, pltpu.VMEM) for array in operands]
    return pl.pallas_call(
        kernel,
        in_specs=[pl.BlockSpec(memory_space=pltpu.VMEM)] * len(operands),
        out_specs=[pl.BlockSpec(memory_space=pltpu.VMEM)] * len(outs),
        out_shape=[pltpu.VMEM(shape, dtype) for shape, dtype in outs],
        compiler_params=pltpu.CompilerParams(vmem_limit_bytes=VMEM_LIMIT),
        cost_estimate=pl.CostEstimate(
            flops=1, bytes_accessed=1, transcendentals=0
        ),
        name=name,
    )(*arrays)


def loading_call(kernel, outs, loaded, operands, scratch, loads, name):
    arrays = [pltpu.with_memory_space_constraint(array, pltpu.HBM) for array in loaded]
    arrays += [pltpu.with_memory_space_constraint(array, pltpu.VMEM) for array in operands]
    return pl.pallas_call(
        kernel,
        in_specs=[pl.BlockSpec(memory_space=pltpu.HBM)] * len(loaded)
        + [pl.BlockSpec(memory_space=pltpu.VMEM)] * len(operands),
        out_specs=[pl.BlockSpec(memory_space=pltpu.VMEM)] * len(outs),
        out_shape=[pltpu.VMEM(shape, dtype) for shape, dtype in outs],
        scratch_shapes=[*scratch, pltpu.SemaphoreType.DMA((loads,))],
        compiler_params=pltpu.CompilerParams(vmem_limit_bytes=VMEM_LIMIT),
        cost_estimate=pl.CostEstimate(flops=1, bytes_accessed=1, transcendentals=0),
        name=name,
    )(*arrays)


def turned(values, cosine, sine):
    half = DH // 2
    parts = []
    for start in range(0, values.shape[1], DH):
        low = values[:, start : start + half]
        high = values[:, start + half : start + DH]
        parts.append((low * cosine - high * sine).astype(BF16))
        parts.append((high * cosine + low * sine).astype(BF16))
    return jnp.concatenate(parts, axis=1)


def angles(coarse, fine, first, count):
    at = first // FINE
    far = coarse[:, pl.ds(at, count // FINE), :]
    near = fine[...]
    cos_c, sin_c = far[0][:, None, :], far[1][:, None, :]
    cos_f, sin_f = near[0][None], near[1][None]
    cosine = cos_c * cos_f - sin_c * sin_f
    sine = sin_c * cos_f + cos_c * sin_f
    return cosine.reshape(count, DH // 2), sine.reshape(count, DH // 2)


def decay_sums(log_decay, decay):
    heads, rows = log_decay.shape
    place_s = lax.broadcasted_iota(jnp.int32, (BLOCK, BLOCK), 0)
    place_t = lax.broadcasted_iota(jnp.int32, (BLOCK, BLOCK), 1)
    upper = jnp.where(place_s <= place_t, 1.0, 0.0).astype(BF16)
    value = jnp.concatenate([log_decay[...], jnp.zeros((8 - heads, rows), F32)], axis=0)
    parts = []
    for _ in range(3):
        parts.append(value.astype(BF16))
        value = value - parts[-1].astype(F32)
    stacked = jnp.concatenate([part.astype(F32) for part in parts], axis=0).astype(BF16)
    for start in range(0, rows, BLOCK):
        sums = mm(stacked[:, start : start + BLOCK], upper)
        decay[:, start : start + BLOCK] = sums[:8] + sums[8:16] + sums[16:]


def turn(first, second):
    (cos_a, sin_a), (cos_b, sin_b) = first, second
    return cos_a * cos_b - sin_a * sin_b, sin_a * cos_b + cos_a * sin_b


def joined(first, second):
    return tuple(jnp.concatenate(pair, axis=0) for pair in zip(first, second))


def angle_tables(coarse, fine):
    half, seeds = DH // 2, 8
    index = lax.broadcasted_iota(jnp.int32, (seeds, half), 1).astype(F32)
    frequency = jnp.exp(index * (-math.log(10000.0) / half))
    place = lax.broadcasted_iota(jnp.int32, (seeds, half), 0).astype(F32)
    offset = (lax.axis_index("ctx") * (coarse.shape[1] * FINE)).astype(F32)
    near = jnp.cos(place * frequency), jnp.sin(place * frequency)
    base = jnp.cos(offset * frequency), jnp.sin(offset * frequency)
    step = turn([part[seeds - 1 : seeds] for part in near], [part[1:2] for part in near])
    while near[0].shape[0] < FINE:
        near = joined(near, turn(near, step))
        step = turn(step, step)
    far = tuple(part[:1] for part in base)
    while far[0].shape[0] < coarse.shape[1]:
        far = joined(far, turn(far, step))
        step = turn(step, step)
    for table, parts in ((coarse, far), (fine, near)):
        table[0], table[1] = (part[: table.shape[1]] for part in parts)


class Loads:
    def __init__(self, arrived):
        self.arrived, self.count = arrived, 0

    def start(self, source, target):
        copy = pltpu.make_async_copy(source, target, self.arrived.at[self.count])
        self.count += 1
        copy.start()
        return copy


def key_value_own_kernel(
    x_far, wk_far, wv_far, log_decay_far, wo_far, wq_far, wg_far,
    x_own, x_other, acc_k, acc_v, decay, coarse, fine, wo, wq, wg, wk, wv, log_decay, arrived,
):
    rows, part = x_own.shape
    core = lax.axis_index("fsdp")
    loads = Loads(arrived)

    def tile(x, half, start):
        at = pl.ds(start, BLOCK)
        columns = pl.ds(pl.multiple_of(half * part, part), part)
        return loads.start(x_far.at[at, columns], x.at[at])

    starts = range(0, rows, BLOCK)
    logs, key = loads.start(log_decay_far, log_decay), loads.start(wk_far, wk)
    tiles = [tile(x_own, core, 0)]
    logs.wait()
    tiles += [tile(x_own, core, start) for start in starts[1:]]
    value = loads.start(wv_far, wv)
    angle_tables(coarse, fine)
    decay_sums(log_decay, decay)
    key.wait()
    tiles[0].wait()
    others = [tile(x_other, 1 - core, 0)]
    others += [loads.start(far, near) for far, near in ((wo_far, wo), (wq_far, wq), (wg_far, wg))]
    for number, start in enumerate(starts):
        at = slice(start, start + BLOCK)
        if number:
            tiles[number].wait()
        acc_k[at, :] = mm(x_own[at, :], wk[...])
    value.wait()
    for start in starts:
        at = slice(start, start + BLOCK)
        acc_v[at, :] = mm(x_own[at, :], wv[...])
    for copy in others:
        copy.wait()


def block_ends(decay, start, stop):
    ends = [decay[:, end - 1 : end] for end in range(start + BLOCK, stop + 1, BLOCK)]
    return functools.reduce(lambda a, b: a + b, ends, jnp.zeros((decay.shape[0], 1), F32))


def pack_message(message, states, logs):
    for head, state in enumerate(states):
        message[head * DH : (head + 1) * DH, :] = state.astype(BF16)
    large = logs.astype(BF16).astype(F32)
    parts = jnp.concatenate([large, logs - large], axis=0)
    message[len(states) * DH :, :] = jnp.broadcast_to(parts, (EXTRA, DH)).astype(BF16)


def message_log(message, heads):
    tail = message[heads * DH :, :].astype(F32)
    return (tail[: EXTRA // 2] + tail[EXTRA // 2 :])[:, :1]


def exchanges(ctx, hop):
    lower = range(ctx - hop)
    if hop == 1:
        return [], list(lower), []
    early = [at for at in lower if at < hop // 2]
    even = [at for at in lower if at >= hop // 2 and at // hop % 2 == 0]
    odd = [at for at in lower if at // hop % 2 == 1]
    return early, even, odd


def is_upper(lowers, hop):
    place = lax.axis_index("ctx")
    found = place < 0
    for lower in lowers:
        found = jnp.logical_or(found, place == lower + hop)
    return found


def arrived_state(arrivals, sets, hop, span):
    parts = [jnp.where(is_upper(lowers, hop), ref[span, :].astype(F32), 0.0) for ref, lowers in zip(arrivals, sets)]
    return functools.reduce(lambda a, b: a + b, parts)


def arrived_log(arrivals, sets, hop, heads):
    parts = [jnp.where(is_upper(lowers, hop), message_log(ref, heads), 0.0) for ref, lowers in zip(arrivals, sets)]
    return functools.reduce(lambda a, b: a + b, parts)


def key_value_kernel(
    heads, x_far, x_first, wk, wv, acc_k, acc_v, decay, coarse, fine,
    x_rest, k_out, v_out, before_out, state_out, message, arrived,
):
    part = wk.shape[0]
    blocks = acc_k.shape[0] // BLOCK
    loads = Loads(arrived)
    columns = pl.ds(pl.multiple_of((1 - lax.axis_index("fsdp")) * part, part), part)
    rest = [
        loads.start(x_far.at[pl.ds(block * BLOCK, BLOCK), columns], x_rest.at[pl.ds((block - 1) * BLOCK, BLOCK)])
        for block in range(1, blocks)
    ]
    state_out[...] = jnp.zeros_like(state_out)
    for block in range(blocks):
        start = block * BLOCK
        at = slice(start, start + BLOCK)
        columns = decay[:, at].T
        ending = columns[BLOCK - 1 : BLOCK, :]
        faded = jnp.exp(ending - columns)
        if block:
            rest[block - 1].wait()
        x = x_rest[start - BLOCK : start, :] if block else x_first[...]
        cosine, sine = angles(coarse, fine, start, BLOCK)
        keys = turned(acc_k[at, :] + mm(x, wk[...]), cosine, sine)
        k_out[at, :] = keys
        values = (acc_v[at, :] + mm(x, wv[...])).astype(BF16)
        v_out[at, :] = values
        for head in range(heads):
            span = slice(head * DH, (head + 1) * DH)
            weighted = (keys[:, span].astype(F32) * faded[:, head : head + 1]).astype(BF16)
            old = state_out[span, :]
            before_out[block, span, :] = old.astype(BF16)
            state_out[span, :] = jnp.exp(ending[:, head : head + 1]) * old + mm_tn(weighted, values[:, span])
    states = [state_out[head * DH : (head + 1) * DH, :] for head in range(heads)]
    pack_message(message, states, block_ends(decay, 0, acc_k.shape[0]))


def combine_kernel(heads, hop, sets, first, last, state, sent, *refs):
    if not first:
        old_entering, refs = refs[0], refs[1:]
    arrivals, entering, message = refs[: len(sets)], refs[len(sets)], refs[len(sets) + 1]
    window_log, log = message_log(sent, heads), arrived_log(arrivals, sets, hop, heads)
    before_log = jnp.zeros_like(log) if first else old_entering[heads * DH :, :1]
    states = []
    for head in range(heads):
        span, row = slice(head * DH, (head + 1) * DH), slice(head, head + 1)
        arrived = arrived_state(arrivals, sets, hop, span)
        if first:
            entering[span, :] = arrived
        else:
            entering[span, :] = old_entering[span, :] + jnp.exp(before_log[row]) * arrived
        states.append(state[span, :] + jnp.exp(window_log[row]) * arrived)
        if last:
            message[span, :] = states[-1].astype(BF16)
        else:
            refs[len(sets) + 2][span, :] = states[-1]
    entering[heads * DH :, :] = jnp.broadcast_to(before_log + log, (8, DH))
    if not last:
        pack_message(message, states, window_log + log)


def query_gate_kernel(
    heads, block, x_own, x_other, wq, wq_far, wg, wg_far, decay, coarse, fine, k, v, q_out, g_out, intra_out
):
    start = block * BLOCK
    lines = decay[:, start : start + BLOCK]
    columns = lines.T

    at = slice(start, start + BLOCK)
    cosine, sine = angles(coarse, fine, start, BLOCK)
    far = slice(max(start - BLOCK, 0), max(start - BLOCK, 0) + BLOCK)
    queries = mm(x_own[at, :], wq[...]) + mm(x_other[far, :], wq_far[...])
    q_out[...] = turned(queries, cosine, sine)
    gates = mm(x_own[at, :], wg[...]) + mm(x_other[far, :], wg_far[...])
    gates = gates.astype(BF16).astype(F32)
    g_out[...] = gates / (1.0 + jnp.exp(-gates))
    for piece in range(BLOCK // TILE):
        low, last = piece * TILE, (piece + 1) * TILE
        place_t = lax.broadcasted_iota(jnp.int32, (TILE, last), 0) + low
        place_s = lax.broadcasted_iota(jnp.int32, (TILE, last), 1)
        causal = place_t >= place_s
        for head in range(heads):
            span = slice(head * DH, (head + 1) * DH)
            scores = mm_nt(q_out[low:last, span], k[start : start + last, span])
            differ = columns[low:last, head : head + 1] - lines[head : head + 1, :last]
            weights = jnp.where(causal, jnp.exp(jnp.where(causal, differ, 0.0)), 0.0)
            intra_out[low:last, span] = mm((scores * weights).astype(BF16), v[start : start + last, span])


def hidden_kernel(heads, hop, sets, starts, decay, before, entering, *refs):
    arrivals, refs, token = refs[: len(sets)], refs[len(sets) : -1], refs[-1]
    projected, outs = refs[: -len(starts)], refs[-len(starts) :]
    token[...] = jnp.zeros_like(token)
    for head in range(heads):
        span = slice(head * DH, (head + 1) * DH)
        entering_log = entering[heads * DH + head : heads * DH + head + 1, :1]
        state = entering[span, :] + jnp.exp(entering_log) * arrived_state(arrivals, sets, hop, span)
        for start, out in zip(starts, outs):
            block = start // BLOCK
            q, gate, intra = projected[3 * block : 3 * block + 3]
            at = slice(start % BLOCK, start % BLOCK + TILE)
            column = jnp.exp(decay[:, start : start + TILE].T[:, head : head + 1])
            scale_log = jnp.zeros((1, 1), F32)
            for earlier in range(block):
                end = (earlier + 1) * BLOCK
                scale_log = scale_log + decay[head : head + 1, end - 1 : end]
            prior = (jnp.exp(scale_log) * state + before[block, span, :].astype(F32)).astype(BF16)
            retained = intra[at, span] + column * mm(q[at, span], prior)
            center = retained - jnp.mean(retained, axis=1, keepdims=True)
            spread = jnp.mean(center * center, axis=1, keepdims=True)
            out[:, span] = (gate[at, span] * center * lax.rsqrt(spread + 1e-5)).astype(BF16)


def columns_kernel(first, second, out):
    cols = out.shape[1] // 2
    place, core = lax.axis_index("tp"), lax.axis_index("fsdp")
    high, low = place // 2, place % 2

    @pl.when(core == 0)
    def _():
        at = pl.ds(pl.multiple_of((1 - low) * cols, cols), cols)
        out[:, :cols] = first[:, at]
        out[:, cols:] = second[:, at]

    @pl.when(core == 1)
    def _():
        out[...] = jnp.where(high == 0, first[...], second[...])


def arrange_kernel(mine, other, low_out, high_out):
    cols = mine.shape[1] // 2
    place, core = lax.axis_index("tp"), lax.axis_index("fsdp")
    for gathered, bit, out in ((core == 0, place // 2, low_out), (core == 1, place % 2, high_out)):
        give = pl.ds(pl.multiple_of((1 - bit) * cols, cols), cols)
        keep = pl.ds(pl.multiple_of(bit * cols, cols), cols)
        out[:, :cols] = jnp.where(gathered, mine[:, give], other[:, give])
        out[:, cols:] = jnp.where(gathered, mine[:, keep], other[:, keep])


def own_kernel(order, own_first, own_second, *refs):
    pieces, outs = refs[: len(order)], refs[len(order) :]
    cols = pieces[0].shape[1]
    place, core = lax.axis_index("tp"), lax.axis_index("fsdp")
    high, low = place // 2, place % 2
    here = core == high
    mine = pl.ds(pl.multiple_of(low * cols, cols), cols)
    flipped = pl.ds(pl.multiple_of((1 - low) * cols, cols), cols)
    keep = jnp.where(here, own_first[:, mine], own_second[:, mine])
    gives = [
        jnp.where(here, own_second[:, mine], own_first[:, mine]),
        jnp.where(here, own_first[:, flipped], own_second[:, flipped]),
    ]
    for (half, number), piece in zip(order, pieces):
        at = slice(number * TILE, (number + 1) * TILE)
        outs[half][at, :cols] = mm(piece[...], gives[half])
        outs[half][at, cols:] = mm(piece[...], keep)


def give_kernel(number, own, far, weight, out):
    cols = out.shape[1]
    at = slice(number * TILE, (number + 1) * TILE)
    out[...] = (own[at, :cols] + mm(far[...], weight[:, :cols])).astype(BF16)


def keep_kernel(order, *refs):
    count = len(order)
    fars, owns, weights, outs = refs[:count], refs[count : count + 2], refs[count + 2 : count + 4], refs[count + 4 :]
    for (half, number), far in zip(order, fars):
        cols = far.shape[1]
        at = slice(number * TILE, (number + 1) * TILE)
        outs[half][at, :] = owns[half][at, cols:] + mm(far[...], weights[half][:, cols:])


def finish_kernel(order, *refs):
    count = len(order)
    gots, keeps, out, ready, written = refs[:count], refs[count : count + 2], refs[-3], refs[-2], refs[-1]
    copies = []
    for slot, ((half, number), got) in enumerate(zip(order, gots)):
        keep = keeps[half]
        at = slice(number * TILE, (number + 1) * TILE)
        ready[slot] = (keep[at, :] + got[...].astype(F32)).astype(BF16)
        start = half * keep.shape[0] + number * TILE
        copies.append(pltpu.make_async_copy(ready.at[slot], out.at[0, pl.ds(start, TILE)], written.at[slot]))
        copies[-1].start()
    for copy in copies:
        copy.wait()


def after(value, *others):
    return lax.optimization_barrier((value, *others))[0]


def on_device(tokens, query_weight, key_weight, value_weight, gate_weight, out_weight, log_decay):
    x = tokens[0]
    rows, width = x.shape
    part, cols = query_weight.shape
    heads = cols // DH
    blocks = rows // BLOCK
    ctx, tp, cores = lax.axis_size("ctx"), lax.axis_size("tp"), lax.axis_size("fsdp")
    assert tp == 4 and cores == 2 and ctx >= 4 and ctx & (ctx - 1) == 0
    near_mask, far_mask = 1, 2
    tables = [((2, rows // FINE, DH // 2), F32), ((2, FINE, DH // 2), F32)]

    key_far = swap(key_weight, "fsdp", 1)
    value_far = swap(value_weight, "fsdp", 1)

    x_own, x_first, acc_k, acc_v, decay, coarse, fine, out_first, own_q, own_g = loading_call(
        key_value_own_kernel,
        [((rows, part), BF16), ((BLOCK, part), BF16), ((rows, cols), F32), ((rows, cols), F32), ((8, rows), F32)]
        + tables
        + [(out_weight.shape, BF16), ((part, cols), BF16), ((part, cols), BF16)],
        [x, key_weight, value_weight, log_decay[0].T, out_weight, query_weight, gate_weight],
        [],
        [pltpu.VMEM((part, cols), BF16)] * 2 + [pltpu.VMEM((heads, rows), F32)],
        rows // BLOCK + 7,
        "key_value_own",
    )
    state_shape, message_shape = (heads * DH, DH), (heads * DH + EXTRA, DH)
    x_rest, keys, values, before, window, message = loading_call(
        functools.partial(key_value_kernel, heads),
        [((rows - BLOCK, part), BF16)]
        + [((rows, cols), BF16)] * 2
        + [((blocks, heads * DH, DH), BF16), (state_shape, F32), (message_shape, BF16)],
        [x],
        [x_first, key_far, value_far, acc_k, acc_v, decay, coarse, fine],
        [],
        rows // BLOCK - 1,
        "key_value",
    )
    far_q, far_g = swap(own_q, "fsdp", 1), swap(own_g, "fsdp", 1)

    def query_gate(block, decay):
        return kernel_call(
            functools.partial(query_gate_kernel, heads, block),
            [((BLOCK, cols), BF16), ((BLOCK, cols), F32), ((BLOCK, cols), F32)],
            [x_own, x_rest if block else x_first, own_q, far_q, own_g, far_g, decay, coarse, fine, keys, values],
            "query_gate",
        )

    def exchange(message, lowers, hop):
        pairs = [(at, at + hop) for at in lowers]
        if hop > 1:
            pairs += [(upper, at) for at, upper in pairs]
        return lax.ppermute(message, "ctx", pairs)

    projected = list(query_gate(0, decay))
    window = after(window, projected[0])
    entering, hop, early, first_message = None, 1, [], message
    while True:
        first_set, *later_sets = exchanges(ctx, hop)
        later_sets = [lowers for lowers in later_sets if lowers]
        sets = later_sets + ([first_set] if first_set else [])
        arrivals = [exchange(message, lowers, hop) for lowers in later_sets] + early
        if 2 * hop >= ctx:
            break
        unchanged = exchanges(ctx, 2 * hop)[0]
        early = [exchange(message, unchanged, 2 * hop)]
        old = [] if entering is None else [entering]
        last = 4 * hop >= ctx
        entering, message, *windows = kernel_call(
            functools.partial(combine_kernel, heads, hop, sets, entering is None, last),
            [((heads * DH + 8, DH), F32)]
            + ([(state_shape, BF16)] if last else [(message_shape, BF16), (state_shape, F32)]),
            [window, message, *old, *arrivals],
            "combine",
        )
        window = windows[0] if windows else None
        hop *= 2

    own_second = swap(out_first, "fsdp", 1)
    [for_partner] = kernel_call(
        columns_kernel,
        [(out_weight.shape, BF16)],
        [after(out_first, first_message), own_second],
        "columns",
    )
    pairs = [(at * cores + at_core, (at ^ mask) * cores + at_core) for at in range(tp) for at_core, mask in enumerate((near_mask, far_mask))]
    out_mine = lax.ppermute(for_partner, ("tp", "fsdp"), pairs)

    held = after(decay, message, *early)
    for block in range(1, blocks):
        projected += query_gate(block, held)

    count = rows // 2 // TILE
    masks = (near_mask, far_mask)
    hidden, far = [[], []], [[], []]
    for number in range(count):
        held = after(decay, swap(pair[2], "fsdp", 1)) if number else decay
        pair = kernel_call(
            functools.partial(hidden_kernel, heads, hop, sets, [(half * count + number) * TILE for half in range(2)]),
            [((TILE, cols), BF16)] * 2 + [((16, 128), BF16)],
            [held, before, entering, *arrivals, *projected],
            "hidden",
        )
        if number == 0:
            out_other = swap(after(out_mine, pair[0]), "fsdp", 1)
        for half in range(2):
            hidden[half].append(pair[half])
            far[half].append(swap(pair[half], "tp", masks[half]))
    weights = kernel_call(
        arrange_kernel,
        [((cols, 2 * cols), BF16)] * 2,
        [out_mine, out_other],
        "arrange",
    )
    order = [(half, number) for number in reversed(range(count)) for half in (1, 0)]
    owns = kernel_call(
        functools.partial(own_kernel, order),
        [((count * TILE, 2 * cols), F32)] * 2,
        [out_first, own_second, *(hidden[half][number] for half, number in order)],
        "own_products",
    )
    gots = []
    for half, number in order:
        [give] = kernel_call(
            functools.partial(give_kernel, number),
            [((TILE, cols), BF16)],
            [owns[half], far[half][number], weights[half]],
            "give",
        )
        gots.append(swap(give, "tp", masks[1 - half]))
    keeps = kernel_call(
        functools.partial(keep_kernel, order),
        [((count * TILE, cols), F32)] * 2,
        [*(far[half][number] for half, number in order), *owns, *weights],
        "keep",
    )
    result = None
    for part_order, part_gots in ((order[2:], gots[2:]), (order[:2], gots[:2])):
        arrays = [pltpu.with_memory_space_constraint(array, pltpu.VMEM) for array in (*part_gots, *keeps)]
        held = [] if result is None else [result]
        result = pl.pallas_call(
            functools.partial(finish_kernel, part_order),
            in_specs=[pl.BlockSpec(memory_space=pltpu.VMEM)] * len(arrays)
            + [pl.BlockSpec(memory_space=pltpu.HBM)] * len(held),
            out_specs=pl.BlockSpec(memory_space=pltpu.HBM),
            out_shape=jax.ShapeDtypeStruct((1, rows, cols), BF16),
            input_output_aliases={len(arrays): 0} if held else {},
            scratch_shapes=[
                pltpu.VMEM((len(part_order), TILE, cols), BF16),
                pltpu.SemaphoreType.DMA((len(part_order),)),
            ],
            compiler_params=pltpu.CompilerParams(vmem_limit_bytes=VMEM_LIMIT),
            name="finish",
        )(*arrays, *held)
    return result


def solution(mesh):
    in_specs = (
        P("fsdp", "ctx", None),
        P("fsdp", "tp"),
        P("fsdp", "tp"),
        P("fsdp", "tp"),
        P("fsdp", "tp"),
        P("tp", "fsdp"),
        P("fsdp", "ctx", "tp"),
    )
    out_specs = P("fsdp", "ctx", "tp")
    return jax.shard_map(
        on_device, mesh=mesh, in_specs=in_specs, out_specs=out_specs, check_vma=False
    )
```

```python
import functools
import math

import jax
import jax.numpy as jnp
from jax import lax
from jax.experimental import pallas as pl
from jax.experimental.pallas import tpu as pltpu
from jax.sharding import PartitionSpec as P

DH = 256
BLOCK = 512
TILE = 256
FINE = 32
EXTRA = 16
VMEM_LIMIT = 14 * 1024 * 1024
F32 = jnp.float32
BF16 = jnp.bfloat16


def mm(left, right):
    return jnp.dot(left, right, preferred_element_type=F32)


def mm_nt(left, right):
    return lax.dot_general(left, right, (((1,), (1,)), ((), ())), preferred_element_type=F32)


def mm_tn(left, right):
    return lax.dot_general(left, right, (((0,), (0,)), ((), ())), preferred_element_type=F32)


def swap(value, axis, mask):
    size = lax.axis_size(axis)
    return lax.ppermute(value, axis, [(place, place ^ mask) for place in range(size)])


def kernel_call(kernel, outs, operands, name):
    arrays = [pltpu.with_memory_space_constraint(array, pltpu.VMEM) for array in operands]
    return pl.pallas_call(
        kernel,
        in_specs=[pl.BlockSpec(memory_space=pltpu.VMEM)] * len(operands),
        out_specs=[pl.BlockSpec(memory_space=pltpu.VMEM)] * len(outs),
        out_shape=[pltpu.VMEM(shape, dtype) for shape, dtype in outs],
        compiler_params=pltpu.CompilerParams(vmem_limit_bytes=VMEM_LIMIT),
        cost_estimate=pl.CostEstimate(
            flops=1, bytes_accessed=1, transcendentals=0
        ),
        name=name,
    )(*arrays)


def loading_call(kernel, outs, loaded, operands, scratch, loads, name):
    arrays = [pltpu.with_memory_space_constraint(array, pltpu.HBM) for array in loaded]
    arrays += [pltpu.with_memory_space_constraint(array, pltpu.VMEM) for array in operands]
    return pl.pallas_call(
        kernel,
        in_specs=[pl.BlockSpec(memory_space=pltpu.HBM)] * len(loaded)
        + [pl.BlockSpec(memory_space=pltpu.VMEM)] * len(operands),
        out_specs=[pl.BlockSpec(memory_space=pltpu.VMEM)] * len(outs),
        out_shape=[pltpu.VMEM(shape, dtype) for shape, dtype in outs],
        scratch_shapes=[*scratch, pltpu.SemaphoreType.DMA((loads,))],
        compiler_params=pltpu.CompilerParams(vmem_limit_bytes=VMEM_LIMIT),
        cost_estimate=pl.CostEstimate(flops=1, bytes_accessed=1, transcendentals=0),
        name=name,
    )(*arrays)


def turned(values, cosine, sine):
    half = DH // 2
    parts = []
    for start in range(0, values.shape[1], DH):
        low = values[:, start : start + half]
        high = values[:, start + half : start + DH]
        parts.append((low * cosine - high * sine).astype(BF16))
        parts.append((high * cosine + low * sine).astype(BF16))
    return jnp.concatenate(parts, axis=1)


def angles(coarse, fine, first, count):
    at = first // FINE
    far = coarse[:, pl.ds(at, count // FINE), :]
    near = fine[...]
    cos_c, sin_c = far[0][:, None, :], far[1][:, None, :]
    cos_f, sin_f = near[0][None], near[1][None]
    cosine = cos_c * cos_f - sin_c * sin_f
    sine = sin_c * cos_f + cos_c * sin_f
    return cosine.reshape(count, DH // 2), sine.reshape(count, DH // 2)


def decay_sums(log_decay, decay):
    heads, rows = log_decay.shape
    place_s = lax.broadcasted_iota(jnp.int32, (BLOCK, BLOCK), 0)
    place_t = lax.broadcasted_iota(jnp.int32, (BLOCK, BLOCK), 1)
    upper = jnp.where(place_s <= place_t, 1.0, 0.0).astype(BF16)
    value = jnp.concatenate([log_decay[...], jnp.zeros((8 - heads, rows), F32)], axis=0)
    parts = []
    for _ in range(3):
        parts.append(value.astype(BF16))
        value = value - parts[-1].astype(F32)
    stacked = jnp.concatenate([part.astype(F32) for part in parts], axis=0).astype(BF16)
    for start in range(0, rows, BLOCK):
        sums = mm(stacked[:, start : start + BLOCK], upper)
        decay[:, start : start + BLOCK] = sums[:8] + sums[8:16] + sums[16:]


def turn(first, second):
    (cos_a, sin_a), (cos_b, sin_b) = first, second
    return cos_a * cos_b - sin_a * sin_b, sin_a * cos_b + cos_a * sin_b


def joined(first, second):
    return tuple(jnp.concatenate(pair, axis=0) for pair in zip(first, second))


def angle_tables(coarse, fine):
    half, seeds = DH // 2, 8
    index = lax.broadcasted_iota(jnp.int32, (seeds, half), 1).astype(F32)
    frequency = jnp.exp(index * (-math.log(10000.0) / half))
    place = lax.broadcasted_iota(jnp.int32, (seeds, half), 0).astype(F32)
    offset = (lax.axis_index("ctx") * (coarse.shape[1] * FINE)).astype(F32)
    near = jnp.cos(place * frequency), jnp.sin(place * frequency)
    base = jnp.cos(offset * frequency), jnp.sin(offset * frequency)
    step = turn([part[seeds - 1 : seeds] for part in near], [part[1:2] for part in near])
    while near[0].shape[0] < FINE:
        near = joined(near, turn(near, step))
        step = turn(step, step)
    far = tuple(part[:1] for part in base)
    while far[0].shape[0] < coarse.shape[1]:
        far = joined(far, turn(far, step))
        step = turn(step, step)
    for table, parts in ((coarse, far), (fine, near)):
        table[0], table[1] = (part[: table.shape[1]] for part in parts)


class Loads:
    def __init__(self, arrived):
        self.arrived, self.count = arrived, 0

    def start(self, source, target):
        copy = pltpu.make_async_copy(source, target, self.arrived.at[self.count])
        self.count += 1
        copy.start()
        return copy


def half_of(x, rows, half):
    part = x.shape[1] // 2
    return x[rows, pl.ds(pl.multiple_of(half * part, part), part)]


def key_value_own_kernel(
    x_far, wk_far, wv_far, log_decay_far, wo_far, wq_far, wg_far,
    x, acc_k, acc_v, decay, coarse, fine, wo, wq, wg, wk, wv, log_decay, arrived,
):
    core = lax.axis_index("fsdp")
    loads = Loads(arrived)
    starts = range(0, x.shape[0], TILE)
    logs, key = loads.start(log_decay_far, log_decay), loads.start(wk_far, wk)
    tiles = [loads.start(x_far.at[pl.ds(0, TILE)], x.at[pl.ds(0, TILE)])]
    logs.wait()
    tiles += [loads.start(x_far.at[pl.ds(start, TILE)], x.at[pl.ds(start, TILE)]) for start in starts[1:]]
    value = loads.start(wv_far, wv)
    angle_tables(coarse, fine)
    decay_sums(log_decay, decay)
    key.wait()
    tiles[0].wait()
    others = [loads.start(far, near) for far, near in ((wo_far, wo), (wq_far, wq), (wg_far, wg))]
    for number, start in enumerate(starts):
        at = slice(start, start + TILE)
        if number:
            tiles[number].wait()
        acc_k[at, :] = mm(half_of(x, at, core), wk[...])
    value.wait()
    for start in range(0, x.shape[0], BLOCK):
        at = slice(start, start + BLOCK)
        acc_v[at, :] = mm(half_of(x, at, core), wv[...])
    for copy in others:
        copy.wait()


def block_ends(decay, start, stop):
    ends = [decay[:, end - 1 : end] for end in range(start + BLOCK, stop + 1, BLOCK)]
    return functools.reduce(lambda a, b: a + b, ends, jnp.zeros((decay.shape[0], 1), F32))


def pack_message(message, states, logs):
    for head, state in enumerate(states):
        message[head * DH : (head + 1) * DH, :] = state.astype(BF16)
    large = logs.astype(BF16).astype(F32)
    parts = jnp.concatenate([large, logs - large], axis=0)
    message[len(states) * DH :, :] = jnp.broadcast_to(parts, (EXTRA, DH)).astype(BF16)


def message_log(message, heads):
    tail = message[heads * DH :, :].astype(F32)
    return (tail[: EXTRA // 2] + tail[EXTRA // 2 :])[:, :1]


def exchanges(ctx, hop):
    lower = range(ctx - hop)
    if hop == 1:
        return [], list(lower), []
    early = [at for at in lower if at < hop // 2]
    even = [at for at in lower if at >= hop // 2 and at // hop % 2 == 0]
    odd = [at for at in lower if at // hop % 2 == 1]
    return early, even, odd


def is_upper(lowers, hop):
    place = lax.axis_index("ctx")
    found = place < 0
    for lower in lowers:
        found = jnp.logical_or(found, place == lower + hop)
    return found


def arrived_state(arrivals, sets, hop, span):
    parts = [jnp.where(is_upper(lowers, hop), ref[span, :].astype(F32), 0.0) for ref, lowers in zip(arrivals, sets)]
    return functools.reduce(lambda a, b: a + b, parts)


def arrived_log(arrivals, sets, hop, heads):
    parts = [jnp.where(is_upper(lowers, hop), message_log(ref, heads), 0.0) for ref, lowers in zip(arrivals, sets)]
    return functools.reduce(lambda a, b: a + b, parts)


def key_value_kernel(
    heads, x, wk, wv, acc_k, acc_v, decay, coarse, fine, k_out, v_out, before_out, state_out, message
):
    blocks, other = acc_k.shape[0] // BLOCK, 1 - lax.axis_index("fsdp")
    state_out[...] = jnp.zeros_like(state_out)
    for block in range(blocks):
        start = block * BLOCK
        at = slice(start, start + BLOCK)
        columns = decay[:, at].T
        ending = columns[BLOCK - 1 : BLOCK, :]
        faded = jnp.exp(ending - columns)
        rows = half_of(x, at, other)
        cosine, sine = angles(coarse, fine, start, BLOCK)
        keys = turned(acc_k[at, :] + mm(rows, wk[...]), cosine, sine)
        k_out[at, :] = keys
        values = (acc_v[at, :] + mm(rows, wv[...])).astype(BF16)
        v_out[at, :] = values
        for head in range(heads):
            span = slice(head * DH, (head + 1) * DH)
            weighted = (keys[:, span].astype(F32) * faded[:, head : head + 1]).astype(BF16)
            old = state_out[span, :]
            before_out[block, span, :] = old.astype(BF16)
            state_out[span, :] = jnp.exp(ending[:, head : head + 1]) * old + mm_tn(weighted, values[:, span])
    states = [state_out[head * DH : (head + 1) * DH, :] for head in range(heads)]
    pack_message(message, states, block_ends(decay, 0, acc_k.shape[0]))


def combine_kernel(heads, hop, sets, first, last, state, sent, *refs):
    if not first:
        old_entering, refs = refs[0], refs[1:]
    arrivals, entering, message = refs[: len(sets)], refs[len(sets)], refs[len(sets) + 1]
    window_log, log = message_log(sent, heads), arrived_log(arrivals, sets, hop, heads)
    before_log = jnp.zeros_like(log) if first else old_entering[heads * DH :, :1]
    states = []
    for head in range(heads):
        span, row = slice(head * DH, (head + 1) * DH), slice(head, head + 1)
        arrived = arrived_state(arrivals, sets, hop, span)
        if first:
            entering[span, :] = arrived
        else:
            entering[span, :] = old_entering[span, :] + jnp.exp(before_log[row]) * arrived
        states.append(state[span, :] + jnp.exp(window_log[row]) * arrived)
        if last:
            message[span, :] = states[-1].astype(BF16)
        else:
            refs[len(sets) + 2][span, :] = states[-1]
    entering[heads * DH :, :] = jnp.broadcast_to(before_log + log, (8, DH))
    if not last:
        pack_message(message, states, window_log + log)


def query_gate_kernel(
    heads, block, x, wq, wq_far, wg, wg_far, decay, coarse, fine, k, v, q_out, g_out, intra_out
):
    start = block * BLOCK
    lines = decay[:, start : start + BLOCK]
    columns = lines.T

    at = slice(start, start + BLOCK)
    cosine, sine = angles(coarse, fine, start, BLOCK)
    core = lax.axis_index("fsdp")
    own, far = half_of(x, at, core), half_of(x, at, 1 - core)
    queries = mm(own, wq[...]) + mm(far, wq_far[...])
    q_out[...] = turned(queries, cosine, sine)
    gates = mm(own, wg[...]) + mm(far, wg_far[...])
    gates = gates.astype(BF16).astype(F32)
    g_out[...] = gates / (1.0 + jnp.exp(-gates))
    for piece in range(BLOCK // TILE):
        low, last = piece * TILE, (piece + 1) * TILE
        place_t = lax.broadcasted_iota(jnp.int32, (TILE, last), 0) + low
        place_s = lax.broadcasted_iota(jnp.int32, (TILE, last), 1)
        causal = place_t >= place_s
        for head in range(heads):
            span = slice(head * DH, (head + 1) * DH)
            scores = mm_nt(q_out[low:last, span], k[start : start + last, span])
            differ = columns[low:last, head : head + 1] - lines[head : head + 1, :last]
            weights = jnp.where(causal, jnp.exp(jnp.where(causal, differ, 0.0)), 0.0)
            intra_out[low:last, span] = mm((scores * weights).astype(BF16), v[start : start + last, span])


def hidden_kernel(heads, hop, sets, starts, decay, before, entering, *refs):
    arrivals, refs, token = refs[: len(sets)], refs[len(sets) : -1], refs[-1]
    projected, outs = refs[: -len(starts)], refs[-len(starts) :]
    token[...] = jnp.zeros_like(token)
    for head in range(heads):
        span = slice(head * DH, (head + 1) * DH)
        entering_log = entering[heads * DH + head : heads * DH + head + 1, :1]
        state = entering[span, :] + jnp.exp(entering_log) * arrived_state(arrivals, sets, hop, span)
        for start, out in zip(starts, outs):
            block = start // BLOCK
            q, gate, intra = projected[3 * block : 3 * block + 3]
            at = slice(start % BLOCK, start % BLOCK + TILE)
            column = jnp.exp(decay[:, start : start + TILE].T[:, head : head + 1])
            scale_log = jnp.zeros((1, 1), F32)
            for earlier in range(block):
                end = (earlier + 1) * BLOCK
                scale_log = scale_log + decay[head : head + 1, end - 1 : end]
            prior = (jnp.exp(scale_log) * state + before[block, span, :].astype(F32)).astype(BF16)
            retained = intra[at, span] + column * mm(q[at, span], prior)
            center = retained - jnp.mean(retained, axis=1, keepdims=True)
            spread = jnp.mean(center * center, axis=1, keepdims=True)
            out[:, span] = (gate[at, span] * center * lax.rsqrt(spread + 1e-5)).astype(BF16)


def columns_kernel(first, second, out):
    cols = out.shape[1] // 2
    place, core = lax.axis_index("tp"), lax.axis_index("fsdp")
    high, low = place // 2, place % 2

    @pl.when(core == 0)
    def _():
        at = pl.ds(pl.multiple_of((1 - low) * cols, cols), cols)
        out[:, :cols] = first[:, at]
        out[:, cols:] = second[:, at]

    @pl.when(core == 1)
    def _():
        out[...] = jnp.where(high == 0, first[...], second[...])


def arrange_kernel(mine, other, low_out, high_out):
    cols = mine.shape[1] // 2
    place, core = lax.axis_index("tp"), lax.axis_index("fsdp")
    for gathered, bit, out in ((core == 0, place // 2, low_out), (core == 1, place % 2, high_out)):
        give = pl.ds(pl.multiple_of((1 - bit) * cols, cols), cols)
        keep = pl.ds(pl.multiple_of(bit * cols, cols), cols)
        out[:, :cols] = jnp.where(gathered, mine[:, give], other[:, give])
        out[:, cols:] = jnp.where(gathered, mine[:, keep], other[:, keep])


def own_kernel(order, own_first, own_second, *refs):
    pieces, outs = refs[: len(order)], refs[len(order) :]
    cols = pieces[0].shape[1]
    place, core = lax.axis_index("tp"), lax.axis_index("fsdp")
    high, low = place // 2, place % 2
    here = core == high
    mine = pl.ds(pl.multiple_of(low * cols, cols), cols)
    flipped = pl.ds(pl.multiple_of((1 - low) * cols, cols), cols)
    keep = jnp.where(here, own_first[:, mine], own_second[:, mine])
    gives = [
        jnp.where(here, own_second[:, mine], own_first[:, mine]),
        jnp.where(here, own_first[:, flipped], own_second[:, flipped]),
    ]
    for (half, number), piece in zip(order, pieces):
        at = slice(number * TILE, (number + 1) * TILE)
        outs[half][at, :cols] = mm(piece[...], gives[half])
        outs[half][at, cols:] = mm(piece[...], keep)


def give_kernel(number, own, far, weight, out):
    cols = out.shape[1]
    at = slice(number * TILE, (number + 1) * TILE)
    out[...] = (own[at, :cols] + mm(far[...], weight[:, :cols])).astype(BF16)


def keep_kernel(order, *refs):
    count = len(order)
    fars, owns, weights, outs = refs[:count], refs[count : count + 2], refs[count + 2 : count + 4], refs[count + 4 :]
    for (half, number), far in zip(order, fars):
        cols = far.shape[1]
        at = slice(number * TILE, (number + 1) * TILE)
        outs[half][at, :] = owns[half][at, cols:] + mm(far[...], weights[half][:, cols:])


def finish_kernel(order, *refs):
    count = len(order)
    gots, keeps, out, ready, written = refs[:count], refs[count : count + 2], refs[-3], refs[-2], refs[-1]
    copies = []
    for slot, ((half, number), got) in enumerate(zip(order, gots)):
        keep = keeps[half]
        at = slice(number * TILE, (number + 1) * TILE)
        ready[slot] = (keep[at, :] + got[...].astype(F32)).astype(BF16)
        start = half * keep.shape[0] + number * TILE
        copies.append(pltpu.make_async_copy(ready.at[slot], out.at[0, pl.ds(start, TILE)], written.at[slot]))
        copies[-1].start()
    for copy in copies:
        copy.wait()


def after(value, *others):
    return lax.optimization_barrier((value, *others))[0]


def on_device(tokens, query_weight, key_weight, value_weight, gate_weight, out_weight, log_decay):
    x = tokens[0]
    rows, width = x.shape
    part, cols = query_weight.shape
    heads = cols // DH
    blocks = rows // BLOCK
    ctx, tp, cores = lax.axis_size("ctx"), lax.axis_size("tp"), lax.axis_size("fsdp")
    assert tp == 4 and cores == 2 and ctx >= 4 and ctx & (ctx - 1) == 0
    near_mask, far_mask = 1, 2
    tables = [((2, rows // FINE, DH // 2), F32), ((2, FINE, DH // 2), F32)]

    key_far = swap(key_weight, "fsdp", 1)
    value_far = swap(value_weight, "fsdp", 1)

    x, acc_k, acc_v, decay, coarse, fine, out_first, own_q, own_g = loading_call(
        key_value_own_kernel,
        [((rows, width), BF16), ((rows, cols), F32), ((rows, cols), F32), ((8, rows), F32)]
        + tables
        + [(out_weight.shape, BF16), ((part, cols), BF16), ((part, cols), BF16)],
        [x, key_weight, value_weight, log_decay[0].T, out_weight, query_weight, gate_weight],
        [],
        [pltpu.VMEM((part, cols), BF16)] * 2 + [pltpu.VMEM((heads, rows), F32)],
        rows // TILE + 6,
        "key_value_own",
    )
    state_shape, message_shape = (heads * DH, DH), (heads * DH + EXTRA, DH)
    keys, values, before, window, message = kernel_call(
        functools.partial(key_value_kernel, heads),
        [((rows, cols), BF16)] * 2
        + [((blocks, heads * DH, DH), BF16), (state_shape, F32), (message_shape, BF16)],
        [x, key_far, value_far, acc_k, acc_v, decay, coarse, fine],
        "key_value",
    )
    far_q, far_g = swap(own_q, "fsdp", 1), swap(own_g, "fsdp", 1)

    def query_gate(block, decay):
        return kernel_call(
            functools.partial(query_gate_kernel, heads, block),
            [((BLOCK, cols), BF16), ((BLOCK, cols), F32), ((BLOCK, cols), F32)],
            [x, own_q, far_q, own_g, far_g, decay, coarse, fine, keys, values],
            "query_gate",
        )

    def exchange(message, lowers, hop):
        pairs = [(at, at + hop) for at in lowers]
        if hop > 1:
            pairs += [(upper, at) for at, upper in pairs]
        return lax.ppermute(message, "ctx", pairs)

    projected = list(query_gate(0, decay))
    window = after(window, projected[0])
    entering, hop, early, first_message = None, 1, [], message
    while True:
        first_set, *later_sets = exchanges(ctx, hop)
        later_sets = [lowers for lowers in later_sets if lowers]
        sets = later_sets + ([first_set] if first_set else [])
        arrivals = [exchange(message, lowers, hop) for lowers in later_sets] + early
        if 2 * hop >= ctx:
            break
        unchanged = exchanges(ctx, 2 * hop)[0]
        early = [exchange(message, unchanged, 2 * hop)]
        old = [] if entering is None else [entering]
        last = 4 * hop >= ctx
        entering, message, *windows = kernel_call(
            functools.partial(combine_kernel, heads, hop, sets, entering is None, last),
            [((heads * DH + 8, DH), F32)]
            + ([(state_shape, BF16)] if last else [(message_shape, BF16), (state_shape, F32)]),
            [window, message, *old, *arrivals],
            "combine",
        )
        window = windows[0] if windows else None
        hop *= 2

    own_second = swap(out_first, "fsdp", 1)
    [for_partner] = kernel_call(
        columns_kernel,
        [(out_weight.shape, BF16)],
        [after(out_first, first_message), own_second],
        "columns",
    )
    pairs = [(at * cores + at_core, (at ^ mask) * cores + at_core) for at in range(tp) for at_core, mask in enumerate((near_mask, far_mask))]
    out_mine = lax.ppermute(for_partner, ("tp", "fsdp"), pairs)

    held = after(decay, message, *early)
    for block in range(1, blocks):
        projected += query_gate(block, held)

    count = rows // 2 // TILE
    masks = (near_mask, far_mask)
    hidden, far = [[], []], [[], []]
    for number in range(count):
        held = after(decay, swap(pair[2], "fsdp", 1)) if number else decay
        pair = kernel_call(
            functools.partial(hidden_kernel, heads, hop, sets, [(half * count + number) * TILE for half in range(2)]),
            [((TILE, cols), BF16)] * 2 + [((16, 128), BF16)],
            [held, before, entering, *arrivals, *projected],
            "hidden",
        )
        if number == 0:
            out_other = swap(after(out_mine, pair[0]), "fsdp", 1)
        for half in range(2):
            hidden[half].append(pair[half])
            far[half].append(swap(pair[half], "tp", masks[half]))
    weights = kernel_call(
        arrange_kernel,
        [((cols, 2 * cols), BF16)] * 2,
        [out_mine, out_other],
        "arrange",
    )
    order = [(half, number) for number in reversed(range(count)) for half in (1, 0)]
    owns = kernel_call(
        functools.partial(own_kernel, order),
        [((count * TILE, 2 * cols), F32)] * 2,
        [out_first, own_second, *(hidden[half][number] for half, number in order)],
        "own_products",
    )
    gots = []
    for half, number in order:
        [give] = kernel_call(
            functools.partial(give_kernel, number),
            [((TILE, cols), BF16)],
            [owns[half], far[half][number], weights[half]],
            "give",
        )
        gots.append(swap(give, "tp", masks[1 - half]))
    keeps = kernel_call(
        functools.partial(keep_kernel, order),
        [((count * TILE, cols), F32)] * 2,
        [*(far[half][number] for half, number in order), *owns, *weights],
        "keep",
    )
    result = None
    for part_order, part_gots in ((order[2:], gots[2:]), (order[:2], gots[:2])):
        arrays = [pltpu.with_memory_space_constraint(array, pltpu.VMEM) for array in (*part_gots, *keeps)]
        held = [] if result is None else [result]
        result = pl.pallas_call(
            functools.partial(finish_kernel, part_order),
            in_specs=[pl.BlockSpec(memory_space=pltpu.VMEM)] * len(arrays)
            + [pl.BlockSpec(memory_space=pltpu.HBM)] * len(held),
            out_specs=pl.BlockSpec(memory_space=pltpu.HBM),
            out_shape=jax.ShapeDtypeStruct((1, rows, cols), BF16),
            input_output_aliases={len(arrays): 0} if held else {},
            scratch_shapes=[
                pltpu.VMEM((len(part_order), TILE, cols), BF16),
                pltpu.SemaphoreType.DMA((len(part_order),)),
            ],
            compiler_params=pltpu.CompilerParams(vmem_limit_bytes=VMEM_LIMIT),
            name="finish",
        )(*arrays, *held)
    return result


def solution(mesh):
    in_specs = (
        P("fsdp", "ctx", None),
        P("fsdp", "tp"),
        P("fsdp", "tp"),
        P("fsdp", "tp"),
        P("fsdp", "tp"),
        P("tp", "fsdp"),
        P("fsdp", "ctx", "tp"),
    )
    out_specs = P("fsdp", "ctx", "tp")
    return jax.shard_map(
        on_device, mesh=mesh, in_specs=in_specs, out_specs=out_specs, check_vma=False
    )
```

```python
import functools
import math

import jax
import jax.numpy as jnp
from jax import lax
from jax.experimental import pallas as pl
from jax.experimental.pallas import tpu as pltpu
from jax.sharding import PartitionSpec as P

DH = 256
BLOCK = 512
TILE = 256
FINE = 32
EXTRA = 16
VMEM_LIMIT = 14 * 1024 * 1024
F32 = jnp.float32
BF16 = jnp.bfloat16


def mm(left, right):
    return jnp.dot(left, right, preferred_element_type=F32)


def mm_nt(left, right):
    return lax.dot_general(left, right, (((1,), (1,)), ((), ())), preferred_element_type=F32)


def mm_tn(left, right):
    return lax.dot_general(left, right, (((0,), (0,)), ((), ())), preferred_element_type=F32)


def swap(value, axis, mask):
    size = lax.axis_size(axis)
    return lax.ppermute(value, axis, [(place, place ^ mask) for place in range(size)])


def kernel_call(kernel, outs, operands, name):
    arrays = [pltpu.with_memory_space_constraint(array, pltpu.VMEM) for array in operands]
    return pl.pallas_call(
        kernel,
        in_specs=[pl.BlockSpec(memory_space=pltpu.VMEM)] * len(operands),
        out_specs=[pl.BlockSpec(memory_space=pltpu.VMEM)] * len(outs),
        out_shape=[pltpu.VMEM(shape, dtype) for shape, dtype in outs],
        compiler_params=pltpu.CompilerParams(vmem_limit_bytes=VMEM_LIMIT),
        cost_estimate=pl.CostEstimate(
            flops=1, bytes_accessed=1, transcendentals=0
        ),
        name=name,
    )(*arrays)


def loading_call(kernel, outs, loaded, operands, scratch, loads, name):
    arrays = [pltpu.with_memory_space_constraint(array, pltpu.HBM) for array in loaded]
    arrays += [pltpu.with_memory_space_constraint(array, pltpu.VMEM) for array in operands]
    return pl.pallas_call(
        kernel,
        in_specs=[pl.BlockSpec(memory_space=pltpu.HBM)] * len(loaded)
        + [pl.BlockSpec(memory_space=pltpu.VMEM)] * len(operands),
        out_specs=[pl.BlockSpec(memory_space=pltpu.VMEM)] * len(outs),
        out_shape=[pltpu.VMEM(shape, dtype) for shape, dtype in outs],
        scratch_shapes=[*scratch, pltpu.SemaphoreType.DMA((loads,))],
        compiler_params=pltpu.CompilerParams(vmem_limit_bytes=VMEM_LIMIT),
        cost_estimate=pl.CostEstimate(flops=1, bytes_accessed=1, transcendentals=0),
        name=name,
    )(*arrays)


def turned(values, cosine, sine):
    half = DH // 2
    parts = []
    for start in range(0, values.shape[1], DH):
        low = values[:, start : start + half]
        high = values[:, start + half : start + DH]
        parts.append((low * cosine - high * sine).astype(BF16))
        parts.append((high * cosine + low * sine).astype(BF16))
    return jnp.concatenate(parts, axis=1)


def angles(coarse, fine, first, count):
    at = first // FINE
    far = coarse[:, pl.ds(at, count // FINE), :]
    near = fine[...]
    cos_c, sin_c = far[0][:, None, :], far[1][:, None, :]
    cos_f, sin_f = near[0][None], near[1][None]
    cosine = cos_c * cos_f - sin_c * sin_f
    sine = sin_c * cos_f + cos_c * sin_f
    return cosine.reshape(count, DH // 2), sine.reshape(count, DH // 2)


def decay_sums(log_decay, decay):
    heads, rows = log_decay.shape
    place_s = lax.broadcasted_iota(jnp.int32, (BLOCK, BLOCK), 0)
    place_t = lax.broadcasted_iota(jnp.int32, (BLOCK, BLOCK), 1)
    upper = jnp.where(place_s <= place_t, 1.0, 0.0).astype(BF16)
    value = jnp.concatenate([log_decay[...], jnp.zeros((8 - heads, rows), F32)], axis=0)
    parts = []
    for _ in range(3):
        parts.append(value.astype(BF16))
        value = value - parts[-1].astype(F32)
    stacked = jnp.concatenate([part.astype(F32) for part in parts], axis=0).astype(BF16)
    for start in range(0, rows, BLOCK):
        sums = mm(stacked[:, start : start + BLOCK], upper)
        decay[:, start : start + BLOCK] = sums[:8] + sums[8:16] + sums[16:]


def turn(first, second):
    (cos_a, sin_a), (cos_b, sin_b) = first, second
    return cos_a * cos_b - sin_a * sin_b, sin_a * cos_b + cos_a * sin_b


def joined(first, second):
    return tuple(jnp.concatenate(pair, axis=0) for pair in zip(first, second))


def angle_tables(coarse, fine):
    half, seeds = DH // 2, 8
    index = lax.broadcasted_iota(jnp.int32, (seeds, half), 1).astype(F32)
    frequency = jnp.exp(index * (-math.log(10000.0) / half))
    place = lax.broadcasted_iota(jnp.int32, (seeds, half), 0).astype(F32)
    offset = (lax.axis_index("ctx") * (coarse.shape[1] * FINE)).astype(F32)
    near = jnp.cos(place * frequency), jnp.sin(place * frequency)
    base = jnp.cos(offset * frequency), jnp.sin(offset * frequency)
    step = turn([part[seeds - 1 : seeds] for part in near], [part[1:2] for part in near])
    while near[0].shape[0] < FINE:
        near = joined(near, turn(near, step))
        step = turn(step, step)
    far = tuple(part[:1] for part in base)
    while far[0].shape[0] < coarse.shape[1]:
        far = joined(far, turn(far, step))
        step = turn(step, step)
    for table, parts in ((coarse, far), (fine, near)):
        table[0], table[1] = (part[: table.shape[1]] for part in parts)


class Loads:
    def __init__(self, arrived):
        self.arrived, self.count = arrived, 0

    def start(self, source, target):
        copy = pltpu.make_async_copy(source, target, self.arrived.at[self.count])
        self.count += 1
        copy.start()
        return copy


def half_of(x, rows, half):
    part = x.shape[1] // 2
    return x[rows, pl.ds(pl.multiple_of(half * part, part), part)]


def key_value_own_kernel(
    x_far, wk_far, wv_far, log_decay_far, wo_far, wq_far, wg_far,
    x, acc_k, acc_v, decay, coarse, fine, wo, wq, wg, wk, wv, log_decay, arrived,
):
    core = lax.axis_index("fsdp")
    loads = Loads(arrived)
    starts = range(0, x.shape[0], TILE)
    logs, key = loads.start(log_decay_far, log_decay), loads.start(wk_far, wk)
    tiles = [loads.start(x_far.at[pl.ds(0, TILE)], x.at[pl.ds(0, TILE)])]
    angle_tables(coarse, fine)
    logs.wait()
    tiles += [loads.start(x_far.at[pl.ds(start, TILE)], x.at[pl.ds(start, TILE)]) for start in starts[1:]]
    value = loads.start(wv_far, wv)
    key.wait()
    tiles[0].wait()
    others = [loads.start(far, near) for far, near in ((wo_far, wo), (wq_far, wq), (wg_far, wg))]
    for number, start in enumerate(starts):
        at = slice(start, start + TILE)
        if number:
            tiles[number].wait()
        acc_k[at, :] = mm(half_of(x, at, core), wk[...])
    value.wait()
    for start in range(0, x.shape[0], BLOCK):
        at = slice(start, start + BLOCK)
        acc_v[at, :] = mm(half_of(x, at, core), wv[...])
    decay_sums(log_decay, decay)
    for copy in others:
        copy.wait()


def block_ends(decay, start, stop):
    ends = [decay[:, end - 1 : end] for end in range(start + BLOCK, stop + 1, BLOCK)]
    return functools.reduce(lambda a, b: a + b, ends, jnp.zeros((decay.shape[0], 1), F32))


def pack_message(message, states, logs):
    for head, state in enumerate(states):
        message[head * DH : (head + 1) * DH, :] = state.astype(BF16)
    large = logs.astype(BF16).astype(F32)
    parts = jnp.concatenate([large, logs - large], axis=0)
    message[len(states) * DH :, :] = jnp.broadcast_to(parts, (EXTRA, DH)).astype(BF16)


def message_log(message, heads):
    tail = message[heads * DH :, :].astype(F32)
    return (tail[: EXTRA // 2] + tail[EXTRA // 2 :])[:, :1]


def exchanges(ctx, hop):
    lower = range(ctx - hop)
    if hop == 1:
        return [], list(lower), []
    early = [at for at in lower if at < hop // 2]
    even = [at for at in lower if at >= hop // 2 and at // hop % 2 == 0]
    odd = [at for at in lower if at // hop % 2 == 1]
    return early, even, odd


def is_upper(lowers, hop):
    place = lax.axis_index("ctx")
    found = place < 0
    for lower in lowers:
        found = jnp.logical_or(found, place == lower + hop)
    return found


def arrived_state(arrivals, sets, hop, span):
    parts = [jnp.where(is_upper(lowers, hop), ref[span, :].astype(F32), 0.0) for ref, lowers in zip(arrivals, sets)]
    return functools.reduce(lambda a, b: a + b, parts)


def arrived_log(arrivals, sets, hop, heads):
    parts = [jnp.where(is_upper(lowers, hop), message_log(ref, heads), 0.0) for ref, lowers in zip(arrivals, sets)]
    return functools.reduce(lambda a, b: a + b, parts)


def key_value_kernel(
    heads, x, wk, wv, acc_k, acc_v, decay, coarse, fine, k_out, v_out, before_out, state_out, message
):
    blocks, other = acc_k.shape[0] // BLOCK, 1 - lax.axis_index("fsdp")
    state_out[...] = jnp.zeros_like(state_out)
    for block in range(blocks):
        start = block * BLOCK
        at = slice(start, start + BLOCK)
        columns = decay[:, at].T
        ending = columns[BLOCK - 1 : BLOCK, :]
        faded = jnp.exp(ending - columns)
        rows = half_of(x, at, other)
        cosine, sine = angles(coarse, fine, start, BLOCK)
        keys = turned(acc_k[at, :] + mm(rows, wk[...]), cosine, sine)
        k_out[at, :] = keys
        values = (acc_v[at, :] + mm(rows, wv[...])).astype(BF16)
        v_out[at, :] = values
        for head in range(heads):
            span = slice(head * DH, (head + 1) * DH)
            weighted = (keys[:, span].astype(F32) * faded[:, head : head + 1]).astype(BF16)
            old = state_out[span, :]
            before_out[block, span, :] = old.astype(BF16)
            state_out[span, :] = jnp.exp(ending[:, head : head + 1]) * old + mm_tn(weighted, values[:, span])
    states = [state_out[head * DH : (head + 1) * DH, :] for head in range(heads)]
    pack_message(message, states, block_ends(decay, 0, acc_k.shape[0]))


def combine_kernel(heads, hop, sets, first, last, state, sent, *refs):
    if not first:
        old_entering, refs = refs[0], refs[1:]
    arrivals, entering, message = refs[: len(sets)], refs[len(sets)], refs[len(sets) + 1]
    window_log, log = message_log(sent, heads), arrived_log(arrivals, sets, hop, heads)
    before_log = jnp.zeros_like(log) if first else old_entering[heads * DH :, :1]
    states = []
    for head in range(heads):
        span, row = slice(head * DH, (head + 1) * DH), slice(head, head + 1)
        arrived = arrived_state(arrivals, sets, hop, span)
        if first:
            entering[span, :] = arrived
        else:
            entering[span, :] = old_entering[span, :] + jnp.exp(before_log[row]) * arrived
        states.append(state[span, :] + jnp.exp(window_log[row]) * arrived)
        if last:
            message[span, :] = states[-1].astype(BF16)
        else:
            refs[len(sets) + 2][span, :] = states[-1]
    entering[heads * DH :, :] = jnp.broadcast_to(before_log + log, (8, DH))
    if not last:
        pack_message(message, states, window_log + log)


def query_gate_kernel(
    heads, block, x, wq, wq_far, wg, wg_far, decay, coarse, fine, k, v, q_out, g_out, intra_out
):
    start = block * BLOCK
    lines = decay[:, start : start + BLOCK]
    columns = lines.T

    at = slice(start, start + BLOCK)
    cosine, sine = angles(coarse, fine, start, BLOCK)
    core = lax.axis_index("fsdp")
    own, far = half_of(x, at, core), half_of(x, at, 1 - core)
    queries = mm(own, wq[...]) + mm(far, wq_far[...])
    q_out[...] = turned(queries, cosine, sine)
    gates = mm(own, wg[...]) + mm(far, wg_far[...])
    gates = gates.astype(BF16).astype(F32)
    g_out[...] = gates / (1.0 + jnp.exp(-gates))
    for piece in range(BLOCK // TILE):
        low, last = piece * TILE, (piece + 1) * TILE
        place_t = lax.broadcasted_iota(jnp.int32, (TILE, last), 0) + low
        place_s = lax.broadcasted_iota(jnp.int32, (TILE, last), 1)
        causal = place_t >= place_s
        for head in range(heads):
            span = slice(head * DH, (head + 1) * DH)
            scores = mm_nt(q_out[low:last, span], k[start : start + last, span])
            differ = columns[low:last, head : head + 1] - lines[head : head + 1, :last]
            weights = jnp.where(causal, jnp.exp(jnp.where(causal, differ, 0.0)), 0.0)
            intra_out[low:last, span] = mm((scores * weights).astype(BF16), v[start : start + last, span])


def hidden_kernel(heads, hop, sets, starts, decay, before, entering, *refs):
    arrivals, refs, token = refs[: len(sets)], refs[len(sets) : -1], refs[-1]
    projected, outs = refs[: -len(starts)], refs[-len(starts) :]
    token[...] = jnp.zeros_like(token)
    for head in range(heads):
        span = slice(head * DH, (head + 1) * DH)
        entering_log = entering[heads * DH + head : heads * DH + head + 1, :1]
        state = entering[span, :] + jnp.exp(entering_log) * arrived_state(arrivals, sets, hop, span)
        for start, out in zip(starts, outs):
            block = start // BLOCK
            q, gate, intra = projected[3 * block : 3 * block + 3]
            at = slice(start % BLOCK, start % BLOCK + TILE)
            column = jnp.exp(decay[:, start : start + TILE].T[:, head : head + 1])
            scale_log = jnp.zeros((1, 1), F32)
            for earlier in range(block):
                end = (earlier + 1) * BLOCK
                scale_log = scale_log + decay[head : head + 1, end - 1 : end]
            prior = (jnp.exp(scale_log) * state + before[block, span, :].astype(F32)).astype(BF16)
            retained = intra[at, span] + column * mm(q[at, span], prior)
            center = retained - jnp.mean(retained, axis=1, keepdims=True)
            spread = jnp.mean(center * center, axis=1, keepdims=True)
            out[:, span] = (gate[at, span] * center * lax.rsqrt(spread + 1e-5)).astype(BF16)


def columns_kernel(first, second, *outs):
    cols = outs[0].shape[1]
    place, core = lax.axis_index("tp"), lax.axis_index("fsdp")
    high, low = place // 2, place % 2

    @pl.when(core == 0)
    def _():
        at = pl.ds(pl.multiple_of((1 - low) * cols, cols), cols)
        outs[0][...] = first[:, at]
        outs[1][...] = second[:, at]

    @pl.when(core == 1)
    def _():
        for number, out in enumerate(outs):
            at = slice(number * cols, (number + 1) * cols)
            out[...] = jnp.where(high == 0, first[:, at], second[:, at])


def arrange_kernel(mine_0, mine_1, other_0, other_1, low_out, high_out):
    cols = mine_0.shape[1]
    place, core = lax.axis_index("tp"), lax.axis_index("fsdp")
    for gathered, bit, out in ((core == 0, place // 2, low_out), (core == 1, place % 2, high_out)):
        blocks = [jnp.where(gathered, mine[...], other[...]) for mine, other in ((mine_0, other_0), (mine_1, other_1))]
        out[:, :cols] = jnp.where(bit == 0, blocks[1], blocks[0])
        out[:, cols:] = jnp.where(bit == 0, blocks[0], blocks[1])


def own_kernel(order, own_first, own_second, *refs):
    pieces, outs = refs[: len(order)], refs[len(order) :]
    cols = pieces[0].shape[1]
    place, core = lax.axis_index("tp"), lax.axis_index("fsdp")
    high, low = place // 2, place % 2
    here = core == high
    mine = pl.ds(pl.multiple_of(low * cols, cols), cols)
    flipped = pl.ds(pl.multiple_of((1 - low) * cols, cols), cols)
    keep = jnp.where(here, own_first[:, mine], own_second[:, mine])
    gives = [
        jnp.where(here, own_second[:, mine], own_first[:, mine]),
        jnp.where(here, own_first[:, flipped], own_second[:, flipped]),
    ]
    for (half, number), piece in zip(order, pieces):
        at = slice(number * TILE, (number + 1) * TILE)
        outs[half][at, :cols] = mm(piece[...], gives[half])
        outs[half][at, cols:] = mm(piece[...], keep)


def give_kernel(number, own, far, weight, out):
    cols = out.shape[1]
    at = slice(number * TILE, (number + 1) * TILE)
    out[...] = (own[at, :cols] + mm(far[...], weight[:, :cols])).astype(BF16)


def keep_kernel(order, *refs):
    count = len(order)
    fars, owns, weights, outs = refs[:count], refs[count : count + 2], refs[count + 2 : count + 4], refs[count + 4 :]
    for (half, number), far in zip(order, fars):
        cols = far.shape[1]
        at = slice(number * TILE, (number + 1) * TILE)
        outs[half][at, :] = owns[half][at, cols:] + mm(far[...], weights[half][:, cols:])


def finish_kernel(order, *refs):
    count = len(order)
    gots, keeps, out, ready, written = refs[:count], refs[count : count + 2], refs[-3], refs[-2], refs[-1]
    copies = []
    for slot, ((half, number), got) in enumerate(zip(order, gots)):
        keep = keeps[half]
        at = slice(number * TILE, (number + 1) * TILE)
        ready[slot] = (keep[at, :] + got[...].astype(F32)).astype(BF16)
        start = half * keep.shape[0] + number * TILE
        copies.append(pltpu.make_async_copy(ready.at[slot], out.at[0, pl.ds(start, TILE)], written.at[slot]))
        copies[-1].start()
    for copy in copies:
        copy.wait()


def after(value, *others):
    return lax.optimization_barrier((value, *others))[0]


def on_device(tokens, query_weight, key_weight, value_weight, gate_weight, out_weight, log_decay):
    x = tokens[0]
    rows, width = x.shape
    part, cols = query_weight.shape
    heads = cols // DH
    blocks = rows // BLOCK
    ctx, tp, cores = lax.axis_size("ctx"), lax.axis_size("tp"), lax.axis_size("fsdp")
    assert tp == 4 and cores == 2 and ctx >= 4 and ctx & (ctx - 1) == 0
    near_mask, far_mask = 1, 2
    tables = [((2, rows // FINE, DH // 2), F32), ((2, FINE, DH // 2), F32)]

    key_far = swap(key_weight, "fsdp", 1)
    value_far = swap(value_weight, "fsdp", 1)

    x, acc_k, acc_v, decay, coarse, fine, out_first, own_q, own_g = loading_call(
        key_value_own_kernel,
        [((rows, width), BF16), ((rows, cols), F32), ((rows, cols), F32), ((8, rows), F32)]
        + tables
        + [(out_weight.shape, BF16), ((part, cols), BF16), ((part, cols), BF16)],
        [x, key_weight, value_weight, log_decay[0].T, out_weight, query_weight, gate_weight],
        [],
        [pltpu.VMEM((part, cols), BF16)] * 2 + [pltpu.VMEM((heads, rows), F32)],
        rows // TILE + 6,
        "key_value_own",
    )
    state_shape, message_shape = (heads * DH, DH), (heads * DH + EXTRA, DH)
    keys, values, before, window, message = kernel_call(
        functools.partial(key_value_kernel, heads),
        [((rows, cols), BF16)] * 2
        + [((blocks, heads * DH, DH), BF16), (state_shape, F32), (message_shape, BF16)],
        [x, key_far, value_far, acc_k, acc_v, decay, coarse, fine],
        "key_value",
    )
    far_q, far_g = swap(own_q, "fsdp", 1), swap(own_g, "fsdp", 1)

    def query_gate(block, decay):
        return kernel_call(
            functools.partial(query_gate_kernel, heads, block),
            [((BLOCK, cols), BF16), ((BLOCK, cols), F32), ((BLOCK, cols), F32)],
            [x, own_q, far_q, own_g, far_g, decay, coarse, fine, keys, values],
            "query_gate",
        )

    def exchange(message, lowers, hop):
        pairs = [(at, at + hop) for at in lowers]
        if hop > 1:
            pairs += [(upper, at) for at, upper in pairs]
        return lax.ppermute(message, "ctx", pairs)

    projected = list(query_gate(0, decay))
    window = after(window, projected[0])
    entering, hop, early, first_message = None, 1, [], message
    while True:
        first_set, *later_sets = exchanges(ctx, hop)
        later_sets = [lowers for lowers in later_sets if lowers]
        sets = later_sets + ([first_set] if first_set else [])
        arrivals = [exchange(message, lowers, hop) for lowers in later_sets] + early
        if 2 * hop >= ctx:
            break
        unchanged = exchanges(ctx, 2 * hop)[0]
        early = [exchange(message, unchanged, 2 * hop)]
        old = [] if entering is None else [entering]
        last = 4 * hop >= ctx
        entering, message, *windows = kernel_call(
            functools.partial(combine_kernel, heads, hop, sets, entering is None, last),
            [((heads * DH + 8, DH), F32)]
            + ([(state_shape, BF16)] if last else [(message_shape, BF16), (state_shape, F32)]),
            [window, message, *old, *arrivals],
            "combine",
        )
        window = windows[0] if windows else None
        hop *= 2

    own_second = swap(out_first, "fsdp", 1)
    for_partner = kernel_call(
        columns_kernel,
        [((cols, cols), BF16)] * 2,
        [after(out_first, first_message), own_second],
        "columns",
    )
    pairs = [(at * cores + at_core, (at ^ mask) * cores + at_core) for at in range(tp) for at_core, mask in enumerate((near_mask, far_mask))]
    out_mine = [lax.ppermute(block, ("tp", "fsdp"), pairs) for block in for_partner]

    held = after(decay, message, *early, out_mine[0])
    for block in range(1, blocks):
        projected += query_gate(block, held)

    count = rows // 2 // TILE
    masks = (near_mask, far_mask)
    hidden, far = [[], []], [[], []]
    for number in range(count):
        held = after(decay, swap(pair[2], "fsdp", 1)) if number else decay
        pair = kernel_call(
            functools.partial(hidden_kernel, heads, hop, sets, [(half * count + number) * TILE for half in range(2)]),
            [((TILE, cols), BF16)] * 2 + [((16, 128), BF16)],
            [held, before, entering, *arrivals, *projected],
            "hidden",
        )
        if number == 0:
            out_other = [swap(after(block, pair[0]), "fsdp", 1) for block in out_mine]
        for half in range(2):
            hidden[half].append(pair[half])
            far[half].append(swap(pair[half], "tp", masks[half]))
    weights = kernel_call(
        arrange_kernel,
        [((cols, 2 * cols), BF16)] * 2,
        [*out_mine, *out_other],
        "arrange",
    )
    order = [(half, number) for number in reversed(range(count)) for half in (1, 0)]
    owns = kernel_call(
        functools.partial(own_kernel, order),
        [((count * TILE, 2 * cols), F32)] * 2,
        [out_first, own_second, *(hidden[half][number] for half, number in order)],
        "own_products",
    )
    gots = []
    for half, number in order:
        [give] = kernel_call(
            functools.partial(give_kernel, number),
            [((TILE, cols), BF16)],
            [owns[half], far[half][number], weights[half]],
            "give",
        )
        gots.append(swap(give, "tp", masks[1 - half]))
    keeps = kernel_call(
        functools.partial(keep_kernel, order),
        [((count * TILE, cols), F32)] * 2,
        [*(far[half][number] for half, number in order), *owns, *weights],
        "keep",
    )
    result = None
    for part_order, part_gots in ((order[2:], gots[2:]), (order[:2], gots[:2])):
        arrays = [pltpu.with_memory_space_constraint(array, pltpu.VMEM) for array in (*part_gots, *keeps)]
        held = [] if result is None else [result]
        result = pl.pallas_call(
            functools.partial(finish_kernel, part_order),
            in_specs=[pl.BlockSpec(memory_space=pltpu.VMEM)] * len(arrays)
            + [pl.BlockSpec(memory_space=pltpu.HBM)] * len(held),
            out_specs=pl.BlockSpec(memory_space=pltpu.HBM),
            out_shape=jax.ShapeDtypeStruct((1, rows, cols), BF16),
            input_output_aliases={len(arrays): 0} if held else {},
            scratch_shapes=[
                pltpu.VMEM((len(part_order), TILE, cols), BF16),
                pltpu.SemaphoreType.DMA((len(part_order),)),
            ],
            compiler_params=pltpu.CompilerParams(vmem_limit_bytes=VMEM_LIMIT),
            name="finish",
        )(*arrays, *held)
    return result


def solution(mesh):
    in_specs = (
        P("fsdp", "ctx", None),
        P("fsdp", "tp"),
        P("fsdp", "tp"),
        P("fsdp", "tp"),
        P("fsdp", "tp"),
        P("tp", "fsdp"),
        P("fsdp", "ctx", "tp"),
    )
    out_specs = P("fsdp", "ctx", "tp")
    return jax.shard_map(
        on_device, mesh=mesh, in_specs=in_specs, out_specs=out_specs, check_vma=False
    )
```

```python
import functools
import math

import jax
import jax.numpy as jnp
from jax import lax
from jax.experimental import pallas as pl
from jax.experimental.pallas import tpu as pltpu
from jax.sharding import PartitionSpec as P

DH = 256
BLOCK = 512
TILE = 256
FINE = 32
EXTRA = 16
VMEM_LIMIT = 14 * 1024 * 1024
F32 = jnp.float32
BF16 = jnp.bfloat16


def mm(left, right):
    return jnp.dot(left, right, preferred_element_type=F32)


def mm_nt(left, right):
    return lax.dot_general(left, right, (((1,), (1,)), ((), ())), preferred_element_type=F32)


def mm_tn(left, right):
    return lax.dot_general(left, right, (((0,), (0,)), ((), ())), preferred_element_type=F32)


def swap(value, axis, mask):
    size = lax.axis_size(axis)
    return lax.ppermute(value, axis, [(place, place ^ mask) for place in range(size)])


def kernel_call(kernel, outs, operands, name):
    arrays = [pltpu.with_memory_space_constraint(array, pltpu.VMEM) for array in operands]
    return pl.pallas_call(
        kernel,
        in_specs=[pl.BlockSpec(memory_space=pltpu.VMEM)] * len(operands),
        out_specs=[pl.BlockSpec(memory_space=pltpu.VMEM)] * len(outs),
        out_shape=[pltpu.VMEM(shape, dtype) for shape, dtype in outs],
        compiler_params=pltpu.CompilerParams(vmem_limit_bytes=VMEM_LIMIT),
        cost_estimate=pl.CostEstimate(
            flops=1, bytes_accessed=1, transcendentals=0
        ),
        name=name,
    )(*arrays)


def loading_call(kernel, outs, loaded, operands, scratch, loads, name):
    arrays = [pltpu.with_memory_space_constraint(array, pltpu.HBM) for array in loaded]
    arrays += [pltpu.with_memory_space_constraint(array, pltpu.VMEM) for array in operands]
    return pl.pallas_call(
        kernel,
        in_specs=[pl.BlockSpec(memory_space=pltpu.HBM)] * len(loaded)
        + [pl.BlockSpec(memory_space=pltpu.VMEM)] * len(operands),
        out_specs=[pl.BlockSpec(memory_space=pltpu.VMEM)] * len(outs),
        out_shape=[pltpu.VMEM(shape, dtype) for shape, dtype in outs],
        scratch_shapes=[*scratch, pltpu.SemaphoreType.DMA((loads,))],
        compiler_params=pltpu.CompilerParams(vmem_limit_bytes=VMEM_LIMIT),
        cost_estimate=pl.CostEstimate(flops=1, bytes_accessed=1, transcendentals=0),
        name=name,
    )(*arrays)


def turned(values, cosine, sine):
    half = DH // 2
    parts = []
    for start in range(0, values.shape[1], DH):
        low = values[:, start : start + half]
        high = values[:, start + half : start + DH]
        parts.append((low * cosine - high * sine).astype(BF16))
        parts.append((high * cosine + low * sine).astype(BF16))
    return jnp.concatenate(parts, axis=1)


def angles(coarse, fine, first, count):
    at = first // FINE
    far = coarse[:, pl.ds(at, count // FINE), :]
    near = fine[...]
    cos_c, sin_c = far[0][:, None, :], far[1][:, None, :]
    cos_f, sin_f = near[0][None], near[1][None]
    cosine = cos_c * cos_f - sin_c * sin_f
    sine = sin_c * cos_f + cos_c * sin_f
    return cosine.reshape(count, DH // 2), sine.reshape(count, DH // 2)


def decay_sums(log_decay, decay):
    heads, rows = log_decay.shape
    place_s = lax.broadcasted_iota(jnp.int32, (BLOCK, BLOCK), 0)
    place_t = lax.broadcasted_iota(jnp.int32, (BLOCK, BLOCK), 1)
    upper = jnp.where(place_s <= place_t, 1.0, 0.0).astype(BF16)
    value = jnp.concatenate([log_decay[...], jnp.zeros((8 - heads, rows), F32)], axis=0)
    parts = []
    for _ in range(3):
        parts.append(value.astype(BF16))
        value = value - parts[-1].astype(F32)
    stacked = jnp.concatenate([part.astype(F32) for part in parts], axis=0).astype(BF16)
    for start in range(0, rows, BLOCK):
        sums = mm(stacked[:, start : start + BLOCK], upper)
        decay[:, start : start + BLOCK] = sums[:8] + sums[8:16] + sums[16:]


def turn(first, second):
    (cos_a, sin_a), (cos_b, sin_b) = first, second
    return cos_a * cos_b - sin_a * sin_b, sin_a * cos_b + cos_a * sin_b


def joined(first, second):
    return tuple(jnp.concatenate(pair, axis=0) for pair in zip(first, second))


def angle_tables(coarse, fine):
    half, seeds = DH // 2, 8
    index = lax.broadcasted_iota(jnp.int32, (seeds, half), 1).astype(F32)
    frequency = jnp.exp(index * (-math.log(10000.0) / half))
    place = lax.broadcasted_iota(jnp.int32, (seeds, half), 0).astype(F32)
    offset = (lax.axis_index("ctx") * (coarse.shape[1] * FINE)).astype(F32)
    near = jnp.cos(place * frequency), jnp.sin(place * frequency)
    base = jnp.cos(offset * frequency), jnp.sin(offset * frequency)
    step = turn([part[seeds - 1 : seeds] for part in near], [part[1:2] for part in near])
    while near[0].shape[0] < FINE:
        near = joined(near, turn(near, step))
        step = turn(step, step)
    far = tuple(part[:1] for part in base)
    while far[0].shape[0] < coarse.shape[1]:
        far = joined(far, turn(far, step))
        step = turn(step, step)
    for table, parts in ((coarse, far), (fine, near)):
        table[0], table[1] = (part[: table.shape[1]] for part in parts)


class Loads:
    def __init__(self, arrived):
        self.arrived, self.count = arrived, 0

    def start(self, source, target):
        copy = pltpu.make_async_copy(source, target, self.arrived.at[self.count])
        self.count += 1
        copy.start()
        return copy


def half_of(x, rows, half):
    part = x.shape[1] // 2
    return x[rows, pl.ds(pl.multiple_of(half * part, part), part)]


def key_value_own_kernel(
    x_far, wk_far, wv_far, log_decay_far, wo_far,
    x, acc_k, acc_v, decay, coarse, fine, wo, wk, wv, log_decay, arrived,
):
    core = lax.axis_index("fsdp")
    loads = Loads(arrived)
    starts = range(0, x.shape[0], TILE)
    logs, key = loads.start(log_decay_far, log_decay), loads.start(wk_far, wk)
    tiles = [loads.start(x_far.at[pl.ds(0, TILE)], x.at[pl.ds(0, TILE)])]
    tiles += [loads.start(x_far.at[pl.ds(start, TILE)], x.at[pl.ds(start, TILE)]) for start in starts[1:]]
    value = loads.start(wv_far, wv)
    others = [loads.start(far, near) for far, near in ((wo_far, wo),)]
    angle_tables(coarse, fine)
    logs.wait()
    key.wait()
    for start in range(0, x.shape[0], BLOCK):
        at = slice(start, start + BLOCK)
        for copy in tiles[start // TILE : (start + BLOCK) // TILE]:
            copy.wait()
        acc_k[at, :] = mm(half_of(x, at, core), wk[...])
    value.wait()
    for start in range(0, x.shape[0], BLOCK):
        at = slice(start, start + BLOCK)
        acc_v[at, :] = mm(half_of(x, at, core), wv[...])
    decay_sums(log_decay, decay)
    for copy in others:
        copy.wait()


def block_ends(decay, start, stop):
    ends = [decay[:, end - 1 : end] for end in range(start + BLOCK, stop + 1, BLOCK)]
    return functools.reduce(lambda a, b: a + b, ends, jnp.zeros((decay.shape[0], 1), F32))


def pack_message(message, states, logs):
    for head, state in enumerate(states):
        message[head * DH : (head + 1) * DH, :] = state.astype(BF16)
    large = logs.astype(BF16).astype(F32)
    parts = jnp.concatenate([large, logs - large], axis=0)
    message[len(states) * DH :, :] = jnp.broadcast_to(parts, (EXTRA, DH)).astype(BF16)


def message_log(message, heads):
    tail = message[heads * DH :, :].astype(F32)
    return (tail[: EXTRA // 2] + tail[EXTRA // 2 :])[:, :1]


def exchanges(ctx, hop):
    lower = range(ctx - hop)
    if hop == 1:
        return [], list(lower), []
    early = [at for at in lower if at < hop // 2]
    even = [at for at in lower if at >= hop // 2 and at // hop % 2 == 0]
    odd = [at for at in lower if at // hop % 2 == 1]
    return early, even, odd


def is_upper(lowers, hop):
    place = lax.axis_index("ctx")
    found = place < 0
    for lower in lowers:
        found = jnp.logical_or(found, place == lower + hop)
    return found


def arrived_state(arrivals, sets, hop, span):
    parts = [jnp.where(is_upper(lowers, hop), ref[span, :].astype(F32), 0.0) for ref, lowers in zip(arrivals, sets)]
    return functools.reduce(lambda a, b: a + b, parts)


def arrived_log(arrivals, sets, hop, heads):
    parts = [jnp.where(is_upper(lowers, hop), message_log(ref, heads), 0.0) for ref, lowers in zip(arrivals, sets)]
    return functools.reduce(lambda a, b: a + b, parts)


def key_value_kernel(
    heads, wq_far, wg_far, x, wk, wv, acc_k, acc_v, decay, coarse, fine,
    wq, wg, k_out, v_out, before_out, state_out, message, arrived,
):
    loads = Loads(arrived)
    others = [loads.start(wq_far, wq), loads.start(wg_far, wg)]
    blocks, other = acc_k.shape[0] // BLOCK, 1 - lax.axis_index("fsdp")
    state_out[...] = jnp.zeros_like(state_out)
    for block in range(blocks):
        start = block * BLOCK
        at = slice(start, start + BLOCK)
        columns = decay[:, at].T
        ending = columns[BLOCK - 1 : BLOCK, :]
        faded = jnp.exp(ending - columns)
        rows = half_of(x, at, other)
        cosine, sine = angles(coarse, fine, start, BLOCK)
        keys = turned(acc_k[at, :] + mm(rows, wk[...]), cosine, sine)
        k_out[at, :] = keys
        values = (acc_v[at, :] + mm(rows, wv[...])).astype(BF16)
        v_out[at, :] = values
        for head in range(heads):
            span = slice(head * DH, (head + 1) * DH)
            weighted = (keys[:, span].astype(F32) * faded[:, head : head + 1]).astype(BF16)
            old = state_out[span, :]
            before_out[block, span, :] = old.astype(BF16)
            state_out[span, :] = jnp.exp(ending[:, head : head + 1]) * old + mm_tn(weighted, values[:, span])
    states = [state_out[head * DH : (head + 1) * DH, :] for head in range(heads)]
    pack_message(message, states, block_ends(decay, 0, acc_k.shape[0]))
    for copy in others:
        copy.wait()


def combine_kernel(heads, hop, sets, first, last, state, sent, *refs):
    if not first:
        old_entering, refs = refs[0], refs[1:]
    arrivals, entering, message = refs[: len(sets)], refs[len(sets)], refs[len(sets) + 1]
    window_log, log = message_log(sent, heads), arrived_log(arrivals, sets, hop, heads)
    before_log = jnp.zeros_like(log) if first else old_entering[heads * DH :, :1]
    states = []
    for head in range(heads):
        span, row = slice(head * DH, (head + 1) * DH), slice(head, head + 1)
        arrived = arrived_state(arrivals, sets, hop, span)
        if first:
            entering[span, :] = arrived
        else:
            entering[span, :] = old_entering[span, :] + jnp.exp(before_log[row]) * arrived
        states.append(state[span, :] + jnp.exp(window_log[row]) * arrived)
        if last:
            message[span, :] = states[-1].astype(BF16)
        else:
            refs[len(sets) + 2][span, :] = states[-1]
    entering[heads * DH :, :] = jnp.broadcast_to(before_log + log, (8, DH))
    if not last:
        pack_message(message, states, window_log + log)


def query_gate_kernel(
    heads, block, x, wq, wq_far, wg, wg_far, decay, coarse, fine, k, v, q_out, g_out, intra_out
):
    start = block * BLOCK
    lines = decay[:, start : start + BLOCK]
    columns = lines.T

    at = slice(start, start + BLOCK)
    cosine, sine = angles(coarse, fine, start, BLOCK)
    core = lax.axis_index("fsdp")
    own, far = half_of(x, at, core), half_of(x, at, 1 - core)
    queries = mm(own, wq[...]) + mm(far, wq_far[...])
    q_out[...] = turned(queries, cosine, sine)
    gates = mm(own, wg[...]) + mm(far, wg_far[...])
    gates = gates.astype(BF16).astype(F32)
    g_out[...] = gates / (1.0 + jnp.exp(-gates))
    for piece in range(BLOCK // TILE):
        low, last = piece * TILE, (piece + 1) * TILE
        place_t = lax.broadcasted_iota(jnp.int32, (TILE, last), 0) + low
        place_s = lax.broadcasted_iota(jnp.int32, (TILE, last), 1)
        causal = place_t >= place_s
        for head in range(heads):
            span = slice(head * DH, (head + 1) * DH)
            scores = mm_nt(q_out[low:last, span], k[start : start + last, span])
            differ = columns[low:last, head : head + 1] - lines[head : head + 1, :last]
            weights = jnp.where(causal, jnp.exp(jnp.where(causal, differ, 0.0)), 0.0)
            intra_out[low:last, span] = mm((scores * weights).astype(BF16), v[start : start + last, span])


def hidden_kernel(heads, hop, sets, starts, decay, before, entering, *refs):
    arrivals, refs, token = refs[: len(sets)], refs[len(sets) : -1], refs[-1]
    projected, outs = refs[: -len(starts)], refs[-len(starts) :]
    token[...] = jnp.zeros_like(token)
    for head in range(heads):
        span = slice(head * DH, (head + 1) * DH)
        entering_log = entering[heads * DH + head : heads * DH + head + 1, :1]
        state = entering[span, :] + jnp.exp(entering_log) * arrived_state(arrivals, sets, hop, span)
        for start, out in zip(starts, outs):
            block = start // BLOCK
            q, gate, intra = projected[3 * block : 3 * block + 3]
            at = slice(start % BLOCK, start % BLOCK + TILE)
            column = jnp.exp(decay[:, start : start + TILE].T[:, head : head + 1])
            scale_log = jnp.zeros((1, 1), F32)
            for earlier in range(block):
                end = (earlier + 1) * BLOCK
                scale_log = scale_log + decay[head : head + 1, end - 1 : end]
            prior = (jnp.exp(scale_log) * state + before[block, span, :].astype(F32)).astype(BF16)
            retained = intra[at, span] + column * mm(q[at, span], prior)
            center = retained - jnp.mean(retained, axis=1, keepdims=True)
            spread = jnp.mean(center * center, axis=1, keepdims=True)
            out[:, span] = (gate[at, span] * center * lax.rsqrt(spread + 1e-5)).astype(BF16)


def columns_kernel(first, second, *outs):
    cols = outs[0].shape[1]
    place, core = lax.axis_index("tp"), lax.axis_index("fsdp")
    high, low = place // 2, place % 2

    @pl.when(core == 0)
    def _():
        at = pl.ds(pl.multiple_of((1 - low) * cols, cols), cols)
        outs[0][...] = first[:, at]
        outs[1][...] = second[:, at]

    @pl.when(core == 1)
    def _():
        for number, out in enumerate(outs):
            at = slice(number * cols, (number + 1) * cols)
            out[...] = jnp.where(high == 0, first[:, at], second[:, at])


def arrange_kernel(mine_0, mine_1, other_0, other_1, low_out, high_out):
    cols = mine_0.shape[1]
    place, core = lax.axis_index("tp"), lax.axis_index("fsdp")
    for gathered, bit, out in ((core == 0, place // 2, low_out), (core == 1, place % 2, high_out)):
        blocks = [jnp.where(gathered, mine[...], other[...]) for mine, other in ((mine_0, other_0), (mine_1, other_1))]
        out[:, :cols] = jnp.where(bit == 0, blocks[1], blocks[0])
        out[:, cols:] = jnp.where(bit == 0, blocks[0], blocks[1])


def own_kernel(order, own_first, own_second, *refs):
    pieces, outs = refs[: len(order)], refs[len(order) :]
    cols = pieces[0].shape[1]
    place, core = lax.axis_index("tp"), lax.axis_index("fsdp")
    high, low = place // 2, place % 2
    here = core == high
    mine = pl.ds(pl.multiple_of(low * cols, cols), cols)
    flipped = pl.ds(pl.multiple_of((1 - low) * cols, cols), cols)
    keep = jnp.where(here, own_first[:, mine], own_second[:, mine])
    gives = [
        jnp.where(here, own_second[:, mine], own_first[:, mine]),
        jnp.where(here, own_first[:, flipped], own_second[:, flipped]),
    ]
    for (half, number), piece in zip(order, pieces):
        at = slice(number * TILE, (number + 1) * TILE)
        outs[half][at, :cols] = mm(piece[...], gives[half])
        outs[half][at, cols:] = mm(piece[...], keep)


def give_kernel(number, own, far, weight, out):
    cols = out.shape[1]
    at = slice(number * TILE, (number + 1) * TILE)
    out[...] = (own[at, :cols] + mm(far[...], weight[:, :cols])).astype(BF16)


def keep_kernel(order, *refs):
    count = len(order)
    fars, owns, weights, outs = refs[:count], refs[count : count + 2], refs[count + 2 : count + 4], refs[count + 4 :]
    for (half, number), far in zip(order, fars):
        cols = far.shape[1]
        at = slice(number * TILE, (number + 1) * TILE)
        outs[half][at, :] = owns[half][at, cols:] + mm(far[...], weights[half][:, cols:])


def finish_kernel(order, *refs):
    count = len(order)
    gots, keeps, out, ready, written = refs[:count], refs[count : count + 2], refs[-3], refs[-2], refs[-1]
    copies = []
    for slot, ((half, number), got) in enumerate(zip(order, gots)):
        keep = keeps[half]
        at = slice(number * TILE, (number + 1) * TILE)
        ready[slot] = (keep[at, :] + got[...].astype(F32)).astype(BF16)
        start = half * keep.shape[0] + number * TILE
        copies.append(pltpu.make_async_copy(ready.at[slot], out.at[0, pl.ds(start, TILE)], written.at[slot]))
        copies[-1].start()
    for copy in copies:
        copy.wait()


def after(value, *others):
    return lax.optimization_barrier((value, *others))[0]


def on_device(tokens, query_weight, key_weight, value_weight, gate_weight, out_weight, log_decay):
    x = tokens[0]
    rows, width = x.shape
    part, cols = query_weight.shape
    heads = cols // DH
    blocks = rows // BLOCK
    ctx, tp, cores = lax.axis_size("ctx"), lax.axis_size("tp"), lax.axis_size("fsdp")
    assert tp == 4 and cores == 2 and ctx >= 4 and ctx & (ctx - 1) == 0
    near_mask, far_mask = 1, 2
    tables = [((2, rows // FINE, DH // 2), F32), ((2, FINE, DH // 2), F32)]

    key_far = swap(key_weight, "fsdp", 1)
    value_far = swap(value_weight, "fsdp", 1)

    x, acc_k, acc_v, decay, coarse, fine, out_first = loading_call(
        key_value_own_kernel,
        [((rows, width), BF16), ((rows, cols), F32), ((rows, cols), F32), ((8, rows), F32)]
        + tables
        + [(out_weight.shape, BF16)],
        [x, key_weight, value_weight, log_decay[0].T, out_weight],
        [],
        [pltpu.VMEM((part, cols), BF16)] * 2 + [pltpu.VMEM((heads, rows), F32)],
        rows // TILE + 4,
        "key_value_own",
    )
    state_shape, message_shape = (heads * DH, DH), (heads * DH + EXTRA, DH)
    own_q, own_g, keys, values, before, window, message = loading_call(
        functools.partial(key_value_kernel, heads),
        [((part, cols), BF16)] * 2
        + [((rows, cols), BF16)] * 2
        + [((blocks, heads * DH, DH), BF16), (state_shape, F32), (message_shape, BF16)],
        [query_weight, gate_weight],
        [x, key_far, value_far, acc_k, acc_v, decay, coarse, fine],
        [],
        2,
        "key_value",
    )
    far_q, far_g = swap(own_q, "fsdp", 1), swap(own_g, "fsdp", 1)

    def query_gate(block, decay):
        return kernel_call(
            functools.partial(query_gate_kernel, heads, block),
            [((BLOCK, cols), BF16), ((BLOCK, cols), F32), ((BLOCK, cols), F32)],
            [x, own_q, far_q, own_g, far_g, decay, coarse, fine, keys, values],
            "query_gate",
        )

    def exchange(message, lowers, hop):
        pairs = [(at, at + hop) for at in lowers]
        if hop > 1:
            pairs += [(upper, at) for at, upper in pairs]
        return lax.ppermute(message, "ctx", pairs)

    projected = list(query_gate(0, decay))
    window = after(window, projected[0])
    entering, hop, early, first_message = None, 1, [], message
    while True:
        first_set, *later_sets = exchanges(ctx, hop)
        later_sets = [lowers for lowers in later_sets if lowers]
        sets = later_sets + ([first_set] if first_set else [])
        arrivals = [exchange(message, lowers, hop) for lowers in later_sets] + early
        if 2 * hop >= ctx:
            break
        unchanged = exchanges(ctx, 2 * hop)[0]
        early = [exchange(message, unchanged, 2 * hop)]
        old = [] if entering is None else [entering]
        last = 4 * hop >= ctx
        entering, message, *windows = kernel_call(
            functools.partial(combine_kernel, heads, hop, sets, entering is None, last),
            [((heads * DH + 8, DH), F32)]
            + ([(state_shape, BF16)] if last else [(message_shape, BF16), (state_shape, F32)]),
            [window, message, *old, *arrivals],
            "combine",
        )
        window = windows[0] if windows else None
        hop *= 2

    own_second = swap(out_first, "fsdp", 1)
    for_partner = kernel_call(
        columns_kernel,
        [((cols, cols), BF16)] * 2,
        [after(out_first, first_message), own_second],
        "columns",
    )
    pairs = [(at * cores + at_core, (at ^ mask) * cores + at_core) for at in range(tp) for at_core, mask in enumerate((near_mask, far_mask))]
    out_mine = [lax.ppermute(block, ("tp", "fsdp"), pairs) for block in for_partner]

    held = after(decay, message, *early, out_mine[0])
    for block in range(1, blocks):
        projected += query_gate(block, held)

    count = rows // 2 // TILE
    masks = (near_mask, far_mask)
    hidden, far = [[], []], [[], []]
    for number in range(count):
        held = after(decay, swap(pair[2], "fsdp", 1)) if number else decay
        pair = kernel_call(
            functools.partial(hidden_kernel, heads, hop, sets, [(half * count + number) * TILE for half in range(2)]),
            [((TILE, cols), BF16)] * 2 + [((16, 128), BF16)],
            [held, before, entering, *arrivals, *projected],
            "hidden",
        )
        if number == 0:
            out_other = [swap(after(block, pair[0]), "fsdp", 1) for block in out_mine]
        for half in range(2):
            hidden[half].append(pair[half])
            far[half].append(swap(pair[half], "tp", masks[half]))
    weights = kernel_call(
        arrange_kernel,
        [((cols, 2 * cols), BF16)] * 2,
        [*out_mine, *out_other],
        "arrange",
    )
    order = [(half, number) for number in reversed(range(count)) for half in (1, 0)]
    owns = kernel_call(
        functools.partial(own_kernel, order),
        [((count * TILE, 2 * cols), F32)] * 2,
        [out_first, own_second, *(hidden[half][number] for half, number in order)],
        "own_products",
    )
    gots = []
    for half, number in order:
        [give] = kernel_call(
            functools.partial(give_kernel, number),
            [((TILE, cols), BF16)],
            [owns[half], far[half][number], weights[half]],
            "give",
        )
        gots.append(swap(give, "tp", masks[1 - half]))
    keeps = kernel_call(
        functools.partial(keep_kernel, order),
        [((count * TILE, cols), F32)] * 2,
        [*(far[half][number] for half, number in order), *owns, *weights],
        "keep",
    )
    result = None
    for part_order, part_gots in ((order[2:], gots[2:]), (order[:2], gots[:2])):
        arrays = [pltpu.with_memory_space_constraint(array, pltpu.VMEM) for array in (*part_gots, *keeps)]
        held = [] if result is None else [result]
        result = pl.pallas_call(
            functools.partial(finish_kernel, part_order),
            in_specs=[pl.BlockSpec(memory_space=pltpu.VMEM)] * len(arrays)
            + [pl.BlockSpec(memory_space=pltpu.HBM)] * len(held),
            out_specs=pl.BlockSpec(memory_space=pltpu.HBM),
            out_shape=jax.ShapeDtypeStruct((1, rows, cols), BF16),
            input_output_aliases={len(arrays): 0} if held else {},
            scratch_shapes=[
                pltpu.VMEM((len(part_order), TILE, cols), BF16),
                pltpu.SemaphoreType.DMA((len(part_order),)),
            ],
            compiler_params=pltpu.CompilerParams(vmem_limit_bytes=VMEM_LIMIT),
            name="finish",
        )(*arrays, *held)
    return result


def solution(mesh):
    in_specs = (
        P("fsdp", "ctx", None),
        P("fsdp", "tp"),
        P("fsdp", "tp"),
        P("fsdp", "tp"),
        P("fsdp", "tp"),
        P("tp", "fsdp"),
        P("fsdp", "ctx", "tp"),
    )
    out_specs = P("fsdp", "ctx", "tp")
    return jax.shard_map(
        on_device, mesh=mesh, in_specs=in_specs, out_specs=out_specs, check_vma=False
    )
```

```python
import functools
import math

import jax
import jax.numpy as jnp
from jax import lax
from jax.experimental import pallas as pl
from jax.experimental.pallas import tpu as pltpu
from jax.sharding import PartitionSpec as P

DH = 256
BLOCK = 512
TILE = 256
FINE = 32
EXTRA = 16
VMEM_LIMIT = 14 * 1024 * 1024
F32 = jnp.float32
BF16 = jnp.bfloat16


def mm(left, right):
    return jnp.dot(left, right, preferred_element_type=F32)


def mm_nt(left, right):
    return lax.dot_general(left, right, (((1,), (1,)), ((), ())), preferred_element_type=F32)


def mm_tn(left, right):
    return lax.dot_general(left, right, (((0,), (0,)), ((), ())), preferred_element_type=F32)


def swap(value, axis, mask):
    size = lax.axis_size(axis)
    return lax.ppermute(value, axis, [(place, place ^ mask) for place in range(size)])


def kernel_call(kernel, outs, operands, name):
    arrays = [pltpu.with_memory_space_constraint(array, pltpu.VMEM) for array in operands]
    return pl.pallas_call(
        kernel,
        in_specs=[pl.BlockSpec(memory_space=pltpu.VMEM)] * len(operands),
        out_specs=[pl.BlockSpec(memory_space=pltpu.VMEM)] * len(outs),
        out_shape=[pltpu.VMEM(shape, dtype) for shape, dtype in outs],
        compiler_params=pltpu.CompilerParams(vmem_limit_bytes=VMEM_LIMIT),
        cost_estimate=pl.CostEstimate(
            flops=1, bytes_accessed=1, transcendentals=0
        ),
        name=name,
    )(*arrays)


def loading_call(kernel, outs, loaded, operands, scratch, loads, name):
    arrays = [pltpu.with_memory_space_constraint(array, pltpu.HBM) for array in loaded]
    arrays += [pltpu.with_memory_space_constraint(array, pltpu.VMEM) for array in operands]
    return pl.pallas_call(
        kernel,
        in_specs=[pl.BlockSpec(memory_space=pltpu.HBM)] * len(loaded)
        + [pl.BlockSpec(memory_space=pltpu.VMEM)] * len(operands),
        out_specs=[pl.BlockSpec(memory_space=pltpu.VMEM)] * len(outs),
        out_shape=[pltpu.VMEM(shape, dtype) for shape, dtype in outs],
        scratch_shapes=[*scratch, pltpu.SemaphoreType.DMA((loads,))],
        compiler_params=pltpu.CompilerParams(vmem_limit_bytes=VMEM_LIMIT),
        cost_estimate=pl.CostEstimate(flops=1, bytes_accessed=1, transcendentals=0),
        name=name,
    )(*arrays)


def turned(values, cosine, sine):
    half = DH // 2
    parts = []
    for start in range(0, values.shape[1], DH):
        low = values[:, start : start + half]
        high = values[:, start + half : start + DH]
        parts.append((low * cosine - high * sine).astype(BF16))
        parts.append((high * cosine + low * sine).astype(BF16))
    return jnp.concatenate(parts, axis=1)


def angles(coarse, fine, first, count):
    at = first // FINE
    far = coarse[:, pl.ds(at, count // FINE), :]
    near = fine[...]
    cos_c, sin_c = far[0][:, None, :], far[1][:, None, :]
    cos_f, sin_f = near[0][None], near[1][None]
    cosine = cos_c * cos_f - sin_c * sin_f
    sine = sin_c * cos_f + cos_c * sin_f
    return cosine.reshape(count, DH // 2), sine.reshape(count, DH // 2)


def decay_sums(log_decay, decay):
    heads, rows = log_decay.shape
    place_s = lax.broadcasted_iota(jnp.int32, (BLOCK, BLOCK), 0)
    place_t = lax.broadcasted_iota(jnp.int32, (BLOCK, BLOCK), 1)
    upper = jnp.where(place_s <= place_t, 1.0, 0.0).astype(BF16)
    value = jnp.concatenate([log_decay[...], jnp.zeros((8 - heads, rows), F32)], axis=0)
    parts = []
    for _ in range(3):
        parts.append(value.astype(BF16))
        value = value - parts[-1].astype(F32)
    stacked = jnp.concatenate([part.astype(F32) for part in parts], axis=0).astype(BF16)
    for start in range(0, rows, BLOCK):
        sums = mm(stacked[:, start : start + BLOCK], upper)
        decay[:, start : start + BLOCK] = sums[:8] + sums[8:16] + sums[16:]


def turn(first, second):
    (cos_a, sin_a), (cos_b, sin_b) = first, second
    return cos_a * cos_b - sin_a * sin_b, sin_a * cos_b + cos_a * sin_b


def joined(first, second):
    return tuple(jnp.concatenate(pair, axis=0) for pair in zip(first, second))


def angle_tables(coarse, fine):
    half, seeds = DH // 2, 8
    index = lax.broadcasted_iota(jnp.int32, (seeds, half), 1).astype(F32)
    frequency = jnp.exp(index * (-math.log(10000.0) / half))
    place = lax.broadcasted_iota(jnp.int32, (seeds, half), 0).astype(F32)
    offset = (lax.axis_index("ctx") * (coarse.shape[1] * FINE)).astype(F32)
    near = jnp.cos(place * frequency), jnp.sin(place * frequency)
    base = jnp.cos(offset * frequency), jnp.sin(offset * frequency)
    step = turn([part[seeds - 1 : seeds] for part in near], [part[1:2] for part in near])
    while near[0].shape[0] < FINE:
        near = joined(near, turn(near, step))
        step = turn(step, step)
    far = tuple(part[:1] for part in base)
    while far[0].shape[0] < coarse.shape[1]:
        far = joined(far, turn(far, step))
        step = turn(step, step)
    for table, parts in ((coarse, far), (fine, near)):
        table[0], table[1] = (part[: table.shape[1]] for part in parts)


class Loads:
    def __init__(self, arrived):
        self.arrived, self.count = arrived, 0

    def start(self, source, target):
        copy = pltpu.make_async_copy(source, target, self.arrived.at[self.count])
        self.count += 1
        copy.start()
        return copy


def key_value_own_kernel(
    x_far, wk_far, wv_far, log_decay_far, wo_far,
    x_own, x_other, acc_k, acc_v, decay, coarse, fine, wo, wk, wv, log_decay, arrived,
):
    rows, part = x_own.shape
    core = lax.axis_index("fsdp")
    loads = Loads(arrived)

    def tile(x, half, start):
        at = pl.ds(start, BLOCK)
        columns = pl.ds(pl.multiple_of(half * part, part), part)
        return loads.start(x_far.at[at, columns], x.at[at])

    starts = range(0, rows, BLOCK)
    key, logs = loads.start(wk_far, wk), loads.start(log_decay_far, log_decay)
    tiles = [tile(x_own, core, start) for start in starts]
    value = loads.start(wv_far, wv)
    others = [tile(x_other, 1 - core, start) for start in starts] + [loads.start(wo_far, wo)]
    angle_tables(coarse, fine)
    logs.wait()
    decay_sums(log_decay, decay)
    key.wait()
    for copy, start in zip(tiles, starts):
        at = slice(start, start + BLOCK)
        copy.wait()
        acc_k[at, :] = mm(x_own[at, :], wk[...])
    value.wait()
    for start in starts:
        at = slice(start, start + BLOCK)
        acc_v[at, :] = mm(x_own[at, :], wv[...])
    for copy in others:
        copy.wait()


def block_ends(decay, start, stop):
    ends = [decay[:, end - 1 : end] for end in range(start + BLOCK, stop + 1, BLOCK)]
    return functools.reduce(lambda a, b: a + b, ends, jnp.zeros((decay.shape[0], 1), F32))


def pack_message(message, states, logs):
    for head, state in enumerate(states):
        message[head * DH : (head + 1) * DH, :] = state.astype(BF16)
    large = logs.astype(BF16).astype(F32)
    parts = jnp.concatenate([large, logs - large], axis=0)
    message[len(states) * DH :, :] = jnp.broadcast_to(parts, (EXTRA, DH)).astype(BF16)


def message_log(message, heads):
    tail = message[heads * DH :, :].astype(F32)
    return (tail[: EXTRA // 2] + tail[EXTRA // 2 :])[:, :1]


def exchanges(ctx, hop):
    lower = range(ctx - hop)
    if hop == 1:
        return [], list(lower), []
    early = [at for at in lower if at < hop // 2]
    even = [at for at in lower if at >= hop // 2 and at // hop % 2 == 0]
    odd = [at for at in lower if at // hop % 2 == 1]
    return early, even, odd


def is_upper(lowers, hop):
    place = lax.axis_index("ctx")
    found = place < 0
    for lower in lowers:
        found = jnp.logical_or(found, place == lower + hop)
    return found


def arrived_state(arrivals, sets, hop, span):
    parts = [jnp.where(is_upper(lowers, hop), ref[span, :].astype(F32), 0.0) for ref, lowers in zip(arrivals, sets)]
    return functools.reduce(lambda a, b: a + b, parts)


def arrived_log(arrivals, sets, hop, heads):
    parts = [jnp.where(is_upper(lowers, hop), message_log(ref, heads), 0.0) for ref, lowers in zip(arrivals, sets)]
    return functools.reduce(lambda a, b: a + b, parts)


def key_value_kernel(
    heads, wq_far, wg_far, x, wk, wv, acc_k, acc_v, decay, coarse, fine,
    wq, wg, k_out, v_out, before_out, state_out, message, arrived,
):
    loads = Loads(arrived)
    others = [loads.start(wq_far, wq), loads.start(wg_far, wg)]
    blocks = acc_k.shape[0] // BLOCK
    state_out[...] = jnp.zeros_like(state_out)
    for block in range(blocks):
        start = block * BLOCK
        at = slice(start, start + BLOCK)
        columns = decay[:, at].T
        ending = columns[BLOCK - 1 : BLOCK, :]
        faded = jnp.exp(ending - columns)
        rows = x[at, :]
        cosine, sine = angles(coarse, fine, start, BLOCK)
        keys = turned(acc_k[at, :] + mm(rows, wk[...]), cosine, sine)
        k_out[at, :] = keys
        values = (acc_v[at, :] + mm(rows, wv[...])).astype(BF16)
        v_out[at, :] = values
        for head in range(heads):
            span = slice(head * DH, (head + 1) * DH)
            weighted = (keys[:, span].astype(F32) * faded[:, head : head + 1]).astype(BF16)
            old = state_out[span, :]
            before_out[block, span, :] = old.astype(BF16)
            state_out[span, :] = jnp.exp(ending[:, head : head + 1]) * old + mm_tn(weighted, values[:, span])
    states = [state_out[head * DH : (head + 1) * DH, :] for head in range(heads)]
    pack_message(message, states, block_ends(decay, 0, acc_k.shape[0]))
    for copy in others:
        copy.wait()


def combine_kernel(heads, hop, sets, first, last, state, sent, *refs):
    if not first:
        old_entering, refs = refs[0], refs[1:]
    arrivals, entering, message = refs[: len(sets)], refs[len(sets)], refs[len(sets) + 1]
    window_log, log = message_log(sent, heads), arrived_log(arrivals, sets, hop, heads)
    before_log = jnp.zeros_like(log) if first else old_entering[heads * DH :, :1]
    states = []
    for head in range(heads):
        span, row = slice(head * DH, (head + 1) * DH), slice(head, head + 1)
        arrived = arrived_state(arrivals, sets, hop, span)
        if first:
            entering[span, :] = arrived
        else:
            entering[span, :] = old_entering[span, :] + jnp.exp(before_log[row]) * arrived
        states.append(state[span, :] + jnp.exp(window_log[row]) * arrived)
        if last:
            message[span, :] = states[-1].astype(BF16)
        else:
            refs[len(sets) + 2][span, :] = states[-1]
    entering[heads * DH :, :] = jnp.broadcast_to(before_log + log, (8, DH))
    if not last:
        pack_message(message, states, window_log + log)


def query_gate_kernel(
    heads, block, x_own, x_other, wq, wq_far, wg, wg_far, decay, coarse, fine, k, v, q_out, g_out, intra_out
):
    start = block * BLOCK
    lines = decay[:, start : start + BLOCK]
    columns = lines.T

    at = slice(start, start + BLOCK)
    cosine, sine = angles(coarse, fine, start, BLOCK)
    own, far = x_own[at, :], x_other[at, :]
    queries = mm(own, wq[...]) + mm(far, wq_far[...])
    q_out[...] = turned(queries, cosine, sine)
    gates = mm(own, wg[...]) + mm(far, wg_far[...])
    gates = gates.astype(BF16).astype(F32)
    g_out[...] = gates / (1.0 + jnp.exp(-gates))
    for piece in range(BLOCK // TILE):
        low, last = piece * TILE, (piece + 1) * TILE
        place_t = lax.broadcasted_iota(jnp.int32, (TILE, last), 0) + low
        place_s = lax.broadcasted_iota(jnp.int32, (TILE, last), 1)
        causal = place_t >= place_s
        for head in range(heads):
            span = slice(head * DH, (head + 1) * DH)
            scores = mm_nt(q_out[low:last, span], k[start : start + last, span])
            differ = columns[low:last, head : head + 1] - lines[head : head + 1, :last]
            weights = jnp.where(causal, jnp.exp(jnp.where(causal, differ, 0.0)), 0.0)
            intra_out[low:last, span] = mm((scores * weights).astype(BF16), v[start : start + last, span])


def hidden_kernel(heads, hop, sets, starts, decay, before, entering, *refs):
    arrivals, refs, token = refs[: len(sets)], refs[len(sets) : -1], refs[-1]
    projected, outs = refs[: -len(starts)], refs[-len(starts) :]
    token[...] = jnp.zeros_like(token)
    for head in range(heads):
        span = slice(head * DH, (head + 1) * DH)
        entering_log = entering[heads * DH + head : heads * DH + head + 1, :1]
        state = entering[span, :] + jnp.exp(entering_log) * arrived_state(arrivals, sets, hop, span)
        for start, out in zip(starts, outs):
            block = start // BLOCK
            q, gate, intra = projected[3 * block : 3 * block + 3]
            at = slice(start % BLOCK, start % BLOCK + TILE)
            column = jnp.exp(decay[:, start : start + TILE].T[:, head : head + 1])
            scale_log = jnp.zeros((1, 1), F32)
            for earlier in range(block):
                end = (earlier + 1) * BLOCK
                scale_log = scale_log + decay[head : head + 1, end - 1 : end]
            prior = (jnp.exp(scale_log) * state + before[block, span, :].astype(F32)).astype(BF16)
            retained = intra[at, span] + column * mm(q[at, span], prior)
            center = retained - jnp.mean(retained, axis=1, keepdims=True)
            spread = jnp.mean(center * center, axis=1, keepdims=True)
            out[:, span] = (gate[at, span] * center * lax.rsqrt(spread + 1e-5)).astype(BF16)


def columns_kernel(first, second, *outs):
    cols = outs[0].shape[1]
    place, core = lax.axis_index("tp"), lax.axis_index("fsdp")
    high, low = place // 2, place % 2

    @pl.when(core == 0)
    def _():
        at = pl.ds(pl.multiple_of((1 - low) * cols, cols), cols)
        outs[0][...] = first[:, at]
        outs[1][...] = second[:, at]

    @pl.when(core == 1)
    def _():
        for number, out in enumerate(outs):
            at = slice(number * cols, (number + 1) * cols)
            out[...] = jnp.where(high == 0, first[:, at], second[:, at])


def arrange_kernel(mine_0, mine_1, other_0, other_1, low_out, high_out):
    cols = mine_0.shape[1]
    place, core = lax.axis_index("tp"), lax.axis_index("fsdp")
    for gathered, bit, out in ((core == 0, place // 2, low_out), (core == 1, place % 2, high_out)):
        blocks = [jnp.where(gathered, mine[...], other[...]) for mine, other in ((mine_0, other_0), (mine_1, other_1))]
        out[:, :cols] = jnp.where(bit == 0, blocks[1], blocks[0])
        out[:, cols:] = jnp.where(bit == 0, blocks[0], blocks[1])


def own_kernel(order, own_first, own_second, *refs):
    pieces, outs = refs[: len(order)], refs[len(order) :]
    cols = pieces[0].shape[1]
    place, core = lax.axis_index("tp"), lax.axis_index("fsdp")
    high, low = place // 2, place % 2
    here = core == high
    mine = pl.ds(pl.multiple_of(low * cols, cols), cols)
    flipped = pl.ds(pl.multiple_of((1 - low) * cols, cols), cols)
    keep = jnp.where(here, own_first[:, mine], own_second[:, mine])
    gives = [
        jnp.where(here, own_second[:, mine], own_first[:, mine]),
        jnp.where(here, own_first[:, flipped], own_second[:, flipped]),
    ]
    for (half, number), piece in zip(order, pieces):
        at = slice(number * TILE, (number + 1) * TILE)
        outs[half][at, :cols] = mm(piece[...], gives[half])
        outs[half][at, cols:] = mm(piece[...], keep)


def give_kernel(number, own, far, weight, out):
    cols = out.shape[1]
    at = slice(number * TILE, (number + 1) * TILE)
    out[...] = (own[at, :cols] + mm(far[...], weight[:, :cols])).astype(BF16)


def keep_kernel(order, *refs):
    count = len(order)
    fars, owns, weights, outs = refs[:count], refs[count : count + 2], refs[count + 2 : count + 4], refs[count + 4 :]
    for (half, number), far in zip(order, fars):
        cols = far.shape[1]
        at = slice(number * TILE, (number + 1) * TILE)
        outs[half][at, :] = owns[half][at, cols:] + mm(far[...], weights[half][:, cols:])


def finish_kernel(order, *refs):
    count = len(order)
    gots, keeps, out, ready, written = refs[:count], refs[count : count + 2], refs[-3], refs[-2], refs[-1]
    copies = []
    for slot, ((half, number), got) in enumerate(zip(order, gots)):
        keep = keeps[half]
        at = slice(number * TILE, (number + 1) * TILE)
        ready[slot] = (keep[at, :] + got[...].astype(F32)).astype(BF16)
        start = half * keep.shape[0] + number * TILE
        copies.append(pltpu.make_async_copy(ready.at[slot], out.at[0, pl.ds(start, TILE)], written.at[slot]))
        copies[-1].start()
    for copy in copies:
        copy.wait()


def after(value, *others):
    return lax.optimization_barrier((value, *others))[0]


def on_device(tokens, query_weight, key_weight, value_weight, gate_weight, out_weight, log_decay):
    x = tokens[0]
    rows, width = x.shape
    part, cols = query_weight.shape
    heads = cols // DH
    blocks = rows // BLOCK
    ctx, tp, cores = lax.axis_size("ctx"), lax.axis_size("tp"), lax.axis_size("fsdp")
    assert tp == 4 and cores == 2 and ctx >= 4 and ctx & (ctx - 1) == 0
    near_mask, far_mask = 1, 2
    tables = [((2, rows // FINE, DH // 2), F32), ((2, FINE, DH // 2), F32)]

    key_far = swap(key_weight, "fsdp", 1)
    value_far = swap(value_weight, "fsdp", 1)

    x_own, x_other, acc_k, acc_v, decay, coarse, fine, out_first = loading_call(
        key_value_own_kernel,
        [((rows, part), BF16)] * 2 + [((rows, cols), F32)] * 2 + [((8, rows), F32)]
        + tables
        + [(out_weight.shape, BF16)],
        [x, key_weight, value_weight, log_decay[0].T, out_weight],
        [],
        [pltpu.VMEM((part, cols), BF16)] * 2 + [pltpu.VMEM((heads, rows), F32)],
        2 * (rows // BLOCK) + 4,
        "key_value_own",
    )
    state_shape, message_shape = (heads * DH, DH), (heads * DH + EXTRA, DH)
    own_q, own_g, keys, values, before, window, message = loading_call(
        functools.partial(key_value_kernel, heads),
        [((part, cols), BF16)] * 2
        + [((rows, cols), BF16)] * 2
        + [((blocks, heads * DH, DH), BF16), (state_shape, F32), (message_shape, BF16)],
        [query_weight, gate_weight],
        [x_other, key_far, value_far, acc_k, acc_v, decay, coarse, fine],
        [],
        2,
        "key_value",
    )
    far_q, far_g = swap(own_q, "fsdp", 1), swap(own_g, "fsdp", 1)

    def query_gate(block, decay):
        return kernel_call(
            functools.partial(query_gate_kernel, heads, block),
            [((BLOCK, cols), BF16), ((BLOCK, cols), F32), ((BLOCK, cols), F32)],
            [x_own, x_other, own_q, far_q, own_g, far_g, decay, coarse, fine, keys, values],
            "query_gate",
        )

    def exchange(message, lowers, hop):
        pairs = [(at, at + hop) for at in lowers]
        if hop > 1:
            pairs += [(upper, at) for at, upper in pairs]
        return lax.ppermute(message, "ctx", pairs)

    projected = list(query_gate(0, decay))
    window = after(window, projected[0])
    entering, hop, early, first_message = None, 1, [], message
    while True:
        first_set, *later_sets = exchanges(ctx, hop)
        later_sets = [lowers for lowers in later_sets if lowers]
        sets = later_sets + ([first_set] if first_set else [])
        arrivals = [exchange(message, lowers, hop) for lowers in later_sets] + early
        if 2 * hop >= ctx:
            break
        unchanged = exchanges(ctx, 2 * hop)[0]
        early = [exchange(message, unchanged, 2 * hop)]
        old = [] if entering is None else [entering]
        last = 4 * hop >= ctx
        entering, message, *windows = kernel_call(
            functools.partial(combine_kernel, heads, hop, sets, entering is None, last),
            [((heads * DH + 8, DH), F32)]
            + ([(state_shape, BF16)] if last else [(message_shape, BF16), (state_shape, F32)]),
            [window, message, *old, *arrivals],
            "combine",
        )
        window = windows[0] if windows else None
        hop *= 2

    own_second = swap(out_first, "fsdp", 1)
    for_partner = kernel_call(
        columns_kernel,
        [((cols, cols), BF16)] * 2,
        [after(out_first, first_message), own_second],
        "columns",
    )
    pairs = [(at * cores + at_core, (at ^ mask) * cores + at_core) for at in range(tp) for at_core, mask in enumerate((near_mask, far_mask))]
    out_mine = [lax.ppermute(block, ("tp", "fsdp"), pairs) for block in for_partner]

    held = after(decay, message, *early, out_mine[0])
    for block in range(1, blocks):
        projected += query_gate(block, held)

    count = rows // 2 // TILE
    masks = (near_mask, far_mask)
    hidden, far = [[], []], [[], []]
    for number in range(count):
        held = after(decay, swap(pair[2], "fsdp", 1)) if number else decay
        pair = kernel_call(
            functools.partial(hidden_kernel, heads, hop, sets, [(half * count + number) * TILE for half in range(2)]),
            [((TILE, cols), BF16)] * 2 + [((16, 128), BF16)],
            [held, before, entering, *arrivals, *projected],
            "hidden",
        )
        if number == 0:
            out_other = [swap(after(block, pair[0]), "fsdp", 1) for block in out_mine]
        for half in range(2):
            hidden[half].append(pair[half])
            far[half].append(swap(pair[half], "tp", masks[half]))
    weights = kernel_call(
        arrange_kernel,
        [((cols, 2 * cols), BF16)] * 2,
        [*out_mine, *out_other],
        "arrange",
    )
    order = [(half, number) for number in reversed(range(count)) for half in (1, 0)]
    owns = kernel_call(
        functools.partial(own_kernel, order),
        [((count * TILE, 2 * cols), F32)] * 2,
        [out_first, own_second, *(hidden[half][number] for half, number in order)],
        "own_products",
    )
    gots = []
    for half, number in order:
        [give] = kernel_call(
            functools.partial(give_kernel, number),
            [((TILE, cols), BF16)],
            [owns[half], far[half][number], weights[half]],
            "give",
        )
        gots.append(swap(give, "tp", masks[1 - half]))
    keeps = kernel_call(
        functools.partial(keep_kernel, order),
        [((count * TILE, cols), F32)] * 2,
        [*(far[half][number] for half, number in order), *owns, *weights],
        "keep",
    )
    result = None
    for part_order, part_gots in ((order[2:], gots[2:]), (order[:2], gots[:2])):
        arrays = [pltpu.with_memory_space_constraint(array, pltpu.VMEM) for array in (*part_gots, *keeps)]
        held = [] if result is None else [result]
        result = pl.pallas_call(
            functools.partial(finish_kernel, part_order),
            in_specs=[pl.BlockSpec(memory_space=pltpu.VMEM)] * len(arrays)
            + [pl.BlockSpec(memory_space=pltpu.HBM)] * len(held),
            out_specs=pl.BlockSpec(memory_space=pltpu.HBM),
            out_shape=jax.ShapeDtypeStruct((1, rows, cols), BF16),
            input_output_aliases={len(arrays): 0} if held else {},
            scratch_shapes=[
                pltpu.VMEM((len(part_order), TILE, cols), BF16),
                pltpu.SemaphoreType.DMA((len(part_order),)),
            ],
            compiler_params=pltpu.CompilerParams(vmem_limit_bytes=VMEM_LIMIT),
            name="finish",
        )(*arrays, *held)
    return result


def solution(mesh):
    in_specs = (
        P("fsdp", "ctx", None),
        P("fsdp", "tp"),
        P("fsdp", "tp"),
        P("fsdp", "tp"),
        P("fsdp", "tp"),
        P("tp", "fsdp"),
        P("fsdp", "ctx", "tp"),
    )
    out_specs = P("fsdp", "ctx", "tp")
    return jax.shard_map(
        on_device, mesh=mesh, in_specs=in_specs, out_specs=out_specs, check_vma=False
    )
```

```python
import functools
import math

import jax
import jax.numpy as jnp
from jax import lax
from jax.experimental import pallas as pl
from jax.experimental.pallas import tpu as pltpu
from jax.sharding import PartitionSpec as P

DH = 256
BLOCK = 512
TILE = 256
FINE = 32
EXTRA = 16
VMEM_LIMIT = 14 * 1024 * 1024
F32 = jnp.float32
BF16 = jnp.bfloat16


def mm(left, right):
    return jnp.dot(left, right, preferred_element_type=F32)


def mm_nt(left, right):
    return lax.dot_general(left, right, (((1,), (1,)), ((), ())), preferred_element_type=F32)


def mm_tn(left, right):
    return lax.dot_general(left, right, (((0,), (0,)), ((), ())), preferred_element_type=F32)


def swap(value, axis, mask):
    size = lax.axis_size(axis)
    return lax.ppermute(value, axis, [(place, place ^ mask) for place in range(size)])


def kernel_call(kernel, outs, operands, name):
    arrays = [pltpu.with_memory_space_constraint(array, pltpu.VMEM) for array in operands]
    return pl.pallas_call(
        kernel,
        in_specs=[pl.BlockSpec(memory_space=pltpu.VMEM)] * len(operands),
        out_specs=[pl.BlockSpec(memory_space=pltpu.VMEM)] * len(outs),
        out_shape=[pltpu.VMEM(shape, dtype) for shape, dtype in outs],
        compiler_params=pltpu.CompilerParams(vmem_limit_bytes=VMEM_LIMIT),
        cost_estimate=pl.CostEstimate(
            flops=1, bytes_accessed=1, transcendentals=0
        ),
        name=name,
    )(*arrays)


def loading_call(kernel, outs, loaded, operands, scratch, loads, name):
    arrays = [pltpu.with_memory_space_constraint(array, pltpu.HBM) for array in loaded]
    arrays += [pltpu.with_memory_space_constraint(array, pltpu.VMEM) for array in operands]
    return pl.pallas_call(
        kernel,
        in_specs=[pl.BlockSpec(memory_space=pltpu.HBM)] * len(loaded)
        + [pl.BlockSpec(memory_space=pltpu.VMEM)] * len(operands),
        out_specs=[pl.BlockSpec(memory_space=pltpu.VMEM)] * len(outs),
        out_shape=[pltpu.VMEM(shape, dtype) for shape, dtype in outs],
        scratch_shapes=[*scratch, pltpu.SemaphoreType.DMA((loads,))],
        compiler_params=pltpu.CompilerParams(vmem_limit_bytes=VMEM_LIMIT),
        cost_estimate=pl.CostEstimate(flops=1, bytes_accessed=1, transcendentals=0),
        name=name,
    )(*arrays)


def turned(values, cosine, sine):
    half = DH // 2
    parts = []
    for start in range(0, values.shape[1], DH):
        low = values[:, start : start + half]
        high = values[:, start + half : start + DH]
        parts.append((low * cosine - high * sine).astype(BF16))
        parts.append((high * cosine + low * sine).astype(BF16))
    return jnp.concatenate(parts, axis=1)


def angles(coarse, fine, first, count):
    at = first // FINE
    far = coarse[:, pl.ds(at, count // FINE), :]
    near = fine[...]
    cos_c, sin_c = far[0][:, None, :], far[1][:, None, :]
    cos_f, sin_f = near[0][None], near[1][None]
    cosine = cos_c * cos_f - sin_c * sin_f
    sine = sin_c * cos_f + cos_c * sin_f
    return cosine.reshape(count, DH // 2), sine.reshape(count, DH // 2)


def decay_sums(log_decay, decay):
    heads, rows = log_decay.shape
    place_s = lax.broadcasted_iota(jnp.int32, (BLOCK, BLOCK), 0)
    place_t = lax.broadcasted_iota(jnp.int32, (BLOCK, BLOCK), 1)
    upper = jnp.where(place_s <= place_t, 1.0, 0.0).astype(BF16)
    value = jnp.concatenate([log_decay[...], jnp.zeros((8 - heads, rows), F32)], axis=0)
    parts = []
    for _ in range(3):
        parts.append(value.astype(BF16))
        value = value - parts[-1].astype(F32)
    stacked = jnp.concatenate([part.astype(F32) for part in parts], axis=0).astype(BF16)
    for start in range(0, rows, BLOCK):
        sums = mm(stacked[:, start : start + BLOCK], upper)
        decay[:, start : start + BLOCK] = sums[:8] + sums[8:16] + sums[16:]


def turn(first, second):
    (cos_a, sin_a), (cos_b, sin_b) = first, second
    return cos_a * cos_b - sin_a * sin_b, sin_a * cos_b + cos_a * sin_b


def joined(first, second):
    return tuple(jnp.concatenate(pair, axis=0) for pair in zip(first, second))


def angle_tables(coarse, fine):
    half, seeds = DH // 2, 8
    index = lax.broadcasted_iota(jnp.int32, (seeds, half), 1).astype(F32)
    frequency = jnp.exp(index * (-math.log(10000.0) / half))
    place = lax.broadcasted_iota(jnp.int32, (seeds, half), 0).astype(F32)
    offset = (lax.axis_index("ctx") * (coarse.shape[1] * FINE)).astype(F32)
    near = jnp.cos(place * frequency), jnp.sin(place * frequency)
    base = jnp.cos(offset * frequency), jnp.sin(offset * frequency)
    step = turn([part[seeds - 1 : seeds] for part in near], [part[1:2] for part in near])
    while near[0].shape[0] < FINE:
        near = joined(near, turn(near, step))
        step = turn(step, step)
    far = tuple(part[:1] for part in base)
    while far[0].shape[0] < coarse.shape[1]:
        far = joined(far, turn(far, step))
        step = turn(step, step)
    for table, parts in ((coarse, far), (fine, near)):
        table[0], table[1] = (part[: table.shape[1]] for part in parts)


class Loads:
    def __init__(self, arrived):
        self.arrived, self.count = arrived, 0

    def start(self, source, target):
        copy = pltpu.make_async_copy(source, target, self.arrived.at[self.count])
        self.count += 1
        copy.start()
        return copy


def key_value_own_kernel(
    x_far, wk_far, wv_far, log_decay_far, wo_far,
    x_own, x_other, acc_k, acc_v, decay, coarse, fine, wo, wk, wv, log_decay, arrived,
):
    rows, part = x_own.shape
    core = lax.axis_index("fsdp")
    loads = Loads(arrived)

    def tile(x, half, start):
        at = pl.ds(start, BLOCK)
        columns = pl.ds(pl.multiple_of(half * part, part), part)
        return loads.start(x_far.at[at, columns], x.at[at])

    starts = range(0, rows, BLOCK)
    key, logs = loads.start(wk_far, wk), loads.start(log_decay_far, log_decay)
    tiles = [tile(x_own, core, start) for start in starts]
    value = loads.start(wv_far, wv)
    others = [tile(x_other, 1 - core, start) for start in starts] + [loads.start(wo_far, wo)]
    angle_tables(coarse, fine)
    logs.wait()
    decay_sums(log_decay, decay)
    key.wait()
    for copy, start in zip(tiles, starts):
        at = slice(start, start + BLOCK)
        copy.wait()
        acc_k[at, :] = mm(x_own[at, :], wk[...])
    value.wait()
    for start in starts:
        at = slice(start, start + BLOCK)
        acc_v[at, :] = mm(x_own[at, :], wv[...])
    for copy in others:
        copy.wait()


def block_ends(decay, start, stop):
    ends = [decay[:, end - 1 : end] for end in range(start + BLOCK, stop + 1, BLOCK)]
    return functools.reduce(lambda a, b: a + b, ends, jnp.zeros((decay.shape[0], 1), F32))


def pack_message(message, states, logs):
    for head, state in enumerate(states):
        message[head * DH : (head + 1) * DH, :] = state.astype(BF16)
    large = logs.astype(BF16).astype(F32)
    parts = jnp.concatenate([large, logs - large], axis=0)
    message[len(states) * DH :, :] = jnp.broadcast_to(parts, (EXTRA, DH)).astype(BF16)


def message_log(message, heads):
    tail = message[heads * DH :, :].astype(F32)
    return (tail[: EXTRA // 2] + tail[EXTRA // 2 :])[:, :1]


def exchanges(ctx, hop):
    lower = range(ctx - hop)
    if hop == 1:
        return [], list(lower), []
    early = [at for at in lower if at < hop // 2]
    even = [at for at in lower if at >= hop // 2 and at // hop % 2 == 0]
    odd = [at for at in lower if at // hop % 2 == 1]
    return early, even, odd


def is_upper(lowers, hop):
    place = lax.axis_index("ctx")
    found = place < 0
    for lower in lowers:
        found = jnp.logical_or(found, place == lower + hop)
    return found


def arrived_state(arrivals, sets, hop, span):
    parts = [jnp.where(is_upper(lowers, hop), ref[span, :].astype(F32), 0.0) for ref, lowers in zip(arrivals, sets)]
    return functools.reduce(lambda a, b: a + b, parts)


def arrived_log(arrivals, sets, hop, heads):
    parts = [jnp.where(is_upper(lowers, hop), message_log(ref, heads), 0.0) for ref, lowers in zip(arrivals, sets)]
    return functools.reduce(lambda a, b: a + b, parts)


def key_value_kernel(
    heads, wq_far, wg_far, x, wk, wv, acc_k, acc_v, decay, coarse, fine,
    wq, wg, k_out, v_out, before_out, state_out, message, arrived,
):
    loads = Loads(arrived)
    others = [loads.start(wq_far, wq), loads.start(wg_far, wg)]
    blocks = acc_k.shape[0] // BLOCK
    state_out[...] = jnp.zeros_like(state_out)
    for block in range(blocks):
        start = block * BLOCK
        at = slice(start, start + BLOCK)
        columns = decay[:, at].T
        ending = columns[BLOCK - 1 : BLOCK, :]
        faded = jnp.exp(ending - columns)
        rows = x[at, :]
        cosine, sine = angles(coarse, fine, start, BLOCK)
        keys = turned(acc_k[at, :] + mm(rows, wk[...]), cosine, sine)
        k_out[at, :] = keys
        values = (acc_v[at, :] + mm(rows, wv[...])).astype(BF16)
        v_out[at, :] = values
        for head in range(heads):
            span = slice(head * DH, (head + 1) * DH)
            weighted = (keys[:, span].astype(F32) * faded[:, head : head + 1]).astype(BF16)
            old = state_out[span, :]
            before_out[block, span, :] = old.astype(BF16)
            state_out[span, :] = jnp.exp(ending[:, head : head + 1]) * old + mm_tn(weighted, values[:, span])
    states = [state_out[head * DH : (head + 1) * DH, :] for head in range(heads)]
    pack_message(message, states, block_ends(decay, 0, acc_k.shape[0]))
    for copy in others:
        copy.wait()


def combine_kernel(heads, hop, sets, first, last, state, sent, *refs):
    if not first:
        old_entering, refs = refs[0], refs[1:]
    arrivals, entering, message = refs[: len(sets)], refs[len(sets)], refs[len(sets) + 1]
    window_log, log = message_log(sent, heads), arrived_log(arrivals, sets, hop, heads)
    before_log = jnp.zeros_like(log) if first else old_entering[heads * DH :, :1]
    states = []
    for head in range(heads):
        span, row = slice(head * DH, (head + 1) * DH), slice(head, head + 1)
        arrived = arrived_state(arrivals, sets, hop, span)
        if first:
            entering[span, :] = arrived
        else:
            entering[span, :] = old_entering[span, :] + jnp.exp(before_log[row]) * arrived
        states.append(state[span, :] + jnp.exp(window_log[row]) * arrived)
        if last:
            message[span, :] = states[-1].astype(BF16)
        else:
            refs[len(sets) + 2][span, :] = states[-1]
    entering[heads * DH :, :] = jnp.broadcast_to(before_log + log, (8, DH))
    if not last:
        pack_message(message, states, window_log + log)


def query_gate_kernel(
    heads, block, x_own, x_other, wq, wq_far, wg, wg_far, decay, coarse, fine, k, v, q_out, g_out, intra_out
):
    start = block * BLOCK
    lines = decay[:, start : start + BLOCK]
    columns = lines.T

    at = slice(start, start + BLOCK)
    cosine, sine = angles(coarse, fine, start, BLOCK)
    own, far = x_own[at, :], x_other[at, :]
    queries = mm(own, wq[...]) + mm(far, wq_far[...])
    q_out[...] = turned(queries, cosine, sine)
    gates = mm(own, wg[...]) + mm(far, wg_far[...])
    gates = gates.astype(BF16).astype(F32)
    g_out[...] = gates / (1.0 + jnp.exp(-gates))
    for piece in range(BLOCK // TILE):
        low, last = piece * TILE, (piece + 1) * TILE
        place_t = lax.broadcasted_iota(jnp.int32, (TILE, last), 0) + low
        place_s = lax.broadcasted_iota(jnp.int32, (TILE, last), 1)
        causal = place_t >= place_s
        for head in range(heads):
            span = slice(head * DH, (head + 1) * DH)
            scores = mm_nt(q_out[low:last, span], k[start : start + last, span])
            differ = columns[low:last, head : head + 1] - lines[head : head + 1, :last]
            weights = jnp.where(causal, jnp.exp(jnp.where(causal, differ, 0.0)), 0.0)
            intra_out[low:last, span] = mm((scores * weights).astype(BF16), v[start : start + last, span])


def hidden_kernel(heads, hop, sets, starts, decay, before, entering, *refs):
    arrivals, refs, token = refs[: len(sets)], refs[len(sets) : -1], refs[-1]
    projected, outs = refs[: -len(starts)], refs[-len(starts) :]
    token[...] = jnp.zeros_like(token)
    core = lax.axis_index("fsdp")
    for head in range(heads):
        span = slice(head * DH, (head + 1) * DH)
        entering_log = entering[heads * DH + head : heads * DH + head + 1, :1]
        state = entering[span, :] + jnp.exp(entering_log) * arrived_state(arrivals, sets, hop, span)
        pieces = []
        for start in starts:
            block = start // BLOCK
            q, gate, intra = projected[3 * block : 3 * block + 3]
            at = slice(start % BLOCK, start % BLOCK + TILE)
            column = jnp.exp(decay[:, start : start + TILE].T[:, head : head + 1])
            scale_log = jnp.zeros((1, 1), F32)
            for earlier in range(block):
                end = (earlier + 1) * BLOCK
                scale_log = scale_log + decay[head : head + 1, end - 1 : end]
            prior = (jnp.exp(scale_log) * state + before[block, span, :].astype(F32)).astype(BF16)
            retained = intra[at, span] + column * mm(q[at, span], prior)
            center = retained - jnp.mean(retained, axis=1, keepdims=True)
            spread = jnp.mean(center * center, axis=1, keepdims=True)
            pieces.append((gate[at, span] * center * lax.rsqrt(spread + 1e-5)).astype(BF16))
        for role, out in enumerate(outs):
            out[:, span] = jnp.where(core == 0, pieces[role], pieces[1 - role])


def columns_kernel(first, second, *outs):
    cols = outs[0].shape[1]
    place, core = lax.axis_index("tp"), lax.axis_index("fsdp")
    high, low = place // 2, place % 2

    @pl.when(core == 0)
    def _():
        at = pl.ds(pl.multiple_of((1 - low) * cols, cols), cols)
        outs[0][...] = first[:, at]
        outs[1][...] = second[:, at]

    @pl.when(core == 1)
    def _():
        for number, out in enumerate(outs):
            at = slice(number * cols, (number + 1) * cols)
            out[...] = jnp.where(high == 0, first[:, at], second[:, at])


def arrange_kernel(mine_0, mine_1, other_0, other_1, *outs):
    cols = mine_0.shape[1]
    place, core = lax.axis_index("tp"), lax.axis_index("fsdp")
    for role, (blocks, out) in enumerate(zip(((mine_0, mine_1), (other_0, other_1)), outs)):
        bit = jnp.where(core == role, place // 2, place % 2)
        out[:, :cols] = jnp.where(bit == 0, blocks[1][...], blocks[0][...])
        out[:, cols:] = jnp.where(bit == 0, blocks[0][...], blocks[1][...])


def own_kernel(order, own_first, own_second, *refs):
    pieces, outs = refs[: len(order)], refs[len(order) :]
    cols = pieces[0].shape[1]
    place, core = lax.axis_index("tp"), lax.axis_index("fsdp")
    high, low = place // 2, place % 2
    here = core == high
    mine = pl.ds(pl.multiple_of(low * cols, cols), cols)
    flipped = pl.ds(pl.multiple_of((1 - low) * cols, cols), cols)
    keep = jnp.where(here, own_first[:, mine], own_second[:, mine])
    low_give = jnp.where(here, own_second[:, mine], own_first[:, mine])
    high_give = jnp.where(here, own_first[:, flipped], own_second[:, flipped])
    gives = [jnp.where(core == role, low_give, high_give) for role in range(2)]
    for (role, number), piece in zip(order, pieces):
        at = slice(number * TILE, (number + 1) * TILE)
        outs[role][at, :cols] = mm(piece[...], gives[role])
        outs[role][at, cols:] = mm(piece[...], keep)


def give_kernel(number, own, far, weight, out):
    cols = out.shape[1]
    at = slice(number * TILE, (number + 1) * TILE)
    out[...] = (own[at, :cols] + mm(far[...], weight[:, :cols])).astype(BF16)


def keep_kernel(order, *refs):
    count = len(order)
    fars, owns, weights, outs = refs[:count], refs[count : count + 2], refs[count + 2 : count + 4], refs[count + 4 :]
    for (role, number), far in zip(order, fars):
        cols = far.shape[1]
        at = slice(number * TILE, (number + 1) * TILE)
        outs[role][at, :] = owns[role][at, cols:] + mm(far[...], weights[role][:, cols:])


def finish_kernel(order, *refs):
    count = len(order)
    gots, keeps, out, ready, written = refs[:count], refs[count : count + 2], refs[-3], refs[-2], refs[-1]
    core, copies = lax.axis_index("fsdp"), []
    for slot, ((role, number), got) in enumerate(zip(order, gots)):
        keep = keeps[role]
        at = slice(number * TILE, (number + 1) * TILE)
        ready[slot] = (keep[at, :] + got[...].astype(F32)).astype(BF16)
        start = pl.multiple_of((role + core) % 2 * keep.shape[0] + number * TILE, TILE)
        copies.append(pltpu.make_async_copy(ready.at[slot], out.at[0, pl.ds(start, TILE)], written.at[slot]))
        copies[-1].start()
    for copy in copies:
        copy.wait()


def after(value, *others):
    return lax.optimization_barrier((value, *others))[0]


def on_device(tokens, query_weight, key_weight, value_weight, gate_weight, out_weight, log_decay):
    x = tokens[0]
    rows, width = x.shape
    part, cols = query_weight.shape
    heads = cols // DH
    blocks = rows // BLOCK
    ctx, tp, cores = lax.axis_size("ctx"), lax.axis_size("tp"), lax.axis_size("fsdp")
    assert tp == 4 and cores == 2 and ctx >= 4 and ctx & (ctx - 1) == 0
    partners = [
        [(at * cores + core, (at ^ (1 << (role + core) % 2)) * cores + core) for at in range(tp) for core in range(cores)]
        for role in range(2)
    ]

    def trade(value, role):
        return lax.ppermute(value, ("tp", "fsdp"), partners[role])

    tables = [((2, rows // FINE, DH // 2), F32), ((2, FINE, DH // 2), F32)]

    key_far = swap(key_weight, "fsdp", 1)
    value_far = swap(value_weight, "fsdp", 1)

    x_own, x_other, acc_k, acc_v, decay, coarse, fine, out_first = loading_call(
        key_value_own_kernel,
        [((rows, part), BF16)] * 2 + [((rows, cols), F32)] * 2 + [((8, rows), F32)]
        + tables
        + [(out_weight.shape, BF16)],
        [x, key_weight, value_weight, log_decay[0].T, out_weight],
        [],
        [pltpu.VMEM((part, cols), BF16)] * 2 + [pltpu.VMEM((heads, rows), F32)],
        2 * (rows // BLOCK) + 4,
        "key_value_own",
    )
    state_shape, message_shape = (heads * DH, DH), (heads * DH + EXTRA, DH)
    own_q, own_g, keys, values, before, window, message = loading_call(
        functools.partial(key_value_kernel, heads),
        [((part, cols), BF16)] * 2
        + [((rows, cols), BF16)] * 2
        + [((blocks, heads * DH, DH), BF16), (state_shape, F32), (message_shape, BF16)],
        [query_weight, gate_weight],
        [x_other, key_far, value_far, acc_k, acc_v, decay, coarse, fine],
        [],
        2,
        "key_value",
    )
    far_q, far_g = swap(own_q, "fsdp", 1), swap(own_g, "fsdp", 1)

    def query_gate(block, decay):
        return kernel_call(
            functools.partial(query_gate_kernel, heads, block),
            [((BLOCK, cols), BF16), ((BLOCK, cols), F32), ((BLOCK, cols), F32)],
            [x_own, x_other, own_q, far_q, own_g, far_g, decay, coarse, fine, keys, values],
            "query_gate",
        )

    def exchange(message, lowers, hop):
        pairs = [(at, at + hop) for at in lowers]
        if hop > 1:
            pairs += [(upper, at) for at, upper in pairs]
        return lax.ppermute(message, "ctx", pairs)

    projected = list(query_gate(0, decay))
    window = after(window, projected[0])
    entering, hop, early, first_message = None, 1, [], message
    while True:
        first_set, *later_sets = exchanges(ctx, hop)
        later_sets = [lowers for lowers in later_sets if lowers]
        sets = later_sets + ([first_set] if first_set else [])
        arrivals = [exchange(message, lowers, hop) for lowers in later_sets] + early
        if 2 * hop >= ctx:
            break
        unchanged = exchanges(ctx, 2 * hop)[0]
        early = [exchange(message, unchanged, 2 * hop)]
        old = [] if entering is None else [entering]
        last = 4 * hop >= ctx
        entering, message, *windows = kernel_call(
            functools.partial(combine_kernel, heads, hop, sets, entering is None, last),
            [((heads * DH + 8, DH), F32)]
            + ([(state_shape, BF16)] if last else [(message_shape, BF16), (state_shape, F32)]),
            [window, message, *old, *arrivals],
            "combine",
        )
        window = windows[0] if windows else None
        hop *= 2

    own_second = swap(out_first, "fsdp", 1)
    for_partner = kernel_call(
        columns_kernel,
        [((cols, cols), BF16)] * 2,
        [after(out_first, first_message), own_second],
        "columns",
    )
    out_mine = [trade(block, 0) for block in for_partner]

    held = after(decay, message, *early, out_mine[0])
    for block in range(1, blocks):
        projected += query_gate(block, held)

    count = rows // 2 // TILE
    hidden, far = [[], []], [[], []]
    for number in range(count):
        held = after(decay, swap(pair[2], "fsdp", 1)) if number else decay
        pair = kernel_call(
            functools.partial(hidden_kernel, heads, hop, sets, [(half * count + number) * TILE for half in range(2)]),
            [((TILE, cols), BF16)] * 2 + [((16, 128), BF16)],
            [held, before, entering, *arrivals, *projected],
            "hidden",
        )
        if number == 0:
            out_other = [swap(after(block, pair[0]), "fsdp", 1) for block in out_mine]
        for role in range(2):
            hidden[role].append(pair[role])
            far[role].append(trade(pair[role], role))
    weights = kernel_call(
        arrange_kernel,
        [((cols, 2 * cols), BF16)] * 2,
        [*out_mine, *out_other],
        "arrange",
    )
    order = [(role, number) for number in reversed(range(count)) for role in (1, 0)]
    owns = kernel_call(
        functools.partial(own_kernel, order),
        [((count * TILE, 2 * cols), F32)] * 2,
        [out_first, own_second, *(hidden[role][number] for role, number in order)],
        "own_products",
    )
    gots = []
    for role, number in order:
        [give] = kernel_call(
            functools.partial(give_kernel, number),
            [((TILE, cols), BF16)],
            [owns[role], far[role][number], weights[role]],
            "give",
        )
        gots.append(trade(give, 1 - role))
    keeps = kernel_call(
        functools.partial(keep_kernel, order),
        [((count * TILE, cols), F32)] * 2,
        [*(far[role][number] for role, number in order), *owns, *weights],
        "keep",
    )
    result = None
    for part_order, part_gots in ((order[2:], gots[2:]), (order[:2], gots[:2])):
        arrays = [pltpu.with_memory_space_constraint(array, pltpu.VMEM) for array in (*part_gots, *keeps)]
        held = [] if result is None else [result]
        result = pl.pallas_call(
            functools.partial(finish_kernel, part_order),
            in_specs=[pl.BlockSpec(memory_space=pltpu.VMEM)] * len(arrays)
            + [pl.BlockSpec(memory_space=pltpu.HBM)] * len(held),
            out_specs=pl.BlockSpec(memory_space=pltpu.HBM),
            out_shape=jax.ShapeDtypeStruct((1, rows, cols), BF16),
            input_output_aliases={len(arrays): 0} if held else {},
            scratch_shapes=[
                pltpu.VMEM((len(part_order), TILE, cols), BF16),
                pltpu.SemaphoreType.DMA((len(part_order),)),
            ],
            compiler_params=pltpu.CompilerParams(vmem_limit_bytes=VMEM_LIMIT),
            name="finish",
        )(*arrays, *held)
    return result


def solution(mesh):
    in_specs = (
        P("fsdp", "ctx", None),
        P("fsdp", "tp"),
        P("fsdp", "tp"),
        P("fsdp", "tp"),
        P("fsdp", "tp"),
        P("tp", "fsdp"),
        P("fsdp", "ctx", "tp"),
    )
    out_specs = P("fsdp", "ctx", "tp")
    return jax.shard_map(
        on_device, mesh=mesh, in_specs=in_specs, out_specs=out_specs, check_vma=False
    )
```

```python
import functools
import math

import jax
import jax.numpy as jnp
from jax import lax
from jax.experimental import pallas as pl
from jax.experimental.pallas import tpu as pltpu
from jax.sharding import PartitionSpec as P

DH = 256
BLOCK = 512
TILE = 256
FINE = 32
EXTRA = 16
VMEM_LIMIT = 14 * 1024 * 1024
F32 = jnp.float32
BF16 = jnp.bfloat16


def mm(left, right):
    return jnp.dot(left, right, preferred_element_type=F32)


def mm_nt(left, right):
    return lax.dot_general(left, right, (((1,), (1,)), ((), ())), preferred_element_type=F32)


def mm_tn(left, right):
    return lax.dot_general(left, right, (((0,), (0,)), ((), ())), preferred_element_type=F32)


def swap(value, axis, mask):
    size = lax.axis_size(axis)
    return lax.ppermute(value, axis, [(place, place ^ mask) for place in range(size)])


def kernel_call(kernel, outs, operands, name):
    arrays = [pltpu.with_memory_space_constraint(array, pltpu.VMEM) for array in operands]
    return pl.pallas_call(
        kernel,
        in_specs=[pl.BlockSpec(memory_space=pltpu.VMEM)] * len(operands),
        out_specs=[pl.BlockSpec(memory_space=pltpu.VMEM)] * len(outs),
        out_shape=[pltpu.VMEM(shape, dtype) for shape, dtype in outs],
        compiler_params=pltpu.CompilerParams(vmem_limit_bytes=VMEM_LIMIT),
        cost_estimate=pl.CostEstimate(
            flops=1, bytes_accessed=1, transcendentals=0
        ),
        name=name,
    )(*arrays)


def loading_call(kernel, outs, loaded, operands, scratch, loads, name):
    arrays = [pltpu.with_memory_space_constraint(array, pltpu.HBM) for array in loaded]
    arrays += [pltpu.with_memory_space_constraint(array, pltpu.VMEM) for array in operands]
    return pl.pallas_call(
        kernel,
        in_specs=[pl.BlockSpec(memory_space=pltpu.HBM)] * len(loaded)
        + [pl.BlockSpec(memory_space=pltpu.VMEM)] * len(operands),
        out_specs=[pl.BlockSpec(memory_space=pltpu.VMEM)] * len(outs),
        out_shape=[pltpu.VMEM(shape, dtype) for shape, dtype in outs],
        scratch_shapes=[*scratch, pltpu.SemaphoreType.DMA((loads,))],
        compiler_params=pltpu.CompilerParams(vmem_limit_bytes=VMEM_LIMIT),
        cost_estimate=pl.CostEstimate(flops=1, bytes_accessed=1, transcendentals=0),
        name=name,
    )(*arrays)


def turned(values, cosine, sine):
    half = DH // 2
    parts = []
    for start in range(0, values.shape[1], DH):
        low = values[:, start : start + half]
        high = values[:, start + half : start + DH]
        parts.append((low * cosine - high * sine).astype(BF16))
        parts.append((high * cosine + low * sine).astype(BF16))
    return jnp.concatenate(parts, axis=1)


def angles(coarse, fine, first, count):
    at = first // FINE
    far = coarse[:, pl.ds(at, count // FINE), :]
    near = fine[...]
    cos_c, sin_c = far[0][:, None, :], far[1][:, None, :]
    cos_f, sin_f = near[0][None], near[1][None]
    cosine = cos_c * cos_f - sin_c * sin_f
    sine = sin_c * cos_f + cos_c * sin_f
    return cosine.reshape(count, DH // 2), sine.reshape(count, DH // 2)


def decay_sums(log_decay, decay):
    heads, rows = log_decay.shape
    place_s = lax.broadcasted_iota(jnp.int32, (BLOCK, BLOCK), 0)
    place_t = lax.broadcasted_iota(jnp.int32, (BLOCK, BLOCK), 1)
    upper = jnp.where(place_s <= place_t, 1.0, 0.0).astype(BF16)
    value = jnp.concatenate([log_decay[...], jnp.zeros((8 - heads, rows), F32)], axis=0)
    parts = []
    for _ in range(3):
        parts.append(value.astype(BF16))
        value = value - parts[-1].astype(F32)
    stacked = jnp.concatenate([part.astype(F32) for part in parts], axis=0).astype(BF16)
    for start in range(0, rows, BLOCK):
        sums = mm(stacked[:, start : start + BLOCK], upper)
        decay[:, start : start + BLOCK] = sums[:8] + sums[8:16] + sums[16:]


def turn(first, second):
    (cos_a, sin_a), (cos_b, sin_b) = first, second
    return cos_a * cos_b - sin_a * sin_b, sin_a * cos_b + cos_a * sin_b


def joined(first, second):
    return tuple(jnp.concatenate(pair, axis=0) for pair in zip(first, second))


def angle_tables(coarse, fine):
    half, seeds = DH // 2, 8
    index = lax.broadcasted_iota(jnp.int32, (seeds, half), 1).astype(F32)
    frequency = jnp.exp(index * (-math.log(10000.0) / half))
    place = lax.broadcasted_iota(jnp.int32, (seeds, half), 0).astype(F32)
    offset = (lax.axis_index("ctx") * (coarse.shape[1] * FINE)).astype(F32)
    near = jnp.cos(place * frequency), jnp.sin(place * frequency)
    base = jnp.cos(offset * frequency), jnp.sin(offset * frequency)
    step = turn([part[seeds - 1 : seeds] for part in near], [part[1:2] for part in near])
    while near[0].shape[0] < FINE:
        near = joined(near, turn(near, step))
        step = turn(step, step)
    far = tuple(part[:1] for part in base)
    while far[0].shape[0] < coarse.shape[1]:
        far = joined(far, turn(far, step))
        step = turn(step, step)
    for table, parts in ((coarse, far), (fine, near)):
        table[0], table[1] = (part[: table.shape[1]] for part in parts)


class Loads:
    def __init__(self, arrived):
        self.arrived, self.count = arrived, 0

    def start(self, source, target):
        copy = pltpu.make_async_copy(source, target, self.arrived.at[self.count])
        self.count += 1
        copy.start()
        return copy


def key_value_own_kernel(
    x_far, wk_far, wv_far, log_decay_far, wo_far,
    x_own, x_other, acc_k, acc_v, decay, coarse, fine, wo, wk, wv, log_decay, arrived,
):
    rows, part = x_own.shape
    core = lax.axis_index("fsdp")
    loads = Loads(arrived)

    def tile(x, half, start):
        at = pl.ds(start, BLOCK)
        columns = pl.ds(pl.multiple_of(half * part, part), part)
        return loads.start(x_far.at[at, columns], x.at[at])

    starts = range(0, rows, BLOCK)
    key, logs = loads.start(wk_far, wk), loads.start(log_decay_far, log_decay)
    tiles = [tile(x_own, core, start) for start in starts]
    value = loads.start(wv_far, wv)
    others = [tile(x_other, 1 - core, start) for start in starts] + [loads.start(wo_far, wo)]
    angle_tables(coarse, fine)
    logs.wait()
    decay_sums(log_decay, decay)
    key.wait()
    for copy, start in zip(tiles, starts):
        at = slice(start, start + BLOCK)
        copy.wait()
        acc_k[at, :] = mm(x_own[at, :], wk[...])
    value.wait()
    for start in starts:
        at = slice(start, start + BLOCK)
        acc_v[at, :] = mm(x_own[at, :], wv[...])
    for copy in others:
        copy.wait()


def block_ends(decay, start, stop):
    ends = [decay[:, end - 1 : end] for end in range(start + BLOCK, stop + 1, BLOCK)]
    return functools.reduce(lambda a, b: a + b, ends, jnp.zeros((decay.shape[0], 1), F32))


def pack_message(message, states, logs):
    for head, state in enumerate(states):
        message[head * DH : (head + 1) * DH, :] = state.astype(BF16)
    large = logs.astype(BF16).astype(F32)
    parts = jnp.concatenate([large, logs - large], axis=0)
    message[len(states) * DH :, :] = jnp.broadcast_to(parts, (EXTRA, DH)).astype(BF16)


def message_log(message, heads):
    tail = message[heads * DH :, :].astype(F32)
    return (tail[: EXTRA // 2] + tail[EXTRA // 2 :])[:, :1]


def exchanges(ctx, hop):
    lower = range(ctx - hop)
    if hop == 1:
        return [], list(lower), []
    early = [at for at in lower if at < hop // 2]
    even = [at for at in lower if at >= hop // 2 and at // hop % 2 == 0]
    odd = [at for at in lower if at // hop % 2 == 1]
    return early, even, odd


def is_upper(lowers, hop):
    place = lax.axis_index("ctx")
    found = place < 0
    for lower in lowers:
        found = jnp.logical_or(found, place == lower + hop)
    return found


def arrived_state(arrivals, sets, hop, span):
    parts = [jnp.where(is_upper(lowers, hop), ref[span, :].astype(F32), 0.0) for ref, lowers in zip(arrivals, sets)]
    return functools.reduce(lambda a, b: a + b, parts)


def arrived_log(arrivals, sets, hop, heads):
    parts = [jnp.where(is_upper(lowers, hop), message_log(ref, heads), 0.0) for ref, lowers in zip(arrivals, sets)]
    return functools.reduce(lambda a, b: a + b, parts)


def key_value_kernel(
    heads, wq_far, wg_far, x, wk, wv, acc_k, acc_v, decay, coarse, fine,
    wq, wg, k_out, v_out, before_out, state_out, message, arrived,
):
    loads = Loads(arrived)
    others = [loads.start(wq_far, wq), loads.start(wg_far, wg)]
    blocks = acc_k.shape[0] // BLOCK
    state_out[...] = jnp.zeros_like(state_out)
    for block in range(blocks):
        start = block * BLOCK
        at = slice(start, start + BLOCK)
        columns = decay[:, at].T
        ending = columns[BLOCK - 1 : BLOCK, :]
        faded = jnp.exp(ending - columns)
        rows = x[at, :]
        cosine, sine = angles(coarse, fine, start, BLOCK)
        keys = turned(acc_k[at, :] + mm(rows, wk[...]), cosine, sine)
        k_out[at, :] = keys
        values = (acc_v[at, :] + mm(rows, wv[...])).astype(BF16)
        v_out[at, :] = values
        for head in range(heads):
            span = slice(head * DH, (head + 1) * DH)
            weighted = (keys[:, span].astype(F32) * faded[:, head : head + 1]).astype(BF16)
            old = state_out[span, :]
            before_out[block, span, :] = old.astype(BF16)
            state_out[span, :] = jnp.exp(ending[:, head : head + 1]) * old + mm_tn(weighted, values[:, span])
    states = [state_out[head * DH : (head + 1) * DH, :] for head in range(heads)]
    pack_message(message, states, block_ends(decay, 0, acc_k.shape[0]))
    for copy in others:
        copy.wait()


def combine_kernel(heads, hop, sets, first, last, state, sent, *refs):
    if not first:
        old_entering, refs = refs[0], refs[1:]
    arrivals, entering, message = refs[: len(sets)], refs[len(sets)], refs[len(sets) + 1]
    window_log, log = message_log(sent, heads), arrived_log(arrivals, sets, hop, heads)
    before_log = jnp.zeros_like(log) if first else old_entering[heads * DH :, :1]
    states = []
    for head in range(heads):
        span, row = slice(head * DH, (head + 1) * DH), slice(head, head + 1)
        arrived = arrived_state(arrivals, sets, hop, span)
        if first:
            entering[span, :] = arrived
        else:
            entering[span, :] = old_entering[span, :] + jnp.exp(before_log[row]) * arrived
        states.append(state[span, :] + jnp.exp(window_log[row]) * arrived)
        if last:
            message[span, :] = states[-1].astype(BF16)
        else:
            refs[len(sets) + 2][span, :] = states[-1]
    entering[heads * DH :, :] = jnp.broadcast_to(before_log + log, (8, DH))
    if not last:
        pack_message(message, states, window_log + log)


def query_gate_kernel(
    heads, block, x_own, x_other, wq, wq_far, wg, wg_far, decay, coarse, fine, k, v, q_out, g_out, intra_out
):
    start = block * BLOCK
    lines = decay[:, start : start + BLOCK]
    columns = lines.T

    at = slice(start, start + BLOCK)
    cosine, sine = angles(coarse, fine, start, BLOCK)
    own, far = x_own[at, :], x_other[at, :]
    queries = mm(own, wq[...]) + mm(far, wq_far[...])
    q_out[...] = turned(queries, cosine, sine)
    gates = mm(own, wg[...]) + mm(far, wg_far[...])
    gates = gates.astype(BF16).astype(F32)
    g_out[...] = gates / (1.0 + jnp.exp(-gates))
    for piece in range(BLOCK // TILE):
        low, last = piece * TILE, (piece + 1) * TILE
        place_t = lax.broadcasted_iota(jnp.int32, (TILE, last), 0) + low
        place_s = lax.broadcasted_iota(jnp.int32, (TILE, last), 1)
        causal = place_t >= place_s
        for head in range(heads):
            span = slice(head * DH, (head + 1) * DH)
            scores = mm_nt(q_out[low:last, span], k[start : start + last, span])
            differ = columns[low:last, head : head + 1] - lines[head : head + 1, :last]
            weights = jnp.where(causal, jnp.exp(jnp.where(causal, differ, 0.0)), 0.0)
            intra_out[low:last, span] = mm((scores * weights).astype(BF16), v[start : start + last, span])


def hidden_kernel(heads, hop, sets, role, first, decay, before, entering, *refs):
    arrivals, projected, out, token = refs[: len(sets)], refs[len(sets) : -2], refs[-2], refs[-1]
    token[...] = jnp.zeros_like(token)

    def piece(start):
        block = start // BLOCK
        q, gate, intra = projected[3 * block : 3 * block + 3]
        at = slice(start % BLOCK, start % BLOCK + TILE)
        columns = jnp.exp(decay[:, start : start + TILE].T)
        scales = jnp.exp(block_ends(decay, 0, block * BLOCK))
        for head in range(heads):
            span, row = slice(head * DH, (head + 1) * DH), slice(head, head + 1)
            fade = jnp.exp(entering[heads * DH + head : heads * DH + head + 1, :1])
            state = entering[span, :] + fade * arrived_state(arrivals, sets, hop, span)
            prior = (scales[row] * state + before[block, span, :].astype(F32)).astype(BF16)
            retained = intra[at, span] + columns[:, row] * mm(q[at, span], prior)
            center = retained - jnp.mean(retained, axis=1, keepdims=True)
            spread = jnp.mean(center * center, axis=1, keepdims=True)
            out[:, span] = (gate[at, span] * center * lax.rsqrt(spread + 1e-5)).astype(BF16)

    core, middle = lax.axis_index("fsdp"), decay.shape[1] // 2
    pl.when(core == role)(lambda: piece(first))
    pl.when(core != role)(lambda: piece(middle + first))


def columns_kernel(first, second, *outs):
    cols = outs[0].shape[1]
    place, core = lax.axis_index("tp"), lax.axis_index("fsdp")
    high, low = place // 2, place % 2

    @pl.when(core == 0)
    def _():
        at = pl.ds(pl.multiple_of((1 - low) * cols, cols), cols)
        outs[0][...] = first[:, at]
        outs[1][...] = second[:, at]

    @pl.when(core == 1)
    def _():
        for number, out in enumerate(outs):
            at = slice(number * cols, (number + 1) * cols)
            out[...] = jnp.where(high == 0, first[:, at], second[:, at])


def arrange_kernel(mine_0, mine_1, other_0, other_1, *outs):
    cols = mine_0.shape[1]
    place, core = lax.axis_index("tp"), lax.axis_index("fsdp")
    for role, (blocks, out) in enumerate(zip(((mine_0, mine_1), (other_0, other_1)), outs)):
        bit = jnp.where(core == role, place // 2, place % 2)
        out[:, :cols] = jnp.where(bit == 0, blocks[1][...], blocks[0][...])
        out[:, cols:] = jnp.where(bit == 0, blocks[0][...], blocks[1][...])


def own_kernel(order, own_first, own_second, *refs):
    pieces, outs = refs[: len(order)], refs[len(order) :]
    cols = pieces[0].shape[1]
    place, core = lax.axis_index("tp"), lax.axis_index("fsdp")
    high, low = place // 2, place % 2
    here = core == high
    mine = pl.ds(pl.multiple_of(low * cols, cols), cols)
    flipped = pl.ds(pl.multiple_of((1 - low) * cols, cols), cols)
    keep = jnp.where(here, own_first[:, mine], own_second[:, mine])
    low_give = jnp.where(here, own_second[:, mine], own_first[:, mine])
    high_give = jnp.where(here, own_first[:, flipped], own_second[:, flipped])
    gives = [jnp.where(core == role, low_give, high_give) for role in range(2)]
    for (role, number), piece in zip(order, pieces):
        at = slice(number * TILE, (number + 1) * TILE)
        outs[role][at, :cols] = mm(piece[...], gives[role])
        outs[role][at, cols:] = mm(piece[...], keep)


def give_kernel(number, own, far, weight, out):
    cols = out.shape[1]
    at = slice(number * TILE, (number + 1) * TILE)
    out[...] = (own[at, :cols] + mm(far[...], weight[:, :cols])).astype(BF16)


def keep_kernel(order, *refs):
    count = len(order)
    fars, owns, weights, outs = refs[:count], refs[count : count + 2], refs[count + 2 : count + 4], refs[count + 4 :]
    for (role, number), far in zip(order, fars):
        cols = far.shape[1]
        at = slice(number * TILE, (number + 1) * TILE)
        outs[role][at, :] = owns[role][at, cols:] + mm(far[...], weights[role][:, cols:])


def finish_kernel(order, *refs):
    count = len(order)
    gots, keeps, out, ready, written = refs[:count], refs[count : count + 2], refs[-3], refs[-2], refs[-1]
    core, copies = lax.axis_index("fsdp"), []
    for slot, ((role, number), got) in enumerate(zip(order, gots)):
        keep = keeps[role]
        at = slice(number * TILE, (number + 1) * TILE)
        ready[slot] = (keep[at, :] + got[...].astype(F32)).astype(BF16)
        start = pl.multiple_of((role + core) % 2 * keep.shape[0] + number * TILE, TILE)
        copies.append(pltpu.make_async_copy(ready.at[slot], out.at[0, pl.ds(start, TILE)], written.at[slot]))
        copies[-1].start()
    for copy in copies:
        copy.wait()


def after(value, *others):
    return lax.optimization_barrier((value, *others))[0]


def on_device(tokens, query_weight, key_weight, value_weight, gate_weight, out_weight, log_decay):
    x = tokens[0]
    rows, width = x.shape
    part, cols = query_weight.shape
    heads = cols // DH
    blocks = rows // BLOCK
    ctx, tp, cores = lax.axis_size("ctx"), lax.axis_size("tp"), lax.axis_size("fsdp")
    assert tp == 4 and cores == 2 and ctx >= 4 and ctx & (ctx - 1) == 0
    partners = [
        [(at * cores + core, (at ^ (1 << (role + core) % 2)) * cores + core) for at in range(tp) for core in range(cores)]
        for role in range(2)
    ]

    def trade(value, role):
        return lax.ppermute(value, ("tp", "fsdp"), partners[role])

    tables = [((2, rows // FINE, DH // 2), F32), ((2, FINE, DH // 2), F32)]

    key_far = swap(key_weight, "fsdp", 1)
    value_far = swap(value_weight, "fsdp", 1)

    x_own, x_other, acc_k, acc_v, decay, coarse, fine, out_first = loading_call(
        key_value_own_kernel,
        [((rows, part), BF16)] * 2 + [((rows, cols), F32)] * 2 + [((8, rows), F32)]
        + tables
        + [(out_weight.shape, BF16)],
        [x, key_weight, value_weight, log_decay[0].T, out_weight],
        [],
        [pltpu.VMEM((part, cols), BF16)] * 2 + [pltpu.VMEM((heads, rows), F32)],
        2 * (rows // BLOCK) + 4,
        "key_value_own",
    )
    state_shape, message_shape = (heads * DH, DH), (heads * DH + EXTRA, DH)
    own_q, own_g, keys, values, before, window, message = loading_call(
        functools.partial(key_value_kernel, heads),
        [((part, cols), BF16)] * 2
        + [((rows, cols), BF16)] * 2
        + [((blocks, heads * DH, DH), BF16), (state_shape, F32), (message_shape, BF16)],
        [query_weight, gate_weight],
        [x_other, key_far, value_far, acc_k, acc_v, decay, coarse, fine],
        [],
        2,
        "key_value",
    )
    far_q, far_g = swap(own_q, "fsdp", 1), swap(own_g, "fsdp", 1)

    def query_gate(block, decay):
        return kernel_call(
            functools.partial(query_gate_kernel, heads, block),
            [((BLOCK, cols), BF16), ((BLOCK, cols), F32), ((BLOCK, cols), F32)],
            [x_own, x_other, own_q, far_q, own_g, far_g, decay, coarse, fine, keys, values],
            "query_gate",
        )

    def exchange(message, lowers, hop):
        pairs = [(at, at + hop) for at in lowers]
        if hop > 1:
            pairs += [(upper, at) for at, upper in pairs]
        return lax.ppermute(message, "ctx", pairs)

    projected = list(query_gate(0, decay))
    window = after(window, projected[0])
    entering, hop, early, first_message = None, 1, [], message
    while True:
        first_set, *later_sets = exchanges(ctx, hop)
        later_sets = [lowers for lowers in later_sets if lowers]
        sets = later_sets + ([first_set] if first_set else [])
        arrivals = [exchange(message, lowers, hop) for lowers in later_sets] + early
        if 2 * hop >= ctx:
            break
        unchanged = exchanges(ctx, 2 * hop)[0]
        early = [exchange(message, unchanged, 2 * hop)]
        old = [] if entering is None else [entering]
        last = 4 * hop >= ctx
        entering, message, *windows = kernel_call(
            functools.partial(combine_kernel, heads, hop, sets, entering is None, last),
            [((heads * DH + 8, DH), F32)]
            + ([(state_shape, BF16)] if last else [(message_shape, BF16), (state_shape, F32)]),
            [window, message, *old, *arrivals],
            "combine",
        )
        window = windows[0] if windows else None
        hop *= 2

    own_second = swap(out_first, "fsdp", 1)
    for_partner = kernel_call(
        columns_kernel,
        [((cols, cols), BF16)] * 2,
        [after(out_first, first_message), own_second],
        "columns",
    )
    out_mine = [trade(block, 0) for block in for_partner]

    held = after(decay, message, *early, out_mine[0])
    for block in range(1, blocks):
        projected += query_gate(block, held)

    count = rows // 2 // TILE
    hidden, far = [[], []], [[], []]
    token = None
    for number, role in [(number, role) for number in range(count) for role in range(2)]:
        held = decay if token is None else after(decay, swap(token, "fsdp", 1))
        piece, token = kernel_call(
            functools.partial(hidden_kernel, heads, hop, sets, role, number * TILE),
            [((TILE, cols), BF16), ((16, 128), BF16)],
            [held, before, entering, *arrivals, *projected],
            "hidden",
        )
        if number == 0 and role == 0:
            out_other = [swap(after(block, piece), "fsdp", 1) for block in out_mine]
        hidden[role].append(piece)
        far[role].append(trade(piece, role))
    weights = kernel_call(
        arrange_kernel,
        [((cols, 2 * cols), BF16)] * 2,
        [*out_mine, *out_other],
        "arrange",
    )
    order = [(role, number) for number in reversed(range(count)) for role in (1, 0)]
    owns = kernel_call(
        functools.partial(own_kernel, order),
        [((count * TILE, 2 * cols), F32)] * 2,
        [out_first, own_second, *(hidden[role][number] for role, number in order)],
        "own_products",
    )
    gots = []
    for role, number in order:
        [give] = kernel_call(
            functools.partial(give_kernel, number),
            [((TILE, cols), BF16)],
            [owns[role], far[role][number], weights[role]],
            "give",
        )
        gots.append(trade(give, 1 - role))
    keeps = kernel_call(
        functools.partial(keep_kernel, order),
        [((count * TILE, cols), F32)] * 2,
        [*(far[role][number] for role, number in order), *owns, *weights],
        "keep",
    )
    result = None
    for part_order, part_gots in ((order[2:], gots[2:]), (order[:2], gots[:2])):
        arrays = [pltpu.with_memory_space_constraint(array, pltpu.VMEM) for array in (*part_gots, *keeps)]
        held = [] if result is None else [result]
        result = pl.pallas_call(
            functools.partial(finish_kernel, part_order),
            in_specs=[pl.BlockSpec(memory_space=pltpu.VMEM)] * len(arrays)
            + [pl.BlockSpec(memory_space=pltpu.HBM)] * len(held),
            out_specs=pl.BlockSpec(memory_space=pltpu.HBM),
            out_shape=jax.ShapeDtypeStruct((1, rows, cols), BF16),
            input_output_aliases={len(arrays): 0} if held else {},
            scratch_shapes=[
                pltpu.VMEM((len(part_order), TILE, cols), BF16),
                pltpu.SemaphoreType.DMA((len(part_order),)),
            ],
            compiler_params=pltpu.CompilerParams(vmem_limit_bytes=VMEM_LIMIT),
            name="finish",
        )(*arrays, *held)
    return result


def solution(mesh):
    in_specs = (
        P("fsdp", "ctx", None),
        P("fsdp", "tp"),
        P("fsdp", "tp"),
        P("fsdp", "tp"),
        P("fsdp", "tp"),
        P("tp", "fsdp"),
        P("fsdp", "ctx", "tp"),
    )
    out_specs = P("fsdp", "ctx", "tp")
    return jax.shard_map(
        on_device, mesh=mesh, in_specs=in_specs, out_specs=out_specs, check_vma=False
    )
```

```python
import functools
import math

import jax
import jax.numpy as jnp
from jax import lax
from jax.experimental import pallas as pl
from jax.experimental.pallas import tpu as pltpu
from jax.sharding import PartitionSpec as P

DH = 256
BLOCK = 512
TILE = 256
FINE = 32
EXTRA = 16
VMEM_LIMIT = 14 * 1024 * 1024
F32 = jnp.float32
BF16 = jnp.bfloat16


def mm(left, right):
    return jnp.dot(left, right, preferred_element_type=F32)


def mm_nt(left, right):
    return lax.dot_general(left, right, (((1,), (1,)), ((), ())), preferred_element_type=F32)


def mm_tn(left, right):
    return lax.dot_general(left, right, (((0,), (0,)), ((), ())), preferred_element_type=F32)


def swap(value, axis, mask):
    size = lax.axis_size(axis)
    return lax.ppermute(value, axis, [(place, place ^ mask) for place in range(size)])


def kernel_call(kernel, outs, operands, name, scratch=()):
    arrays = [pltpu.with_memory_space_constraint(array, pltpu.VMEM) for array in operands]
    return pl.pallas_call(
        kernel,
        in_specs=[pl.BlockSpec(memory_space=pltpu.VMEM)] * len(operands),
        out_specs=[pl.BlockSpec(memory_space=pltpu.VMEM)] * len(outs),
        out_shape=[pltpu.VMEM(shape, dtype) for shape, dtype in outs],
        scratch_shapes=list(scratch),
        compiler_params=pltpu.CompilerParams(vmem_limit_bytes=VMEM_LIMIT),
        cost_estimate=pl.CostEstimate(flops=1, bytes_accessed=1, transcendentals=0),
        name=name,
    )(*arrays)


def loading_call(kernel, outs, loaded, operands, scratch, loads, name):
    arrays = [pltpu.with_memory_space_constraint(array, pltpu.HBM) for array in loaded]
    arrays += [pltpu.with_memory_space_constraint(array, pltpu.VMEM) for array in operands]
    return pl.pallas_call(
        kernel,
        in_specs=[pl.BlockSpec(memory_space=pltpu.HBM)] * len(loaded)
        + [pl.BlockSpec(memory_space=pltpu.VMEM)] * len(operands),
        out_specs=[pl.BlockSpec(memory_space=pltpu.VMEM)] * len(outs),
        out_shape=[pltpu.VMEM(shape, dtype) for shape, dtype in outs],
        scratch_shapes=[*scratch, pltpu.SemaphoreType.DMA((loads,))],
        compiler_params=pltpu.CompilerParams(vmem_limit_bytes=VMEM_LIMIT),
        cost_estimate=pl.CostEstimate(flops=1, bytes_accessed=1, transcendentals=0),
        name=name,
    )(*arrays)


def turned(values, cosine, sine):
    half = DH // 2
    parts = []
    for start in range(0, values.shape[1], DH):
        low = values[:, start : start + half]
        high = values[:, start + half : start + DH]
        parts.append((low * cosine - high * sine).astype(BF16))
        parts.append((high * cosine + low * sine).astype(BF16))
    return jnp.concatenate(parts, axis=1)


def angles(coarse, fine, first, count):
    at = first // FINE
    far = coarse[:, pl.ds(at, count // FINE), :]
    near = fine[...]
    cos_c, sin_c = far[0][:, None, :], far[1][:, None, :]
    cos_f, sin_f = near[0][None], near[1][None]
    cosine = cos_c * cos_f - sin_c * sin_f
    sine = sin_c * cos_f + cos_c * sin_f
    return cosine.reshape(count, DH // 2), sine.reshape(count, DH // 2)


def decay_sums(log_decay, decay):
    heads, rows = log_decay.shape
    place_s = lax.broadcasted_iota(jnp.int32, (BLOCK, BLOCK), 0)
    place_t = lax.broadcasted_iota(jnp.int32, (BLOCK, BLOCK), 1)
    upper = jnp.where(place_s <= place_t, 1.0, 0.0).astype(BF16)
    value = jnp.concatenate([log_decay[...], jnp.zeros((8 - heads, rows), F32)], axis=0)
    parts = []
    for _ in range(3):
        parts.append(value.astype(BF16))
        value = value - parts[-1].astype(F32)
    stacked = jnp.concatenate([part.astype(F32) for part in parts], axis=0).astype(BF16)
    for start in range(0, rows, BLOCK):
        sums = mm(stacked[:, start : start + BLOCK], upper)
        decay[:, start : start + BLOCK] = sums[:8] + sums[8:16] + sums[16:]


def turn(first, second):
    (cos_a, sin_a), (cos_b, sin_b) = first, second
    return cos_a * cos_b - sin_a * sin_b, sin_a * cos_b + cos_a * sin_b


def joined(first, second):
    return tuple(jnp.concatenate(pair, axis=0) for pair in zip(first, second))


def angle_tables(coarse, fine):
    half, seeds = DH // 2, 8
    index = lax.broadcasted_iota(jnp.int32, (seeds, half), 1).astype(F32)
    frequency = jnp.exp(index * (-math.log(10000.0) / half))
    place = lax.broadcasted_iota(jnp.int32, (seeds, half), 0).astype(F32)
    offset = (lax.axis_index("ctx") * (coarse.shape[1] * FINE)).astype(F32)
    near = jnp.cos(place * frequency), jnp.sin(place * frequency)
    base = jnp.cos(offset * frequency), jnp.sin(offset * frequency)
    step = turn([part[seeds - 1 : seeds] for part in near], [part[1:2] for part in near])
    while near[0].shape[0] < FINE:
        near = joined(near, turn(near, step))
        step = turn(step, step)
    far = tuple(part[:1] for part in base)
    while far[0].shape[0] < coarse.shape[1]:
        far = joined(far, turn(far, step))
        step = turn(step, step)
    for table, parts in ((coarse, far), (fine, near)):
        table[0], table[1] = (part[: table.shape[1]] for part in parts)


class Loads:
    def __init__(self, arrived):
        self.arrived, self.count = arrived, 0

    def start(self, source, target):
        copy = pltpu.make_async_copy(source, target, self.arrived.at[self.count])
        self.count += 1
        copy.start()
        return copy


def key_value_own_kernel(
    x_far, wk_far, wv_far, log_decay_far, wo_far,
    x_own, x_other, acc_k, acc_v, decay, coarse, fine, wo, wk, wv, log_decay, arrived,
):
    rows, part = x_own.shape
    core = lax.axis_index("fsdp")
    loads = Loads(arrived)

    def tile(x, half, start):
        at = pl.ds(start, BLOCK)
        columns = pl.ds(pl.multiple_of(half * part, part), part)
        return loads.start(x_far.at[at, columns], x.at[at])

    starts = range(0, rows, BLOCK)
    key, logs = loads.start(wk_far, wk), loads.start(log_decay_far, log_decay)
    tiles = [tile(x_own, core, start) for start in starts]
    value = loads.start(wv_far, wv)
    others = [tile(x_other, 1 - core, start) for start in starts] + [loads.start(wo_far, wo)]
    angle_tables(coarse, fine)
    logs.wait()
    decay_sums(log_decay, decay)
    key.wait()
    for copy, start in zip(tiles, starts):
        at = slice(start, start + BLOCK)
        copy.wait()
        acc_k[at, :] = mm(x_own[at, :], wk[...])
    value.wait()
    acc_v[...] = mm(x_own[...], wv[...])
    for copy in others:
        copy.wait()


def block_ends(decay, start, stop):
    ends = [decay[:, end - 1 : end] for end in range(start + BLOCK, stop + 1, BLOCK)]
    return functools.reduce(lambda a, b: a + b, ends, jnp.zeros((decay.shape[0], 1), F32))


def pack_message(message, states, logs):
    for head, state in enumerate(states):
        message[head * DH : (head + 1) * DH, :] = state.astype(BF16)
    large = logs.astype(BF16).astype(F32)
    parts = jnp.concatenate([large, logs - large], axis=0)
    message[len(states) * DH :, :] = jnp.broadcast_to(parts, (EXTRA, DH)).astype(BF16)


def message_log(message, heads):
    tail = message[heads * DH :, :].astype(F32)
    return (tail[: EXTRA // 2] + tail[EXTRA // 2 :])[:, :1]


def exchanges(ctx, hop):
    lower = range(ctx - hop)
    if hop == 1:
        return [], list(lower), []
    early = [at for at in lower if at < hop // 2]
    even = [at for at in lower if at >= hop // 2 and at // hop % 2 == 0]
    odd = [at for at in lower if at // hop % 2 == 1]
    return early, even, odd


def is_upper(lowers, hop):
    place = lax.axis_index("ctx")
    found = place < 0
    for lower in lowers:
        found = jnp.logical_or(found, place == lower + hop)
    return found


def arrived_state(arrivals, sets, hop, span):
    parts = [jnp.where(is_upper(lowers, hop), ref[span, :].astype(F32), 0.0) for ref, lowers in zip(arrivals, sets)]
    return functools.reduce(lambda a, b: a + b, parts)


def arrived_log(arrivals, sets, hop, heads):
    parts = [jnp.where(is_upper(lowers, hop), message_log(ref, heads), 0.0) for ref, lowers in zip(arrivals, sets)]
    return functools.reduce(lambda a, b: a + b, parts)


def key_value_kernel(
    heads, wq_far, wg_far, x, wk, wv, acc_k, acc_v, decay, coarse, fine,
    wq, wg, k_out, v_out, before_out, state_out, message, arrived,
):
    loads = Loads(arrived)
    others = [loads.start(wq_far, wq), loads.start(wg_far, wg)]
    blocks = acc_k.shape[0] // BLOCK
    state_out[...] = jnp.zeros_like(state_out)
    for block in range(blocks):
        start = block * BLOCK
        at = slice(start, start + BLOCK)
        columns = decay[:, at].T
        ending = columns[BLOCK - 1 : BLOCK, :]
        faded = jnp.exp(ending - columns)
        rows = x[at, :]
        cosine, sine = angles(coarse, fine, start, BLOCK)
        keys = turned(acc_k[at, :] + mm(rows, wk[...]), cosine, sine)
        k_out[at, :] = keys
        values = (acc_v[at, :] + mm(rows, wv[...])).astype(BF16)
        v_out[at, :] = values
        for head in range(heads):
            span = slice(head * DH, (head + 1) * DH)
            weighted = (keys[:, span].astype(F32) * faded[:, head : head + 1]).astype(BF16)
            old = state_out[span, :]
            before_out[block, span, :] = old.astype(BF16)
            state_out[span, :] = jnp.exp(ending[:, head : head + 1]) * old + mm_tn(weighted, values[:, span])
    states = [state_out[head * DH : (head + 1) * DH, :] for head in range(heads)]
    pack_message(message, states, block_ends(decay, 0, acc_k.shape[0]))
    for copy in others:
        copy.wait()


def combine_kernel(heads, hop, sets, first, last, state, sent, *refs):
    if not first:
        old_entering, refs = refs[0], refs[1:]
    arrivals, entering, message = refs[: len(sets)], refs[len(sets)], refs[len(sets) + 1]
    window_log, log = message_log(sent, heads), arrived_log(arrivals, sets, hop, heads)
    before_log = jnp.zeros_like(log) if first else old_entering[heads * DH :, :1]
    states = []
    for head in range(heads):
        span, row = slice(head * DH, (head + 1) * DH), slice(head, head + 1)
        arrived = arrived_state(arrivals, sets, hop, span)
        if first:
            entering[span, :] = arrived
        else:
            entering[span, :] = old_entering[span, :] + jnp.exp(before_log[row]) * arrived
        states.append(state[span, :] + jnp.exp(window_log[row]) * arrived)
        if last:
            message[span, :] = states[-1].astype(BF16)
        else:
            refs[len(sets) + 2][span, :] = states[-1]
    entering[heads * DH :, :] = jnp.broadcast_to(before_log + log, (8, DH))
    if not last:
        pack_message(message, states, window_log + log)


def query_gate_kernel(
    heads, block, x_own, x_other, wq, wq_far, wg, wg_far, decay, coarse, fine, k, v, q_out, g_out, intra_out, q
):
    start = block * BLOCK
    lines = decay[:, start : start + BLOCK]
    columns = lines.T

    at = slice(start, start + BLOCK)
    cosine, sine = angles(coarse, fine, start, BLOCK)
    own, far = x_own[at, :], x_other[at, :]
    queries = mm(own, wq[...]) + mm(far, wq_far[...])
    q[...] = turned(queries, cosine, sine)
    faded = jnp.exp(columns)
    for head in range(heads):
        span = slice(head * DH, (head + 1) * DH)
        q_out[:, span] = (q[:, span].astype(F32) * faded[:, head : head + 1]).astype(BF16)
    gates = mm(own, wg[...]) + mm(far, wg_far[...])
    gates = gates.astype(BF16).astype(F32)
    g_out[...] = gates / (1.0 + jnp.exp(-gates))
    for piece in range(BLOCK // TILE):
        low, last = piece * TILE, (piece + 1) * TILE
        place_t = lax.broadcasted_iota(jnp.int32, (TILE, last), 0) + low
        place_s = lax.broadcasted_iota(jnp.int32, (TILE, last), 1)
        causal = place_t >= place_s
        for head in range(heads):
            span = slice(head * DH, (head + 1) * DH)
            scores = mm_nt(q[low:last, span], k[start : start + last, span])
            differ = columns[low:last, head : head + 1] - lines[head : head + 1, :last]
            weights = jnp.where(causal, jnp.exp(jnp.where(causal, differ, 0.0)), 0.0)
            intra_out[low:last, span] = mm((scores * weights).astype(BF16), v[start : start + last, span])


def hidden_kernel(heads, hop, sets, role, first, decay, before, entering, *refs):
    arrivals, projected, out, token = refs[: len(sets)], refs[len(sets) : -2], refs[-2], refs[-1]
    token[...] = jnp.zeros_like(token)

    def piece(start):
        block = start // BLOCK
        q, gate, intra = projected[3 * block : 3 * block + 3]
        at = slice(start % BLOCK, start % BLOCK + TILE)
        scales = jnp.exp(block_ends(decay, 0, block * BLOCK))
        for head in range(heads):
            span, row = slice(head * DH, (head + 1) * DH), slice(head, head + 1)
            fade = jnp.exp(entering[heads * DH + head : heads * DH + head + 1, :1])
            state = entering[span, :] + fade * arrived_state(arrivals, sets, hop, span)
            prior = (scales[row] * state + before[block, span, :].astype(F32)).astype(BF16)
            retained = intra[at, span] + mm(q[at, span], prior)
            center = retained - jnp.mean(retained, axis=1, keepdims=True)
            spread = jnp.mean(center * center, axis=1, keepdims=True)
            out[:, span] = (gate[at, span] * center * lax.rsqrt(spread + 1e-5)).astype(BF16)

    core, middle = lax.axis_index("fsdp"), decay.shape[1] // 2
    pl.when(core == role)(lambda: piece(first))
    pl.when(core != role)(lambda: piece(middle + first))


def columns_kernel(first, second, *outs):
    cols = outs[0].shape[1]
    place, core = lax.axis_index("tp"), lax.axis_index("fsdp")
    high, low = place // 2, place % 2

    @pl.when(core == 0)
    def _():
        at = pl.ds(pl.multiple_of((1 - low) * cols, cols), cols)
        outs[0][...] = first[:, at]
        outs[1][...] = second[:, at]

    @pl.when(core == 1)
    def _():
        for number, out in enumerate(outs):
            at = slice(number * cols, (number + 1) * cols)
            out[...] = jnp.where(high == 0, first[:, at], second[:, at])


def arrange_kernel(mine_0, mine_1, other_0, other_1, *outs):
    cols = mine_0.shape[1]
    place, core = lax.axis_index("tp"), lax.axis_index("fsdp")
    for role, (blocks, out) in enumerate(zip(((mine_0, mine_1), (other_0, other_1)), outs)):
        bit = jnp.where(core == role, place // 2, place % 2)
        out[:, :cols] = jnp.where(bit == 0, blocks[1][...], blocks[0][...])
        out[:, cols:] = jnp.where(bit == 0, blocks[0][...], blocks[1][...])


def own_kernel(order, own_first, own_second, *refs):
    pieces, outs = refs[: len(order)], refs[len(order) :]
    cols = pieces[0].shape[1]
    place, core = lax.axis_index("tp"), lax.axis_index("fsdp")
    high, low = place // 2, place % 2
    here = core == high
    mine = pl.ds(pl.multiple_of(low * cols, cols), cols)
    flipped = pl.ds(pl.multiple_of((1 - low) * cols, cols), cols)
    keep = jnp.where(here, own_first[:, mine], own_second[:, mine])
    low_give = jnp.where(here, own_second[:, mine], own_first[:, mine])
    high_give = jnp.where(here, own_first[:, flipped], own_second[:, flipped])
    gives = [jnp.where(core == role, low_give, high_give) for role in range(2)]
    for (role, number), piece in zip(order, pieces):
        at = slice(number * TILE, (number + 1) * TILE)
        outs[role][at, :cols] = mm(piece[...], gives[role])
        outs[role][at, cols:] = mm(piece[...], keep)


def give_kernel(number, own, far, weight, out):
    cols = out.shape[1]
    at = slice(number * TILE, (number + 1) * TILE)
    out[...] = (own[at, :cols] + mm(far[...], weight[:, :cols])).astype(BF16)


def keep_kernel(order, *refs):
    count = len(order)
    fars, owns, weights, outs = refs[:count], refs[count : count + 2], refs[count + 2 : count + 4], refs[count + 4 :]
    for (role, number), far in zip(order, fars):
        cols = far.shape[1]
        at = slice(number * TILE, (number + 1) * TILE)
        outs[role][at, :] = owns[role][at, cols:] + mm(far[...], weights[role][:, cols:])


def finish_kernel(order, *refs):
    count = len(order)
    gots, keeps, out, ready, written = refs[:count], refs[count : count + 2], refs[-3], refs[-2], refs[-1]
    core, copies = lax.axis_index("fsdp"), []
    for slot, ((role, number), got) in enumerate(zip(order, gots)):
        keep = keeps[role]
        at = slice(number * TILE, (number + 1) * TILE)
        ready[slot] = (keep[at, :] + got[...].astype(F32)).astype(BF16)
        start = pl.multiple_of((role + core) % 2 * keep.shape[0] + number * TILE, TILE)
        copies.append(pltpu.make_async_copy(ready.at[slot], out.at[0, pl.ds(start, TILE)], written.at[slot]))
        copies[-1].start()
    for copy in copies:
        copy.wait()


def after(value, *others):
    return lax.optimization_barrier((value, *others))[0]


def on_device(tokens, query_weight, key_weight, value_weight, gate_weight, out_weight, log_decay):
    x = tokens[0]
    rows, width = x.shape
    part, cols = query_weight.shape
    heads = cols // DH
    blocks = rows // BLOCK
    ctx, tp, cores = lax.axis_size("ctx"), lax.axis_size("tp"), lax.axis_size("fsdp")
    assert tp == 4 and cores == 2 and ctx >= 4 and ctx & (ctx - 1) == 0
    partners = [
        [(at * cores + core, (at ^ (1 << (role + core) % 2)) * cores + core) for at in range(tp) for core in range(cores)]
        for role in range(2)
    ]

    def trade(value, role):
        return lax.ppermute(value, ("tp", "fsdp"), partners[role])

    tables = [((2, rows // FINE, DH // 2), F32), ((2, FINE, DH // 2), F32)]

    key_far = swap(key_weight, "fsdp", 1)
    value_far = swap(value_weight, "fsdp", 1)

    x_own, x_other, acc_k, acc_v, decay, coarse, fine, out_first = loading_call(
        key_value_own_kernel,
        [((rows, part), BF16)] * 2 + [((rows, cols), F32)] * 2 + [((8, rows), F32)]
        + tables
        + [(out_weight.shape, BF16)],
        [x, key_weight, value_weight, log_decay[0].T, out_weight],
        [],
        [pltpu.VMEM((part, cols), BF16)] * 2 + [pltpu.VMEM((heads, rows), F32)],
        2 * (rows // BLOCK) + 4,
        "key_value_own",
    )
    state_shape, message_shape = (heads * DH, DH), (heads * DH + EXTRA, DH)
    own_q, own_g, keys, values, before, window, message = loading_call(
        functools.partial(key_value_kernel, heads),
        [((part, cols), BF16)] * 2
        + [((rows, cols), BF16)] * 2
        + [((blocks, heads * DH, DH), BF16), (state_shape, F32), (message_shape, BF16)],
        [query_weight, gate_weight],
        [x_other, key_far, value_far, acc_k, acc_v, decay, coarse, fine],
        [],
        2,
        "key_value",
    )
    far_q, far_g = swap(own_q, "fsdp", 1), swap(own_g, "fsdp", 1)

    def query_gate(block, decay):
        return kernel_call(
            functools.partial(query_gate_kernel, heads, block),
            [((BLOCK, cols), BF16), ((BLOCK, cols), F32), ((BLOCK, cols), F32)],
            [x_own, x_other, own_q, far_q, own_g, far_g, decay, coarse, fine, keys, values],
            "query_gate",
            [pltpu.VMEM((BLOCK, cols), BF16)],
        )

    def exchange(message, lowers, hop):
        pairs = [(at, at + hop) for at in lowers]
        if hop > 1:
            pairs += [(upper, at) for at, upper in pairs]
        return lax.ppermute(message, "ctx", pairs)

    projected = list(query_gate(0, decay))
    window = after(window, projected[0])
    entering, hop, early, first_message = None, 1, [], message
    while True:
        first_set, *later_sets = exchanges(ctx, hop)
        later_sets = [lowers for lowers in later_sets if lowers]
        sets = later_sets + ([first_set] if first_set else [])
        arrivals = [exchange(message, lowers, hop) for lowers in later_sets] + early
        if 2 * hop >= ctx:
            break
        unchanged = exchanges(ctx, 2 * hop)[0]
        early = [exchange(message, unchanged, 2 * hop)]
        old = [] if entering is None else [entering]
        last = 4 * hop >= ctx
        entering, message, *windows = kernel_call(
            functools.partial(combine_kernel, heads, hop, sets, entering is None, last),
            [((heads * DH + 8, DH), F32)]
            + ([(state_shape, BF16)] if last else [(message_shape, BF16), (state_shape, F32)]),
            [window, message, *old, *arrivals],
            "combine",
        )
        window = windows[0] if windows else None
        hop *= 2

    own_second = swap(out_first, "fsdp", 1)
    for_partner = kernel_call(
        columns_kernel,
        [((cols, cols), BF16)] * 2,
        [after(out_first, first_message), own_second],
        "columns",
    )
    out_mine = [trade(block, 0) for block in for_partner]

    held = after(decay, message, *early, out_mine[0])
    for block in range(1, blocks):
        projected += query_gate(block, held)

    count = rows // 2 // TILE
    hidden, far = [[], []], [[], []]
    token = None
    for number, role in [(number, role) for number in range(count) for role in range(2)]:
        held = decay if token is None else after(decay, swap(token, "fsdp", 1))
        piece, token = kernel_call(
            functools.partial(hidden_kernel, heads, hop, sets, role, number * TILE),
            [((TILE, cols), BF16), ((16, 128), BF16)],
            [held, before, entering, *arrivals, *projected],
            "hidden",
        )
        if number == 0 and role == 0:
            out_other = [swap(after(block, piece), "fsdp", 1) for block in out_mine]
        hidden[role].append(piece)
        far[role].append(trade(piece, role))
    weights = kernel_call(
        arrange_kernel,
        [((cols, 2 * cols), BF16)] * 2,
        [*out_mine, *out_other],
        "arrange",
    )
    order = [(role, number) for number in reversed(range(count)) for role in (1, 0)]
    owns = kernel_call(
        functools.partial(own_kernel, order),
        [((count * TILE, 2 * cols), F32)] * 2,
        [out_first, own_second, *(hidden[role][number] for role, number in order)],
        "own_products",
    )
    gots = []
    for role, number in order:
        [give] = kernel_call(
            functools.partial(give_kernel, number),
            [((TILE, cols), BF16)],
            [owns[role], far[role][number], weights[role]],
            "give",
        )
        gots.append(trade(give, 1 - role))
    keeps = kernel_call(
        functools.partial(keep_kernel, order),
        [((count * TILE, cols), F32)] * 2,
        [*(far[role][number] for role, number in order), *owns, *weights],
        "keep",
    )
    result = None
    for part_order, part_gots in ((order[2:], gots[2:]), (order[:2], gots[:2])):
        arrays = [pltpu.with_memory_space_constraint(array, pltpu.VMEM) for array in (*part_gots, *keeps)]
        held = [] if result is None else [result]
        result = pl.pallas_call(
            functools.partial(finish_kernel, part_order),
            in_specs=[pl.BlockSpec(memory_space=pltpu.VMEM)] * len(arrays)
            + [pl.BlockSpec(memory_space=pltpu.HBM)] * len(held),
            out_specs=pl.BlockSpec(memory_space=pltpu.HBM),
            out_shape=jax.ShapeDtypeStruct((1, rows, cols), BF16),
            input_output_aliases={len(arrays): 0} if held else {},
            scratch_shapes=[
                pltpu.VMEM((len(part_order), TILE, cols), BF16),
                pltpu.SemaphoreType.DMA((len(part_order),)),
            ],
            compiler_params=pltpu.CompilerParams(vmem_limit_bytes=VMEM_LIMIT),
            name="finish",
        )(*arrays, *held)
    return result


def solution(mesh):
    in_specs = (
        P("fsdp", "ctx", None),
        P("fsdp", "tp"),
        P("fsdp", "tp"),
        P("fsdp", "tp"),
        P("fsdp", "tp"),
        P("tp", "fsdp"),
        P("fsdp", "ctx", "tp"),
    )
    out_specs = P("fsdp", "ctx", "tp")
    return jax.shard_map(
        on_device, mesh=mesh, in_specs=in_specs, out_specs=out_specs, check_vma=False
    )
```

```python
import functools
import math

import jax
import jax.numpy as jnp
from jax import lax
from jax.experimental import pallas as pl
from jax.experimental.pallas import tpu as pltpu
from jax.sharding import PartitionSpec as P

DH = 256
BLOCK = 512
TILE = 256
FINE = 32
EXTRA = 16
VMEM_LIMIT = 14 * 1024 * 1024
F32 = jnp.float32
BF16 = jnp.bfloat16


def mm(left, right):
    return jnp.dot(left, right, preferred_element_type=F32)


def mm_nt(left, right):
    return lax.dot_general(left, right, (((1,), (1,)), ((), ())), preferred_element_type=F32)


def mm_tn(left, right):
    return lax.dot_general(left, right, (((0,), (0,)), ((), ())), preferred_element_type=F32)


def swap(value, axis, mask):
    size = lax.axis_size(axis)
    return lax.ppermute(value, axis, [(place, place ^ mask) for place in range(size)])


def kernel_call(kernel, outs, operands, name):
    arrays = [pltpu.with_memory_space_constraint(array, pltpu.VMEM) for array in operands]
    return pl.pallas_call(
        kernel,
        in_specs=[pl.BlockSpec(memory_space=pltpu.VMEM)] * len(operands),
        out_specs=[pl.BlockSpec(memory_space=pltpu.VMEM)] * len(outs),
        out_shape=[pltpu.VMEM(shape, dtype) for shape, dtype in outs],
        compiler_params=pltpu.CompilerParams(vmem_limit_bytes=VMEM_LIMIT),
        cost_estimate=pl.CostEstimate(
            flops=1, bytes_accessed=1, transcendentals=0
        ),
        name=name,
    )(*arrays)


def loading_call(kernel, outs, loaded, operands, scratch, loads, name):
    arrays = [pltpu.with_memory_space_constraint(array, pltpu.HBM) for array in loaded]
    arrays += [pltpu.with_memory_space_constraint(array, pltpu.VMEM) for array in operands]
    return pl.pallas_call(
        kernel,
        in_specs=[pl.BlockSpec(memory_space=pltpu.HBM)] * len(loaded)
        + [pl.BlockSpec(memory_space=pltpu.VMEM)] * len(operands),
        out_specs=[pl.BlockSpec(memory_space=pltpu.VMEM)] * len(outs),
        out_shape=[pltpu.VMEM(shape, dtype) for shape, dtype in outs],
        scratch_shapes=[*scratch, pltpu.SemaphoreType.DMA((loads,))],
        compiler_params=pltpu.CompilerParams(vmem_limit_bytes=VMEM_LIMIT),
        cost_estimate=pl.CostEstimate(flops=1, bytes_accessed=1, transcendentals=0),
        name=name,
    )(*arrays)


def turned(values, cosine, sine):
    half = DH // 2
    parts = []
    for start in range(0, values.shape[1], DH):
        low = values[:, start : start + half]
        high = values[:, start + half : start + DH]
        parts.append((low * cosine - high * sine).astype(BF16))
        parts.append((high * cosine + low * sine).astype(BF16))
    return jnp.concatenate(parts, axis=1)


def angles(coarse, fine, first, count):
    at = first // FINE
    far = coarse[:, pl.ds(at, count // FINE), :]
    near = fine[...]
    cos_c, sin_c = far[0][:, None, :], far[1][:, None, :]
    cos_f, sin_f = near[0][None], near[1][None]
    cosine = cos_c * cos_f - sin_c * sin_f
    sine = sin_c * cos_f + cos_c * sin_f
    return cosine.reshape(count, DH // 2), sine.reshape(count, DH // 2)


def decay_sums(log_decay, decay):
    heads, rows = log_decay.shape
    place_s = lax.broadcasted_iota(jnp.int32, (BLOCK, BLOCK), 0)
    place_t = lax.broadcasted_iota(jnp.int32, (BLOCK, BLOCK), 1)
    upper = jnp.where(place_s <= place_t, 1.0, 0.0).astype(BF16)
    value = jnp.concatenate([log_decay[...], jnp.zeros((8 - heads, rows), F32)], axis=0)
    parts = []
    for _ in range(3):
        parts.append(value.astype(BF16))
        value = value - parts[-1].astype(F32)
    stacked = jnp.concatenate([part.astype(F32) for part in parts], axis=0).astype(BF16)
    for start in range(0, rows, BLOCK):
        sums = mm(stacked[:, start : start + BLOCK], upper)
        decay[:, start : start + BLOCK] = sums[:8] + sums[8:16] + sums[16:]


def turn(first, second):
    (cos_a, sin_a), (cos_b, sin_b) = first, second
    return cos_a * cos_b - sin_a * sin_b, sin_a * cos_b + cos_a * sin_b


def joined(first, second):
    return tuple(jnp.concatenate(pair, axis=0) for pair in zip(first, second))


def angle_tables(coarse, fine):
    half, seeds = DH // 2, 8
    index = lax.broadcasted_iota(jnp.int32, (seeds, half), 1).astype(F32)
    frequency = jnp.exp(index * (-math.log(10000.0) / half))
    place = lax.broadcasted_iota(jnp.int32, (seeds, half), 0).astype(F32)
    offset = (lax.axis_index("ctx") * (coarse.shape[1] * FINE)).astype(F32)
    near = jnp.cos(place * frequency), jnp.sin(place * frequency)
    base = jnp.cos(offset * frequency), jnp.sin(offset * frequency)
    step = turn([part[seeds - 1 : seeds] for part in near], [part[1:2] for part in near])
    while near[0].shape[0] < FINE:
        near = joined(near, turn(near, step))
        step = turn(step, step)
    far = tuple(part[:1] for part in base)
    while far[0].shape[0] < coarse.shape[1]:
        far = joined(far, turn(far, step))
        step = turn(step, step)
    for table, parts in ((coarse, far), (fine, near)):
        table[0], table[1] = (part[: table.shape[1]] for part in parts)


class Loads:
    def __init__(self, arrived):
        self.arrived, self.count = arrived, 0

    def start(self, source, target):
        copy = pltpu.make_async_copy(source, target, self.arrived.at[self.count])
        self.count += 1
        copy.start()
        return copy


def key_value_own_kernel(
    x_far, wk_far, wv_far, log_decay_far, wo_far,
    x_own, x_other, acc_k, acc_v, decay, coarse, fine, wo, wk, wv, log_decay, arrived,
):
    rows, part = x_own.shape
    core = lax.axis_index("fsdp")
    loads = Loads(arrived)

    def tile(x, half, start):
        at = pl.ds(start, BLOCK)
        columns = pl.ds(pl.multiple_of(half * part, part), part)
        return loads.start(x_far.at[at, columns], x.at[at])

    starts = range(0, rows, BLOCK)
    key, logs = loads.start(wk_far, wk), loads.start(log_decay_far, log_decay)
    tiles = [tile(x_own, core, start) for start in starts]
    value = loads.start(wv_far, wv)
    others = [tile(x_other, 1 - core, start) for start in starts] + [loads.start(wo_far, wo)]
    angle_tables(coarse, fine)
    logs.wait()
    decay_sums(log_decay, decay)
    key.wait()
    for copy, start in zip(tiles, starts):
        at = slice(start, start + BLOCK)
        copy.wait()
        acc_k[at, :] = mm(x_own[at, :], wk[...])
    value.wait()
    for start in starts:
        at = slice(start, start + BLOCK)
        acc_v[at, :] = mm(x_own[at, :], wv[...])
    for copy in others:
        copy.wait()


def block_ends(decay, start, stop):
    ends = [decay[:, end - 1 : end] for end in range(start + BLOCK, stop + 1, BLOCK)]
    return functools.reduce(lambda a, b: a + b, ends, jnp.zeros((decay.shape[0], 1), F32))


def pack_message(message, states, logs):
    for head, state in enumerate(states):
        message[head * DH : (head + 1) * DH, :] = state.astype(BF16)
    large = logs.astype(BF16).astype(F32)
    parts = jnp.concatenate([large, logs - large], axis=0)
    message[len(states) * DH :, :] = jnp.broadcast_to(parts, (EXTRA, DH)).astype(BF16)


def message_log(message, heads):
    tail = message[heads * DH :, :].astype(F32)
    return (tail[: EXTRA // 2] + tail[EXTRA // 2 :])[:, :1]


def exchanges(ctx, hop):
    lower = range(ctx - hop)
    if hop == 1:
        return [], list(lower), []
    early = [at for at in lower if at < hop // 2]
    even = [at for at in lower if at >= hop // 2 and at // hop % 2 == 0]
    odd = [at for at in lower if at // hop % 2 == 1]
    return early, even, odd


def is_upper(lowers, hop):
    place = lax.axis_index("ctx")
    found = place < 0
    for lower in lowers:
        found = jnp.logical_or(found, place == lower + hop)
    return found


def arrived_state(arrivals, sets, hop, span):
    parts = [jnp.where(is_upper(lowers, hop), ref[span, :].astype(F32), 0.0) for ref, lowers in zip(arrivals, sets)]
    return functools.reduce(lambda a, b: a + b, parts)


def arrived_log(arrivals, sets, hop, heads):
    parts = [jnp.where(is_upper(lowers, hop), message_log(ref, heads), 0.0) for ref, lowers in zip(arrivals, sets)]
    return functools.reduce(lambda a, b: a + b, parts)


def key_value_kernel(
    heads, wq_far, wg_far, x, wk, wv, acc_k, acc_v, decay, coarse, fine,
    wq, wg, k_out, v_out, before_out, state_out, message, arrived,
):
    loads = Loads(arrived)
    others = [loads.start(wq_far, wq), loads.start(wg_far, wg)]
    blocks = acc_k.shape[0] // BLOCK
    state_out[...] = jnp.zeros_like(state_out)
    for block in range(blocks):
        start = block * BLOCK
        at = slice(start, start + BLOCK)
        columns = decay[:, at].T
        ending = columns[BLOCK - 1 : BLOCK, :]
        faded = jnp.exp(ending - columns)
        rows = x[at, :]
        cosine, sine = angles(coarse, fine, start, BLOCK)
        keys = turned(acc_k[at, :] + mm(rows, wk[...]), cosine, sine)
        k_out[at, :] = keys
        values = (acc_v[at, :] + mm(rows, wv[...])).astype(BF16)
        v_out[at, :] = values
        for head in range(heads):
            span = slice(head * DH, (head + 1) * DH)
            weighted = (keys[:, span].astype(F32) * faded[:, head : head + 1]).astype(BF16)
            old = state_out[span, :]
            before_out[block, span, :] = old.astype(BF16)
            state_out[span, :] = jnp.exp(ending[:, head : head + 1]) * old + mm_tn(weighted, values[:, span])
    states = [state_out[head * DH : (head + 1) * DH, :] for head in range(heads)]
    pack_message(message, states, block_ends(decay, 0, acc_k.shape[0]))
    for copy in others:
        copy.wait()


def combine_kernel(heads, hop, sets, first, last, state, sent, *refs):
    if not first:
        old_entering, refs = refs[0], refs[1:]
    arrivals, entering, message = refs[: len(sets)], refs[len(sets)], refs[len(sets) + 1]
    window_log, log = message_log(sent, heads), arrived_log(arrivals, sets, hop, heads)
    before_log = jnp.zeros_like(log) if first else old_entering[heads * DH :, :1]
    states = []
    for head in range(heads):
        span, row = slice(head * DH, (head + 1) * DH), slice(head, head + 1)
        arrived = arrived_state(arrivals, sets, hop, span)
        if first:
            entering[span, :] = arrived
        else:
            entering[span, :] = old_entering[span, :] + jnp.exp(before_log[row]) * arrived
        states.append(state[span, :] + jnp.exp(window_log[row]) * arrived)
        if last:
            message[span, :] = states[-1].astype(BF16)
        else:
            refs[len(sets) + 2][span, :] = states[-1]
    entering[heads * DH :, :] = jnp.broadcast_to(before_log + log, (8, DH))
    if not last:
        pack_message(message, states, window_log + log)


def query_gate_kernel(
    heads, block, x_own, x_other, wq, wq_far, wg, wg_far, decay, coarse, fine, k, v, q_out, g_out, intra_out
):
    start = block * BLOCK
    lines = decay[:, start : start + BLOCK]
    columns = lines.T

    at = slice(start, start + BLOCK)
    cosine, sine = angles(coarse, fine, start, BLOCK)
    own, far = x_own[at, :], x_other[at, :]
    queries = mm(own, wq[...]) + mm(far, wq_far[...])
    q_out[...] = turned(queries, cosine, sine)
    gates = mm(own, wg[...]) + mm(far, wg_far[...])
    gates = gates.astype(BF16).astype(F32)
    g_out[...] = gates / (1.0 + jnp.exp(-gates))
    for piece in range(BLOCK // TILE):
        low, last = piece * TILE, (piece + 1) * TILE
        place_t = lax.broadcasted_iota(jnp.int32, (TILE, last), 0) + low
        place_s = lax.broadcasted_iota(jnp.int32, (TILE, last), 1)
        causal = place_t >= place_s
        for head in range(heads):
            span = slice(head * DH, (head + 1) * DH)
            scores = mm_nt(q_out[low:last, span], k[start : start + last, span])
            differ = columns[low:last, head : head + 1] - lines[head : head + 1, :last]
            weights = jnp.where(causal, jnp.exp(jnp.where(causal, differ, 0.0)), 0.0)
            intra_out[low:last, span] = mm((scores * weights).astype(BF16), v[start : start + last, span])


def hidden_kernel(heads, hop, sets, role, first, decay, before, entering, *refs):
    arrivals, projected, out, token = refs[: len(sets)], refs[len(sets) : -2], refs[-2], refs[-1]
    token[...] = jnp.zeros_like(token)

    def piece(start):
        block = start // BLOCK
        q, gate, intra = projected[3 * block : 3 * block + 3]
        at = slice(start % BLOCK, start % BLOCK + TILE)
        columns = jnp.exp(decay[:, start : start + TILE].T)
        scales = jnp.exp(block_ends(decay, 0, block * BLOCK))
        for head in range(heads):
            span, row = slice(head * DH, (head + 1) * DH), slice(head, head + 1)
            fade = jnp.exp(entering[heads * DH + head : heads * DH + head + 1, :1])
            state = entering[span, :] + fade * arrived_state(arrivals, sets, hop, span)
            prior = (scales[row] * state + before[block, span, :].astype(F32)).astype(BF16)
            retained = intra[at, span] + columns[:, row] * mm(q[at, span], prior)
            center = retained - jnp.mean(retained, axis=1, keepdims=True)
            spread = jnp.mean(center * center, axis=1, keepdims=True)
            out[:, span] = (gate[at, span] * center * lax.rsqrt(spread + 1e-5)).astype(BF16)

    core, middle = lax.axis_index("fsdp"), decay.shape[1] // 2
    pl.when(core == role)(lambda: piece(first))
    pl.when(core != role)(lambda: piece(middle + first))


def columns_kernel(first, second, *outs):
    cols = outs[0].shape[1]
    place, core = lax.axis_index("tp"), lax.axis_index("fsdp")
    high, low = place // 2, place % 2

    @pl.when(core == 0)
    def _():
        at = pl.ds(pl.multiple_of((1 - low) * cols, cols), cols)
        outs[0][...] = first[:, at]
        outs[1][...] = second[:, at]

    @pl.when(core == 1)
    def _():
        for number, out in enumerate(outs):
            at = slice(number * cols, (number + 1) * cols)
            out[...] = jnp.where(high == 0, first[:, at], second[:, at])


def arrange_kernel(mine_0, mine_1, other_0, other_1, *outs):
    cols = mine_0.shape[1]
    place, core = lax.axis_index("tp"), lax.axis_index("fsdp")
    for role, (blocks, out) in enumerate(zip(((mine_0, mine_1), (other_0, other_1)), outs)):
        bit = jnp.where(core == role, place // 2, place % 2)
        out[:, :cols] = jnp.where(bit == 0, blocks[1][...], blocks[0][...])
        out[:, cols:] = jnp.where(bit == 0, blocks[0][...], blocks[1][...])


def own_kernel(order, own_first, own_second, *refs):
    pieces, outs = refs[: len(order)], refs[len(order) :]
    cols = pieces[0].shape[1]
    place, core = lax.axis_index("tp"), lax.axis_index("fsdp")
    high, low = place // 2, place % 2
    here = core == high
    mine = pl.ds(pl.multiple_of(low * cols, cols), cols)
    flipped = pl.ds(pl.multiple_of((1 - low) * cols, cols), cols)
    keep = jnp.where(here, own_first[:, mine], own_second[:, mine])
    low_give = jnp.where(here, own_second[:, mine], own_first[:, mine])
    high_give = jnp.where(here, own_first[:, flipped], own_second[:, flipped])
    gives = [jnp.where(core == role, low_give, high_give) for role in range(2)]
    for (role, number), piece in zip(order, pieces):
        at = slice(number * TILE, (number + 1) * TILE)
        outs[role][at, :cols] = mm(piece[...], gives[role])
        outs[role][at, cols:] = mm(piece[...], keep)


def give_kernel(number, own, far, weight, out):
    cols = out.shape[1]
    at = slice(number * TILE, (number + 1) * TILE)
    out[...] = (own[at, :cols] + mm(far[...], weight[:, :cols])).astype(BF16)


def keep_kernel(order, *refs):
    count = len(order)
    fars, owns, weights, outs = refs[:count], refs[count : count + 2], refs[count + 2 : count + 4], refs[count + 4 :]
    for (role, number), far in zip(order, fars):
        cols = far.shape[1]
        at = slice(number * TILE, (number + 1) * TILE)
        outs[role][at, :] = owns[role][at, cols:] + mm(far[...], weights[role][:, cols:])


def finish_kernel(order, *refs):
    count = len(order)
    gots, keeps, out, ready, written = refs[:count], refs[count : count + 2], refs[-3], refs[-2], refs[-1]
    core, copies = lax.axis_index("fsdp"), []
    for slot, ((role, number), got) in enumerate(zip(order, gots)):
        keep = keeps[role]
        at = slice(number * TILE, (number + 1) * TILE)
        ready[slot] = (keep[at, :] + got[...].astype(F32)).astype(BF16)
        start = pl.multiple_of((role + core) % 2 * keep.shape[0] + number * TILE, TILE)
        copies.append(pltpu.make_async_copy(ready.at[slot], out.at[0, pl.ds(start, TILE)], written.at[slot]))
        copies[-1].start()
    for copy in copies:
        copy.wait()


def after(value, *others):
    return lax.optimization_barrier((value, *others))[0]


def on_device(tokens, query_weight, key_weight, value_weight, gate_weight, out_weight, log_decay):
    x = tokens[0]
    rows, width = x.shape
    part, cols = query_weight.shape
    heads = cols // DH
    blocks = rows // BLOCK
    ctx, tp, cores = lax.axis_size("ctx"), lax.axis_size("tp"), lax.axis_size("fsdp")
    assert tp == 4 and cores == 2 and ctx >= 4 and ctx & (ctx - 1) == 0
    partners = [
        [(at * cores + core, (at ^ (1 << (role + core) % 2)) * cores + core) for at in range(tp) for core in range(cores)]
        for role in range(2)
    ]

    def trade(value, role):
        return lax.ppermute(value, ("tp", "fsdp"), partners[role])

    tables = [((2, rows // FINE, DH // 2), F32), ((2, FINE, DH // 2), F32)]

    key_far = swap(key_weight, "fsdp", 1)
    value_far = swap(value_weight, "fsdp", 1)

    x_own, x_other, acc_k, acc_v, decay, coarse, fine, out_first = loading_call(
        key_value_own_kernel,
        [((rows, part), BF16)] * 2 + [((rows, cols), F32)] * 2 + [((8, rows), F32)]
        + tables
        + [(out_weight.shape, BF16)],
        [x, key_weight, value_weight, log_decay[0].T, out_weight],
        [],
        [pltpu.VMEM((part, cols), BF16)] * 2 + [pltpu.VMEM((heads, rows), F32)],
        2 * (rows // BLOCK) + 4,
        "key_value_own",
    )
    state_shape, message_shape = (heads * DH, DH), (heads * DH + EXTRA, DH)
    own_q, own_g, keys, values, before, window, message = loading_call(
        functools.partial(key_value_kernel, heads),
        [((part, cols), BF16)] * 2
        + [((rows, cols), BF16)] * 2
        + [((blocks, heads * DH, DH), BF16), (state_shape, F32), (message_shape, BF16)],
        [query_weight, gate_weight],
        [x_other, key_far, value_far, acc_k, acc_v, decay, coarse, fine],
        [],
        2,
        "key_value",
    )
    far_q, far_g = swap(own_q, "fsdp", 1), swap(own_g, "fsdp", 1)

    def query_gate(block, decay):
        return kernel_call(
            functools.partial(query_gate_kernel, heads, block),
            [((BLOCK, cols), BF16), ((BLOCK, cols), F32), ((BLOCK, cols), F32)],
            [x_own, x_other, own_q, far_q, own_g, far_g, decay, coarse, fine, keys, values],
            "query_gate",
        )

    def exchange(message, lowers, hop):
        pairs = [(at, at + hop) for at in lowers]
        pairs += [(upper, at) for at, upper in pairs] if hop > 1 else [(ctx - 1, 0)]
        return lax.ppermute(message, "ctx", pairs)

    projected = list(query_gate(0, decay))
    window = after(window, projected[0])
    entering, hop, early, first_message = None, 1, [], message
    while True:
        first_set, *later_sets = exchanges(ctx, hop)
        later_sets = [lowers for lowers in later_sets if lowers]
        sets = later_sets + ([first_set] if first_set else [])
        arrivals = [exchange(message, lowers, hop) for lowers in later_sets] + early
        if 2 * hop >= ctx:
            break
        unchanged = exchanges(ctx, 2 * hop)[0]
        early = [exchange(message, unchanged, 2 * hop)]
        old = [] if entering is None else [entering]
        last = 4 * hop >= ctx
        entering, message, *windows = kernel_call(
            functools.partial(combine_kernel, heads, hop, sets, entering is None, last),
            [((heads * DH + 8, DH), F32)]
            + ([(state_shape, BF16)] if last else [(message_shape, BF16), (state_shape, F32)]),
            [window, message, *old, *arrivals],
            "combine",
        )
        window = windows[0] if windows else None
        hop *= 2

    own_second = swap(out_first, "fsdp", 1)
    for_partner = kernel_call(
        columns_kernel,
        [((cols, cols), BF16)] * 2,
        [after(out_first, first_message), own_second],
        "columns",
    )
    out_mine = [trade(block, 0) for block in for_partner]

    held = after(decay, message, *early, out_mine[0])
    for block in range(1, blocks):
        projected += query_gate(block, held)

    count = rows // 2 // TILE
    hidden, far = [[], []], [[], []]
    token = None
    for number, role in [(number, role) for number in range(count) for role in range(2)]:
        held = decay if token is None else after(decay, swap(token, "fsdp", 1))
        piece, token = kernel_call(
            functools.partial(hidden_kernel, heads, hop, sets, role, number * TILE),
            [((TILE, cols), BF16), ((16, 128), BF16)],
            [held, before, entering, *arrivals, *projected],
            "hidden",
        )
        if number == 0 and role == 0:
            out_other = [swap(after(block, piece), "fsdp", 1) for block in out_mine]
        hidden[role].append(piece)
        far[role].append(trade(piece, role))
    weights = kernel_call(
        arrange_kernel,
        [((cols, 2 * cols), BF16)] * 2,
        [*out_mine, *out_other],
        "arrange",
    )
    order = [(role, number) for number in reversed(range(count)) for role in (1, 0)]
    owns = kernel_call(
        functools.partial(own_kernel, order),
        [((count * TILE, 2 * cols), F32)] * 2,
        [out_first, own_second, *(hidden[role][number] for role, number in order)],
        "own_products",
    )
    gots = []
    for role, number in order:
        [give] = kernel_call(
            functools.partial(give_kernel, number),
            [((TILE, cols), BF16)],
            [owns[role], far[role][number], weights[role]],
            "give",
        )
        gots.append(trade(give, 1 - role))
    keeps = kernel_call(
        functools.partial(keep_kernel, order),
        [((count * TILE, cols), F32)] * 2,
        [*(far[role][number] for role, number in order), *owns, *weights],
        "keep",
    )
    result = None
    for part_order, part_gots in ((order[2:], gots[2:]), (order[:2], gots[:2])):
        arrays = [pltpu.with_memory_space_constraint(array, pltpu.VMEM) for array in (*part_gots, *keeps)]
        held = [] if result is None else [result]
        result = pl.pallas_call(
            functools.partial(finish_kernel, part_order),
            in_specs=[pl.BlockSpec(memory_space=pltpu.VMEM)] * len(arrays)
            + [pl.BlockSpec(memory_space=pltpu.HBM)] * len(held),
            out_specs=pl.BlockSpec(memory_space=pltpu.HBM),
            out_shape=jax.ShapeDtypeStruct((1, rows, cols), BF16),
            input_output_aliases={len(arrays): 0} if held else {},
            scratch_shapes=[
                pltpu.VMEM((len(part_order), TILE, cols), BF16),
                pltpu.SemaphoreType.DMA((len(part_order),)),
            ],
            compiler_params=pltpu.CompilerParams(vmem_limit_bytes=VMEM_LIMIT),
            name="finish",
        )(*arrays, *held)
    return result


def solution(mesh):
    in_specs = (
        P("fsdp", "ctx", None),
        P("fsdp", "tp"),
        P("fsdp", "tp"),
        P("fsdp", "tp"),
        P("fsdp", "tp"),
        P("tp", "fsdp"),
        P("fsdp", "ctx", "tp"),
    )
    out_specs = P("fsdp", "ctx", "tp")
    return jax.shard_map(
        on_device, mesh=mesh, in_specs=in_specs, out_specs=out_specs, check_vma=False
    )
```

```python
import functools
import math

import jax
import jax.numpy as jnp
from jax import lax
from jax.experimental import pallas as pl
from jax.experimental.pallas import tpu as pltpu
from jax.sharding import PartitionSpec as P

DH = 256
BLOCK = 512
TILE = 256
FINE = 32
EXTRA = 16
VMEM_LIMIT = 14 * 1024 * 1024
F32 = jnp.float32
BF16 = jnp.bfloat16


def mm(left, right):
    return jnp.dot(left, right, preferred_element_type=F32)


def mm_nt(left, right):
    return lax.dot_general(left, right, (((1,), (1,)), ((), ())), preferred_element_type=F32)


def mm_tn(left, right):
    return lax.dot_general(left, right, (((0,), (0,)), ((), ())), preferred_element_type=F32)


def swap(value, axis, mask):
    size = lax.axis_size(axis)
    return lax.ppermute(value, axis, [(place, place ^ mask) for place in range(size)])


def kernel_call(kernel, outs, operands, name):
    arrays = [pltpu.with_memory_space_constraint(array, pltpu.VMEM) for array in operands]
    return pl.pallas_call(
        kernel,
        in_specs=[pl.BlockSpec(memory_space=pltpu.VMEM)] * len(operands),
        out_specs=[pl.BlockSpec(memory_space=pltpu.VMEM)] * len(outs),
        out_shape=[pltpu.VMEM(shape, dtype) for shape, dtype in outs],
        compiler_params=pltpu.CompilerParams(vmem_limit_bytes=VMEM_LIMIT),
        cost_estimate=pl.CostEstimate(
            flops=1, bytes_accessed=1, transcendentals=0
        ),
        name=name,
    )(*arrays)


def loading_call(kernel, outs, loaded, operands, scratch, loads, name):
    arrays = [pltpu.with_memory_space_constraint(array, pltpu.HBM) for array in loaded]
    arrays += [pltpu.with_memory_space_constraint(array, pltpu.VMEM) for array in operands]
    return pl.pallas_call(
        kernel,
        in_specs=[pl.BlockSpec(memory_space=pltpu.HBM)] * len(loaded)
        + [pl.BlockSpec(memory_space=pltpu.VMEM)] * len(operands),
        out_specs=[pl.BlockSpec(memory_space=pltpu.VMEM)] * len(outs),
        out_shape=[pltpu.VMEM(shape, dtype) for shape, dtype in outs],
        scratch_shapes=[*scratch, pltpu.SemaphoreType.DMA((loads,))],
        compiler_params=pltpu.CompilerParams(vmem_limit_bytes=VMEM_LIMIT),
        cost_estimate=pl.CostEstimate(flops=1, bytes_accessed=1, transcendentals=0),
        name=name,
    )(*arrays)


def turned(values, cosine, sine):
    half = DH // 2
    parts = []
    for start in range(0, values.shape[1], DH):
        low = values[:, start : start + half]
        high = values[:, start + half : start + DH]
        parts.append((low * cosine - high * sine).astype(BF16))
        parts.append((high * cosine + low * sine).astype(BF16))
    return jnp.concatenate(parts, axis=1)


def angles(coarse, fine, first, count):
    at = first // FINE
    far = coarse[:, pl.ds(at, count // FINE), :]
    near = fine[...]
    cos_c, sin_c = far[0][:, None, :], far[1][:, None, :]
    cos_f, sin_f = near[0][None], near[1][None]
    cosine = cos_c * cos_f - sin_c * sin_f
    sine = sin_c * cos_f + cos_c * sin_f
    return cosine.reshape(count, DH // 2), sine.reshape(count, DH // 2)


def decay_sums(log_decay, decay):
    heads, rows = log_decay.shape
    place_s = lax.broadcasted_iota(jnp.int32, (BLOCK, BLOCK), 0)
    place_t = lax.broadcasted_iota(jnp.int32, (BLOCK, BLOCK), 1)
    upper = jnp.where(place_s <= place_t, 1.0, 0.0).astype(BF16)
    value = jnp.concatenate([log_decay[...], jnp.zeros((8 - heads, rows), F32)], axis=0)
    parts = []
    for _ in range(3):
        parts.append(value.astype(BF16))
        value = value - parts[-1].astype(F32)
    stacked = jnp.concatenate([part.astype(F32) for part in parts], axis=0).astype(BF16)
    for start in range(0, rows, BLOCK):
        sums = mm(stacked[:, start : start + BLOCK], upper)
        decay[:, start : start + BLOCK] = sums[:8] + sums[8:16] + sums[16:]


def turn(first, second):
    (cos_a, sin_a), (cos_b, sin_b) = first, second
    return cos_a * cos_b - sin_a * sin_b, sin_a * cos_b + cos_a * sin_b


def joined(first, second):
    return tuple(jnp.concatenate(pair, axis=0) for pair in zip(first, second))


def angle_tables(coarse, fine):
    half, seeds = DH // 2, 8
    index = lax.broadcasted_iota(jnp.int32, (seeds, half), 1).astype(F32)
    frequency = jnp.exp(index * (-math.log(10000.0) / half))
    place = lax.broadcasted_iota(jnp.int32, (seeds, half), 0).astype(F32)
    offset = (lax.axis_index("ctx") * (coarse.shape[1] * FINE)).astype(F32)
    near = jnp.cos(place * frequency), jnp.sin(place * frequency)
    base = jnp.cos(offset * frequency), jnp.sin(offset * frequency)
    step = turn([part[seeds - 1 : seeds] for part in near], [part[1:2] for part in near])
    while near[0].shape[0] < FINE:
        near = joined(near, turn(near, step))
        step = turn(step, step)
    far = tuple(part[:1] for part in base)
    while far[0].shape[0] < coarse.shape[1]:
        far = joined(far, turn(far, step))
        step = turn(step, step)
    for table, parts in ((coarse, far), (fine, near)):
        table[0], table[1] = (part[: table.shape[1]] for part in parts)


class Loads:
    def __init__(self, arrived):
        self.arrived, self.count = arrived, 0

    def start(self, source, target):
        copy = pltpu.make_async_copy(source, target, self.arrived.at[self.count])
        self.count += 1
        copy.start()
        return copy


def key_value_own_kernel(
    x_far, wk_far, wv_far, log_decay_far, wo_far,
    x_own, x_other, acc_k, acc_v, decay, coarse, fine, wo, wk, wv, log_decay, arrived,
):
    rows, part = x_own.shape
    core = lax.axis_index("fsdp")
    loads = Loads(arrived)

    def tile(x, half, start):
        at = pl.ds(start, BLOCK)
        columns = pl.ds(pl.multiple_of(half * part, part), part)
        return loads.start(x_far.at[at, columns], x.at[at])

    starts = range(0, rows, BLOCK)
    key, logs = loads.start(wk_far, wk), loads.start(log_decay_far, log_decay)
    tiles = [tile(x_own, core, start) for start in starts]
    value = loads.start(wv_far, wv)
    others = [tile(x_other, 1 - core, start) for start in starts] + [loads.start(wo_far, wo)]
    angle_tables(coarse, fine)
    logs.wait()
    decay_sums(log_decay, decay)
    key.wait()
    for copy, start in zip(tiles, starts):
        at = slice(start, start + BLOCK)
        copy.wait()
        acc_k[at, :] = mm(x_own[at, :], wk[...])
    value.wait()
    for start in starts:
        at = slice(start, start + BLOCK)
        acc_v[at, :] = mm(x_own[at, :], wv[...])
    for copy in others:
        copy.wait()


def block_ends(decay, start, stop):
    ends = [decay[:, end - 1 : end] for end in range(start + BLOCK, stop + 1, BLOCK)]
    return functools.reduce(lambda a, b: a + b, ends, jnp.zeros((decay.shape[0], 1), F32))


def pack_message(message, states, logs):
    for head, state in enumerate(states):
        message[head * DH : (head + 1) * DH, :] = state.astype(BF16)
    large = logs.astype(BF16).astype(F32)
    parts = jnp.concatenate([large, logs - large], axis=0)
    message[len(states) * DH :, :] = jnp.broadcast_to(parts, (EXTRA, DH)).astype(BF16)


def message_log(message, heads):
    tail = message[heads * DH :, :].astype(F32)
    return (tail[: EXTRA // 2] + tail[EXTRA // 2 :])[:, :1]


def exchanges(ctx, hop):
    lower = range(ctx - hop)
    if hop == 1:
        return [], list(lower), []
    early = [at for at in lower if at < hop // 2]
    even = [at for at in lower if at >= hop // 2 and at // hop % 2 == 0]
    odd = [at for at in lower if at // hop % 2 == 1]
    return early, even, odd


def is_upper(lowers, hop):
    place = lax.axis_index("ctx")
    found = place < 0
    for lower in lowers:
        found = jnp.logical_or(found, place == lower + hop)
    return found


def arrived_state(arrivals, sets, hop, span):
    parts = [jnp.where(is_upper(lowers, hop), ref[span, :].astype(F32), 0.0) for ref, lowers in zip(arrivals, sets)]
    return functools.reduce(lambda a, b: a + b, parts)


def arrived_log(arrivals, sets, hop, heads):
    parts = [jnp.where(is_upper(lowers, hop), message_log(ref, heads), 0.0) for ref, lowers in zip(arrivals, sets)]
    return functools.reduce(lambda a, b: a + b, parts)


def key_value_kernel(
    heads, wq_far, wg_far, x, wk, wv, acc_k, acc_v, decay, coarse, fine,
    wq, wg, k_out, v_out, before_out, state_out, message, arrived,
):
    loads = Loads(arrived)
    others = [loads.start(wq_far, wq), loads.start(wg_far, wg)]
    blocks = acc_k.shape[0] // BLOCK
    state_out[...] = jnp.zeros_like(state_out)
    for block in range(blocks):
        start = block * BLOCK
        at = slice(start, start + BLOCK)
        columns = decay[:, at].T
        ending = columns[BLOCK - 1 : BLOCK, :]
        faded = jnp.exp(ending - columns)
        rows = x[at, :]
        cosine, sine = angles(coarse, fine, start, BLOCK)
        keys = turned(acc_k[at, :] + mm(rows, wk[...]), cosine, sine)
        k_out[at, :] = keys
        values = (acc_v[at, :] + mm(rows, wv[...])).astype(BF16)
        v_out[at, :] = values
        for head in range(heads):
            span = slice(head * DH, (head + 1) * DH)
            weighted = (keys[:, span].astype(F32) * faded[:, head : head + 1]).astype(BF16)
            old = state_out[span, :]
            before_out[block, span, :] = old.astype(BF16)
            state_out[span, :] = jnp.exp(ending[:, head : head + 1]) * old + mm_tn(weighted, values[:, span])
    states = [state_out[head * DH : (head + 1) * DH, :] for head in range(heads)]
    pack_message(message, states, block_ends(decay, 0, acc_k.shape[0]))
    for copy in others:
        copy.wait()


def combine_kernel(heads, hop, sets, first, last, state, sent, *refs):
    if not first:
        old_entering, refs = refs[0], refs[1:]
    arrivals, entering, message = refs[: len(sets)], refs[len(sets)], refs[len(sets) + 1]
    window_log, log = message_log(sent, heads), arrived_log(arrivals, sets, hop, heads)
    before_log = jnp.zeros_like(log) if first else old_entering[heads * DH :, :1]
    states = []
    for head in range(heads):
        span, row = slice(head * DH, (head + 1) * DH), slice(head, head + 1)
        arrived = arrived_state(arrivals, sets, hop, span)
        if first:
            entering[span, :] = arrived
        else:
            entering[span, :] = old_entering[span, :] + jnp.exp(before_log[row]) * arrived
        states.append(state[span, :] + jnp.exp(window_log[row]) * arrived)
        if last:
            message[span, :] = states[-1].astype(BF16)
        else:
            refs[len(sets) + 2][span, :] = states[-1]
    entering[heads * DH :, :] = jnp.broadcast_to(before_log + log, (8, DH))
    if not last:
        pack_message(message, states, window_log + log)


def query_gate_kernel(
    heads, block, x_own, x_other, wq, wq_far, wg, wg_far, decay, coarse, fine, k, v, q_out, g_out, intra_out
):
    start = block * BLOCK
    lines = decay[:, start : start + BLOCK]
    columns = lines.T

    at = slice(start, start + BLOCK)
    cosine, sine = angles(coarse, fine, start, BLOCK)
    own, far = x_own[at, :], x_other[at, :]
    queries = mm(own, wq[...]) + mm(far, wq_far[...])
    q_out[...] = turned(queries, cosine, sine)
    gates = mm(own, wg[...]) + mm(far, wg_far[...])
    gates = gates.astype(BF16).astype(F32)
    g_out[...] = gates / (1.0 + jnp.exp(-gates))
    for piece in range(BLOCK // TILE):
        low, last = piece * TILE, (piece + 1) * TILE
        place_t = lax.broadcasted_iota(jnp.int32, (TILE, last), 0) + low
        place_s = lax.broadcasted_iota(jnp.int32, (TILE, last), 1)
        causal = place_t >= place_s
        for head in range(heads):
            span = slice(head * DH, (head + 1) * DH)
            scores = mm_nt(q_out[low:last, span], k[start : start + last, span])
            differ = columns[low:last, head : head + 1] - lines[head : head + 1, :last]
            weights = jnp.where(causal, jnp.exp(jnp.where(causal, differ, 0.0)), 0.0)
            intra_out[low:last, span] = mm((scores * weights).astype(BF16), v[start : start + last, span])


def hidden_kernel(heads, hop, sets, role, first, decay, before, entering, *refs):
    arrivals, projected, out, token = refs[: len(sets)], refs[len(sets) : -2], refs[-2], refs[-1]
    token[...] = jnp.zeros_like(token)

    def piece(start):
        block = start // BLOCK
        q, gate, intra = projected[3 * block : 3 * block + 3]
        at = slice(start % BLOCK, start % BLOCK + TILE)
        columns = jnp.exp(decay[:, start : start + TILE].T)
        scales = jnp.exp(block_ends(decay, 0, block * BLOCK))
        for head in range(heads):
            span, row = slice(head * DH, (head + 1) * DH), slice(head, head + 1)
            fade = jnp.exp(entering[heads * DH + head : heads * DH + head + 1, :1])
            state = entering[span, :] + fade * arrived_state(arrivals, sets, hop, span)
            prior = (scales[row] * state + before[block, span, :].astype(F32)).astype(BF16)
            retained = intra[at, span] + columns[:, row] * mm(q[at, span], prior)
            center = retained - jnp.mean(retained, axis=1, keepdims=True)
            spread = jnp.mean(center * center, axis=1, keepdims=True)
            out[:, span] = (gate[at, span] * center * lax.rsqrt(spread + 1e-5)).astype(BF16)

    core, middle = lax.axis_index("fsdp"), decay.shape[1] // 2
    pl.when(core == role)(lambda: piece(first))
    pl.when(core != role)(lambda: piece(middle + first))


def columns_kernel(first, second, *outs):
    cols = outs[0].shape[1]
    place, core = lax.axis_index("tp"), lax.axis_index("fsdp")
    high, low = place // 2, place % 2

    @pl.when(core == 0)
    def _():
        at = pl.ds(pl.multiple_of((1 - low) * cols, cols), cols)
        outs[0][...] = first[:, at]
        outs[1][...] = second[:, at]

    @pl.when(core == 1)
    def _():
        for number, out in enumerate(outs):
            at = slice(number * cols, (number + 1) * cols)
            out[...] = jnp.where(high == 0, first[:, at], second[:, at])


def arrange_kernel(mine_0, mine_1, other_0, other_1, *outs):
    cols = mine_0.shape[1]
    place, core = lax.axis_index("tp"), lax.axis_index("fsdp")
    for role, (blocks, out) in enumerate(zip(((mine_0, mine_1), (other_0, other_1)), outs)):
        bit = jnp.where(core == role, place // 2, place % 2)
        out[:, :cols] = jnp.where(bit == 0, blocks[1][...], blocks[0][...])
        out[:, cols:] = jnp.where(bit == 0, blocks[0][...], blocks[1][...])


def own_kernel(order, own_first, own_second, *refs):
    pieces, outs = refs[: len(order)], refs[len(order) :]
    cols = pieces[0].shape[1]
    place, core = lax.axis_index("tp"), lax.axis_index("fsdp")
    high, low = place // 2, place % 2
    here = core == high
    mine = pl.ds(pl.multiple_of(low * cols, cols), cols)
    flipped = pl.ds(pl.multiple_of((1 - low) * cols, cols), cols)
    keep = jnp.where(here, own_first[:, mine], own_second[:, mine])
    low_give = jnp.where(here, own_second[:, mine], own_first[:, mine])
    high_give = jnp.where(here, own_first[:, flipped], own_second[:, flipped])
    gives = [jnp.where(core == role, low_give, high_give) for role in range(2)]
    for (role, number), piece in zip(order, pieces):
        at = slice(number * TILE, (number + 1) * TILE)
        outs[role][at, :cols] = mm(piece[...], gives[role])
        outs[role][at, cols:] = mm(piece[...], keep)


def give_kernel(number, own, far, weight, out):
    cols = out.shape[1]
    at = slice(number * TILE, (number + 1) * TILE)
    out[...] = (own[at, :cols] + mm(far[...], weight[:, :cols])).astype(BF16)


def keep_kernel(order, *refs):
    count = len(order)
    fars, owns, weights, outs = refs[:count], refs[count : count + 2], refs[count + 2 : count + 4], refs[count + 4 :]
    for (role, number), far in zip(order, fars):
        cols = far.shape[1]
        at = slice(number * TILE, (number + 1) * TILE)
        outs[role][at, :] = owns[role][at, cols:] + mm(far[...], weights[role][:, cols:])


def finish_kernel(order, *refs):
    count = len(order)
    gots, keeps, out, ready, written = refs[:count], refs[count : count + 2], refs[-3], refs[-2], refs[-1]
    core, copies = lax.axis_index("fsdp"), []
    for slot, ((role, number), got) in enumerate(zip(order, gots)):
        keep = keeps[role]
        at = slice(number * TILE, (number + 1) * TILE)
        ready[slot] = (keep[at, :] + got[...].astype(F32)).astype(BF16)
        start = pl.multiple_of((role + core) % 2 * keep.shape[0] + number * TILE, TILE)
        copies.append(pltpu.make_async_copy(ready.at[slot], out.at[0, pl.ds(start, TILE)], written.at[slot]))
        copies[-1].start()
    for copy in copies:
        copy.wait()


def after(value, *others):
    return lax.optimization_barrier((value, *others))[0]


def on_device(tokens, query_weight, key_weight, value_weight, gate_weight, out_weight, log_decay):
    x = tokens[0]
    rows, width = x.shape
    part, cols = query_weight.shape
    heads = cols // DH
    blocks = rows // BLOCK
    ctx, tp, cores = lax.axis_size("ctx"), lax.axis_size("tp"), lax.axis_size("fsdp")
    assert tp == 4 and cores == 2 and ctx >= 4 and ctx & (ctx - 1) == 0
    partners = [
        [(at * cores + core, (at ^ (1 << (role + core) % 2)) * cores + core) for at in range(tp) for core in range(cores)]
        for role in range(2)
    ]

    def trade(value, role):
        return lax.ppermute(value, ("tp", "fsdp"), partners[role])

    tables = [((2, rows // FINE, DH // 2), F32), ((2, FINE, DH // 2), F32)]

    key_far = swap(key_weight, "fsdp", 1)
    value_far = swap(value_weight, "fsdp", 1)

    x_own, x_other, acc_k, acc_v, decay, coarse, fine, out_first = loading_call(
        key_value_own_kernel,
        [((rows, part), BF16)] * 2 + [((rows, cols), F32)] * 2 + [((8, rows), F32)]
        + tables
        + [(out_weight.shape, BF16)],
        [x, key_weight, value_weight, log_decay[0].T, out_weight],
        [],
        [pltpu.VMEM((part, cols), BF16)] * 2 + [pltpu.VMEM((heads, rows), F32)],
        2 * (rows // BLOCK) + 4,
        "key_value_own",
    )
    state_shape, message_shape = (heads * DH, DH), (heads * DH + EXTRA, DH)
    own_q, own_g, keys, values, before, window, message = loading_call(
        functools.partial(key_value_kernel, heads),
        [((part, cols), BF16)] * 2
        + [((rows, cols), BF16)] * 2
        + [((blocks, heads * DH, DH), BF16), (state_shape, F32), (message_shape, BF16)],
        [query_weight, gate_weight],
        [x_other, key_far, value_far, acc_k, acc_v, decay, coarse, fine],
        [],
        2,
        "key_value",
    )
    far_q, far_g = swap(own_q, "fsdp", 1), swap(own_g, "fsdp", 1)

    def query_gate(block, decay):
        return kernel_call(
            functools.partial(query_gate_kernel, heads, block),
            [((BLOCK, cols), BF16), ((BLOCK, cols), F32), ((BLOCK, cols), F32)],
            [x_own, x_other, own_q, far_q, own_g, far_g, decay, coarse, fine, keys, values],
            "query_gate",
        )

    def exchange(message, lowers, hop, two_way=True):
        pairs = [(at, at + hop) for at in lowers]
        if two_way:
            pairs += [(upper, at) for at, upper in pairs] if hop > 1 else [(ctx - 1, 0)]
        return lax.ppermute(message, "ctx", pairs)

    projected = list(query_gate(0, decay))
    window = after(window, projected[0])
    entering, hop, early, first_message = None, 1, [], message
    while True:
        first_set, *later_sets = exchanges(ctx, hop)
        later_sets = [lowers for lowers in later_sets if lowers]
        sets = later_sets + ([first_set] if first_set else [])
        arrivals = [exchange(message, lowers, hop) for lowers in later_sets] + early
        if 2 * hop >= ctx:
            break
        unchanged = exchanges(ctx, 2 * hop)[0]
        early = [exchange(message, unchanged, 2 * hop, two_way=False)]
        old = [] if entering is None else [entering]
        last = 4 * hop >= ctx
        entering, message, *windows = kernel_call(
            functools.partial(combine_kernel, heads, hop, sets, entering is None, last),
            [((heads * DH + 8, DH), F32)]
            + ([(state_shape, BF16)] if last else [(message_shape, BF16), (state_shape, F32)]),
            [window, message, *old, *arrivals],
            "combine",
        )
        window = windows[0] if windows else None
        hop *= 2

    own_second = swap(out_first, "fsdp", 1)
    for_partner = kernel_call(
        columns_kernel,
        [((cols, cols), BF16)] * 2,
        [after(out_first, first_message), own_second],
        "columns",
    )
    out_mine = [trade(block, 0) for block in for_partner]

    held = after(decay, message, *early, out_mine[0])
    for block in range(1, blocks):
        projected += query_gate(block, held)

    count = rows // 2 // TILE
    hidden, far = [[], []], [[], []]
    token = None
    for number, role in [(number, role) for number in range(count) for role in range(2)]:
        held = decay if token is None else after(decay, swap(token, "fsdp", 1))
        piece, token = kernel_call(
            functools.partial(hidden_kernel, heads, hop, sets, role, number * TILE),
            [((TILE, cols), BF16), ((16, 128), BF16)],
            [held, before, entering, *arrivals, *projected],
            "hidden",
        )
        if number == 0 and role == 0:
            out_other = [swap(after(block, piece), "fsdp", 1) for block in out_mine]
        hidden[role].append(piece)
        far[role].append(trade(piece, role))
    weights = kernel_call(
        arrange_kernel,
        [((cols, 2 * cols), BF16)] * 2,
        [*out_mine, *out_other],
        "arrange",
    )
    order = [(role, number) for number in reversed(range(count)) for role in (1, 0)]
    owns = kernel_call(
        functools.partial(own_kernel, order),
        [((count * TILE, 2 * cols), F32)] * 2,
        [out_first, own_second, *(hidden[role][number] for role, number in order)],
        "own_products",
    )
    gots = []
    for role, number in order:
        [give] = kernel_call(
            functools.partial(give_kernel, number),
            [((TILE, cols), BF16)],
            [owns[role], far[role][number], weights[role]],
            "give",
        )
        gots.append(trade(give, 1 - role))
    keeps = kernel_call(
        functools.partial(keep_kernel, order),
        [((count * TILE, cols), F32)] * 2,
        [*(far[role][number] for role, number in order), *owns, *weights],
        "keep",
    )
    result = None
    for part_order, part_gots in ((order[2:], gots[2:]), (order[:2], gots[:2])):
        arrays = [pltpu.with_memory_space_constraint(array, pltpu.VMEM) for array in (*part_gots, *keeps)]
        held = [] if result is None else [result]
        result = pl.pallas_call(
            functools.partial(finish_kernel, part_order),
            in_specs=[pl.BlockSpec(memory_space=pltpu.VMEM)] * len(arrays)
            + [pl.BlockSpec(memory_space=pltpu.HBM)] * len(held),
            out_specs=pl.BlockSpec(memory_space=pltpu.HBM),
            out_shape=jax.ShapeDtypeStruct((1, rows, cols), BF16),
            input_output_aliases={len(arrays): 0} if held else {},
            scratch_shapes=[
                pltpu.VMEM((len(part_order), TILE, cols), BF16),
                pltpu.SemaphoreType.DMA((len(part_order),)),
            ],
            compiler_params=pltpu.CompilerParams(vmem_limit_bytes=VMEM_LIMIT),
            name="finish",
        )(*arrays, *held)
    return result


def solution(mesh):
    in_specs = (
        P("fsdp", "ctx", None),
        P("fsdp", "tp"),
        P("fsdp", "tp"),
        P("fsdp", "tp"),
        P("fsdp", "tp"),
        P("tp", "fsdp"),
        P("fsdp", "ctx", "tp"),
    )
    out_specs = P("fsdp", "ctx", "tp")
    return jax.shard_map(
        on_device, mesh=mesh, in_specs=in_specs, out_specs=out_specs, check_vma=False
    )
```

```python
import functools
import math

import jax
import jax.numpy as jnp
from jax import lax
from jax.experimental import pallas as pl
from jax.experimental.pallas import tpu as pltpu
from jax.sharding import PartitionSpec as P

DH = 256
BLOCK = 512
TILE = 256
FINE = 32
EXTRA = 16
VMEM_LIMIT = 14 * 1024 * 1024
F32 = jnp.float32
BF16 = jnp.bfloat16


def mm(left, right):
    return jnp.dot(left, right, preferred_element_type=F32)


def mm_nt(left, right):
    return lax.dot_general(left, right, (((1,), (1,)), ((), ())), preferred_element_type=F32)


def mm_tn(left, right):
    return lax.dot_general(left, right, (((0,), (0,)), ((), ())), preferred_element_type=F32)


def swap(value, axis, mask):
    size = lax.axis_size(axis)
    return lax.ppermute(value, axis, [(place, place ^ mask) for place in range(size)])


def kernel_call(kernel, outs, operands, name):
    arrays = [pltpu.with_memory_space_constraint(array, pltpu.VMEM) for array in operands]
    return pl.pallas_call(
        kernel,
        in_specs=[pl.BlockSpec(memory_space=pltpu.VMEM)] * len(operands),
        out_specs=[pl.BlockSpec(memory_space=pltpu.VMEM)] * len(outs),
        out_shape=[pltpu.VMEM(shape, dtype) for shape, dtype in outs],
        compiler_params=pltpu.CompilerParams(vmem_limit_bytes=VMEM_LIMIT),
        cost_estimate=pl.CostEstimate(
            flops=1, bytes_accessed=1, transcendentals=0
        ),
        name=name,
    )(*arrays)


def loading_call(kernel, outs, loaded, operands, scratch, loads, name):
    arrays = [pltpu.with_memory_space_constraint(array, pltpu.HBM) for array in loaded]
    arrays += [pltpu.with_memory_space_constraint(array, pltpu.VMEM) for array in operands]
    return pl.pallas_call(
        kernel,
        in_specs=[pl.BlockSpec(memory_space=pltpu.HBM)] * len(loaded)
        + [pl.BlockSpec(memory_space=pltpu.VMEM)] * len(operands),
        out_specs=[pl.BlockSpec(memory_space=pltpu.VMEM)] * len(outs),
        out_shape=[pltpu.VMEM(shape, dtype) for shape, dtype in outs],
        scratch_shapes=[*scratch, pltpu.SemaphoreType.DMA((loads,))],
        compiler_params=pltpu.CompilerParams(vmem_limit_bytes=VMEM_LIMIT),
        cost_estimate=pl.CostEstimate(flops=1, bytes_accessed=1, transcendentals=0),
        name=name,
    )(*arrays)


def turned(values, cosine, sine):
    half = DH // 2
    parts = []
    for start in range(0, values.shape[1], DH):
        low = values[:, start : start + half]
        high = values[:, start + half : start + DH]
        parts.append((low * cosine - high * sine).astype(BF16))
        parts.append((high * cosine + low * sine).astype(BF16))
    return jnp.concatenate(parts, axis=1)


def angles(coarse, fine, first, count):
    at = first // FINE
    far = coarse[:, pl.ds(at, count // FINE), :]
    near = fine[...]
    cos_c, sin_c = far[0][:, None, :], far[1][:, None, :]
    cos_f, sin_f = near[0][None], near[1][None]
    cosine = cos_c * cos_f - sin_c * sin_f
    sine = sin_c * cos_f + cos_c * sin_f
    return cosine.reshape(count, DH // 2), sine.reshape(count, DH // 2)


def decay_sums(log_decay, decay):
    heads, rows = log_decay.shape
    place_s = lax.broadcasted_iota(jnp.int32, (BLOCK, BLOCK), 0)
    place_t = lax.broadcasted_iota(jnp.int32, (BLOCK, BLOCK), 1)
    upper = jnp.where(place_s <= place_t, 1.0, 0.0).astype(BF16)
    value = jnp.concatenate([log_decay[...], jnp.zeros((8 - heads, rows), F32)], axis=0)
    parts = []
    for _ in range(3):
        parts.append(value.astype(BF16))
        value = value - parts[-1].astype(F32)
    stacked = jnp.concatenate([part.astype(F32) for part in parts], axis=0).astype(BF16)
    for start in range(0, rows, BLOCK):
        sums = mm(stacked[:, start : start + BLOCK], upper)
        decay[:, start : start + BLOCK] = sums[:8] + sums[8:16] + sums[16:]


def turn(first, second):
    (cos_a, sin_a), (cos_b, sin_b) = first, second
    return cos_a * cos_b - sin_a * sin_b, sin_a * cos_b + cos_a * sin_b


def joined(first, second):
    return tuple(jnp.concatenate(pair, axis=0) for pair in zip(first, second))


def angle_tables(coarse, fine):
    half, seeds = DH // 2, 8
    index = lax.broadcasted_iota(jnp.int32, (seeds, half), 1).astype(F32)
    frequency = jnp.exp(index * (-math.log(10000.0) / half))
    place = lax.broadcasted_iota(jnp.int32, (seeds, half), 0).astype(F32)
    offset = (lax.axis_index("ctx") * (coarse.shape[1] * FINE)).astype(F32)
    near = jnp.cos(place * frequency), jnp.sin(place * frequency)
    base = jnp.cos(offset * frequency), jnp.sin(offset * frequency)
    step = turn([part[seeds - 1 : seeds] for part in near], [part[1:2] for part in near])
    while near[0].shape[0] < FINE:
        near = joined(near, turn(near, step))
        step = turn(step, step)
    far = tuple(part[:1] for part in base)
    while far[0].shape[0] < coarse.shape[1]:
        far = joined(far, turn(far, step))
        step = turn(step, step)
    for table, parts in ((coarse, far), (fine, near)):
        table[0], table[1] = (part[: table.shape[1]] for part in parts)


class Loads:
    def __init__(self, arrived):
        self.arrived, self.count = arrived, 0

    def start(self, source, target):
        copy = pltpu.make_async_copy(source, target, self.arrived.at[self.count])
        self.count += 1
        copy.start()
        return copy


def key_value_own_kernel(
    x_far, wk_far, wv_far, log_decay_far, wo_far,
    x_own, x_other, acc_k, acc_v, decay, coarse, fine, wo, wk, wv, log_decay, arrived,
):
    rows, part = x_own.shape
    core = lax.axis_index("fsdp")
    loads = Loads(arrived)

    def tile(x, half, start):
        at = pl.ds(start, BLOCK)
        columns = pl.ds(pl.multiple_of(half * part, part), part)
        return loads.start(x_far.at[at, columns], x.at[at])

    starts = range(0, rows, BLOCK)
    key, logs = loads.start(wk_far, wk), loads.start(log_decay_far, log_decay)
    tiles = [tile(x_own, core, start) for start in starts]
    value = loads.start(wv_far, wv)
    others = [tile(x_other, 1 - core, start) for start in starts] + [loads.start(wo_far, wo)]
    angle_tables(coarse, fine)
    logs.wait()
    decay_sums(log_decay, decay)
    key.wait()
    for copy, start in zip(tiles, starts):
        at = slice(start, start + BLOCK)
        copy.wait()
        acc_k[at, :] = mm(x_own[at, :], wk[...])
    value.wait()
    for start in starts:
        at = slice(start, start + BLOCK)
        acc_v[at, :] = mm(x_own[at, :], wv[...])
    for copy in others:
        copy.wait()


def block_ends(decay, start, stop):
    ends = [decay[:, end - 1 : end] for end in range(start + BLOCK, stop + 1, BLOCK)]
    return functools.reduce(lambda a, b: a + b, ends, jnp.zeros((decay.shape[0], 1), F32))


def pack_message(message, states, logs):
    for head, state in enumerate(states):
        message[head * DH : (head + 1) * DH, :] = state.astype(BF16)
    large = logs.astype(BF16).astype(F32)
    parts = jnp.concatenate([large, logs - large], axis=0)
    message[len(states) * DH :, :] = jnp.broadcast_to(parts, (EXTRA, DH)).astype(BF16)


def message_log(message, heads):
    tail = message[heads * DH :, :].astype(F32)
    return (tail[: EXTRA // 2] + tail[EXTRA // 2 :])[:, :1]


def exchanges(ctx, hop):
    lower = range(ctx - hop)
    if hop == 1:
        return [], list(lower), []
    early = [at for at in lower if at < hop // 2]
    even = [at for at in lower if at >= hop // 2 and at // hop % 2 == 0]
    odd = [at for at in lower if at // hop % 2 == 1]
    return early, even, odd


def is_upper(lowers, hop):
    place = lax.axis_index("ctx")
    found = place < 0
    for lower in lowers:
        found = jnp.logical_or(found, place == lower + hop)
    return found


def arrived_state(arrivals, sets, hop, span):
    parts = [jnp.where(is_upper(lowers, hop), ref[span, :].astype(F32), 0.0) for ref, lowers in zip(arrivals, sets)]
    return functools.reduce(lambda a, b: a + b, parts)


def arrived_log(arrivals, sets, hop, heads):
    parts = [jnp.where(is_upper(lowers, hop), message_log(ref, heads), 0.0) for ref, lowers in zip(arrivals, sets)]
    return functools.reduce(lambda a, b: a + b, parts)


def key_value_kernel(
    heads, wq_far, wg_far, x, wk, wv, acc_k, acc_v, decay, coarse, fine,
    wq, wg, k_out, v_out, before_out, state_out, message, arrived,
):
    loads = Loads(arrived)
    others = [loads.start(wq_far, wq), loads.start(wg_far, wg)]
    blocks = acc_k.shape[0] // BLOCK
    state_out[...] = jnp.zeros_like(state_out)
    for block in range(blocks):
        start = block * BLOCK
        at = slice(start, start + BLOCK)
        columns = decay[:, at].T
        ending = columns[BLOCK - 1 : BLOCK, :]
        faded = jnp.exp(ending - columns)
        rows = x[at, :]
        cosine, sine = angles(coarse, fine, start, BLOCK)
        keys = turned(acc_k[at, :] + mm(rows, wk[...]), cosine, sine)
        k_out[at, :] = keys
        values = (acc_v[at, :] + mm(rows, wv[...])).astype(BF16)
        v_out[at, :] = values
        for head in range(heads):
            span = slice(head * DH, (head + 1) * DH)
            weighted = (keys[:, span].astype(F32) * faded[:, head : head + 1]).astype(BF16)
            old = state_out[span, :]
            before_out[block, span, :] = old.astype(BF16)
            state_out[span, :] = jnp.exp(ending[:, head : head + 1]) * old + mm_tn(weighted, values[:, span])
    states = [state_out[head * DH : (head + 1) * DH, :] for head in range(heads)]
    pack_message(message, states, block_ends(decay, 0, acc_k.shape[0]))
    for copy in others:
        copy.wait()


def combine_kernel(heads, hop, sets, first, last, state, sent, *refs):
    if not first:
        old_entering, refs = refs[0], refs[1:]
    arrivals, entering, message = refs[: len(sets)], refs[len(sets)], refs[len(sets) + 1]
    window_log, log = message_log(sent, heads), arrived_log(arrivals, sets, hop, heads)
    before_log = jnp.zeros_like(log) if first else old_entering[heads * DH :, :1]
    states = []
    for head in range(heads):
        span, row = slice(head * DH, (head + 1) * DH), slice(head, head + 1)
        arrived = arrived_state(arrivals, sets, hop, span)
        if first:
            entering[span, :] = arrived
        else:
            entering[span, :] = old_entering[span, :] + jnp.exp(before_log[row]) * arrived
        states.append(state[span, :] + jnp.exp(window_log[row]) * arrived)
        if last:
            message[span, :] = states[-1].astype(BF16)
        else:
            refs[len(sets) + 2][span, :] = states[-1]
    entering[heads * DH :, :] = jnp.broadcast_to(before_log + log, (8, DH))
    if not last:
        pack_message(message, states, window_log + log)


def query_gate_kernel(
    heads, block, x_own, x_other, wq, wq_far, wg, wg_far, decay, coarse, fine, k, v, q_out, g_out, intra_out
):
    start = block * BLOCK
    lines = decay[:, start : start + BLOCK]
    columns = lines.T

    at = slice(start, start + BLOCK)
    cosine, sine = angles(coarse, fine, start, BLOCK)
    own, far = x_own[at, :], x_other[at, :]
    queries = mm(own, wq[...]) + mm(far, wq_far[...])
    q_out[...] = turned(queries, cosine, sine)
    gates = mm(own, wg[...]) + mm(far, wg_far[...])
    gates = gates.astype(BF16).astype(F32)
    g_out[...] = gates / (1.0 + jnp.exp(-gates))
    for piece in range(BLOCK // TILE):
        low, last = piece * TILE, (piece + 1) * TILE
        place_t = lax.broadcasted_iota(jnp.int32, (TILE, last), 0) + low
        place_s = lax.broadcasted_iota(jnp.int32, (TILE, last), 1)
        causal = place_t >= place_s
        for head in range(heads):
            span = slice(head * DH, (head + 1) * DH)
            scores = mm_nt(q_out[low:last, span], k[start : start + last, span])
            differ = columns[low:last, head : head + 1] - lines[head : head + 1, :last]
            weights = jnp.where(causal, jnp.exp(jnp.where(causal, differ, 0.0)), 0.0)
            intra_out[low:last, span] = mm((scores * weights).astype(BF16), v[start : start + last, span])


def hidden_kernel(heads, hop, sets, role, first, decay, before, entering, *refs):
    arrivals, projected, out, token = refs[: len(sets)], refs[len(sets) : -2], refs[-2], refs[-1]
    token[...] = jnp.zeros_like(token)

    def piece(start):
        block = start // BLOCK
        q, gate, intra = projected[3 * block : 3 * block + 3]
        at = slice(start % BLOCK, start % BLOCK + TILE)
        columns = jnp.exp(decay[:, start : start + TILE].T)
        scales = jnp.exp(block_ends(decay, 0, block * BLOCK))
        for head in range(heads):
            span, row = slice(head * DH, (head + 1) * DH), slice(head, head + 1)
            fade = jnp.exp(entering[heads * DH + head : heads * DH + head + 1, :1])
            state = entering[span, :] + fade * arrived_state(arrivals, sets, hop, span)
            prior = (scales[row] * state + before[block, span, :].astype(F32)).astype(BF16)
            retained = intra[at, span] + columns[:, row] * mm(q[at, span], prior)
            center = retained - jnp.mean(retained, axis=1, keepdims=True)
            spread = jnp.mean(center * center, axis=1, keepdims=True)
            out[:, span] = (gate[at, span] * center * lax.rsqrt(spread + 1e-5)).astype(BF16)

    core, middle = lax.axis_index("fsdp"), decay.shape[1] // 2
    pl.when(core == role)(lambda: piece(first))
    pl.when(core != role)(lambda: piece(middle + first))


def columns_kernel(first, second, *outs):
    cols = outs[0].shape[1]
    place, core = lax.axis_index("tp"), lax.axis_index("fsdp")
    high, low = place // 2, place % 2

    @pl.when(core == 0)
    def _():
        at = pl.ds(pl.multiple_of((1 - low) * cols, cols), cols)
        outs[0][...] = first[:, at]
        outs[1][...] = second[:, at]

    @pl.when(core == 1)
    def _():
        for number, out in enumerate(outs):
            at = slice(number * cols, (number + 1) * cols)
            out[...] = jnp.where(high == 0, first[:, at], second[:, at])


def arrange_kernel(mine_0, mine_1, other_0, other_1, *outs):
    cols = mine_0.shape[1]
    place, core = lax.axis_index("tp"), lax.axis_index("fsdp")
    for role, (blocks, out) in enumerate(zip(((mine_0, mine_1), (other_0, other_1)), outs)):
        bit = jnp.where(core == role, place // 2, place % 2)
        out[:, :cols] = jnp.where(bit == 0, blocks[1][...], blocks[0][...])
        out[:, cols:] = jnp.where(bit == 0, blocks[0][...], blocks[1][...])


def own_kernel(order, own_first, own_second, *refs):
    pieces, outs = refs[: len(order)], refs[len(order) :]
    cols = pieces[0].shape[1]
    place, core = lax.axis_index("tp"), lax.axis_index("fsdp")
    high, low = place // 2, place % 2
    here = core == high
    mine = pl.ds(pl.multiple_of(low * cols, cols), cols)
    flipped = pl.ds(pl.multiple_of((1 - low) * cols, cols), cols)
    keep = jnp.where(here, own_first[:, mine], own_second[:, mine])
    low_give = jnp.where(here, own_second[:, mine], own_first[:, mine])
    high_give = jnp.where(here, own_first[:, flipped], own_second[:, flipped])
    gives = [jnp.where(core == role, low_give, high_give) for role in range(2)]
    for (role, number), piece in zip(order, pieces):
        at = slice(number * TILE, (number + 1) * TILE)
        outs[role][at, :cols] = mm(piece[...], gives[role])
        outs[role][at, cols:] = mm(piece[...], keep)


def give_kernel(number, own, far, weight, out):
    cols = out.shape[1]
    at = slice(number * TILE, (number + 1) * TILE)
    out[...] = (own[at, :cols] + mm(far[...], weight[:, :cols])).astype(BF16)


def keep_kernel(order, *refs):
    count = len(order)
    fars, owns, weights, outs = refs[:count], refs[count : count + 2], refs[count + 2 : count + 4], refs[count + 4 :]
    for (role, number), far in zip(order, fars):
        cols = far.shape[1]
        at = slice(number * TILE, (number + 1) * TILE)
        outs[role][at, :] = owns[role][at, cols:] + mm(far[...], weights[role][:, cols:])


def finish_kernel(order, *refs):
    count = len(order)
    gots, keeps, out, ready, written = refs[:count], refs[count : count + 2], refs[-3], refs[-2], refs[-1]
    core, copies = lax.axis_index("fsdp"), []
    for slot, ((role, number), got) in enumerate(zip(order, gots)):
        keep = keeps[role]
        at = slice(number * TILE, (number + 1) * TILE)
        ready[slot] = (keep[at, :] + got[...].astype(F32)).astype(BF16)
        start = pl.multiple_of((role + core) % 2 * keep.shape[0] + number * TILE, TILE)
        copies.append(pltpu.make_async_copy(ready.at[slot], out.at[0, pl.ds(start, TILE)], written.at[slot]))
        copies[-1].start()
    for copy in copies:
        copy.wait()


def after(value, *others):
    return lax.optimization_barrier((value, *others))[0]


def on_device(tokens, query_weight, key_weight, value_weight, gate_weight, out_weight, log_decay):
    x = tokens[0]
    rows, width = x.shape
    part, cols = query_weight.shape
    heads = cols // DH
    blocks = rows // BLOCK
    ctx, tp, cores = lax.axis_size("ctx"), lax.axis_size("tp"), lax.axis_size("fsdp")
    assert tp == 4 and cores == 2 and ctx >= 4 and ctx & (ctx - 1) == 0
    partners = [
        [(at * cores + core, (at ^ (1 << (role + core) % 2)) * cores + core) for at in range(tp) for core in range(cores)]
        for role in range(2)
    ]

    def trade(value, role):
        return lax.ppermute(value, ("tp", "fsdp"), partners[role])

    tables = [((2, rows // FINE, DH // 2), F32), ((2, FINE, DH // 2), F32)]

    key_far = swap(key_weight, "fsdp", 1)
    value_far = swap(value_weight, "fsdp", 1)

    x_own, x_other, acc_k, acc_v, decay, coarse, fine, out_first = loading_call(
        key_value_own_kernel,
        [((rows, part), BF16)] * 2 + [((rows, cols), F32)] * 2 + [((8, rows), F32)]
        + tables
        + [(out_weight.shape, BF16)],
        [x, key_weight, value_weight, log_decay[0].T, out_weight],
        [],
        [pltpu.VMEM((part, cols), BF16)] * 2 + [pltpu.VMEM((heads, rows), F32)],
        2 * (rows // BLOCK) + 4,
        "key_value_own",
    )
    state_shape, message_shape = (heads * DH, DH), (heads * DH + EXTRA, DH)
    own_q, own_g, keys, values, before, window, message = loading_call(
        functools.partial(key_value_kernel, heads),
        [((part, cols), BF16)] * 2
        + [((rows, cols), BF16)] * 2
        + [((blocks, heads * DH, DH), BF16), (state_shape, F32), (message_shape, BF16)],
        [query_weight, gate_weight],
        [x_other, key_far, value_far, acc_k, acc_v, decay, coarse, fine],
        [],
        2,
        "key_value",
    )
    far_q, far_g = swap(own_q, "fsdp", 1), swap(own_g, "fsdp", 1)

    def query_gate(block, decay):
        return kernel_call(
            functools.partial(query_gate_kernel, heads, block),
            [((BLOCK, cols), BF16), ((BLOCK, cols), F32), ((BLOCK, cols), F32)],
            [x_own, x_other, own_q, far_q, own_g, far_g, decay, coarse, fine, keys, values],
            "query_gate",
        )

    def exchange(message, lowers, hop, everyone=False):
        pairs = [(at, at + hop) for at in lowers]
        if everyone and hop == 1:
            pairs += [(ctx - 1, 0)]
        elif everyone:
            pairs += [(upper, at) for at, upper in pairs]
            busy = {at for pair in pairs for at in pair}
            pairs += [(at, at) for at in range(ctx) if at not in busy]
        return lax.ppermute(message, "ctx", pairs)

    projected = list(query_gate(0, decay))
    window = after(window, projected[0])
    entering, hop, early, first_message = None, 1, [], message
    while True:
        first_set, *later_sets = exchanges(ctx, hop)
        later_sets = [lowers for lowers in later_sets if lowers]
        sets = later_sets + ([first_set] if first_set else [])
        arrivals = [exchange(message, lowers, hop, everyone=hop == 1) for lowers in later_sets] + early
        if 2 * hop >= ctx:
            break
        unchanged = exchanges(ctx, 2 * hop)[0]
        early = [exchange(message, unchanged, 2 * hop, everyone=True)]
        old = [] if entering is None else [entering]
        last = 4 * hop >= ctx
        entering, message, *windows = kernel_call(
            functools.partial(combine_kernel, heads, hop, sets, entering is None, last),
            [((heads * DH + 8, DH), F32)]
            + ([(state_shape, BF16)] if last else [(message_shape, BF16), (state_shape, F32)]),
            [window, message, *old, *arrivals],
            "combine",
        )
        window = windows[0] if windows else None
        hop *= 2

    own_second = swap(out_first, "fsdp", 1)
    for_partner = kernel_call(
        columns_kernel,
        [((cols, cols), BF16)] * 2,
        [after(out_first, first_message), own_second],
        "columns",
    )
    out_mine = [trade(block, 0) for block in for_partner]

    held = after(decay, message, *early, out_mine[0])
    for block in range(1, blocks):
        projected += query_gate(block, held)

    count = rows // 2 // TILE
    hidden, far = [[], []], [[], []]
    token = None
    for number, role in [(number, role) for number in range(count) for role in range(2)]:
        held = decay if token is None else after(decay, swap(token, "fsdp", 1))
        piece, token = kernel_call(
            functools.partial(hidden_kernel, heads, hop, sets, role, number * TILE),
            [((TILE, cols), BF16), ((16, 128), BF16)],
            [held, before, entering, *arrivals, *projected],
            "hidden",
        )
        if number == 0 and role == 0:
            out_other = [swap(after(block, piece), "fsdp", 1) for block in out_mine]
        hidden[role].append(piece)
        far[role].append(trade(piece, role))
    weights = kernel_call(
        arrange_kernel,
        [((cols, 2 * cols), BF16)] * 2,
        [*out_mine, *out_other],
        "arrange",
    )
    order = [(role, number) for number in reversed(range(count)) for role in (1, 0)]
    owns = kernel_call(
        functools.partial(own_kernel, order),
        [((count * TILE, 2 * cols), F32)] * 2,
        [out_first, own_second, *(hidden[role][number] for role, number in order)],
        "own_products",
    )
    gots = []
    for role, number in order:
        [give] = kernel_call(
            functools.partial(give_kernel, number),
            [((TILE, cols), BF16)],
            [owns[role], far[role][number], weights[role]],
            "give",
        )
        gots.append(trade(give, 1 - role))
    keeps = kernel_call(
        functools.partial(keep_kernel, order),
        [((count * TILE, cols), F32)] * 2,
        [*(far[role][number] for role, number in order), *owns, *weights],
        "keep",
    )
    result = None
    for part_order, part_gots in ((order[2:], gots[2:]), (order[:2], gots[:2])):
        arrays = [pltpu.with_memory_space_constraint(array, pltpu.VMEM) for array in (*part_gots, *keeps)]
        held = [] if result is None else [result]
        result = pl.pallas_call(
            functools.partial(finish_kernel, part_order),
            in_specs=[pl.BlockSpec(memory_space=pltpu.VMEM)] * len(arrays)
            + [pl.BlockSpec(memory_space=pltpu.HBM)] * len(held),
            out_specs=pl.BlockSpec(memory_space=pltpu.HBM),
            out_shape=jax.ShapeDtypeStruct((1, rows, cols), BF16),
            input_output_aliases={len(arrays): 0} if held else {},
            scratch_shapes=[
                pltpu.VMEM((len(part_order), TILE, cols), BF16),
                pltpu.SemaphoreType.DMA((len(part_order),)),
            ],
            compiler_params=pltpu.CompilerParams(vmem_limit_bytes=VMEM_LIMIT),
            name="finish",
        )(*arrays, *held)
    return result


def solution(mesh):
    in_specs = (
        P("fsdp", "ctx", None),
        P("fsdp", "tp"),
        P("fsdp", "tp"),
        P("fsdp", "tp"),
        P("fsdp", "tp"),
        P("tp", "fsdp"),
        P("fsdp", "ctx", "tp"),
    )
    out_specs = P("fsdp", "ctx", "tp")
    return jax.shard_map(
        on_device, mesh=mesh, in_specs=in_specs, out_specs=out_specs, check_vma=False
    )
```

```python
import functools
import math

import jax
import jax.numpy as jnp
from jax import lax
from jax.experimental import pallas as pl
from jax.experimental.pallas import tpu as pltpu
from jax.sharding import PartitionSpec as P

DH = 256
BLOCK = 512
TILE = 256
FINE = 32
EXTRA = 16
VMEM_LIMIT = 14 * 1024 * 1024
F32 = jnp.float32
BF16 = jnp.bfloat16


def mm(left, right):
    return jnp.dot(left, right, preferred_element_type=F32)


def mm_nt(left, right):
    return lax.dot_general(left, right, (((1,), (1,)), ((), ())), preferred_element_type=F32)


def mm_tn(left, right):
    return lax.dot_general(left, right, (((0,), (0,)), ((), ())), preferred_element_type=F32)


def swap(value, axis, mask):
    size = lax.axis_size(axis)
    return lax.ppermute(value, axis, [(place, place ^ mask) for place in range(size)])


def kernel_call(kernel, outs, operands, name):
    arrays = [pltpu.with_memory_space_constraint(array, pltpu.VMEM) for array in operands]
    return pl.pallas_call(
        kernel,
        in_specs=[pl.BlockSpec(memory_space=pltpu.VMEM)] * len(operands),
        out_specs=[pl.BlockSpec(memory_space=pltpu.VMEM)] * len(outs),
        out_shape=[pltpu.VMEM(shape, dtype) for shape, dtype in outs],
        compiler_params=pltpu.CompilerParams(vmem_limit_bytes=VMEM_LIMIT),
        cost_estimate=pl.CostEstimate(
            flops=1, bytes_accessed=1, transcendentals=0
        ),
        name=name,
    )(*arrays)


def loading_call(kernel, outs, loaded, operands, scratch, loads, name):
    arrays = [pltpu.with_memory_space_constraint(array, pltpu.HBM) for array in loaded]
    arrays += [pltpu.with_memory_space_constraint(array, pltpu.VMEM) for array in operands]
    return pl.pallas_call(
        kernel,
        in_specs=[pl.BlockSpec(memory_space=pltpu.HBM)] * len(loaded)
        + [pl.BlockSpec(memory_space=pltpu.VMEM)] * len(operands),
        out_specs=[pl.BlockSpec(memory_space=pltpu.VMEM)] * len(outs),
        out_shape=[pltpu.VMEM(shape, dtype) for shape, dtype in outs],
        scratch_shapes=[*scratch, pltpu.SemaphoreType.DMA((loads,))],
        compiler_params=pltpu.CompilerParams(vmem_limit_bytes=VMEM_LIMIT),
        cost_estimate=pl.CostEstimate(flops=1, bytes_accessed=1, transcendentals=0),
        name=name,
    )(*arrays)


def turned(values, cosine, sine):
    half = DH // 2
    parts = []
    for start in range(0, values.shape[1], DH):
        low = values[:, start : start + half]
        high = values[:, start + half : start + DH]
        parts.append((low * cosine - high * sine).astype(BF16))
        parts.append((high * cosine + low * sine).astype(BF16))
    return jnp.concatenate(parts, axis=1)


def angles(coarse, fine, first, count):
    at = first // FINE
    far = coarse[:, pl.ds(at, count // FINE), :]
    near = fine[...]
    cos_c, sin_c = far[0][:, None, :], far[1][:, None, :]
    cos_f, sin_f = near[0][None], near[1][None]
    cosine = cos_c * cos_f - sin_c * sin_f
    sine = sin_c * cos_f + cos_c * sin_f
    return cosine.reshape(count, DH // 2), sine.reshape(count, DH // 2)


def decay_sums(log_decay, decay):
    heads, rows = log_decay.shape
    place_s = lax.broadcasted_iota(jnp.int32, (BLOCK, BLOCK), 0)
    place_t = lax.broadcasted_iota(jnp.int32, (BLOCK, BLOCK), 1)
    upper = jnp.where(place_s <= place_t, 1.0, 0.0).astype(BF16)
    value = jnp.concatenate([log_decay[...], jnp.zeros((8 - heads, rows), F32)], axis=0)
    parts = []
    for _ in range(3):
        parts.append(value.astype(BF16))
        value = value - parts[-1].astype(F32)
    stacked = jnp.concatenate([part.astype(F32) for part in parts], axis=0).astype(BF16)
    for start in range(0, rows, BLOCK):
        sums = mm(stacked[:, start : start + BLOCK], upper)
        decay[:, start : start + BLOCK] = sums[:8] + sums[8:16] + sums[16:]


def turn(first, second):
    (cos_a, sin_a), (cos_b, sin_b) = first, second
    return cos_a * cos_b - sin_a * sin_b, sin_a * cos_b + cos_a * sin_b


def joined(first, second):
    return tuple(jnp.concatenate(pair, axis=0) for pair in zip(first, second))


def angle_tables(coarse, fine):
    half, seeds = DH // 2, 8
    index = lax.broadcasted_iota(jnp.int32, (seeds, half), 1).astype(F32)
    frequency = jnp.exp(index * (-math.log(10000.0) / half))
    place = lax.broadcasted_iota(jnp.int32, (seeds, half), 0).astype(F32)
    offset = (lax.axis_index("ctx") * (coarse.shape[1] * FINE)).astype(F32)
    near = jnp.cos(place * frequency), jnp.sin(place * frequency)
    base = jnp.cos(offset * frequency), jnp.sin(offset * frequency)
    step = turn([part[seeds - 1 : seeds] for part in near], [part[1:2] for part in near])
    while near[0].shape[0] < FINE:
        near = joined(near, turn(near, step))
        step = turn(step, step)
    far = tuple(part[:1] for part in base)
    while far[0].shape[0] < coarse.shape[1]:
        far = joined(far, turn(far, step))
        step = turn(step, step)
    for table, parts in ((coarse, far), (fine, near)):
        table[0], table[1] = (part[: table.shape[1]] for part in parts)


class Loads:
    def __init__(self, arrived):
        self.arrived, self.count = arrived, 0

    def start(self, source, target):
        copy = pltpu.make_async_copy(source, target, self.arrived.at[self.count])
        self.count += 1
        copy.start()
        return copy


def key_value_own_kernel(
    x_far, wk_far, wv_far, log_decay_far, wo_far,
    x_own, x_other, acc_k, acc_v, decay, coarse, fine, wo, wk, wv, log_decay, arrived,
):
    rows, part = x_own.shape
    core = lax.axis_index("fsdp")
    loads = Loads(arrived)

    def tile(x, half, start):
        at = pl.ds(start, BLOCK)
        columns = pl.ds(pl.multiple_of(half * part, part), part)
        return loads.start(x_far.at[at, columns], x.at[at])

    starts = range(0, rows, BLOCK)
    key, logs = loads.start(wk_far, wk), loads.start(log_decay_far, log_decay)
    tiles = [tile(x_own, core, start) for start in starts]
    value = loads.start(wv_far, wv)
    others = [tile(x_other, 1 - core, start) for start in starts] + [loads.start(wo_far, wo)]
    angle_tables(coarse, fine)
    logs.wait()
    decay_sums(log_decay, decay)
    key.wait()
    for copy, start in zip(tiles, starts):
        at = slice(start, start + BLOCK)
        copy.wait()
        acc_k[at, :] = mm(x_own[at, :], wk[...])
    value.wait()
    for start in starts:
        at = slice(start, start + BLOCK)
        acc_v[at, :] = mm(x_own[at, :], wv[...])
    for copy in others:
        copy.wait()


def block_ends(decay, start, stop):
    ends = [decay[:, end - 1 : end] for end in range(start + BLOCK, stop + 1, BLOCK)]
    return functools.reduce(lambda a, b: a + b, ends, jnp.zeros((decay.shape[0], 1), F32))


def pack_message(message, states, logs):
    for head, state in enumerate(states):
        message[head * DH : (head + 1) * DH, :] = state.astype(BF16)
    large = logs.astype(BF16).astype(F32)
    parts = jnp.concatenate([large, logs - large], axis=0)
    message[len(states) * DH :, :] = jnp.broadcast_to(parts, (EXTRA, DH)).astype(BF16)


def message_log(message, heads):
    tail = message[heads * DH :, :].astype(F32)
    return (tail[: EXTRA // 2] + tail[EXTRA // 2 :])[:, :1]


def exchanges(ctx, hop):
    lower = range(ctx - hop)
    if hop == 1:
        return [], list(lower), []
    early = [at for at in lower if at < hop // 2]
    even = [at for at in lower if at >= hop // 2 and at // hop % 2 == 0]
    odd = [at for at in lower if at // hop % 2 == 1]
    return early, even, odd


def is_upper(lowers, hop):
    place = lax.axis_index("ctx")
    found = place < 0
    for lower in lowers:
        found = jnp.logical_or(found, place == lower + hop)
    return found


def arrived_state(arrivals, sets, hop, span):
    parts = [jnp.where(is_upper(lowers, hop), ref[span, :].astype(F32), 0.0) for ref, lowers in zip(arrivals, sets)]
    return functools.reduce(lambda a, b: a + b, parts)


def arrived_log(arrivals, sets, hop, heads):
    parts = [jnp.where(is_upper(lowers, hop), message_log(ref, heads), 0.0) for ref, lowers in zip(arrivals, sets)]
    return functools.reduce(lambda a, b: a + b, parts)


def key_value_kernel(
    heads, wq_far, wg_far, x, wk, wv, acc_k, acc_v, decay, coarse, fine,
    wq, wg, k_out, v_out, before_out, state_out, message, arrived,
):
    loads = Loads(arrived)
    others = [loads.start(wq_far, wq), loads.start(wg_far, wg)]
    blocks = acc_k.shape[0] // BLOCK
    state_out[...] = jnp.zeros_like(state_out)
    for block in range(blocks):
        start = block * BLOCK
        at = slice(start, start + BLOCK)
        columns = decay[:, at].T
        ending = columns[BLOCK - 1 : BLOCK, :]
        faded = jnp.exp(ending - columns)
        rows = x[at, :]
        cosine, sine = angles(coarse, fine, start, BLOCK)
        keys = turned(acc_k[at, :] + mm(rows, wk[...]), cosine, sine)
        k_out[at, :] = keys
        values = (acc_v[at, :] + mm(rows, wv[...])).astype(BF16)
        v_out[at, :] = values
        for head in range(heads):
            span = slice(head * DH, (head + 1) * DH)
            weighted = (keys[:, span].astype(F32) * faded[:, head : head + 1]).astype(BF16)
            old = state_out[span, :]
            before_out[block, span, :] = old.astype(BF16)
            state_out[span, :] = jnp.exp(ending[:, head : head + 1]) * old + mm_tn(weighted, values[:, span])
    states = [state_out[head * DH : (head + 1) * DH, :] for head in range(heads)]
    pack_message(message, states, block_ends(decay, 0, acc_k.shape[0]))
    for copy in others:
        copy.wait()


def combine_kernel(heads, hop, sets, first, last, state, sent, *refs):
    if not first:
        old_entering, refs = refs[0], refs[1:]
    arrivals, entering, message = refs[: len(sets)], refs[len(sets)], refs[len(sets) + 1]
    window_log, log = message_log(sent, heads), arrived_log(arrivals, sets, hop, heads)
    before_log = jnp.zeros_like(log) if first else old_entering[heads * DH :, :1]
    states = []
    for head in range(heads):
        span, row = slice(head * DH, (head + 1) * DH), slice(head, head + 1)
        arrived = arrived_state(arrivals, sets, hop, span)
        if first:
            entering[span, :] = arrived
        else:
            entering[span, :] = old_entering[span, :] + jnp.exp(before_log[row]) * arrived
        states.append(state[span, :] + jnp.exp(window_log[row]) * arrived)
        if last:
            message[span, :] = states[-1].astype(BF16)
        else:
            refs[len(sets) + 2][span, :] = states[-1]
    entering[heads * DH :, :] = jnp.broadcast_to(before_log + log, (8, DH))
    if not last:
        pack_message(message, states, window_log + log)


def query_gate_kernel(
    heads, block, x_own, x_other, wq, wq_far, wg, wg_far, decay, coarse, fine, k, v, q_out, g_out, intra_out
):
    start = block * BLOCK
    lines = decay[:, start : start + BLOCK]
    columns = lines.T

    at = slice(start, start + BLOCK)
    cosine, sine = angles(coarse, fine, start, BLOCK)
    own, far = x_own[at, :], x_other[at, :]
    queries = mm(own, wq[...]) + mm(far, wq_far[...])
    q_out[...] = turned(queries, cosine, sine)
    gates = mm(own, wg[...]) + mm(far, wg_far[...])
    gates = gates.astype(BF16).astype(F32)
    g_out[...] = gates / (1.0 + jnp.exp(-gates))
    for piece in range(BLOCK // TILE):
        low, last = piece * TILE, (piece + 1) * TILE
        place_t = lax.broadcasted_iota(jnp.int32, (TILE, last), 0) + low
        place_s = lax.broadcasted_iota(jnp.int32, (TILE, last), 1)
        causal = place_t >= place_s
        for head in range(heads):
            span = slice(head * DH, (head + 1) * DH)
            scores = mm_nt(q_out[low:last, span], k[start : start + last, span])
            differ = columns[low:last, head : head + 1] - lines[head : head + 1, :last]
            weights = jnp.where(causal, jnp.exp(jnp.where(causal, differ, 0.0)), 0.0)
            intra_out[low:last, span] = mm((scores * weights).astype(BF16), v[start : start + last, span])


def hidden_kernel(heads, hop, sets, role, first, decay, before, entering, *refs):
    arrivals, projected, out, token = refs[: len(sets)], refs[len(sets) : -2], refs[-2], refs[-1]
    token[...] = jnp.zeros_like(token)

    def piece(start):
        block = start // BLOCK
        q, gate, intra = projected[3 * block : 3 * block + 3]
        at = slice(start % BLOCK, start % BLOCK + TILE)
        columns = jnp.exp(decay[:, start : start + TILE].T)
        scales = jnp.exp(block_ends(decay, 0, block * BLOCK))
        for head in range(heads):
            span, row = slice(head * DH, (head + 1) * DH), slice(head, head + 1)
            fade = jnp.exp(entering[heads * DH + head : heads * DH + head + 1, :1])
            state = entering[span, :] + fade * arrived_state(arrivals, sets, hop, span)
            prior = (scales[row] * state + before[block, span, :].astype(F32)).astype(BF16)
            retained = intra[at, span] + columns[:, row] * mm(q[at, span], prior)
            center = retained - jnp.mean(retained, axis=1, keepdims=True)
            spread = jnp.mean(center * center, axis=1, keepdims=True)
            out[:, span] = (gate[at, span] * center * lax.rsqrt(spread + 1e-5)).astype(BF16)

    core, middle = lax.axis_index("fsdp"), decay.shape[1] // 2
    pl.when(core == role)(lambda: piece(first))
    pl.when(core != role)(lambda: piece(middle + first))


def columns_kernel(first, second, *outs):
    cols = outs[0].shape[1]
    place, core = lax.axis_index("tp"), lax.axis_index("fsdp")
    high, low = place // 2, place % 2

    @pl.when(core == 0)
    def _():
        at = pl.ds(pl.multiple_of((1 - low) * cols, cols), cols)
        outs[0][...] = first[:, at]
        outs[1][...] = second[:, at]

    @pl.when(core == 1)
    def _():
        for number, out in enumerate(outs):
            at = slice(number * cols, (number + 1) * cols)
            out[...] = jnp.where(high == 0, first[:, at], second[:, at])


def arrange_kernel(mine_0, mine_1, other_0, other_1, *outs):
    cols = mine_0.shape[1]
    place, core = lax.axis_index("tp"), lax.axis_index("fsdp")
    for role, (blocks, out) in enumerate(zip(((mine_0, mine_1), (other_0, other_1)), outs)):
        bit = jnp.where(core == role, place // 2, place % 2)
        out[:, :cols] = jnp.where(bit == 0, blocks[1][...], blocks[0][...])
        out[:, cols:] = jnp.where(bit == 0, blocks[0][...], blocks[1][...])


def own_kernel(order, own_first, own_second, *refs):
    pieces, outs = refs[: len(order)], refs[len(order) :]
    cols = pieces[0].shape[1]
    place, core = lax.axis_index("tp"), lax.axis_index("fsdp")
    high, low = place // 2, place % 2
    here = core == high
    mine = pl.ds(pl.multiple_of(low * cols, cols), cols)
    flipped = pl.ds(pl.multiple_of((1 - low) * cols, cols), cols)
    keep = jnp.where(here, own_first[:, mine], own_second[:, mine])
    low_give = jnp.where(here, own_second[:, mine], own_first[:, mine])
    high_give = jnp.where(here, own_first[:, flipped], own_second[:, flipped])
    gives = [jnp.where(core == role, low_give, high_give) for role in range(2)]
    for (role, number), piece in zip(order, pieces):
        at = slice(number * TILE, (number + 1) * TILE)
        outs[role][at, :cols] = mm(piece[...], gives[role])
        outs[role][at, cols:] = mm(piece[...], keep)


def give_kernel(number, own, far, weight, out):
    cols = out.shape[1]
    at = slice(number * TILE, (number + 1) * TILE)
    out[...] = (own[at, :cols] + mm(far[...], weight[:, :cols])).astype(BF16)


def keep_kernel(order, *refs):
    count = len(order)
    fars, owns, weights, outs = refs[:count], refs[count : count + 2], refs[count + 2 : count + 4], refs[count + 4 :]
    for (role, number), far in zip(order, fars):
        cols = far.shape[1]
        at = slice(number * TILE, (number + 1) * TILE)
        outs[role][at, :] = owns[role][at, cols:] + mm(far[...], weights[role][:, cols:])


def finish_kernel(order, *refs):
    count = len(order)
    gots, keeps, out, ready, written = refs[:count], refs[count : count + 2], refs[-3], refs[-2], refs[-1]
    core, copies = lax.axis_index("fsdp"), []
    for slot, ((role, number), got) in enumerate(zip(order, gots)):
        keep = keeps[role]
        at = slice(number * TILE, (number + 1) * TILE)
        ready[slot] = (keep[at, :] + got[...].astype(F32)).astype(BF16)
        start = pl.multiple_of((role + core) % 2 * keep.shape[0] + number * TILE, TILE)
        copies.append(pltpu.make_async_copy(ready.at[slot], out.at[0, pl.ds(start, TILE)], written.at[slot]))
        copies[-1].start()
    for copy in copies:
        copy.wait()


def after(value, *others):
    return lax.optimization_barrier((value, *others))[0]


def on_device(tokens, query_weight, key_weight, value_weight, gate_weight, out_weight, log_decay):
    x = tokens[0]
    rows, width = x.shape
    part, cols = query_weight.shape
    heads = cols // DH
    blocks = rows // BLOCK
    ctx, tp, cores = lax.axis_size("ctx"), lax.axis_size("tp"), lax.axis_size("fsdp")
    assert tp == 4 and cores == 2 and ctx >= 4 and ctx & (ctx - 1) == 0
    partners = [
        [(at * cores + core, (at ^ (1 << (role + core) % 2)) * cores + core) for at in range(tp) for core in range(cores)]
        for role in range(2)
    ]

    def trade(value, role):
        return lax.ppermute(value, ("tp", "fsdp"), partners[role])

    tables = [((2, rows // FINE, DH // 2), F32), ((2, FINE, DH // 2), F32)]

    key_far = swap(key_weight, "fsdp", 1)
    value_far = swap(value_weight, "fsdp", 1)

    x_own, x_other, acc_k, acc_v, decay, coarse, fine, out_first = loading_call(
        key_value_own_kernel,
        [((rows, part), BF16)] * 2 + [((rows, cols), F32)] * 2 + [((8, rows), F32)]
        + tables
        + [(out_weight.shape, BF16)],
        [x, key_weight, value_weight, log_decay[0].T, out_weight],
        [],
        [pltpu.VMEM((part, cols), BF16)] * 2 + [pltpu.VMEM((heads, rows), F32)],
        2 * (rows // BLOCK) + 4,
        "key_value_own",
    )
    state_shape, message_shape = (heads * DH, DH), (heads * DH + EXTRA, DH)
    own_q, own_g, keys, values, before, window, message = loading_call(
        functools.partial(key_value_kernel, heads),
        [((part, cols), BF16)] * 2
        + [((rows, cols), BF16)] * 2
        + [((blocks, heads * DH, DH), BF16), (state_shape, F32), (message_shape, BF16)],
        [query_weight, gate_weight],
        [x_other, key_far, value_far, acc_k, acc_v, decay, coarse, fine],
        [],
        2,
        "key_value",
    )
    far_q, far_g = swap(own_q, "fsdp", 1), swap(own_g, "fsdp", 1)

    def query_gate(block, decay):
        return kernel_call(
            functools.partial(query_gate_kernel, heads, block),
            [((BLOCK, cols), BF16), ((BLOCK, cols), F32), ((BLOCK, cols), F32)],
            [x_own, x_other, own_q, far_q, own_g, far_g, decay, coarse, fine, keys, values],
            "query_gate",
        )

    def exchange(message, lowers, hop, two_way=True):
        pairs = [(at, at + hop) for at in lowers]
        if two_way:
            pairs += [(upper, at) for at, upper in pairs] if hop > 1 else [(ctx - 1, 0)]
        return lax.ppermute(message, "ctx", pairs)

    projected = list(query_gate(0, decay))
    window = after(window, projected[0])
    entering, hop, early, first_message = None, 1, [], message
    while True:
        first_set, *later_sets = exchanges(ctx, hop)
        later_sets = [lowers for lowers in later_sets if lowers]
        sets = later_sets + ([first_set] if first_set else [])
        late = after(message, *early) if early else message
        arrivals = [exchange(late, lowers, hop) for lowers in later_sets] + early
        if 2 * hop >= ctx:
            break
        unchanged = exchanges(ctx, 2 * hop)[0]
        early = [exchange(message, unchanged, 2 * hop, two_way=False)]
        old = [] if entering is None else [entering]
        last = 4 * hop >= ctx
        entering, message, *windows = kernel_call(
            functools.partial(combine_kernel, heads, hop, sets, entering is None, last),
            [((heads * DH + 8, DH), F32)]
            + ([(state_shape, BF16)] if last else [(message_shape, BF16), (state_shape, F32)]),
            [window, message, *old, *arrivals],
            "combine",
        )
        window = windows[0] if windows else None
        hop *= 2

    own_second = swap(out_first, "fsdp", 1)
    for_partner = kernel_call(
        columns_kernel,
        [((cols, cols), BF16)] * 2,
        [after(out_first, first_message), own_second],
        "columns",
    )
    out_mine = [trade(block, 0) for block in for_partner]

    held = after(decay, message, *early, out_mine[0])
    for block in range(1, blocks):
        projected += query_gate(block, held)

    count = rows // 2 // TILE
    hidden, far = [[], []], [[], []]
    token = None
    for number, role in [(number, role) for number in range(count) for role in range(2)]:
        held = decay if token is None else after(decay, swap(token, "fsdp", 1))
        piece, token = kernel_call(
            functools.partial(hidden_kernel, heads, hop, sets, role, number * TILE),
            [((TILE, cols), BF16), ((16, 128), BF16)],
            [held, before, entering, *arrivals, *projected],
            "hidden",
        )
        if number == 0 and role == 0:
            out_other = [swap(after(block, piece), "fsdp", 1) for block in out_mine]
        hidden[role].append(piece)
        far[role].append(trade(piece, role))
    weights = kernel_call(
        arrange_kernel,
        [((cols, 2 * cols), BF16)] * 2,
        [*out_mine, *out_other],
        "arrange",
    )
    order = [(role, number) for number in reversed(range(count)) for role in (1, 0)]
    owns = kernel_call(
        functools.partial(own_kernel, order),
        [((count * TILE, 2 * cols), F32)] * 2,
        [out_first, own_second, *(hidden[role][number] for role, number in order)],
        "own_products",
    )
    gots = []
    for role, number in order:
        [give] = kernel_call(
            functools.partial(give_kernel, number),
            [((TILE, cols), BF16)],
            [owns[role], far[role][number], weights[role]],
            "give",
        )
        gots.append(trade(give, 1 - role))
    keeps = kernel_call(
        functools.partial(keep_kernel, order),
        [((count * TILE, cols), F32)] * 2,
        [*(far[role][number] for role, number in order), *owns, *weights],
        "keep",
    )
    result = None
    for part_order, part_gots in ((order[2:], gots[2:]), (order[:2], gots[:2])):
        arrays = [pltpu.with_memory_space_constraint(array, pltpu.VMEM) for array in (*part_gots, *keeps)]
        held = [] if result is None else [result]
        result = pl.pallas_call(
            functools.partial(finish_kernel, part_order),
            in_specs=[pl.BlockSpec(memory_space=pltpu.VMEM)] * len(arrays)
            + [pl.BlockSpec(memory_space=pltpu.HBM)] * len(held),
            out_specs=pl.BlockSpec(memory_space=pltpu.HBM),
            out_shape=jax.ShapeDtypeStruct((1, rows, cols), BF16),
            input_output_aliases={len(arrays): 0} if held else {},
            scratch_shapes=[
                pltpu.VMEM((len(part_order), TILE, cols), BF16),
                pltpu.SemaphoreType.DMA((len(part_order),)),
            ],
            compiler_params=pltpu.CompilerParams(vmem_limit_bytes=VMEM_LIMIT),
            name="finish",
        )(*arrays, *held)
    return result


def solution(mesh):
    in_specs = (
        P("fsdp", "ctx", None),
        P("fsdp", "tp"),
        P("fsdp", "tp"),
        P("fsdp", "tp"),
        P("fsdp", "tp"),
        P("tp", "fsdp"),
        P("fsdp", "ctx", "tp"),
    )
    out_specs = P("fsdp", "ctx", "tp")
    return jax.shard_map(
        on_device, mesh=mesh, in_specs=in_specs, out_specs=out_specs, check_vma=False
    )
```

```python
import functools
import math

import jax
import jax.numpy as jnp
from jax import lax
from jax.experimental import pallas as pl
from jax.experimental.pallas import tpu as pltpu
from jax.sharding import PartitionSpec as P

DH = 256
BLOCK = 512
TILE = 256
FINE = 32
EXTRA = 16
VMEM_LIMIT = 14 * 1024 * 1024
F32 = jnp.float32
BF16 = jnp.bfloat16


def mm(left, right):
    return jnp.dot(left, right, preferred_element_type=F32)


def mm_nt(left, right):
    return lax.dot_general(left, right, (((1,), (1,)), ((), ())), preferred_element_type=F32)


def mm_tn(left, right):
    return lax.dot_general(left, right, (((0,), (0,)), ((), ())), preferred_element_type=F32)


def swap(value, axis, mask):
    size = lax.axis_size(axis)
    return lax.ppermute(value, axis, [(place, place ^ mask) for place in range(size)])


def kernel_call(kernel, outs, operands, name):
    arrays = [pltpu.with_memory_space_constraint(array, pltpu.VMEM) for array in operands]
    return pl.pallas_call(
        kernel,
        in_specs=[pl.BlockSpec(memory_space=pltpu.VMEM)] * len(operands),
        out_specs=[pl.BlockSpec(memory_space=pltpu.VMEM)] * len(outs),
        out_shape=[pltpu.VMEM(shape, dtype) for shape, dtype in outs],
        compiler_params=pltpu.CompilerParams(vmem_limit_bytes=VMEM_LIMIT),
        cost_estimate=pl.CostEstimate(
            flops=1, bytes_accessed=1, transcendentals=0
        ),
        name=name,
    )(*arrays)


def loading_call(kernel, outs, loaded, operands, scratch, loads, name):
    arrays = [pltpu.with_memory_space_constraint(array, pltpu.HBM) for array in loaded]
    arrays += [pltpu.with_memory_space_constraint(array, pltpu.VMEM) for array in operands]
    return pl.pallas_call(
        kernel,
        in_specs=[pl.BlockSpec(memory_space=pltpu.HBM)] * len(loaded)
        + [pl.BlockSpec(memory_space=pltpu.VMEM)] * len(operands),
        out_specs=[pl.BlockSpec(memory_space=pltpu.VMEM)] * len(outs),
        out_shape=[pltpu.VMEM(shape, dtype) for shape, dtype in outs],
        scratch_shapes=[*scratch, pltpu.SemaphoreType.DMA((loads,))],
        compiler_params=pltpu.CompilerParams(vmem_limit_bytes=VMEM_LIMIT),
        cost_estimate=pl.CostEstimate(flops=1, bytes_accessed=1, transcendentals=0),
        name=name,
    )(*arrays)


def turned(values, cosine, sine):
    half = DH // 2
    parts = []
    for start in range(0, values.shape[1], DH):
        low = values[:, start : start + half]
        high = values[:, start + half : start + DH]
        parts.append((low * cosine - high * sine).astype(BF16))
        parts.append((high * cosine + low * sine).astype(BF16))
    return jnp.concatenate(parts, axis=1)


def angles(coarse, fine, first, count):
    at = first // FINE
    far = coarse[:, pl.ds(at, count // FINE), :]
    near = fine[...]
    cos_c, sin_c = far[0][:, None, :], far[1][:, None, :]
    cos_f, sin_f = near[0][None], near[1][None]
    cosine = cos_c * cos_f - sin_c * sin_f
    sine = sin_c * cos_f + cos_c * sin_f
    return cosine.reshape(count, DH // 2), sine.reshape(count, DH // 2)


def decay_sums(log_decay, decay):
    heads, rows = log_decay.shape
    place_s = lax.broadcasted_iota(jnp.int32, (BLOCK, BLOCK), 0)
    place_t = lax.broadcasted_iota(jnp.int32, (BLOCK, BLOCK), 1)
    upper = jnp.where(place_s <= place_t, 1.0, 0.0).astype(BF16)
    value = jnp.concatenate([log_decay[...], jnp.zeros((8 - heads, rows), F32)], axis=0)
    parts = []
    for _ in range(3):
        parts.append(value.astype(BF16))
        value = value - parts[-1].astype(F32)
    stacked = jnp.concatenate([part.astype(F32) for part in parts], axis=0).astype(BF16)
    for start in range(0, rows, BLOCK):
        sums = mm(stacked[:, start : start + BLOCK], upper)
        decay[:, start : start + BLOCK] = sums[:8] + sums[8:16] + sums[16:]


def turn(first, second):
    (cos_a, sin_a), (cos_b, sin_b) = first, second
    return cos_a * cos_b - sin_a * sin_b, sin_a * cos_b + cos_a * sin_b


def joined(first, second):
    return tuple(jnp.concatenate(pair, axis=0) for pair in zip(first, second))


def angle_tables(coarse, fine):
    half, seeds = DH // 2, 8
    index = lax.broadcasted_iota(jnp.int32, (seeds, half), 1).astype(F32)
    frequency = jnp.exp(index * (-math.log(10000.0) / half))
    place = lax.broadcasted_iota(jnp.int32, (seeds, half), 0).astype(F32)
    offset = (lax.axis_index("ctx") * (coarse.shape[1] * FINE)).astype(F32)
    near = jnp.cos(place * frequency), jnp.sin(place * frequency)
    base = jnp.cos(offset * frequency), jnp.sin(offset * frequency)
    step = turn([part[seeds - 1 : seeds] for part in near], [part[1:2] for part in near])
    while near[0].shape[0] < FINE:
        near = joined(near, turn(near, step))
        step = turn(step, step)
    far = tuple(part[:1] for part in base)
    while far[0].shape[0] < coarse.shape[1]:
        far = joined(far, turn(far, step))
        step = turn(step, step)
    for table, parts in ((coarse, far), (fine, near)):
        table[0], table[1] = (part[: table.shape[1]] for part in parts)


class Loads:
    def __init__(self, arrived):
        self.arrived, self.count = arrived, 0

    def start(self, source, target):
        copy = pltpu.make_async_copy(source, target, self.arrived.at[self.count])
        self.count += 1
        copy.start()
        return copy


def key_value_own_kernel(
    x_far, wk_far, wv_far, log_decay_far, wo_far,
    x_own, x_other, acc_k, acc_v, decay, coarse, fine, wo, wk, wv, log_decay, arrived,
):
    rows, part = x_own.shape
    core = lax.axis_index("fsdp")
    loads = Loads(arrived)

    def tile(x, half, start):
        at = pl.ds(start, BLOCK)
        columns = pl.ds(pl.multiple_of(half * part, part), part)
        return loads.start(x_far.at[at, columns], x.at[at])

    starts = range(0, rows, BLOCK)
    key, logs = loads.start(wk_far, wk), loads.start(log_decay_far, log_decay)
    tiles = [tile(x_own, core, start) for start in starts]
    value = loads.start(wv_far, wv)
    others = [tile(x_other, 1 - core, start) for start in starts] + [loads.start(wo_far, wo)]
    angle_tables(coarse, fine)
    logs.wait()
    decay_sums(log_decay, decay)
    key.wait()
    for copy, start in zip(tiles, starts):
        at = slice(start, start + BLOCK)
        copy.wait()
        acc_k[at, :] = mm(x_own[at, :], wk[...])
    value.wait()
    for start in starts:
        at = slice(start, start + BLOCK)
        acc_v[at, :] = mm(x_own[at, :], wv[...])
    for copy in others:
        copy.wait()


def block_ends(decay, start, stop):
    ends = [decay[:, end - 1 : end] for end in range(start + BLOCK, stop + 1, BLOCK)]
    return functools.reduce(lambda a, b: a + b, ends, jnp.zeros((decay.shape[0], 1), F32))


def pack_message(message, states, logs):
    for head, state in enumerate(states):
        message[head * DH : (head + 1) * DH, :] = state.astype(BF16)
    large = logs.astype(BF16).astype(F32)
    parts = jnp.concatenate([large, logs - large], axis=0)
    message[len(states) * DH :, :] = jnp.broadcast_to(parts, (EXTRA, DH)).astype(BF16)


def message_log(message, heads):
    tail = message[heads * DH :, :].astype(F32)
    return (tail[: EXTRA // 2] + tail[EXTRA // 2 :])[:, :1]


def exchanges(ctx, hop):
    lower = range(ctx - hop)
    if hop == 1:
        return [], list(lower), []
    early = [at for at in lower if at < hop // 2]
    even = [at for at in lower if at >= hop // 2 and at // hop % 2 == 0]
    odd = [at for at in lower if at // hop % 2 == 1]
    return early, even, odd


def is_upper(lowers, hop):
    place = lax.axis_index("ctx")
    found = place < 0
    for lower in lowers:
        found = jnp.logical_or(found, place == lower + hop)
    return found


def arrived_state(arrivals, sets, hop, span):
    parts = [jnp.where(is_upper(lowers, hop), ref[span, :].astype(F32), 0.0) for ref, lowers in zip(arrivals, sets)]
    return functools.reduce(lambda a, b: a + b, parts)


def arrived_log(arrivals, sets, hop, heads):
    parts = [jnp.where(is_upper(lowers, hop), message_log(ref, heads), 0.0) for ref, lowers in zip(arrivals, sets)]
    return functools.reduce(lambda a, b: a + b, parts)


def key_value_kernel(
    heads, wq_far, wg_far, x, wk, wv, acc_k, acc_v, decay, coarse, fine,
    wq, wg, k_out, v_out, before_out, state_out, message, arrived,
):
    loads = Loads(arrived)
    others = [loads.start(wq_far, wq), loads.start(wg_far, wg)]
    blocks = acc_k.shape[0] // BLOCK
    state_out[...] = jnp.zeros_like(state_out)
    for block in range(blocks):
        start = block * BLOCK
        at = slice(start, start + BLOCK)
        columns = decay[:, at].T
        ending = columns[BLOCK - 1 : BLOCK, :]
        faded = jnp.exp(ending - columns)
        rows = x[at, :]
        cosine, sine = angles(coarse, fine, start, BLOCK)
        keys = turned(acc_k[at, :] + mm(rows, wk[...]), cosine, sine)
        k_out[at, :] = keys
        values = (acc_v[at, :] + mm(rows, wv[...])).astype(BF16)
        v_out[at, :] = values
        for head in range(heads):
            span = slice(head * DH, (head + 1) * DH)
            weighted = (keys[:, span].astype(F32) * faded[:, head : head + 1]).astype(BF16)
            old = state_out[span, :]
            before_out[block, span, :] = old.astype(BF16)
            state_out[span, :] = jnp.exp(ending[:, head : head + 1]) * old + mm_tn(weighted, values[:, span])
    states = [state_out[head * DH : (head + 1) * DH, :] for head in range(heads)]
    pack_message(message, states, block_ends(decay, 0, acc_k.shape[0]))
    for copy in others:
        copy.wait()


def combine_kernel(heads, hop, sets, first, last, state, sent, *refs):
    if not first:
        old_entering, refs = refs[0], refs[1:]
    arrivals, entering, message = refs[: len(sets)], refs[len(sets)], refs[len(sets) + 1]
    window_log, log = message_log(sent, heads), arrived_log(arrivals, sets, hop, heads)
    before_log = jnp.zeros_like(log) if first else old_entering[heads * DH :, :1]
    states = []
    for head in range(heads):
        span, row = slice(head * DH, (head + 1) * DH), slice(head, head + 1)
        arrived = arrived_state(arrivals, sets, hop, span)
        if first:
            entering[span, :] = arrived
        else:
            entering[span, :] = old_entering[span, :] + jnp.exp(before_log[row]) * arrived
        states.append(state[span, :] + jnp.exp(window_log[row]) * arrived)
        if last:
            message[span, :] = states[-1].astype(BF16)
        else:
            refs[len(sets) + 2][span, :] = states[-1]
    entering[heads * DH :, :] = jnp.broadcast_to(before_log + log, (8, DH))
    if not last:
        pack_message(message, states, window_log + log)


def query_gate_kernel(
    heads, block, x_own, x_other, wq, wq_far, wg, wg_far, decay, coarse, fine, k, v, q_out, g_out, intra_out
):
    start = block * BLOCK
    lines = decay[:, start : start + BLOCK]
    columns = lines.T

    at = slice(start, start + BLOCK)
    cosine, sine = angles(coarse, fine, start, BLOCK)
    own, far = x_own[at, :], x_other[at, :]
    queries = mm(own, wq[...]) + mm(far, wq_far[...])
    q_out[...] = turned(queries, cosine, sine)
    gates = mm(own, wg[...]) + mm(far, wg_far[...])
    gates = gates.astype(BF16).astype(F32)
    g_out[...] = gates / (1.0 + jnp.exp(-gates))
    for piece in range(BLOCK // TILE):
        low, last = piece * TILE, (piece + 1) * TILE
        place_t = lax.broadcasted_iota(jnp.int32, (TILE, last), 0) + low
        place_s = lax.broadcasted_iota(jnp.int32, (TILE, last), 1)
        causal = place_t >= place_s
        for head in range(heads):
            span = slice(head * DH, (head + 1) * DH)
            scores = mm_nt(q_out[low:last, span], k[start : start + last, span])
            differ = columns[low:last, head : head + 1] - lines[head : head + 1, :last]
            weights = jnp.where(causal, jnp.exp(jnp.where(causal, differ, 0.0)), 0.0)
            intra_out[low:last, span] = mm((scores * weights).astype(BF16), v[start : start + last, span])


def hidden_kernel(heads, hop, sets, role, first, decay, before, entering, *refs):
    arrivals, projected, out, token = refs[: len(sets)], refs[len(sets) : -2], refs[-2], refs[-1]
    token[...] = jnp.zeros_like(token)

    def piece(start):
        block = start // BLOCK
        q, gate, intra = projected[3 * block : 3 * block + 3]
        at = slice(start % BLOCK, start % BLOCK + TILE)
        columns = jnp.exp(decay[:, start : start + TILE].T)
        scales = jnp.exp(block_ends(decay, 0, block * BLOCK))
        for head in range(heads):
            span, row = slice(head * DH, (head + 1) * DH), slice(head, head + 1)
            fade = jnp.exp(entering[heads * DH + head : heads * DH + head + 1, :1])
            state = entering[span, :] + fade * arrived_state(arrivals, sets, hop, span)
            prior = (scales[row] * state + before[block, span, :].astype(F32)).astype(BF16)
            retained = intra[at, span] + columns[:, row] * mm(q[at, span], prior)
            center = retained - jnp.mean(retained, axis=1, keepdims=True)
            spread = jnp.mean(center * center, axis=1, keepdims=True)
            out[:, span] = (gate[at, span] * center * lax.rsqrt(spread + 1e-5)).astype(BF16)

    core, middle = lax.axis_index("fsdp"), decay.shape[1] // 2
    pl.when(core == role)(lambda: piece(first))
    pl.when(core != role)(lambda: piece(middle + first))


def columns_kernel(first, second, *outs):
    cols = outs[0].shape[1]
    place, core = lax.axis_index("tp"), lax.axis_index("fsdp")
    high, low = place // 2, place % 2

    @pl.when(core == 0)
    def _():
        at = pl.ds(pl.multiple_of((1 - low) * cols, cols), cols)
        outs[0][...] = first[:, at]
        outs[1][...] = second[:, at]

    @pl.when(core == 1)
    def _():
        for number, out in enumerate(outs):
            at = slice(number * cols, (number + 1) * cols)
            out[...] = jnp.where(high == 0, first[:, at], second[:, at])


def arrange_kernel(mine_0, mine_1, other_0, other_1, *outs):
    cols = mine_0.shape[1]
    place, core = lax.axis_index("tp"), lax.axis_index("fsdp")
    for role, (blocks, out) in enumerate(zip(((mine_0, mine_1), (other_0, other_1)), outs)):
        bit = jnp.where(core == role, place // 2, place % 2)
        out[:, :cols] = jnp.where(bit == 0, blocks[1][...], blocks[0][...])
        out[:, cols:] = jnp.where(bit == 0, blocks[0][...], blocks[1][...])


def own_kernel(order, own_first, own_second, *refs):
    pieces, outs = refs[: len(order)], refs[len(order) :]
    cols = pieces[0].shape[1]
    place, core = lax.axis_index("tp"), lax.axis_index("fsdp")
    high, low = place // 2, place % 2
    here = core == high
    mine = pl.ds(pl.multiple_of(low * cols, cols), cols)
    flipped = pl.ds(pl.multiple_of((1 - low) * cols, cols), cols)
    keep = jnp.where(here, own_first[:, mine], own_second[:, mine])
    low_give = jnp.where(here, own_second[:, mine], own_first[:, mine])
    high_give = jnp.where(here, own_first[:, flipped], own_second[:, flipped])
    gives = [jnp.where(core == role, low_give, high_give) for role in range(2)]
    for (role, number), piece in zip(order, pieces):
        at = slice(number * TILE, (number + 1) * TILE)
        outs[role][at, :cols] = mm(piece[...], gives[role])
        outs[role][at, cols:] = mm(piece[...], keep)


def give_kernel(number, own, far, weight, out):
    cols = out.shape[1]
    at = slice(number * TILE, (number + 1) * TILE)
    out[...] = (own[at, :cols] + mm(far[...], weight[:, :cols])).astype(BF16)


def keep_kernel(order, *refs):
    count = len(order)
    fars, owns, weights, outs = refs[:count], refs[count : count + 2], refs[count + 2 : count + 4], refs[count + 4 :]
    for (role, number), far in zip(order, fars):
        cols = far.shape[1]
        at = slice(number * TILE, (number + 1) * TILE)
        outs[role][at, :] = owns[role][at, cols:] + mm(far[...], weights[role][:, cols:])


def finish_kernel(order, *refs):
    count = len(order)
    gots, keeps, out, ready, written = refs[:count], refs[count : count + 2], refs[-3], refs[-2], refs[-1]
    core, copies = lax.axis_index("fsdp"), []
    for slot, ((role, number), got) in enumerate(zip(order, gots)):
        keep = keeps[role]
        at = slice(number * TILE, (number + 1) * TILE)
        ready[slot] = (keep[at, :] + got[...].astype(F32)).astype(BF16)
        start = pl.multiple_of((role + core) % 2 * keep.shape[0] + number * TILE, TILE)
        copies.append(pltpu.make_async_copy(ready.at[slot], out.at[0, pl.ds(start, TILE)], written.at[slot]))
        copies[-1].start()
    for copy in copies:
        copy.wait()


def after(value, *others):
    return lax.optimization_barrier((value, *others))[0]


def on_device(tokens, query_weight, key_weight, value_weight, gate_weight, out_weight, log_decay):
    x = tokens[0]
    rows, width = x.shape
    part, cols = query_weight.shape
    heads = cols // DH
    blocks = rows // BLOCK
    ctx, tp, cores = lax.axis_size("ctx"), lax.axis_size("tp"), lax.axis_size("fsdp")
    assert tp == 4 and cores == 2 and ctx >= 4 and ctx & (ctx - 1) == 0
    partners = [
        [(at * cores + core, (at ^ (1 << (role + core) % 2)) * cores + core) for at in range(tp) for core in range(cores)]
        for role in range(2)
    ]

    def trade(value, role):
        return lax.ppermute(value, ("tp", "fsdp"), partners[role])

    tables = [((2, rows // FINE, DH // 2), F32), ((2, FINE, DH // 2), F32)]

    key_far = swap(key_weight, "fsdp", 1)
    value_far = swap(value_weight, "fsdp", 1)

    x_own, x_other, acc_k, acc_v, decay, coarse, fine, out_first = loading_call(
        key_value_own_kernel,
        [((rows, part), BF16)] * 2 + [((rows, cols), F32)] * 2 + [((8, rows), F32)]
        + tables
        + [(out_weight.shape, BF16)],
        [x, key_weight, value_weight, log_decay[0].T, out_weight],
        [],
        [pltpu.VMEM((part, cols), BF16)] * 2 + [pltpu.VMEM((heads, rows), F32)],
        2 * (rows // BLOCK) + 4,
        "key_value_own",
    )
    state_shape, message_shape = (heads * DH, DH), (heads * DH + EXTRA, DH)
    own_q, own_g, keys, values, before, window, message = loading_call(
        functools.partial(key_value_kernel, heads),
        [((part, cols), BF16)] * 2
        + [((rows, cols), BF16)] * 2
        + [((blocks, heads * DH, DH), BF16), (state_shape, F32), (message_shape, BF16)],
        [query_weight, gate_weight],
        [x_other, key_far, value_far, acc_k, acc_v, decay, coarse, fine],
        [],
        2,
        "key_value",
    )
    far_q, far_g = swap(own_q, "fsdp", 1), swap(own_g, "fsdp", 1)

    def query_gate(block, decay):
        return kernel_call(
            functools.partial(query_gate_kernel, heads, block),
            [((BLOCK, cols), BF16), ((BLOCK, cols), F32), ((BLOCK, cols), F32)],
            [x_own, x_other, own_q, far_q, own_g, far_g, decay, coarse, fine, keys, values],
            "query_gate",
        )

    def exchange(message, lowers, hop, two_way=True):
        pairs = [(at, at + hop) for at in lowers]
        if two_way:
            pairs += [(upper, at) for at, upper in pairs] if hop > 1 else [(ctx - 1, 0)]
        return lax.ppermute(message, "ctx", pairs)

    projected = list(query_gate(0, decay))
    window = after(window, projected[0])
    entering, hop, early, first_message = None, 1, [], message
    while True:
        first_set, *later_sets = exchanges(ctx, hop)
        later_sets = [lowers for lowers in later_sets if lowers]
        sets = later_sets + ([first_set] if first_set else [])
        late = after(message, *early) if early else message
        arrivals = [exchange(late, lowers, hop) for lowers in later_sets] + early
        if 2 * hop >= ctx:
            break
        unchanged = exchanges(ctx, 2 * hop)[0]
        early = [exchange(message, unchanged, 2 * hop, two_way=False)]
        old = [] if entering is None else [entering]
        last = 4 * hop >= ctx
        entering, message, *windows = kernel_call(
            functools.partial(combine_kernel, heads, hop, sets, entering is None, last),
            [((heads * DH + 8, DH), F32)]
            + ([(state_shape, BF16)] if last else [(message_shape, BF16), (state_shape, F32)]),
            [window, message, *old, *arrivals],
            "combine",
        )
        window = windows[0] if windows else None
        hop *= 2

    own_second = swap(out_first, "fsdp", 1)
    for_partner = kernel_call(
        columns_kernel,
        [((cols, cols), BF16)] * 2,
        [after(out_first, first_message), own_second],
        "columns",
    )
    out_mine = [trade(block, 0) for block in for_partner]

    held = after(decay, message, *early)
    for block in range(1, blocks):
        projected += query_gate(block, held)

    count = rows // 2 // TILE
    hidden, far = [[], []], [[], []]
    token = None
    for number, role in [(number, role) for number in range(count) for role in range(2)]:
        held = decay if token is None else after(decay, swap(token, "fsdp", 1))
        piece, token = kernel_call(
            functools.partial(hidden_kernel, heads, hop, sets, role, number * TILE),
            [((TILE, cols), BF16), ((16, 128), BF16)],
            [held, before, entering, *arrivals, *projected],
            "hidden",
        )
        if number == 0 and role == 0:
            out_other = [swap(after(block, piece), "fsdp", 1) for block in out_mine]
        hidden[role].append(piece)
        far[role].append(trade(piece, role))
    weights = kernel_call(
        arrange_kernel,
        [((cols, 2 * cols), BF16)] * 2,
        [*out_mine, *out_other],
        "arrange",
    )
    order = [(role, number) for number in reversed(range(count)) for role in (1, 0)]
    owns = kernel_call(
        functools.partial(own_kernel, order),
        [((count * TILE, 2 * cols), F32)] * 2,
        [out_first, own_second, *(hidden[role][number] for role, number in order)],
        "own_products",
    )
    gots = []
    for role, number in order:
        [give] = kernel_call(
            functools.partial(give_kernel, number),
            [((TILE, cols), BF16)],
            [owns[role], far[role][number], weights[role]],
            "give",
        )
        gots.append(trade(give, 1 - role))
    keeps = kernel_call(
        functools.partial(keep_kernel, order),
        [((count * TILE, cols), F32)] * 2,
        [*(far[role][number] for role, number in order), *owns, *weights],
        "keep",
    )
    result = None
    for part_order, part_gots in ((order[2:], gots[2:]), (order[:2], gots[:2])):
        arrays = [pltpu.with_memory_space_constraint(array, pltpu.VMEM) for array in (*part_gots, *keeps)]
        held = [] if result is None else [result]
        result = pl.pallas_call(
            functools.partial(finish_kernel, part_order),
            in_specs=[pl.BlockSpec(memory_space=pltpu.VMEM)] * len(arrays)
            + [pl.BlockSpec(memory_space=pltpu.HBM)] * len(held),
            out_specs=pl.BlockSpec(memory_space=pltpu.HBM),
            out_shape=jax.ShapeDtypeStruct((1, rows, cols), BF16),
            input_output_aliases={len(arrays): 0} if held else {},
            scratch_shapes=[
                pltpu.VMEM((len(part_order), TILE, cols), BF16),
                pltpu.SemaphoreType.DMA((len(part_order),)),
            ],
            compiler_params=pltpu.CompilerParams(vmem_limit_bytes=VMEM_LIMIT),
            name="finish",
        )(*arrays, *held)
    return result


def solution(mesh):
    in_specs = (
        P("fsdp", "ctx", None),
        P("fsdp", "tp"),
        P("fsdp", "tp"),
        P("fsdp", "tp"),
        P("fsdp", "tp"),
        P("tp", "fsdp"),
        P("fsdp", "ctx", "tp"),
    )
    out_specs = P("fsdp", "ctx", "tp")
    return jax.shard_map(
        on_device, mesh=mesh, in_specs=in_specs, out_specs=out_specs, check_vma=False
    )
```
